32 devices in a mesh: segment: 4 (over y, x), dp: 8 (over z, core).
Axes of the slice: x: 2, y: 2, z: 4, core: 2. Of those that a mesh axis runs over, the one named last changes fastest.
Arguments:
- patches: bfloat16 [6272, 768], P('dp'), may hold values from -6 to 6
- region_mask: int32 [6272], P('dp'), may hold values 0 or 1
- conv_weight: bfloat16 [2, 9, 768], P(None, None, 'dp'), may hold values from -2 to 2
- conv_bias: bfloat16 [2, 768], P(None, 'dp'), may hold values from -1.75 to 1.75
- mixer_gain: bfloat16 [2, 768], P(None, 'dp'), may hold values from 0.099609375 to 1.8984375
- mixer_shift: bfloat16 [2, 768], P(None, 'dp'), may hold values from -1.75 to 1.75
- triple_weight: bfloat16 [2, 768, 2304], P(None, 'dp'), may hold values from -0.21875 to 0.21875
- triple_bias: bfloat16 [2, 2304], P(None, 'dp'), may hold values from -1.75 to 1.75
- output_weight: bfloat16 [2, 768, 768], P(None, 'dp'), may hold values from -0.625 to 0.625
- output_bias: bfloat16 [2, 768], P(None, 'dp'), may hold values from -1.75 to 1.75
- feed_gain: bfloat16 [2, 768], P(None, 'dp'), may hold values from 0.099609375 to 1.8984375
- feed_shift: bfloat16 [2, 768], P(None, 'dp'), may hold values from -1.75 to 1.75
- expand_weight: bfloat16 [2, 768, 3072], P(None, 'dp'), may hold values from -0.21875 to 0.21875
- expand_bias: bfloat16 [2, 3072], P(None, 'dp'), may hold values from -3 to 3
- reduce_weight: bfloat16 [2, 3072, 768], P(None, 'dp'), may hold values from -0.109375 to 0.109375
- reduce_bias: bfloat16 [2, 768], P(None, 'dp'), may hold values from -1.75 to 1.75
- cotangent: bfloat16 [6272, 768], P('dp'), may hold values from -6 to 6
Outputs:
- section_outputs: bfloat16 [4, 6272, 768], P('segment', 'dp')
- section_grads: bfloat16 [4, 6272, 768], P('segment', 'dp')
- grad_conv_weight: float32 [2, 9, 768], P(None, None, 'dp')
- grad_conv_bias: float32 [2, 768], P(None, 'dp')
- grad_mixer_gain: float32 [2, 768], P(None, 'dp')
- grad_mixer_shift: float32 [2, 768], P(None, 'dp')
- grad_triple_weight: float32 [2, 768, 2304], P(None, 'dp')
- grad_triple_bias: float32 [2, 2304], P(None, 'dp')
- grad_output_weight: float32 [2, 768, 768], P(None, 'dp')
- grad_output_bias: float32 [2, 768], P(None, 'dp')
- grad_feed_gain: float32 [2, 768], P(None, 'dp')
- grad_feed_shift: float32 [2, 768], P(None, 'dp')
- grad_expand_weight: float32 [2, 768, 3072], P(None, 'dp')
- grad_expand_bias: float32 [2, 3072], P(None, 'dp')
- grad_reduce_weight: float32 [2, 3072, 768], P(None, 'dp')
- grad_reduce_bias: float32 [2, 768], P(None, 'dp')
The draws below stay inside these ranges and needn't reach their ends.
All inputs are finite; a program needn't handle non-finite values. No bound on the sum of `region_mask` on one device may be relied on, other than what follows from the above.
Results may differ from the reference program's by a relative error of at most 0.025.
Values may be sent and summed in bfloat16 or wider, within the bound.
A program may use at most 704 MiB of HBM per device.

```python
import jax
import jax.numpy as jnp
from jax import lax

D = 768
FF = 3072
HEADS = 24
GROUPS = 24
HD = 32
SIDE = 7
MICRO = 4
IMG_MB = 4
TOKENS = 6272


def place_ends(entries, rng, smallest, high):
    index_at = [jax.random.randint(jax.random.fold_in(rng, axis), (), 0, length) for axis, length in enumerate(entries.shape)]
    widest = entries.shape.index(max(entries.shape))
    beside = index_at[:widest] + [(index_at[widest] + 1) % entries.shape[widest]] + index_at[widest + 1:]
    return entries.at[tuple(index_at)].set(smallest).at[tuple(beside)].set(high)


def block_scale(rng, extent, cuts, smallest, top_value):
    factor_of, own = 1.0, jax.random.fold_in(rng, 6)
    for position, parts in cuts:
        draws = jnp.exp(jax.random.uniform(jax.random.fold_in(own, position), (parts,), jnp.float32, smallest / len(cuts), top_value / len(cuts)))
        factor_of = factor_of * jnp.repeat(draws, extent[position] // parts).reshape([-1 if axis == position else 1 for axis in range(len(extent))])
    return factor_of


def scatter_about(rng, extent, scale, limit, cuts=(), held_as=jnp.bfloat16):
    entries = scale * jax.random.normal(rng, extent, jnp.float32)
    if cuts:
        entries = entries * block_scale(rng, extent, cuts, -0.22, 0.18)
    return jnp.clip(entries, -limit, limit).astype(held_as)


def setup_inputs(seed: int = 0) -> dict:
    splits = jax.random.split(jax.random.key(seed), 18)
    return {
        "patches": scatter_about(splits[0], (TOKENS, D), 1.0, 6.0, ((0, 8),)),
        "region_mask": place_ends((jax.random.randint(splits[1], (TOKENS,), 0, 4) < 3).astype(jnp.int32), jax.random.fold_in(splits[1], 1), 0, 1),
        "conv_weight": scatter_about(splits[2], (2, 9, D), 9 ** -0.5, 2.0, ((2, 8),)),
        "conv_bias": scatter_about(splits[3], (2, D), 0.3, 1.75, ((1, 8),)),
        "mixer_gain": jnp.clip(1.0 + 0.18 * jax.random.normal(splits[4], (2, D), jnp.float32), 0.099609375, 1.8984375).astype(jnp.bfloat16),
        "mixer_shift": scatter_about(splits[5], (2, D), 0.3, 1.75, ((1, 8),)),
        "triple_weight": scatter_about(splits[6], (2, D, 3 * D), D ** -0.5, 0.21875, ((1, 8),)),
        "triple_bias": scatter_about(splits[7], (2, 3 * D), 0.3, 1.75, ((1, 8),)),
        "output_weight": scatter_about(splits[8], (2, D, D), (D // 8) ** -0.5, 0.625, ((1, 8),)),
        "output_bias": scatter_about(splits[9], (2, D), 0.3, 1.75, ((1, 8),)),
        "feed_gain": jnp.clip(1.0 + 0.18 * jax.random.normal(splits[10], (2, D), jnp.float32), 0.099609375, 1.8984375).astype(jnp.bfloat16),
        "feed_shift": scatter_about(splits[11], (2, D), 0.3, 1.75, ((1, 8),)),
        "expand_weight": scatter_about(splits[12], (2, D, FF), D ** -0.5, 0.21875, ((1, 8),)),
        "expand_bias": scatter_about(splits[13], (2, FF), 0.5, 3.0, ((1, 8),)),
        "reduce_weight": scatter_about(splits[14], (2, FF, D), FF ** -0.5, 0.109375, ((1, 8),)),
        "reduce_bias": scatter_about(splits[15], (2, D), 0.3, 1.75, ((1, 8),)),
        "cotangent": scatter_about(splits[16], (TOKENS, D), 1.0, 6.0, ((0, 8),)),
    }


@jax.custom_vjp
def low(v):
    return lax.optimization_barrier(v.astype(jnp.bfloat16)).astype(jnp.float32)

@jax.custom_vjp
def low_back(v):
    return v

def low_keep(v):
    return (low(v), None)

def low_pass(kept, grad):
    return (grad,)

def back_keep(v):
    return (v, None)

def back_low(kept, grad):
    return (low(grad),)
low.defvjp(low_keep, low_pass)
low_back.defvjp(back_keep, back_low)
EPSILON = 1e-05

def matmul_high(first_operand, second_operand):
    return jnp.dot(first_operand, second_operand, precision=lax.Precision.HIGHEST)

def layer_norm(values, norm_gain, norm_shift):
    center = values - lax.optimization_barrier(jnp.mean(values, axis=-1, keepdims=True))
    spread = lax.optimization_barrier(jnp.mean(center * center, axis=-1, keepdims=True))
    return center * lax.rsqrt(spread + EPSILON) * norm_gain + norm_shift

def position_conv(stream, conv_weight, conv_bias):
    features = stream.shape[-1]
    planes = stream.reshape(-1, SIDE, SIDE, features)
    padded = jnp.pad(planes, ((0, 0), (1, 1), (1, 1), (0, 0)))
    summed = jnp.zeros_like(planes) + conv_bias
    for tap_row in range(3):
        for tap_col in range(3):
            summed = summed + padded[:, tap_row:tap_row + SIDE, tap_col:tap_col + SIDE, :] * conv_weight[tap_row * 3 + tap_col]
    return stream + summed.reshape(stream.shape)

def window_core(triple, keep_mask):
    tokens = triple.shape[0]
    features = triple.shape[1] // 3
    pieces = triple.reshape(tokens // (SIDE * SIDE), SIDE * SIDE, 3, HEADS, HD)
    queries = pieces[:, :, 0]
    key_parts = pieces[:, :, 1]
    value_parts = pieces[:, :, 2]
    scores = low_back(jnp.einsum('iqhd,ikhd->ihqk', queries, key_parts, precision=lax.Precision.HIGHEST) * HD ** (-0.5))
    softmaxed = low(jax.nn.softmax(scores, axis=-1))
    mixture = jnp.einsum('ihqk,ikhd->iqhd', softmaxed, value_parts, precision=lax.Precision.HIGHEST)
    return mixture.reshape(tokens, features)

def channel_core(triple, keep_mask):
    tokens = triple.shape[0]
    features = triple.shape[1] // 3
    images = tokens // (SIDE * SIDE)
    pieces = triple.reshape(images, SIDE * SIDE, 3, GROUPS, HD)
    queries = pieces[:, :, 0]
    masked = pieces[:, :, 1] * keep_mask.reshape(images, SIDE * SIDE, 1, 1)
    value_parts = pieces[:, :, 2]
    scores = low_back(jnp.einsum('itgc,itge->igce', queries, masked, precision=lax.Precision.HIGHEST) * HD ** (-0.5))
    softmaxed = low(jax.nn.softmax(scores, axis=-1))
    mixture = jnp.einsum('igce,itge->itgc', softmaxed, value_parts, precision=lax.Precision.HIGHEST)
    return mixture.reshape(tokens, features)

def mixer_section(stream, layer_params, keep_mask, channel):
    conv_weight, conv_bias, norm_gain, norm_shift, triple_weight, triple_bias, output_weight, output_bias = layer_params[:8]
    shifted = position_conv(stream, conv_weight, conv_bias)
    normed = low(layer_norm(shifted, norm_gain, norm_shift))
    triple = low_back(low(matmul_high(normed, triple_weight) + triple_bias))
    if channel:
        mixture = channel_core(triple, keep_mask)
    else:
        mixture = window_core(triple, keep_mask)
    mixture = low_back(low(mixture))
    return low(shifted + matmul_high(mixture, output_weight) + output_bias)

def feed_section(stream, layer_params):
    norm_gain, norm_shift, expand_weight, expand_bias, reduce_weight, reduce_bias = layer_params[8:]
    normed = low(layer_norm(stream, norm_gain, norm_shift))
    hidden = low_back(matmul_high(normed, expand_weight) + expand_bias)
    active = low(jax.nn.gelu(hidden, approximate=False))
    return low(stream + matmul_high(active, reduce_weight) + reduce_bias)

def forward(params, probes, patches, keep_mask):
    stream = patches
    leaving_list = []
    for section in range(4):
        layer_params = tuple((member[section // 2] for member in params))
        stream = low_back(stream + probes[section])
        if section % 2 == 1:
            stream = feed_section(stream, layer_params)
        else:
            stream = mixer_section(stream, layer_params, keep_mask, section == 2)
        leaving_list.append(stream)
    return jnp.stack(leaving_list)

def block_grads(params, patches, keep_mask, cotangent):
    probes = jnp.zeros((4,) + patches.shape, jnp.float32)

    def closed(param_set, probe_set):
        return forward(param_set, probe_set, patches, keep_mask)
    leaving, pullback = jax.vjp(closed, params, probes)
    out_seeds = jnp.zeros_like(leaving).at[3].set(cotangent)
    grad_params, grad_probes = pullback(out_seeds)
    return (leaving, grad_probes, grad_params)

def reference(patches, region_mask, conv_weight, conv_bias, mixer_gain, mixer_shift, triple_weight, triple_bias, output_weight, output_bias, feed_gain, feed_shift, expand_weight, expand_bias, reduce_weight, reduce_bias, cotangent):
    params = tuple((member.astype(jnp.float32) for member in (conv_weight, conv_bias, mixer_gain, mixer_shift, triple_weight, triple_bias, output_weight, output_bias, feed_gain, feed_shift, expand_weight, expand_bias, reduce_weight, reduce_bias)))
    block_rows = MICRO * IMG_MB * SIDE * SIDE
    blocks = TOKENS // block_rows
    features = patches.shape[1]
    patch_blocks = patches.astype(jnp.float32).reshape(blocks, block_rows, features)
    mask_blocks = region_mask.astype(jnp.float32).reshape(blocks, block_rows)
    seed_blocks = cotangent.astype(jnp.float32).reshape(blocks, block_rows, features)

    def scan_step(running, inputs):
        leaving, grad_probes, grad_params = block_grads(params, inputs[0], inputs[1], inputs[2])
        updated = tuple((first_term + second_term for first_term, second_term in zip(running, grad_params)))
        return (updated, (leaving, grad_probes))
    initial = tuple((jnp.zeros_like(member) for member in params))
    totals, stacked = lax.scan(scan_step, initial, (patch_blocks, mask_blocks, seed_blocks))
    section_outputs = stacked[0].transpose(1, 0, 2, 3).reshape(4, TOKENS, features).astype(jnp.bfloat16)
    section_grads = stacked[1].transpose(1, 0, 2, 3).reshape(4, TOKENS, features).astype(jnp.bfloat16)
    return (section_outputs, section_grads, totals[0], totals[1], totals[2], totals[3], totals[4], totals[5], totals[6], totals[7], totals[8], totals[9], totals[10], totals[11], totals[12], totals[13])
```

```python
from functools import partial

import jax
import jax.numpy as jnp
from jax import lax
from jax.experimental import pallas as pl
from jax.experimental.pallas import tpu as pltpu
from jax.sharding import PartitionSpec as P

HD = 32
SIDE = 7
MICRO = 4
IMG_MB = 4


EPSILON = 1e-05


def as_sent(x):

    def short(part):
        return part.astype(jnp.bfloat16) if part.dtype == jnp.float32 else part

    return jax.tree.map(short, x)


def shifted_2(x, axis, by):
    count = lax.axis_size(axis)
    pairs = [(i, i + by) for i in range(count) if 0 <= i + by < count]
    return lax.ppermute(x, axis, pairs)


def dot_last(first_operand, second_operand):
    return lax.dot_general(
        first_operand, second_operand, (((1,), (1,)), ((), ())), preferred_element_type=jnp.float32
    )


def dot_first(first_operand, second_operand):
    return lax.dot_general(
        first_operand, second_operand, (((0,), (0,)), ((), ())), preferred_element_type=jnp.float32
    )


def layer_norm(values, norm_gain, norm_shift):
    center = values - jnp.mean(values, axis=-1, keepdims=True)
    spread = jnp.mean(center * center, axis=-1, keepdims=True)
    return center * lax.rsqrt(spread + EPSILON) * norm_gain + norm_shift


def position_conv(stream, conv_weight, conv_bias):
    features = stream.shape[-1]
    planes = stream.reshape(-1, SIDE, SIDE, features)
    padded = jnp.pad(planes, ((0, 0), (1, 1), (1, 1), (0, 0)))
    summed = jnp.zeros_like(planes) + conv_bias
    for tap_row in range(3):
        for tap_col in range(3):
            summed = (
                summed
                + padded[:, tap_row : tap_row + SIDE, tap_col : tap_col + SIDE, :]
                * conv_weight[tap_row * 3 + tap_col]
            )
    return stream + summed.reshape(stream.shape)


def front_part(stream, conv_weight, conv_bias, norm_gain, norm_shift):
    shifted = position_conv(stream, conv_weight, conv_bias)
    return (shifted, layer_norm(shifted, norm_gain, norm_shift))


def gelu_exact(values):
    return jax.nn.gelu(values, approximate=False)


def softmax_rows(scores):
    row_max = jnp.max(scores, axis=-1, keepdims=True)
    lifted = jnp.exp(scores - row_max)
    return lifted / jnp.sum(lifted, axis=-1, keepdims=True)


def window_forward(triple):
    tokens = triple.shape[0]
    features = triple.shape[1] // 3
    pieces = triple.reshape(tokens // (SIDE * SIDE), SIDE * SIDE, 3, features // HD, HD)
    queries = pieces[:, :, 0]
    key_parts = pieces[:, :, 1]
    value_parts = pieces[:, :, 2]
    scores = jnp.einsum(
        "iqhd,ikhd->ihqk", queries, key_parts, preferred_element_type=jnp.float32
    ) * HD ** (-0.5)
    softmaxed = softmax_rows(scores)
    softmaxed_low = softmaxed.astype(jnp.bfloat16)
    mixture = jnp.einsum(
        "ihqk,ikhd->iqhd", softmaxed_low, value_parts, preferred_element_type=jnp.float32
    )
    return (
        mixture.reshape(tokens, features),
        (queries, key_parts, value_parts, softmaxed, softmaxed_low),
    )


def window_backward(stored, grad_mixture):
    queries, key_parts, value_parts, softmaxed, softmaxed_low = stored
    grad_pieces = grad_mixture.reshape(queries.shape)
    grad_values = jnp.einsum(
        "ihqk,iqhd->ikhd", softmaxed_low, grad_pieces, preferred_element_type=jnp.float32
    )
    grad_soft = jnp.einsum(
        "iqhd,ikhd->ihqk", grad_pieces, value_parts, preferred_element_type=jnp.float32
    )
    grad_scores = (
        softmaxed * (grad_soft - jnp.sum(grad_soft * softmaxed, axis=-1, keepdims=True))
    ).astype(jnp.bfloat16)
    grad_queries = jnp.einsum(
        "ihqk,ikhd->iqhd", grad_scores, key_parts, preferred_element_type=jnp.float32
    ) * HD ** (-0.5)
    grad_keys = jnp.einsum(
        "ihqk,iqhd->ikhd", grad_scores, queries, preferred_element_type=jnp.float32
    ) * HD ** (-0.5)
    joined = jnp.stack([grad_queries, grad_keys, grad_values], axis=2)
    return joined.reshape(grad_mixture.shape[0], 3 * grad_mixture.shape[1])


def channel_forward(triple, mask_rows):
    tokens = triple.shape[0]
    features = triple.shape[1] // 3
    images = tokens // (SIDE * SIDE)
    pieces = triple.reshape(images, SIDE * SIDE, 3, features // HD, HD)
    queries = pieces[:, :, 0]
    keep_mask = mask_rows.reshape(images, SIDE * SIDE, 1, 1).astype(jnp.bfloat16)
    masked = pieces[:, :, 1] * keep_mask
    value_parts = pieces[:, :, 2]
    scores = jnp.einsum(
        "itgc,itge->igce", queries, masked, preferred_element_type=jnp.float32
    ) * HD ** (-0.5)
    softmaxed = softmax_rows(scores)
    softmaxed_low = softmaxed.astype(jnp.bfloat16)
    mixture = jnp.einsum(
        "igce,itge->itgc", softmaxed_low, value_parts, preferred_element_type=jnp.float32
    )
    return (
        mixture.reshape(tokens, features),
        (queries, masked, value_parts, keep_mask, softmaxed, softmaxed_low),
    )


def channel_backward(stored, grad_mixture):
    queries, masked, value_parts, keep_mask, softmaxed, softmaxed_low = stored
    grad_pieces = grad_mixture.reshape(queries.shape)
    grad_soft = jnp.einsum(
        "itgc,itge->igce", grad_pieces, value_parts, preferred_element_type=jnp.float32
    )
    grad_values = jnp.einsum(
        "igce,itgc->itge", softmaxed_low, grad_pieces, preferred_element_type=jnp.float32
    )
    grad_scores = (
        softmaxed * (grad_soft - jnp.sum(grad_soft * softmaxed, axis=-1, keepdims=True))
    ).astype(jnp.bfloat16)
    grad_queries = jnp.einsum(
        "igce,itge->itgc", grad_scores, masked, preferred_element_type=jnp.float32
    ) * HD ** (-0.5)
    grad_masked = jnp.einsum(
        "igce,itgc->itge", grad_scores, queries, preferred_element_type=jnp.float32
    ) * HD ** (-0.5)
    grad_keys = grad_masked * keep_mask.astype(jnp.float32)
    joined = jnp.stack([grad_queries, grad_keys, grad_values], axis=2)
    return joined.reshape(grad_mixture.shape[0], 3 * grad_mixture.shape[1])


def mixer_inner(stream, weights, mask_rows, channel):
    (
        conv_weight,
        conv_bias,
        norm_gain,
        norm_shift,
        triple_weight,
        triple_bias,
        output_weight,
        output_bias,
    ) = weights[:8]
    widened = stream.astype(jnp.float32)
    (shifted, normed), front_pull = jax.vjp(
        front_part,
        widened,
        conv_weight.astype(jnp.float32),
        conv_bias.astype(jnp.float32),
        norm_gain.astype(jnp.float32),
        norm_shift.astype(jnp.float32),
    )
    normed_low = normed.astype(jnp.bfloat16)
    triple = (
        jnp.dot(normed_low, triple_weight, preferred_element_type=jnp.float32)
        + triple_bias.astype(jnp.float32)
    ).astype(jnp.bfloat16)
    if channel:
        mixture, stored = channel_forward(triple, mask_rows)
    else:
        mixture, stored = window_forward(triple)
    mixture_low = mixture.astype(jnp.bfloat16)
    return (shifted, front_pull, normed_low, stored, mixture_low)


def mixer_forward(stream, weights, mask_rows, channel):
    shifted, front_pull, normed_low, stored, mixture_low = mixer_inner(
        stream, weights, mask_rows, channel
    )
    result = (
        shifted
        + jnp.dot(mixture_low, weights[6], preferred_element_type=jnp.float32)
        + weights[7].astype(jnp.float32)
    )
    return result.astype(jnp.bfloat16)


def mixer_backward(stream, grad_out, weights, mask_rows, channel):
    shifted, front_pull, normed_low, stored, mixture_low = mixer_inner(
        stream, weights, mask_rows, channel
    )
    grad_wide = grad_out.astype(jnp.float32)
    grad_out_bias = jnp.sum(grad_wide, axis=0)
    grad_out_weight = dot_first(mixture_low, grad_out)
    grad_mixture = dot_last(grad_out, weights[6]).astype(jnp.bfloat16)
    if channel:
        grad_triple = channel_backward(stored, grad_mixture).astype(jnp.bfloat16)
    else:
        grad_triple = window_backward(stored, grad_mixture).astype(jnp.bfloat16)
    grad_tri_weight = dot_first(normed_low, grad_triple)
    grad_tri_bias = jnp.sum(grad_triple.astype(jnp.float32), axis=0)
    grad_normed = dot_last(grad_triple, weights[4])
    grad_stream, grad_taps, grad_tap_bias, grad_gain, grad_shift = front_pull(
        (grad_wide, grad_normed)
    )
    zero_tail = tuple((jnp.zeros(member.shape, jnp.float32) for member in weights[8:]))
    return (
        grad_stream.astype(jnp.bfloat16),
        (
            grad_taps,
            grad_tap_bias,
            grad_gain,
            grad_shift,
            grad_tri_weight,
            grad_tri_bias,
            grad_out_weight,
            grad_out_bias,
        )
        + zero_tail,
    )


def feed_inner(stream, weights):
    norm_gain, norm_shift, expand_weight, expand_bias, reduce_weight, reduce_bias = weights[8:]
    widened = stream.astype(jnp.float32)
    normed, norm_pull = jax.vjp(
        layer_norm, widened, norm_gain.astype(jnp.float32), norm_shift.astype(jnp.float32)
    )
    normed_low = normed.astype(jnp.bfloat16)
    hidden = jnp.dot(
        normed_low, expand_weight, preferred_element_type=jnp.float32
    ) + expand_bias.astype(jnp.float32)
    active, gelu_pull = jax.vjp(gelu_exact, hidden)
    return (widened, norm_pull, normed_low, gelu_pull, active.astype(jnp.bfloat16))


def feed_forward(stream, weights):
    widened, norm_pull, normed_low, gelu_pull, active_low = feed_inner(stream, weights)
    result = (
        widened
        + jnp.dot(active_low, weights[12], preferred_element_type=jnp.float32)
        + weights[13].astype(jnp.float32)
    )
    return result.astype(jnp.bfloat16)


def feed_backward(stream, grad_out, weights):
    widened, norm_pull, normed_low, gelu_pull, active_low = feed_inner(stream, weights)
    grad_wide = grad_out.astype(jnp.float32)
    grad_red_bias = jnp.sum(grad_wide, axis=0)
    grad_red_weight = dot_first(active_low, grad_out)
    grad_active = dot_last(grad_out, weights[12])
    grad_hidden = gelu_pull(grad_active)[0].astype(jnp.bfloat16)
    grad_exp_weight = dot_first(normed_low, grad_hidden)
    grad_exp_bias = jnp.sum(grad_hidden.astype(jnp.float32), axis=0)
    grad_normed = dot_last(grad_hidden, weights[10])
    grad_inner, grad_gain, grad_shift = norm_pull(grad_normed)
    zero_head = tuple((jnp.zeros(member.shape, jnp.float32) for member in weights[:8]))
    grad_stream = grad_wide + grad_inner
    return (
        grad_stream.astype(jnp.bfloat16),
        zero_head
        + (grad_gain, grad_shift, grad_exp_weight, grad_exp_bias, grad_red_weight, grad_red_bias),
    )


def section_forward(section, stream, weights, mask_rows):
    if section % 2 == 1:
        return feed_forward(stream, weights)
    return mixer_forward(stream, weights, mask_rows, section == 2)


def section_backward(section, stream, grad_out, weights, mask_rows):
    if section % 2 == 1:
        return feed_backward(stream, grad_out, weights)
    return mixer_backward(stream, grad_out, weights, mask_rows, section == 2)


def spare_forward(stream, weights, mask_rows):
    return jnp.zeros_like(stream)


def spare_backward(stream, grad_out, weights, mask_rows):
    return (
        jnp.zeros_like(stream),
        tuple((jnp.zeros(member.shape, jnp.float32) for member in weights)),
    )


def put_rows(buffer, rows, row_start, is_live):
    former = lax.dynamic_slice_in_dim(buffer, row_start, rows.shape[0], 0)
    return lax.dynamic_update_slice_in_dim(buffer, jnp.where(is_live, rows, former), row_start, 0)


def run_segments(layer_set, patches, region_mask, cotangent, segment_index, segments):
    features = patches.shape[1]
    micro_count = MICRO
    micro_rows = IMG_MB * SIDE * SIDE
    tick_count = micro_count + segments - 1
    forward_branches = [
        partial(section_forward, 0),
        partial(section_forward, 1),
        partial(section_forward, 2),
        partial(section_forward, 3),
        spare_forward,
    ]
    backward_branches = [
        partial(section_backward, 0),
        partial(section_backward, 1),
        partial(section_backward, 2),
        partial(section_backward, 3),
        spare_backward,
    ]
    received = jnp.zeros((micro_rows, features), jnp.bfloat16)
    kept_inputs = jnp.zeros((micro_count * micro_rows, features), jnp.bfloat16)
    outputs_here = jnp.zeros((micro_count * micro_rows, features), jnp.bfloat16)
    for tick_index in range(tick_count):
        micro_index = tick_index - segment_index
        is_live = (micro_index >= 0) & (micro_index < micro_count)
        row_start = jnp.clip(micro_index, 0, micro_count - 1) * micro_rows
        fresh_rows = lax.dynamic_slice_in_dim(patches, row_start, micro_rows, 0)
        mask_rows = lax.dynamic_slice_in_dim(region_mask, row_start, micro_rows, 0)
        entering = jnp.where(segment_index == 0, fresh_rows, received)
        leaving = lax.switch(
            jnp.where(is_live, segment_index, segments),
            forward_branches,
            entering,
            layer_set,
            mask_rows,
        )
        kept_inputs = put_rows(kept_inputs, entering, row_start, is_live)
        outputs_here = put_rows(outputs_here, leaving, row_start, is_live)
        if tick_index + 1 < tick_count:
            received = jax.tree.map(
                lambda part, own: part.astype(own.dtype),
                shifted_2(as_sent(leaving), "segment", 1),
                leaving,
            )
    grad_received = jnp.zeros((micro_rows, features), jnp.bfloat16)
    grads_here = jnp.zeros((micro_count * micro_rows, features), jnp.bfloat16)
    totals = tuple((jnp.zeros(member.shape, jnp.float32) for member in layer_set))
    for tick_index in range(tick_count):
        micro_index = tick_index - (segments - 1 - segment_index)
        is_live = (micro_index >= 0) & (micro_index < micro_count)
        row_start = jnp.clip(micro_index, 0, micro_count - 1) * micro_rows
        seed_rows = lax.dynamic_slice_in_dim(cotangent, row_start, micro_rows, 0)
        mask_rows = lax.dynamic_slice_in_dim(region_mask, row_start, micro_rows, 0)
        arriving = jnp.where(segment_index == segments - 1, seed_rows, grad_received)
        stream = lax.dynamic_slice_in_dim(kept_inputs, row_start, micro_rows, 0)
        grad_stream, grad_terms = lax.switch(
            jnp.where(is_live, segment_index, segments),
            backward_branches,
            stream,
            arriving,
            layer_set,
            mask_rows,
        )
        totals = tuple(
            (first_term + second_term for first_term, second_term in zip(totals, grad_terms))
        )
        grads_here = put_rows(grads_here, grad_stream, row_start, is_live)
        if tick_index + 1 < tick_count:
            grad_received = jax.tree.map(
                lambda part, own: part.astype(own.dtype),
                shifted_2(as_sent(grad_stream), "segment", -1),
                grad_stream,
            )
    return (outputs_here, grads_here, totals)


def body(
    patches,
    region_mask,
    conv_weight,
    conv_bias,
    mixer_gain,
    mixer_shift,
    triple_weight,
    triple_bias,
    output_weight,
    output_bias,
    feed_gain,
    feed_shift,
    expand_weight,
    expand_bias,
    reduce_weight,
    reduce_bias,
    cotangent,
):
    params = (
        conv_weight,
        conv_bias,
        mixer_gain,
        mixer_shift,
        triple_weight,
        triple_bias,
        output_weight,
        output_bias,
        feed_gain,
        feed_shift,
        expand_weight,
        expand_bias,
        reduce_weight,
        reduce_bias,
    )
    segments = lax.axis_size("segment")
    segment_index = lax.axis_index("segment")
    layer_index = segment_index // 2
    slices = tuple(
        (lax.dynamic_index_in_dim(member, layer_index, 0, keepdims=False) for member in params)
    )
    layer_set = (
        lax.all_gather(slices[0], "dp", axis=1, tiled=True),
        lax.all_gather(slices[1], "dp", axis=0, tiled=True),
        lax.all_gather(slices[2], "dp", axis=0, tiled=True),
        lax.all_gather(slices[3], "dp", axis=0, tiled=True),
        lax.all_gather(slices[4], "dp", axis=0, tiled=True),
        lax.all_gather(slices[5], "dp", axis=0, tiled=True),
        lax.all_gather(slices[6], "dp", axis=0, tiled=True),
        lax.all_gather(slices[7], "dp", axis=0, tiled=True),
        lax.all_gather(slices[8], "dp", axis=0, tiled=True),
        lax.all_gather(slices[9], "dp", axis=0, tiled=True),
        lax.all_gather(slices[10], "dp", axis=0, tiled=True),
        lax.all_gather(slices[11], "dp", axis=0, tiled=True),
        lax.all_gather(slices[12], "dp", axis=0, tiled=True),
        lax.all_gather(slices[13], "dp", axis=0, tiled=True),
    )
    outputs_here, grads_here, totals = run_segments(
        layer_set, patches, region_mask, cotangent, segment_index, segments
    )
    reduced = (
        lax.psum_scatter(totals[0], "dp", scatter_dimension=1, tiled=True),
        lax.psum_scatter(totals[1], "dp", scatter_dimension=0, tiled=True),
        lax.psum_scatter(totals[2], "dp", scatter_dimension=0, tiled=True),
        lax.psum_scatter(totals[3], "dp", scatter_dimension=0, tiled=True),
        lax.psum_scatter(totals[4], "dp", scatter_dimension=0, tiled=True),
        lax.psum_scatter(totals[5], "dp", scatter_dimension=0, tiled=True),
        lax.psum_scatter(totals[6], "dp", scatter_dimension=0, tiled=True),
        lax.psum_scatter(totals[7], "dp", scatter_dimension=0, tiled=True),
        lax.psum_scatter(totals[8], "dp", scatter_dimension=0, tiled=True),
        lax.psum_scatter(totals[9], "dp", scatter_dimension=0, tiled=True),
        lax.psum_scatter(totals[10], "dp", scatter_dimension=0, tiled=True),
        lax.psum_scatter(totals[11], "dp", scatter_dimension=0, tiled=True),
        lax.psum_scatter(totals[12], "dp", scatter_dimension=0, tiled=True),
        lax.psum_scatter(totals[13], "dp", scatter_dimension=0, tiled=True),
    )
    placed = tuple(
        (
            jnp.stack(
                [jnp.where(layer_index == 0, member, 0.0), jnp.where(layer_index == 1, member, 0.0)]
            )
            for member in reduced
        )
    )
    section_outputs = outputs_here[None]
    section_grads = grads_here[None]
    summed = (
        lax.psum(placed[0].astype(jnp.bfloat16), "segment").astype(jnp.float32),
        lax.psum(placed[1].astype(jnp.bfloat16), "segment").astype(jnp.float32),
        lax.psum(placed[2].astype(jnp.bfloat16), "segment").astype(jnp.float32),
        lax.psum(placed[3].astype(jnp.bfloat16), "segment").astype(jnp.float32),
        lax.psum(placed[4].astype(jnp.bfloat16), "segment").astype(jnp.float32),
        lax.psum(placed[5].astype(jnp.bfloat16), "segment").astype(jnp.float32),
        lax.psum(placed[6].astype(jnp.bfloat16), "segment").astype(jnp.float32),
        lax.psum(placed[7].astype(jnp.bfloat16), "segment").astype(jnp.float32),
        lax.psum(placed[8].astype(jnp.bfloat16), "segment").astype(jnp.float32),
        lax.psum(placed[9].astype(jnp.bfloat16), "segment").astype(jnp.float32),
        lax.psum(placed[10].astype(jnp.bfloat16), "segment").astype(jnp.float32),
        lax.psum(placed[11].astype(jnp.bfloat16), "segment").astype(jnp.float32),
        lax.psum(placed[12].astype(jnp.bfloat16), "segment").astype(jnp.float32),
        lax.psum(placed[13].astype(jnp.bfloat16), "segment").astype(jnp.float32),
    )
    return (
        section_outputs,
        section_grads,
        summed[0],
        summed[1],
        summed[2],
        summed[3],
        summed[4],
        summed[5],
        summed[6],
        summed[7],
        summed[8],
        summed[9],
        summed[10],
        summed[11],
        summed[12],
        summed[13],
    )


W = 768
IMG = 56
LIVE = 49
ROWS = 224
PAIR = 2 * IMG
LANES = 128
SCALE = HD ** (-0.5)
F32 = jnp.float32
BF16 = jnp.bfloat16
TAPS = [(a, b) for a in range(3) for b in range(3)]


def mm(a, b):
    return lax.dot_general(a, b, (((1,), (0,)), ((), ())), preferred_element_type=F32)


def mm_nt(a, b):
    return lax.dot_general(a, b, (((1,), (1,)), ((), ())), preferred_element_type=F32)


def mm_tn(a, b):
    return lax.dot_general(a, b, (((0,), (0,)), ((), ())), preferred_element_type=F32)


def row_index(rows):
    return lax.broadcasted_iota(jnp.int32, (rows, 1), 0)


def live_rows(rows):
    return lax.rem(row_index(rows), IMG) < LIVE


def column_masks(rows):
    place = lax.rem(row_index(rows), IMG)
    column = lax.rem(place, SIDE)
    live = place < LIVE
    return [(live & (column + b - 1 >= 0) & (column + b - 1 < SIDE)).astype(F32) for b in range(3)]


def rolled(values, by):
    by = by % values.shape[0]
    return values if by == 0 else pltpu.roll(values, by, 0)


def norm_parts(values):
    center = values - jnp.mean(values, axis=-1, keepdims=True)
    spread = jnp.mean(center * center, axis=-1, keepdims=True)
    rstd = lax.rsqrt(spread + EPSILON)
    return center * rstd, rstd


def column_sum(values):
    return jnp.sum(values, axis=0, keepdims=True)


def head_lanes(head):
    lane = lax.broadcasted_iota(jnp.int32, (1, LANES), 1)
    return (lane // HD) == head


def only(values, mask):
    return jnp.where(mask, values, jnp.zeros_like(values))


def mix_forward(layer, channel, u_in, u_out, w, small, mask, bias, c_ref, xhat, rstd, n_ref, t_ref, p_ref, m_ref):
    base = 12 * layer
    row = lambda r: small[layer, r:r + 1, :]
    v = u_in[...].astype(F32)
    masks = column_masks(ROWS)
    total = v + row(9)
    for b in range(3):
        part = jnp.zeros_like(v)
        for a in range(3):
            part = part + row(3 * a + b) * rolled(v, -(SIDE * (a - 1) + b - 1))
        total = total + part * masks[b]
    c = jnp.where(live_rows(ROWS), total, 0.0)
    c_ref[...] = c
    x, r = norm_parts(c)
    xhat[...] = x
    rstd[...] = r
    n_ref[...] = (x * row(10) + row(11)).astype(BF16)

    @pl.loop(0, 3)
    def _(j):
        cols = pl.ds(pl.multiple_of(W * j, W), W)
        t_ref[:, cols] = (mm(n_ref[...], w[base + j]) + small[layer, pl.ds(12 + j, 1), :]).astype(BF16)

    @pl.loop(0, 6)
    def _(g):
        qs = pl.ds(pl.multiple_of(LANES * g, LANES), LANES)
        ks = pl.ds(pl.multiple_of(W + LANES * g, LANES), LANES)
        vs = pl.ds(pl.multiple_of(2 * W + LANES * g, LANES), LANES)
        for pair in range(2):
            rows = slice(PAIR * pair, PAIR * pair + PAIR)
            q, k, val = t_ref[rows, qs], t_ref[rows, ks], t_ref[rows, vs]
            mix = jnp.zeros((PAIR, LANES), F32)
            if channel:
                for im in range(2):
                    here = (row_index(PAIR) // IMG) == im
                    km = k * only(mask[rows, :], here)
                    s = mm_tn(q, km) * SCALE + bias[...]
                    e = jnp.exp(s - jnp.max(s, axis=-1, keepdims=True))
                    p = e / jnp.sum(e, axis=-1, keepdims=True)
                    p_ref[g, 2 * pair + im] = p
                    mix = mix + mm_nt(only(val, here), p.astype(BF16))
            else:
                for head in range(4):
                    lanes = head_lanes(head)
                    s = mm_nt(only(q, lanes), k) * SCALE + bias[...]
                    e = jnp.exp(s - jnp.max(s, axis=-1, keepdims=True))
                    p = e / jnp.sum(e, axis=-1, keepdims=True)
                    p_ref[g, 4 * pair + head] = p
                    mix = mix + mm(p.astype(BF16), only(val, lanes))
            m_ref[rows, qs] = mix.astype(BF16)

    out = c_ref[...] + mm(m_ref[...], w[base + 3]) + row(15)
    u_out[...] = jnp.where(live_rows(ROWS), out, 0.0).astype(BF16)


def mix_backward(layer, channel, u_in, g_in, g_out, w, small, mask, sg, dw, c_ref, xhat, rstd, n_ref, t_ref, p_ref, m_ref, dm_ref, dt_ref, acc):
    base = 12 * layer
    row = lambda r: small[layer, r:r + 1, :]
    g = g_in[...]
    sg[layer, 15:16, :] = column_sum(g.astype(F32))
    dm_ref[...] = mm_nt(g, w[base + 3]).astype(BF16)
    dw(layer, 3, m_ref, lambda: g_in[...])

    @pl.loop(0, 6)
    def _(grp):
        qs = pl.ds(pl.multiple_of(LANES * grp, LANES), LANES)
        ks = pl.ds(pl.multiple_of(W + LANES * grp, LANES), LANES)
        vs = pl.ds(pl.multiple_of(2 * W + LANES * grp, LANES), LANES)
        for pair in range(2):
            rows = slice(PAIR * pair, PAIR * pair + PAIR)
            q, k, val, dm = t_ref[rows, qs], t_ref[rows, ks], t_ref[rows, vs], dm_ref[rows, qs]
            dq = jnp.zeros((PAIR, LANES), F32)
            dk = jnp.zeros((PAIR, LANES), F32)
            dv = jnp.zeros((PAIR, LANES), F32)
            if channel:
                for im in range(2):
                    here = (row_index(PAIR) // IMG) == im
                    keep = only(mask[rows, :], here)
                    km = k * keep
                    p = p_ref[grp, 2 * pair + im]
                    dmh = only(dm, here)
                    dp = mm_tn(dmh, val)
                    dv = dv + mm(dmh, p.astype(BF16))
                    ds = (p * (dp - jnp.sum(dp * p, axis=-1, keepdims=True))).astype(BF16)
                    dq = dq + mm_nt(km, ds)
                    dk = dk + mm(only(q, here), ds) * keep.astype(F32)
            else:
                for head in range(4):
                    lanes = head_lanes(head)
                    p = p_ref[grp, 4 * pair + head]
                    dmh = only(dm, lanes)
                    dp = mm_nt(dmh, val)
                    dv = dv + mm_tn(p.astype(BF16), dmh)
                    ds = (p * (dp - jnp.sum(dp * p, axis=-1, keepdims=True))).astype(BF16)
                    dq = dq + mm(ds, only(k, lanes))
                    dk = dk + mm_tn(ds, only(q, lanes))
            dt_ref[rows, qs] = (dq * SCALE).astype(BF16)
            dt_ref[rows, ks] = (dk * SCALE).astype(BF16)
            dt_ref[rows, vs] = dv.astype(BF16)

    acc[...] = jnp.zeros_like(acc)

    @pl.loop(0, 3)
    def _(j):
        cols = pl.ds(pl.multiple_of(W * j, W), W)
        acc[...] += mm_nt(dt_ref[:, cols], w[base + j])
        sg[layer, pl.ds(12 + j, 1), :] = column_sum(dt_ref[:, cols].astype(F32))
        dw(layer, j, n_ref, lambda: dt_ref[:, cols])

    dn = acc[...]
    x = xhat[...]
    sg[layer, 10:11, :] = column_sum(dn * x)
    sg[layer, 11:12, :] = column_sum(dn)
    e = dn * row(10)
    inner = rstd[...] * (e - jnp.mean(e, axis=-1, keepdims=True) - x * jnp.mean(e * x, axis=-1, keepdims=True))
    dc = jnp.where(live_rows(ROWS), g_in[...].astype(F32) + inner, 0.0)
    sg[layer, 9:10, :] = column_sum(dc)
    v = u_in[...].astype(F32)
    masks = column_masks(ROWS)
    du = dc
    for b in range(3):
        dcm = dc * masks[b]
        for a in range(3):
            moved = rolled(dcm, SIDE * (a - 1) + b - 1)
            tap = 3 * a + b
            du = du + row(tap) * moved
            sg[layer, tap:tap + 1, :] = column_sum(moved * v)
    g_out[...] = jnp.where(live_rows(ROWS), du, 0.0).astype(BF16)


ROOT_HALF = 0.5 ** 0.5
ROOT_TWO_PI = 0.3989422804014327


def ff_forward(layer, u_in, u_out, w, small, xhat, rstd, n_ref, slope, acc):
    base = 12 * layer
    row = lambda r: small[layer, r:r + 1, :]
    x, r = norm_parts(u_in[...].astype(F32))
    xhat[...] = x
    rstd[...] = r
    n_ref[...] = (x * row(16) + row(17)).astype(BF16)
    acc[...] = u_in[...].astype(F32) + row(22)

    @pl.loop(0, 4)
    def _(j):
        cols = pl.ds(pl.multiple_of(W * j, W), W)
        h = mm(n_ref[...], w[base + 4 + j]) + small[layer, pl.ds(18 + j, 1), :]
        cdf = 0.5 + 0.5 * lax.erf(h * ROOT_HALF)
        slope[:, cols] = cdf + h * (ROOT_TWO_PI * jnp.exp(-0.5 * h * h))
        acc[...] += mm((h * cdf).astype(BF16), w[base + 8 + j])

    u_out[...] = jnp.where(live_rows(ROWS), acc[...], 0.0).astype(BF16)


def ff_backward(layer, g_in, g_out, w, small, sg, xhat, rstd, slope, acc):
    base = 12 * layer
    row = lambda r: small[layer, r:r + 1, :]
    sg[layer, 22:23, :] = column_sum(g_in[...].astype(F32))
    acc[...] = jnp.zeros_like(acc)

    @pl.loop(0, 4)
    def _(j):
        cols = pl.ds(pl.multiple_of(W * j, W), W)
        dh = (mm_nt(g_in[...], w[base + 8 + j]) * slope[:, cols]).astype(BF16)
        sg[layer, pl.ds(18 + j, 1), :] = column_sum(dh.astype(F32))
        acc[...] += mm_nt(dh, w[base + 4 + j])

    dn = acc[...]
    x = xhat[...]
    sg[layer, 16:17, :] = column_sum(dn * x)
    sg[layer, 17:18, :] = column_sum(dn)
    e = dn * row(16)
    inner = rstd[...] * (e - jnp.mean(e, axis=-1, keepdims=True) - x * jnp.mean(e * x, axis=-1, keepdims=True))
    g_out[...] = jnp.where(live_rows(ROWS), g_in[...].astype(F32) + inner, 0.0).astype(BF16)


def chain_scratch():
    V = pltpu.VMEM
    mixer = [V((ROWS, W), F32), V((ROWS, 1), F32), V((ROWS, W), BF16), V((ROWS, 3 * W), BF16)]
    feed = [V((ROWS, W), F32), V((ROWS, 1), F32), V((ROWS, W), BF16), V((ROWS, 4 * W), F32)]
    return (mixer + [V((6, 8, PAIR, PAIR), F32), V((ROWS, W), BF16)] + feed + mixer + [V((6, 4, LANES, LANES), F32), V((ROWS, W), BF16)] + feed
            + [V((ROWS, W), F32), V((ROWS, W), F32), V((ROWS, W), BF16), V((ROWS, 3 * W), BF16), V((PAIR, PAIR), F32), V((LANES, LANES), F32)])


def fill_biases(win_bias, chan_bias):
    qi = lax.broadcasted_iota(jnp.int32, (PAIR, PAIR), 0)
    ki = lax.broadcasted_iota(jnp.int32, (PAIR, PAIR), 1)
    win_bias[...] = jnp.where(((qi // IMG) == (ki // IMG)) & (lax.rem(ki, IMG) < LIVE), 0.0, -1e30).astype(F32)
    ci = lax.broadcasted_iota(jnp.int32, (LANES, LANES), 0)
    ei = lax.broadcasted_iota(jnp.int32, (LANES, LANES), 1)
    chan_bias[...] = jnp.where((ci // HD) == (ei // HD), 0.0, -1e30).astype(F32)


class Chain:
    def __init__(self, w, small, mask, u, g, sg, dw, scratch):
        self.w, self.small, self.mask, self.u, self.g, self.sg, self.dw = w, small, mask, u, g, sg, dw
        s = scratch
        self.window, self.feed0, self.channel, self.feed1 = s[0:6], s[6:10], s[10:16], s[16:20]
        self.c_ref, self.acc, self.dm, self.dt, self.win_bias, self.chan_bias = s[20:26]

    def forward(self, k):
        u, w, small = self.u, self.w, self.small
        if k == 0:
            fill_biases(self.win_bias, self.chan_bias)
            mix_forward(0, False, u[0], u[1], w, small, self.mask, self.win_bias, self.c_ref, *self.window)
        if k == 1:
            ff_forward(0, u[1], u[2], w, small, *self.feed0, self.acc)
        if k == 2:
            mix_forward(1, True, u[2], u[3], w, small, self.mask, self.chan_bias, self.c_ref, *self.channel)
        if k == 3:
            ff_forward(1, u[3], u[4], w, small, *self.feed1, self.acc)

    def backward(self, k):
        u, g, w, small, sg = self.u, self.g, self.w, self.small, self.sg
        if k in (0, 2):
            parts = self.channel if k == 2 else self.window
            mix_backward(k // 2, k == 2, u[k], g[k + 1], g[k], w, small, self.mask, sg, self.dw, self.c_ref, *parts, self.dm, self.dt, self.acc)
        else:
            x, r, _, slope = self.feed0 if k == 1 else self.feed1
            ff_backward(k // 2, g[k + 1], g[k], w, small, sg, x, r, slope, self.acc)


MESH = pl.DeviceIdType.MESH
STRIP = 96


def slot(item, line, d):
    red = lax.rem(item, 3) // 2
    block = 12 * (item // 3) + 4 * lax.rem(item, 3) + (1 - red) * line + red * (d // 2)
    row = (1 - red) * STRIP * d + red * (4 * STRIP * lax.rem(d, 2) + STRIP * line)
    return block, row


def other_planes(z):
    near = z + 1 - 2 * (z // 2)
    far = 3 * (1 - z // 2)
    return near, 6 - z - near - far, far


class Place:
    def __init__(self):
        self.s = lax.axis_index("segment")
        self.d = lax.axis_index("dp")
        self.z = self.d // 2
        self.c = lax.rem(self.d, 2)
        self.xn = self.s + 1 - 2 * lax.rem(self.s, 2)
        self.yn = lax.rem(self.s + 2, 4)
        self.dn = 3 - self.s
        self.twin = self.d + 1 - 2 * self.c


def greet_neighbours(at):
    bar = pltpu.get_barrier_semaphore()

    def greet(seg, dev):
        pl.semaphore_signal(bar, inc=1, device_id=(seg, dev), device_id_type=MESH)

    greet(at.xn, at.d)
    greet(at.yn, at.d)
    greet(at.s, at.twin)

    @pl.when(at.z < 3)
    def _():
        greet(at.s, at.d + 2)

    @pl.when(at.z > 0)
    def _():
        greet(at.s, at.d - 2)

    pl.semaphore_wait(bar, 4 + (at.z * (3 - at.z)) // 2)


def remote(src, dst, ssem, rsem, seg, dev):
    return pltpu.make_async_remote_copy(src, dst, ssem, rsem, device_id=(seg, dev), device_id_type=MESH)


def gather_scratch():
    D = pltpu.SemaphoreType.DMA
    return [D((2, 9)), D((6, 5)), D((6, 3, 2)), D((6, 3, 2)), D((6, 4, 4)), D((2, 3, 4)), D((2, 3, 4))]


class Gather:
    def __init__(self, at, shards, wbuf, sems):
        self.at, self.shards, self.w = at, shards, wbuf
        self.lsem, self.zs, self.xs, self.ys, self.pr, self.cs, self.cr = sems
        self.planes = other_planes(at.z)
        self.away = 2 * (at.z // 2) - 1
        self.inner = (at.z == 1) | (at.z == 2)
        self.groups = [(layer, part, k) for layer in range(2) for part in range(3) for k in range(3)]

    def strip(self, item, line, plane):
        block, row = slot(item, line, 2 * plane + self.at.c)
        return self.w.at[block, pl.ds(pl.multiple_of(row, STRIP), STRIP), :]

    def quad_ref(self, layer, part, plane, core):
        if part == 2:
            return self.w.at[12 * layer + 8 + plane, pl.ds(pl.multiple_of(4 * STRIP * core, 4 * STRIP), 4 * STRIP), :]
        row = pl.multiple_of(STRIP * (2 * plane + core), STRIP)
        return self.w.at[pl.ds(12 * layer + 4 * part, 4), pl.ds(row, STRIP), :]

    def quad(self, layer, part, plane, core, k):
        ref = self.quad_ref(layer, part, plane, core)
        return remote(ref, ref, self.cs.at[layer, part, k], self.cr.at[layer, part, plane], self.at.s, self.at.twin)

    def local(self, layer):
        triple, output, expand, reduce = self.shards
        at, w, base = self.at, self.w, 12 * layer
        rows = pl.ds(pl.multiple_of(STRIP * at.d, STRIP), STRIP)
        sems = self.lsem.at
        copies = [pltpu.make_async_copy(triple.at[layer, :, pl.ds(W * j, W)], w.at[base + j, rows, :], sems[layer, j]) for j in range(3)]
        copies.append(pltpu.make_async_copy(output.at[layer], w.at[base + 3, rows, :], sems[layer, 3]))
        copies += [pltpu.make_async_copy(expand.at[layer, :, pl.ds(W * j, W)], w.at[base + 4 + j, rows, :], sems[layer, 4 + j]) for j in range(4)]
        half = pl.ds(pl.multiple_of(4 * STRIP * at.c, 4 * STRIP), 4 * STRIP)
        copies.append(pltpu.make_async_copy(reduce.at[layer], w.at[base + 8 + at.z, half, :], sems[layer, 8]))
        return copies

    def up(self, item):
        ref = self.strip(item, self.at.s, self.at.z)
        return remote(ref, ref, self.zs.at[item, 0], self.pr.at[item, self.at.z, self.at.s], self.at.s, self.at.d + 2)

    def down(self, item):
        ref = self.strip(item, self.at.s, self.at.z)
        return remote(ref, ref, self.zs.at[item, 1], self.pr.at[item, self.at.z, self.at.s], self.at.s, self.at.d - 2)

    def onward(self, item, k):
        step = self.away if k != 1 else -self.away
        ref = self.strip(item, self.at.s, self.planes[k])
        return remote(ref, ref, self.zs.at[item, 2 + k], self.pr.at[item, self.planes[k], self.at.s], self.at.s, self.at.d + 2 * step)

    def to_x(self, item, k, line, j):
        ref = self.strip(item, line, self.planes[k])
        return remote(ref, ref, self.xs.at[item, k, j], self.pr.at[item, self.planes[k], line], self.at.xn, self.at.d)

    def to_y(self, item, k, line, j):
        ref = self.strip(item, line, self.planes[k])
        return remote(ref, ref, self.ys.at[item, k, j], self.pr.at[item, self.planes[k], line], self.at.yn, self.at.d)

    def arrival(self, item, k, line):
        ref = self.strip(item, line, self.planes[k])
        return remote(ref, ref, self.zs.at[item, 0], self.pr.at[item, self.planes[k], line], self.at.s, self.at.twin)

    def ends(self, item, act):
        @pl.when(self.at.z < 3)
        def _():
            act(self.up(item))

        @pl.when(self.at.z > 0)
        def _():
            act(self.down(item))

    def begin(self):
        at = self.at
        copies = [self.local(layer) for layer in range(2)]
        for layer in range(2):
            for copy in copies[layer]:
                copy.start()
        for copy in copies[0]:
            copy.wait()
        self.ends(0, lambda copy: copy.start())
        for part in range(3):
            self.quad(0, part, at.z, at.c, 3).start()
        for copy in copies[1]:
            copy.wait()
        for part in range(3):
            self.quad(1, part, at.z, at.c, 3).start()

    def stage_a(self, layer, part, k):
        item = 3 * layer + part
        self.arrival(item, k, self.at.s).wait_recv()

        @pl.when(self.inner)
        def _():
            self.onward(item, k).start()

        self.to_x(item, k, self.at.s, 0).start()
        self.to_y(item, k, self.at.s, 0).start()

    def stage_b(self, layer, part, k):
        item = 3 * layer + part
        self.arrival(item, k, self.at.xn).wait_recv()
        if (part + k + layer) % 2 == 0:
            self.to_y(item, k, self.at.xn, 1).start()
        self.arrival(item, k, self.at.yn).wait_recv()
        if (part + k + layer) % 2 == 1:
            self.to_x(item, k, self.at.yn, 1).start()

    def stage_c(self, layer, part, k):
        item = 3 * layer + part
        self.arrival(item, k, self.at.dn).wait_recv()
        self.quad(layer, part, self.planes[k], self.at.c, k).start()

    def step(self, g):
        n = len(self.groups)
        if g < n and g % 3 == 0 and g // 3 + 1 < 6:
            self.ends(g // 3 + 1, lambda copy: copy.start())
        if g < n:
            self.stage_a(*self.groups[g])
        if 0 <= g - 1 < n:
            self.stage_b(*self.groups[g - 1])
        if 0 <= g - 2 < n:
            self.stage_c(*self.groups[g - 2])

    def settle(self, layer, part):
        for k in range(3):
            self.quad(layer, part, self.planes[k], 1 - self.at.c, k).wait_recv()
        self.quad(layer, part, self.at.z, 1 - self.at.c, 3).wait_recv()

    def drain(self):
        at = self.at
        for layer in range(2):
            for part in range(3):
                item = 3 * layer + part
                self.ends(item, lambda copy: copy.wait_send())
                self.quad(layer, part, at.z, at.c, 3).wait_send()
                for k in range(3):
                    @pl.when(self.inner)
                    def _():
                        self.onward(item, k).wait_send()

                    self.to_x(item, k, at.s, 0).wait_send()
                    self.to_y(item, k, at.s, 0).wait_send()
                    if (part + k + layer) % 2 == 0:
                        self.to_y(item, k, at.xn, 1).wait_send()
                    else:
                        self.to_x(item, k, at.yn, 1).wait_send()
                    self.quad(layer, part, self.planes[k], at.c, k).wait_send()


def chain_kernel(triple, output, expand, reduce, small, x, mask, gin, u_out, g_out, sg, w_out, w, osem, *scratch):
    at = Place()
    gather = Gather(at, (triple, output, expand, reduce), w, scratch[:7])
    u = [x] + [u_out.at[i] for i in range(4)]
    g = [g_out.at[i] for i in range(4)] + [gin]

    def dw(layer, j, lhs, rhs):
        w[12 * layer + j] = mm_tn(lhs[...], rhs()).astype(BF16)

    chain = Chain(w, small, mask, u, g, sg, dw, scratch[7:])
    sg[...] = jnp.zeros_like(sg)
    greet_neighbours(at)
    gather.begin()
    for step in range(20):
        gather.step(step)
    for layer in range(2):
        for part in range(3):
            gather.settle(layer, part)
    gather.drain()
    for k in range(4):
        chain.forward(k)
    for k in (3, 2, 1, 0):
        chain.backward(k)
    keep = pltpu.make_async_copy(w, w_out, osem)
    keep.start()
    keep.wait()


def chain_call(triple, output, expand, reduce, small, x, mask, gin):
    V = pltpu.VMEM
    S = jax.ShapeDtypeStruct
    anywhere = pl.BlockSpec(memory_space=pl.ANY)
    vmem = pl.BlockSpec(memory_space=V)
    return pl.pallas_call(
        chain_kernel,
        out_shape=(S((4, ROWS, W), BF16), S((4, ROWS, W), BF16), S((2, 24, W), F32), S((24, W, W), BF16)),
        in_specs=[anywhere] * 4 + [vmem] * 4,
        out_specs=[vmem] * 3 + [anywhere],
        scratch_shapes=[V((24, W, W), BF16), pltpu.SemaphoreType.DMA] + gather_scratch() + chain_scratch(),
        compiler_params=pltpu.CompilerParams(collective_id=1, has_side_effects=True, vmem_limit_bytes=63 * 1024 * 1024),
        name="gather_and_chain",
    )(triple, output, expand, reduce, small, x, mask, gin)


def pack_small(conv_weight, conv_bias, mixer_gain, mixer_shift, triple_bias, output_bias, feed_gain, feed_shift, expand_bias, reduce_bias):
    part = conv_bias.shape[1]
    rows = [conv_weight] + [
        v.reshape(2, -1, part)
        for v in (conv_bias, mixer_gain, mixer_shift, triple_bias, output_bias, feed_gain, feed_shift, expand_bias, reduce_bias)
    ]
    return jnp.concatenate(rows, axis=1)


def spread_small(packed):
    n = packed.shape[0]

    def rows(lo, hi):
        return jnp.transpose(packed[:, :, lo:hi], (1, 2, 0, 3)).reshape(2, hi - lo, W)

    def long(lo, hi):
        return jnp.transpose(packed[:, :, lo:hi], (1, 0, 2, 3)).reshape(2, hi - lo, W)

    zero = jnp.zeros((2, 1, W), packed.dtype)
    return jnp.concatenate([rows(0, 12), long(12, 15), rows(15, 18), long(18, 22), rows(22, 23), zero], axis=1)


def pad_images(rows):
    return jnp.pad(rows.reshape(-1, LIVE, rows.shape[1]), ((0, 0), (0, IMG - LIVE), (0, 0))).reshape(-1, rows.shape[1])


def unpad_images(rows):
    lead = rows.shape[:-2]
    return rows.reshape(lead + (-1, IMG, W))[..., :LIVE, :].reshape(lead + (-1, W))


def spread_body(
    patches, region_mask, conv_weight, conv_bias, mixer_gain, mixer_shift, triple_weight, triple_bias, output_weight,
    output_bias, feed_gain, feed_shift, expand_weight, expand_bias, reduce_weight, reduce_bias, cotangent,
):
    s = lax.axis_index("segment")
    d = lax.axis_index("dp")
    packed = pack_small(conv_weight, conv_bias, mixer_gain, mixer_shift, triple_bias, output_bias, feed_gain, feed_shift, expand_bias, reduce_bias)
    small = spread_small(lax.all_gather(packed, "dp", axis=0)).astype(F32)
    own = patches.shape[0] // lax.axis_size("segment")
    mine = lambda v: lax.dynamic_slice_in_dim(v, s * own, own, 0)
    x = pad_images(mine(patches))
    gin = pad_images(mine(cotangent))
    mask = pad_images(mine(region_mask).astype(BF16)[:, None])
    u, g, sg, w = chain_call(triple_weight, output_weight, expand_weight, reduce_weight, small, x, mask, gin)
    sections = lambda v: lax.all_to_all(unpad_images(v), "segment", split_axis=0, concat_axis=1, tiled=True)
    blocks = []
    for layer in range(2):
        e_w, r_w = w[12 * layer + 4:12 * layer + 8], w[12 * layer + 8:12 * layer + 12]
        ui = u[2 * layer].astype(F32)
        go = g[2] if layer == 0 else gin
        hat, _ = norm_parts(ui)
        n = (hat * small[layer, 16] + small[layer, 17]).astype(BF16)
        es, rs = [], []
        for j in range(4):
            h = mm(n, e_w[j]) + small[layer, 18 + j]
            a, pull = jax.vjp(gelu_exact, h)
            dh = pull(mm_nt(go, r_w[j]))[0].astype(BF16)
            es.append(mm_tn(n, dh).astype(BF16))
            rs.append(mm_tn(a.astype(BF16), go).astype(BF16))
        blocks.append((w[12 * layer:12 * layer + 4], jnp.stack(es), jnp.stack(rs)))
    dp = lax.axis_size("dp")
    by_row = lambda v: v.reshape(4, dp, W // dp, W).transpose(1, 2, 0, 3)
    total = jnp.concatenate(
        [jnp.concatenate([by_row(m).reshape(dp, -1, W), by_row(e).reshape(dp, -1, W), r.reshape(dp, -1, W)], axis=1) for m, e, r in blocks], axis=1
    )
    total = lax.psum_scatter(total, "dp", scatter_dimension=0, tiled=True)[0]
    total = lax.psum(total, "segment").astype(F32)
    part = W // dp
    total = total.reshape(2, 3, part * 4, W)
    mix = total[:, 0].reshape(2, part, 4 * W)
    exp = total[:, 1].reshape(2, part, 4 * W)
    red = total[:, 2]
    sg = lax.psum(sg, ("segment", "dp"))
    cut = lambda lo, hi: lax.dynamic_slice_in_dim(sg[:, lo:hi].reshape(2, -1), d * part * (hi - lo), part * (hi - lo), 1)
    taps = lax.dynamic_slice_in_dim(sg[:, :9], d * part, part, 2)
    return (
        sections(u), sections(g), taps, cut(9, 10), cut(10, 11), cut(11, 12), mix[:, :, :3 * W], cut(12, 15), mix[:, :, 3 * W:],
        cut(15, 16), cut(16, 17), cut(17, 18), exp, cut(18, 22), red, cut(22, 23),
    )


def solution(mesh):
    in_specs = (
        P("dp", None),
        P("dp"),
        P(None, None, "dp"),
        P(None, "dp"),
        P(None, "dp"),
        P(None, "dp"),
        P(None, "dp", None),
        P(None, "dp"),
        P(None, "dp", None),
        P(None, "dp"),
        P(None, "dp"),
        P(None, "dp"),
        P(None, "dp", None),
        P(None, "dp"),
        P(None, "dp", None),
        P(None, "dp"),
        P("dp", None),
    )
    out_specs = (
        P("segment", "dp", None),
        P("segment", "dp", None),
        P(None, None, "dp"),
        P(None, "dp"),
        P(None, "dp"),
        P(None, "dp"),
        P(None, "dp", None),
        P(None, "dp"),
        P(None, "dp", None),
        P(None, "dp"),
        P(None, "dp"),
        P(None, "dp"),
        P(None, "dp", None),
        P(None, "dp"),
        P(None, "dp", None),
        P(None, "dp"),
    )
    chosen = spread_body if mesh.shape["dp"] == 8 and mesh.shape["segment"] == 4 else body
    return jax.shard_map(chosen, mesh=mesh, in_specs=in_specs, out_specs=out_specs, check_vma=False)
```

```python
from functools import partial

import jax
import jax.numpy as jnp
from jax import lax
from jax.experimental import pallas as pl
from jax.experimental.pallas import tpu as pltpu
from jax.sharding import PartitionSpec as P

HD = 32
SIDE = 7
MICRO = 4
IMG_MB = 4


EPSILON = 1e-05


def as_sent(x):

    def short(part):
        return part.astype(jnp.bfloat16) if part.dtype == jnp.float32 else part

    return jax.tree.map(short, x)


def shifted_2(x, axis, by):
    count = lax.axis_size(axis)
    pairs = [(i, i + by) for i in range(count) if 0 <= i + by < count]
    return lax.ppermute(x, axis, pairs)


def dot_last(first_operand, second_operand):
    return lax.dot_general(
        first_operand, second_operand, (((1,), (1,)), ((), ())), preferred_element_type=jnp.float32
    )


def dot_first(first_operand, second_operand):
    return lax.dot_general(
        first_operand, second_operand, (((0,), (0,)), ((), ())), preferred_element_type=jnp.float32
    )


def layer_norm(values, norm_gain, norm_shift):
    center = values - jnp.mean(values, axis=-1, keepdims=True)
    spread = jnp.mean(center * center, axis=-1, keepdims=True)
    return center * lax.rsqrt(spread + EPSILON) * norm_gain + norm_shift


def position_conv(stream, conv_weight, conv_bias):
    features = stream.shape[-1]
    planes = stream.reshape(-1, SIDE, SIDE, features)
    padded = jnp.pad(planes, ((0, 0), (1, 1), (1, 1), (0, 0)))
    summed = jnp.zeros_like(planes) + conv_bias
    for tap_row in range(3):
        for tap_col in range(3):
            summed = (
                summed
                + padded[:, tap_row : tap_row + SIDE, tap_col : tap_col + SIDE, :]
                * conv_weight[tap_row * 3 + tap_col]
            )
    return stream + summed.reshape(stream.shape)


def front_part(stream, conv_weight, conv_bias, norm_gain, norm_shift):
    shifted = position_conv(stream, conv_weight, conv_bias)
    return (shifted, layer_norm(shifted, norm_gain, norm_shift))


def gelu_exact(values):
    return jax.nn.gelu(values, approximate=False)


def softmax_rows(scores):
    row_max = jnp.max(scores, axis=-1, keepdims=True)
    lifted = jnp.exp(scores - row_max)
    return lifted / jnp.sum(lifted, axis=-1, keepdims=True)


def window_forward(triple):
    tokens = triple.shape[0]
    features = triple.shape[1] // 3
    pieces = triple.reshape(tokens // (SIDE * SIDE), SIDE * SIDE, 3, features // HD, HD)
    queries = pieces[:, :, 0]
    key_parts = pieces[:, :, 1]
    value_parts = pieces[:, :, 2]
    scores = jnp.einsum(
        "iqhd,ikhd->ihqk", queries, key_parts, preferred_element_type=jnp.float32
    ) * HD ** (-0.5)
    softmaxed = softmax_rows(scores)
    softmaxed_low = softmaxed.astype(jnp.bfloat16)
    mixture = jnp.einsum(
        "ihqk,ikhd->iqhd", softmaxed_low, value_parts, preferred_element_type=jnp.float32
    )
    return (
        mixture.reshape(tokens, features),
        (queries, key_parts, value_parts, softmaxed, softmaxed_low),
    )


def window_backward(stored, grad_mixture):
    queries, key_parts, value_parts, softmaxed, softmaxed_low = stored
    grad_pieces = grad_mixture.reshape(queries.shape)
    grad_values = jnp.einsum(
        "ihqk,iqhd->ikhd", softmaxed_low, grad_pieces, preferred_element_type=jnp.float32
    )
    grad_soft = jnp.einsum(
        "iqhd,ikhd->ihqk", grad_pieces, value_parts, preferred_element_type=jnp.float32
    )
    grad_scores = (
        softmaxed * (grad_soft - jnp.sum(grad_soft * softmaxed, axis=-1, keepdims=True))
    ).astype(jnp.bfloat16)
    grad_queries = jnp.einsum(
        "ihqk,ikhd->iqhd", grad_scores, key_parts, preferred_element_type=jnp.float32
    ) * HD ** (-0.5)
    grad_keys = jnp.einsum(
        "ihqk,iqhd->ikhd", grad_scores, queries, preferred_element_type=jnp.float32
    ) * HD ** (-0.5)
    joined = jnp.stack([grad_queries, grad_keys, grad_values], axis=2)
    return joined.reshape(grad_mixture.shape[0], 3 * grad_mixture.shape[1])


def channel_forward(triple, mask_rows):
    tokens = triple.shape[0]
    features = triple.shape[1] // 3
    images = tokens // (SIDE * SIDE)
    pieces = triple.reshape(images, SIDE * SIDE, 3, features // HD, HD)
    queries = pieces[:, :, 0]
    keep_mask = mask_rows.reshape(images, SIDE * SIDE, 1, 1).astype(jnp.bfloat16)
    masked = pieces[:, :, 1] * keep_mask
    value_parts = pieces[:, :, 2]
    scores = jnp.einsum(
        "itgc,itge->igce", queries, masked, preferred_element_type=jnp.float32
    ) * HD ** (-0.5)
    softmaxed = softmax_rows(scores)
    softmaxed_low = softmaxed.astype(jnp.bfloat16)
    mixture = jnp.einsum(
        "igce,itge->itgc", softmaxed_low, value_parts, preferred_element_type=jnp.float32
    )
    return (
        mixture.reshape(tokens, features),
        (queries, masked, value_parts, keep_mask, softmaxed, softmaxed_low),
    )


def channel_backward(stored, grad_mixture):
    queries, masked, value_parts, keep_mask, softmaxed, softmaxed_low = stored
    grad_pieces = grad_mixture.reshape(queries.shape)
    grad_soft = jnp.einsum(
        "itgc,itge->igce", grad_pieces, value_parts, preferred_element_type=jnp.float32
    )
    grad_values = jnp.einsum(
        "igce,itgc->itge", softmaxed_low, grad_pieces, preferred_element_type=jnp.float32
    )
    grad_scores = (
        softmaxed * (grad_soft - jnp.sum(grad_soft * softmaxed, axis=-1, keepdims=True))
    ).astype(jnp.bfloat16)
    grad_queries = jnp.einsum(
        "igce,itge->itgc", grad_scores, masked, preferred_element_type=jnp.float32
    ) * HD ** (-0.5)
    grad_masked = jnp.einsum(
        "igce,itgc->itge", grad_scores, queries, preferred_element_type=jnp.float32
    ) * HD ** (-0.5)
    grad_keys = grad_masked * keep_mask.astype(jnp.float32)
    joined = jnp.stack([grad_queries, grad_keys, grad_values], axis=2)
    return joined.reshape(grad_mixture.shape[0], 3 * grad_mixture.shape[1])


def mixer_inner(stream, weights, mask_rows, channel):
    (
        conv_weight,
        conv_bias,
        norm_gain,
        norm_shift,
        triple_weight,
        triple_bias,
        output_weight,
        output_bias,
    ) = weights[:8]
    widened = stream.astype(jnp.float32)
    (shifted, normed), front_pull = jax.vjp(
        front_part,
        widened,
        conv_weight.astype(jnp.float32),
        conv_bias.astype(jnp.float32),
        norm_gain.astype(jnp.float32),
        norm_shift.astype(jnp.float32),
    )
    normed_low = normed.astype(jnp.bfloat16)
    triple = (
        jnp.dot(normed_low, triple_weight, preferred_element_type=jnp.float32)
        + triple_bias.astype(jnp.float32)
    ).astype(jnp.bfloat16)
    if channel:
        mixture, stored = channel_forward(triple, mask_rows)
    else:
        mixture, stored = window_forward(triple)
    mixture_low = mixture.astype(jnp.bfloat16)
    return (shifted, front_pull, normed_low, stored, mixture_low)


def mixer_forward(stream, weights, mask_rows, channel):
    shifted, front_pull, normed_low, stored, mixture_low = mixer_inner(
        stream, weights, mask_rows, channel
    )
    result = (
        shifted
        + jnp.dot(mixture_low, weights[6], preferred_element_type=jnp.float32)
        + weights[7].astype(jnp.float32)
    )
    return result.astype(jnp.bfloat16)


def mixer_backward(stream, grad_out, weights, mask_rows, channel):
    shifted, front_pull, normed_low, stored, mixture_low = mixer_inner(
        stream, weights, mask_rows, channel
    )
    grad_wide = grad_out.astype(jnp.float32)
    grad_out_bias = jnp.sum(grad_wide, axis=0)
    grad_out_weight = dot_first(mixture_low, grad_out)
    grad_mixture = dot_last(grad_out, weights[6]).astype(jnp.bfloat16)
    if channel:
        grad_triple = channel_backward(stored, grad_mixture).astype(jnp.bfloat16)
    else:
        grad_triple = window_backward(stored, grad_mixture).astype(jnp.bfloat16)
    grad_tri_weight = dot_first(normed_low, grad_triple)
    grad_tri_bias = jnp.sum(grad_triple.astype(jnp.float32), axis=0)
    grad_normed = dot_last(grad_triple, weights[4])
    grad_stream, grad_taps, grad_tap_bias, grad_gain, grad_shift = front_pull(
        (grad_wide, grad_normed)
    )
    zero_tail = tuple((jnp.zeros(member.shape, jnp.float32) for member in weights[8:]))
    return (
        grad_stream.astype(jnp.bfloat16),
        (
            grad_taps,
            grad_tap_bias,
            grad_gain,
            grad_shift,
            grad_tri_weight,
            grad_tri_bias,
            grad_out_weight,
            grad_out_bias,
        )
        + zero_tail,
    )


def feed_inner(stream, weights):
    norm_gain, norm_shift, expand_weight, expand_bias, reduce_weight, reduce_bias = weights[8:]
    widened = stream.astype(jnp.float32)
    normed, norm_pull = jax.vjp(
        layer_norm, widened, norm_gain.astype(jnp.float32), norm_shift.astype(jnp.float32)
    )
    normed_low = normed.astype(jnp.bfloat16)
    hidden = jnp.dot(
        normed_low, expand_weight, preferred_element_type=jnp.float32
    ) + expand_bias.astype(jnp.float32)
    active, gelu_pull = jax.vjp(gelu_exact, hidden)
    return (widened, norm_pull, normed_low, gelu_pull, active.astype(jnp.bfloat16))


def feed_forward(stream, weights):
    widened, norm_pull, normed_low, gelu_pull, active_low = feed_inner(stream, weights)
    result = (
        widened
        + jnp.dot(active_low, weights[12], preferred_element_type=jnp.float32)
        + weights[13].astype(jnp.float32)
    )
    return result.astype(jnp.bfloat16)


def feed_backward(stream, grad_out, weights):
    widened, norm_pull, normed_low, gelu_pull, active_low = feed_inner(stream, weights)
    grad_wide = grad_out.astype(jnp.float32)
    grad_red_bias = jnp.sum(grad_wide, axis=0)
    grad_red_weight = dot_first(active_low, grad_out)
    grad_active = dot_last(grad_out, weights[12])
    grad_hidden = gelu_pull(grad_active)[0].astype(jnp.bfloat16)
    grad_exp_weight = dot_first(normed_low, grad_hidden)
    grad_exp_bias = jnp.sum(grad_hidden.astype(jnp.float32), axis=0)
    grad_normed = dot_last(grad_hidden, weights[10])
    grad_inner, grad_gain, grad_shift = norm_pull(grad_normed)
    zero_head = tuple((jnp.zeros(member.shape, jnp.float32) for member in weights[:8]))
    grad_stream = grad_wide + grad_inner
    return (
        grad_stream.astype(jnp.bfloat16),
        zero_head
        + (grad_gain, grad_shift, grad_exp_weight, grad_exp_bias, grad_red_weight, grad_red_bias),
    )


def section_forward(section, stream, weights, mask_rows):
    if section % 2 == 1:
        return feed_forward(stream, weights)
    return mixer_forward(stream, weights, mask_rows, section == 2)


def section_backward(section, stream, grad_out, weights, mask_rows):
    if section % 2 == 1:
        return feed_backward(stream, grad_out, weights)
    return mixer_backward(stream, grad_out, weights, mask_rows, section == 2)


def spare_forward(stream, weights, mask_rows):
    return jnp.zeros_like(stream)


def spare_backward(stream, grad_out, weights, mask_rows):
    return (
        jnp.zeros_like(stream),
        tuple((jnp.zeros(member.shape, jnp.float32) for member in weights)),
    )


def put_rows(buffer, rows, row_start, is_live):
    former = lax.dynamic_slice_in_dim(buffer, row_start, rows.shape[0], 0)
    return lax.dynamic_update_slice_in_dim(buffer, jnp.where(is_live, rows, former), row_start, 0)


def run_segments(layer_set, patches, region_mask, cotangent, segment_index, segments):
    features = patches.shape[1]
    micro_count = MICRO
    micro_rows = IMG_MB * SIDE * SIDE
    tick_count = micro_count + segments - 1
    forward_branches = [
        partial(section_forward, 0),
        partial(section_forward, 1),
        partial(section_forward, 2),
        partial(section_forward, 3),
        spare_forward,
    ]
    backward_branches = [
        partial(section_backward, 0),
        partial(section_backward, 1),
        partial(section_backward, 2),
        partial(section_backward, 3),
        spare_backward,
    ]
    received = jnp.zeros((micro_rows, features), jnp.bfloat16)
    kept_inputs = jnp.zeros((micro_count * micro_rows, features), jnp.bfloat16)
    outputs_here = jnp.zeros((micro_count * micro_rows, features), jnp.bfloat16)
    for tick_index in range(tick_count):
        micro_index = tick_index - segment_index
        is_live = (micro_index >= 0) & (micro_index < micro_count)
        row_start = jnp.clip(micro_index, 0, micro_count - 1) * micro_rows
        fresh_rows = lax.dynamic_slice_in_dim(patches, row_start, micro_rows, 0)
        mask_rows = lax.dynamic_slice_in_dim(region_mask, row_start, micro_rows, 0)
        entering = jnp.where(segment_index == 0, fresh_rows, received)
        leaving = lax.switch(
            jnp.where(is_live, segment_index, segments),
            forward_branches,
            entering,
            layer_set,
            mask_rows,
        )
        kept_inputs = put_rows(kept_inputs, entering, row_start, is_live)
        outputs_here = put_rows(outputs_here, leaving, row_start, is_live)
        if tick_index + 1 < tick_count:
            received = jax.tree.map(
                lambda part, own: part.astype(own.dtype),
                shifted_2(as_sent(leaving), "segment", 1),
                leaving,
            )
    grad_received = jnp.zeros((micro_rows, features), jnp.bfloat16)
    grads_here = jnp.zeros((micro_count * micro_rows, features), jnp.bfloat16)
    totals = tuple((jnp.zeros(member.shape, jnp.float32) for member in layer_set))
    for tick_index in range(tick_count):
        micro_index = tick_index - (segments - 1 - segment_index)
        is_live = (micro_index >= 0) & (micro_index < micro_count)
        row_start = jnp.clip(micro_index, 0, micro_count - 1) * micro_rows
        seed_rows = lax.dynamic_slice_in_dim(cotangent, row_start, micro_rows, 0)
        mask_rows = lax.dynamic_slice_in_dim(region_mask, row_start, micro_rows, 0)
        arriving = jnp.where(segment_index == segments - 1, seed_rows, grad_received)
        stream = lax.dynamic_slice_in_dim(kept_inputs, row_start, micro_rows, 0)
        grad_stream, grad_terms = lax.switch(
            jnp.where(is_live, segment_index, segments),
            backward_branches,
            stream,
            arriving,
            layer_set,
            mask_rows,
        )
        totals = tuple(
            (first_term + second_term for first_term, second_term in zip(totals, grad_terms))
        )
        grads_here = put_rows(grads_here, grad_stream, row_start, is_live)
        if tick_index + 1 < tick_count:
            grad_received = jax.tree.map(
                lambda part, own: part.astype(own.dtype),
                shifted_2(as_sent(grad_stream), "segment", -1),
                grad_stream,
            )
    return (outputs_here, grads_here, totals)


def body(
    patches,
    region_mask,
    conv_weight,
    conv_bias,
    mixer_gain,
    mixer_shift,
    triple_weight,
    triple_bias,
    output_weight,
    output_bias,
    feed_gain,
    feed_shift,
    expand_weight,
    expand_bias,
    reduce_weight,
    reduce_bias,
    cotangent,
):
    params = (
        conv_weight,
        conv_bias,
        mixer_gain,
        mixer_shift,
        triple_weight,
        triple_bias,
        output_weight,
        output_bias,
        feed_gain,
        feed_shift,
        expand_weight,
        expand_bias,
        reduce_weight,
        reduce_bias,
    )
    segments = lax.axis_size("segment")
    segment_index = lax.axis_index("segment")
    layer_index = segment_index // 2
    slices = tuple(
        (lax.dynamic_index_in_dim(member, layer_index, 0, keepdims=False) for member in params)
    )
    layer_set = (
        lax.all_gather(slices[0], "dp", axis=1, tiled=True),
        lax.all_gather(slices[1], "dp", axis=0, tiled=True),
        lax.all_gather(slices[2], "dp", axis=0, tiled=True),
        lax.all_gather(slices[3], "dp", axis=0, tiled=True),
        lax.all_gather(slices[4], "dp", axis=0, tiled=True),
        lax.all_gather(slices[5], "dp", axis=0, tiled=True),
        lax.all_gather(slices[6], "dp", axis=0, tiled=True),
        lax.all_gather(slices[7], "dp", axis=0, tiled=True),
        lax.all_gather(slices[8], "dp", axis=0, tiled=True),
        lax.all_gather(slices[9], "dp", axis=0, tiled=True),
        lax.all_gather(slices[10], "dp", axis=0, tiled=True),
        lax.all_gather(slices[11], "dp", axis=0, tiled=True),
        lax.all_gather(slices[12], "dp", axis=0, tiled=True),
        lax.all_gather(slices[13], "dp", axis=0, tiled=True),
    )
    outputs_here, grads_here, totals = run_segments(
        layer_set, patches, region_mask, cotangent, segment_index, segments
    )
    reduced = (
        lax.psum_scatter(totals[0], "dp", scatter_dimension=1, tiled=True),
        lax.psum_scatter(totals[1], "dp", scatter_dimension=0, tiled=True),
        lax.psum_scatter(totals[2], "dp", scatter_dimension=0, tiled=True),
        lax.psum_scatter(totals[3], "dp", scatter_dimension=0, tiled=True),
        lax.psum_scatter(totals[4], "dp", scatter_dimension=0, tiled=True),
        lax.psum_scatter(totals[5], "dp", scatter_dimension=0, tiled=True),
        lax.psum_scatter(totals[6], "dp", scatter_dimension=0, tiled=True),
        lax.psum_scatter(totals[7], "dp", scatter_dimension=0, tiled=True),
        lax.psum_scatter(totals[8], "dp", scatter_dimension=0, tiled=True),
        lax.psum_scatter(totals[9], "dp", scatter_dimension=0, tiled=True),
        lax.psum_scatter(totals[10], "dp", scatter_dimension=0, tiled=True),
        lax.psum_scatter(totals[11], "dp", scatter_dimension=0, tiled=True),
        lax.psum_scatter(totals[12], "dp", scatter_dimension=0, tiled=True),
        lax.psum_scatter(totals[13], "dp", scatter_dimension=0, tiled=True),
    )
    placed = tuple(
        (
            jnp.stack(
                [jnp.where(layer_index == 0, member, 0.0), jnp.where(layer_index == 1, member, 0.0)]
            )
            for member in reduced
        )
    )
    section_outputs = outputs_here[None]
    section_grads = grads_here[None]
    summed = (
        lax.psum(placed[0].astype(jnp.bfloat16), "segment").astype(jnp.float32),
        lax.psum(placed[1].astype(jnp.bfloat16), "segment").astype(jnp.float32),
        lax.psum(placed[2].astype(jnp.bfloat16), "segment").astype(jnp.float32),
        lax.psum(placed[3].astype(jnp.bfloat16), "segment").astype(jnp.float32),
        lax.psum(placed[4].astype(jnp.bfloat16), "segment").astype(jnp.float32),
        lax.psum(placed[5].astype(jnp.bfloat16), "segment").astype(jnp.float32),
        lax.psum(placed[6].astype(jnp.bfloat16), "segment").astype(jnp.float32),
        lax.psum(placed[7].astype(jnp.bfloat16), "segment").astype(jnp.float32),
        lax.psum(placed[8].astype(jnp.bfloat16), "segment").astype(jnp.float32),
        lax.psum(placed[9].astype(jnp.bfloat16), "segment").astype(jnp.float32),
        lax.psum(placed[10].astype(jnp.bfloat16), "segment").astype(jnp.float32),
        lax.psum(placed[11].astype(jnp.bfloat16), "segment").astype(jnp.float32),
        lax.psum(placed[12].astype(jnp.bfloat16), "segment").astype(jnp.float32),
        lax.psum(placed[13].astype(jnp.bfloat16), "segment").astype(jnp.float32),
    )
    return (
        section_outputs,
        section_grads,
        summed[0],
        summed[1],
        summed[2],
        summed[3],
        summed[4],
        summed[5],
        summed[6],
        summed[7],
        summed[8],
        summed[9],
        summed[10],
        summed[11],
        summed[12],
        summed[13],
    )


W = 768
IMG = 56
LIVE = 49
ROWS = 224
PAIR = 2 * IMG
LANES = 128
SCALE = HD ** (-0.5)
F32 = jnp.float32
BF16 = jnp.bfloat16
TAPS = [(a, b) for a in range(3) for b in range(3)]


def mm(a, b):
    return lax.dot_general(a, b, (((1,), (0,)), ((), ())), preferred_element_type=F32)


def mm_nt(a, b):
    return lax.dot_general(a, b, (((1,), (1,)), ((), ())), preferred_element_type=F32)


def mm_tn(a, b):
    return lax.dot_general(a, b, (((0,), (0,)), ((), ())), preferred_element_type=F32)


def row_index(rows):
    return lax.broadcasted_iota(jnp.int32, (rows, 1), 0)


def live_rows(rows):
    return lax.rem(row_index(rows), IMG) < LIVE


def column_masks(rows):
    place = lax.rem(row_index(rows), IMG)
    column = lax.rem(place, SIDE)
    live = place < LIVE
    return [(live & (column + b - 1 >= 0) & (column + b - 1 < SIDE)).astype(F32) for b in range(3)]


def rolled(values, by):
    by = by % values.shape[0]
    return values if by == 0 else pltpu.roll(values, by, 0)


def norm_parts(values):
    center = values - jnp.mean(values, axis=-1, keepdims=True)
    spread = jnp.mean(center * center, axis=-1, keepdims=True)
    rstd = lax.rsqrt(spread + EPSILON)
    return center * rstd, rstd


def column_sum(values):
    return jnp.sum(values, axis=0, keepdims=True)


def head_lanes(head):
    lane = lax.broadcasted_iota(jnp.int32, (1, LANES), 1)
    return (lane // HD) == head


def only(values, mask):
    return jnp.where(mask, values, jnp.zeros_like(values))


def mix_forward(layer, channel, u_in, u_out, w, small, mask, bias, c_ref, xhat, rstd, n_ref, t_ref, p_ref, m_ref):
    base = 12 * layer
    row = lambda r: small[layer, r:r + 1, :]
    v = u_in[...].astype(F32)
    masks = column_masks(ROWS)
    total = v + row(9)
    for b in range(3):
        part = jnp.zeros_like(v)
        for a in range(3):
            part = part + row(3 * a + b) * rolled(v, -(SIDE * (a - 1) + b - 1))
        total = total + part * masks[b]
    c = jnp.where(live_rows(ROWS), total, 0.0)
    c_ref[...] = c
    x, r = norm_parts(c)
    xhat[...] = x
    rstd[...] = r
    n_ref[...] = (x * row(10) + row(11)).astype(BF16)

    @pl.loop(0, 3)
    def _(j):
        cols = pl.ds(pl.multiple_of(W * j, W), W)
        t_ref[:, cols] = (mm(n_ref[...], w[base + j]) + small[layer, pl.ds(12 + j, 1), :]).astype(BF16)

    @pl.loop(0, 6)
    def _(g):
        qs = pl.ds(pl.multiple_of(LANES * g, LANES), LANES)
        ks = pl.ds(pl.multiple_of(W + LANES * g, LANES), LANES)
        vs = pl.ds(pl.multiple_of(2 * W + LANES * g, LANES), LANES)
        for pair in range(2):
            rows = slice(PAIR * pair, PAIR * pair + PAIR)
            q, k, val = t_ref[rows, qs], t_ref[rows, ks], t_ref[rows, vs]
            mix = jnp.zeros((PAIR, LANES), F32)
            if channel:
                for im in range(2):
                    here = (row_index(PAIR) // IMG) == im
                    km = k * only(mask[rows, :], here)
                    s = mm_tn(q, km) * SCALE + bias[...]
                    e = jnp.exp(s - jnp.max(s, axis=-1, keepdims=True))
                    p = e / jnp.sum(e, axis=-1, keepdims=True)
                    p_ref[g, 2 * pair + im] = p
                    mix = mix + mm_nt(only(val, here), p.astype(BF16))
            else:
                for head in range(4):
                    lanes = head_lanes(head)
                    s = mm_nt(only(q, lanes), k) * SCALE + bias[...]
                    e = jnp.exp(s - jnp.max(s, axis=-1, keepdims=True))
                    p = e / jnp.sum(e, axis=-1, keepdims=True)
                    p_ref[g, 4 * pair + head] = p
                    mix = mix + mm(p.astype(BF16), only(val, lanes))
            m_ref[rows, qs] = mix.astype(BF16)

    out = c_ref[...] + mm(m_ref[...], w[base + 3]) + row(15)
    u_out[...] = jnp.where(live_rows(ROWS), out, 0.0).astype(BF16)


def mix_backward(layer, channel, u_in, g_in, g_out, w, small, mask, sg, dw, c_ref, xhat, rstd, n_ref, t_ref, p_ref, m_ref, dm_ref, dt_ref, acc):
    base = 12 * layer
    row = lambda r: small[layer, r:r + 1, :]
    g = g_in[...]
    sg[layer, 15:16, :] = column_sum(g.astype(F32))
    dm_ref[...] = mm_nt(g, w[base + 3]).astype(BF16)
    dw(layer, 3, m_ref, lambda: g_in[...])

    @pl.loop(0, 6)
    def _(grp):
        qs = pl.ds(pl.multiple_of(LANES * grp, LANES), LANES)
        ks = pl.ds(pl.multiple_of(W + LANES * grp, LANES), LANES)
        vs = pl.ds(pl.multiple_of(2 * W + LANES * grp, LANES), LANES)
        for pair in range(2):
            rows = slice(PAIR * pair, PAIR * pair + PAIR)
            q, k, val, dm = t_ref[rows, qs], t_ref[rows, ks], t_ref[rows, vs], dm_ref[rows, qs]
            dq = jnp.zeros((PAIR, LANES), F32)
            dk = jnp.zeros((PAIR, LANES), F32)
            dv = jnp.zeros((PAIR, LANES), F32)
            if channel:
                for im in range(2):
                    here = (row_index(PAIR) // IMG) == im
                    keep = only(mask[rows, :], here)
                    km = k * keep
                    p = p_ref[grp, 2 * pair + im]
                    dmh = only(dm, here)
                    dp = mm_tn(dmh, val)
                    dv = dv + mm(dmh, p.astype(BF16))
                    ds = (p * (dp - jnp.sum(dp * p, axis=-1, keepdims=True))).astype(BF16)
                    dq = dq + mm_nt(km, ds)
                    dk = dk + mm(only(q, here), ds) * keep.astype(F32)
            else:
                for head in range(4):
                    lanes = head_lanes(head)
                    p = p_ref[grp, 4 * pair + head]
                    dmh = only(dm, lanes)
                    dp = mm_nt(dmh, val)
                    dv = dv + mm_tn(p.astype(BF16), dmh)
                    ds = (p * (dp - jnp.sum(dp * p, axis=-1, keepdims=True))).astype(BF16)
                    dq = dq + mm(ds, only(k, lanes))
                    dk = dk + mm_tn(ds, only(q, lanes))
            dt_ref[rows, qs] = (dq * SCALE).astype(BF16)
            dt_ref[rows, ks] = (dk * SCALE).astype(BF16)
            dt_ref[rows, vs] = dv.astype(BF16)

    acc[...] = jnp.zeros_like(acc)

    @pl.loop(0, 3)
    def _(j):
        cols = pl.ds(pl.multiple_of(W * j, W), W)
        acc[...] += mm_nt(dt_ref[:, cols], w[base + j])
        sg[layer, pl.ds(12 + j, 1), :] = column_sum(dt_ref[:, cols].astype(F32))
        dw(layer, j, n_ref, lambda: dt_ref[:, cols])

    dn = acc[...]
    x = xhat[...]
    sg[layer, 10:11, :] = column_sum(dn * x)
    sg[layer, 11:12, :] = column_sum(dn)
    e = dn * row(10)
    inner = rstd[...] * (e - jnp.mean(e, axis=-1, keepdims=True) - x * jnp.mean(e * x, axis=-1, keepdims=True))
    dc = jnp.where(live_rows(ROWS), g_in[...].astype(F32) + inner, 0.0)
    sg[layer, 9:10, :] = column_sum(dc)
    v = u_in[...].astype(F32)
    masks = column_masks(ROWS)
    du = dc
    for b in range(3):
        dcm = dc * masks[b]
        for a in range(3):
            moved = rolled(dcm, SIDE * (a - 1) + b - 1)
            tap = 3 * a + b
            du = du + row(tap) * moved
            sg[layer, tap:tap + 1, :] = column_sum(moved * v)
    g_out[...] = jnp.where(live_rows(ROWS), du, 0.0).astype(BF16)


ROOT_HALF = 0.5 ** 0.5
ROOT_TWO_PI = 0.3989422804014327


def ff_forward(layer, u_in, u_out, w, small, xhat, rstd, n_ref, slope, acc):
    base = 12 * layer
    row = lambda r: small[layer, r:r + 1, :]
    x, r = norm_parts(u_in[...].astype(F32))
    xhat[...] = x
    rstd[...] = r
    n_ref[...] = (x * row(16) + row(17)).astype(BF16)
    acc[...] = u_in[...].astype(F32) + row(22)

    @pl.loop(0, 4)
    def _(j):
        cols = pl.ds(pl.multiple_of(W * j, W), W)
        h = mm(n_ref[...], w[base + 4 + j]) + small[layer, pl.ds(18 + j, 1), :]
        cdf = 0.5 + 0.5 * lax.erf(h * ROOT_HALF)
        slope[:, cols] = cdf + h * (ROOT_TWO_PI * jnp.exp(-0.5 * h * h))
        acc[...] += mm((h * cdf).astype(BF16), w[base + 8 + j])

    u_out[...] = jnp.where(live_rows(ROWS), acc[...], 0.0).astype(BF16)


def ff_backward(layer, g_in, g_out, w, small, sg, xhat, rstd, slope, acc):
    base = 12 * layer
    row = lambda r: small[layer, r:r + 1, :]
    sg[layer, 22:23, :] = column_sum(g_in[...].astype(F32))
    acc[...] = jnp.zeros_like(acc)

    @pl.loop(0, 4)
    def _(j):
        cols = pl.ds(pl.multiple_of(W * j, W), W)
        dh = (mm_nt(g_in[...], w[base + 8 + j]) * slope[:, cols]).astype(BF16)
        sg[layer, pl.ds(18 + j, 1), :] = column_sum(dh.astype(F32))
        acc[...] += mm_nt(dh, w[base + 4 + j])

    dn = acc[...]
    x = xhat[...]
    sg[layer, 16:17, :] = column_sum(dn * x)
    sg[layer, 17:18, :] = column_sum(dn)
    e = dn * row(16)
    inner = rstd[...] * (e - jnp.mean(e, axis=-1, keepdims=True) - x * jnp.mean(e * x, axis=-1, keepdims=True))
    g_out[...] = jnp.where(live_rows(ROWS), g_in[...].astype(F32) + inner, 0.0).astype(BF16)


def chain_scratch():
    V = pltpu.VMEM
    mixer = [V((ROWS, W), F32), V((ROWS, 1), F32), V((ROWS, W), BF16), V((ROWS, 3 * W), BF16)]
    feed = [V((ROWS, W), F32), V((ROWS, 1), F32), V((ROWS, W), BF16), V((ROWS, 4 * W), F32)]
    return (mixer + [V((6, 8, PAIR, PAIR), F32), V((ROWS, W), BF16)] + feed + mixer + [V((6, 4, LANES, LANES), F32), V((ROWS, W), BF16)] + feed
            + [V((ROWS, W), F32), V((ROWS, W), F32), V((ROWS, W), BF16), V((ROWS, 3 * W), BF16), V((PAIR, PAIR), F32), V((LANES, LANES), F32)])


def fill_biases(win_bias, chan_bias):
    qi = lax.broadcasted_iota(jnp.int32, (PAIR, PAIR), 0)
    ki = lax.broadcasted_iota(jnp.int32, (PAIR, PAIR), 1)
    win_bias[...] = jnp.where(((qi // IMG) == (ki // IMG)) & (lax.rem(ki, IMG) < LIVE), 0.0, -1e30).astype(F32)
    ci = lax.broadcasted_iota(jnp.int32, (LANES, LANES), 0)
    ei = lax.broadcasted_iota(jnp.int32, (LANES, LANES), 1)
    chan_bias[...] = jnp.where((ci // HD) == (ei // HD), 0.0, -1e30).astype(F32)


class Chain:
    def __init__(self, w, small, mask, u, g, sg, dw, scratch):
        self.w, self.small, self.mask, self.u, self.g, self.sg, self.dw = w, small, mask, u, g, sg, dw
        s = scratch
        self.window, self.feed0, self.channel, self.feed1 = s[0:6], s[6:10], s[10:16], s[16:20]
        self.c_ref, self.acc, self.dm, self.dt, self.win_bias, self.chan_bias = s[20:26]

    def forward(self, k):
        u, w, small = self.u, self.w, self.small
        if k == 0:
            fill_biases(self.win_bias, self.chan_bias)
            mix_forward(0, False, u[0], u[1], w, small, self.mask, self.win_bias, self.c_ref, *self.window)
        if k == 1:
            ff_forward(0, u[1], u[2], w, small, *self.feed0, self.acc)
        if k == 2:
            mix_forward(1, True, u[2], u[3], w, small, self.mask, self.chan_bias, self.c_ref, *self.channel)
        if k == 3:
            ff_forward(1, u[3], u[4], w, small, *self.feed1, self.acc)

    def backward(self, k):
        u, g, w, small, sg = self.u, self.g, self.w, self.small, self.sg
        if k in (0, 2):
            parts = self.channel if k == 2 else self.window
            mix_backward(k // 2, k == 2, u[k], g[k + 1], g[k], w, small, self.mask, sg, self.dw, self.c_ref, *parts, self.dm, self.dt, self.acc)
        else:
            x, r, _, slope = self.feed0 if k == 1 else self.feed1
            ff_backward(k // 2, g[k + 1], g[k], w, small, sg, x, r, slope, self.acc)


MESH = pl.DeviceIdType.MESH
STRIP = 96


def slot(item, line, d):
    red = lax.rem(item, 3) // 2
    block = 12 * (item // 3) + 4 * lax.rem(item, 3) + (1 - red) * line + red * (d // 2)
    row = (1 - red) * STRIP * d + red * (4 * STRIP * lax.rem(d, 2) + STRIP * line)
    return block, row


def other_planes(z):
    near = z + 1 - 2 * (z // 2)
    far = 3 * (1 - z // 2)
    return near, 6 - z - near - far, far


class Place:
    def __init__(self):
        self.s = lax.axis_index("segment")
        self.d = lax.axis_index("dp")
        self.z = self.d // 2
        self.c = lax.rem(self.d, 2)
        self.xn = self.s + 1 - 2 * lax.rem(self.s, 2)
        self.yn = lax.rem(self.s + 2, 4)
        self.dn = 3 - self.s
        self.twin = self.d + 1 - 2 * self.c


def greet_neighbours(at):
    bar = pltpu.get_barrier_semaphore()

    def greet(seg, dev):
        pl.semaphore_signal(bar, inc=1, device_id=(seg, dev), device_id_type=MESH)

    greet(at.xn, at.d)
    greet(at.yn, at.d)
    greet(at.s, at.twin)

    @pl.when(at.z < 3)
    def _():
        greet(at.s, at.d + 2)

    @pl.when(at.z > 0)
    def _():
        greet(at.s, at.d - 2)

    pl.semaphore_wait(bar, 4 + (at.z * (3 - at.z)) // 2)


def remote(src, dst, ssem, rsem, seg, dev):
    return pltpu.make_async_remote_copy(src, dst, ssem, rsem, device_id=(seg, dev), device_id_type=MESH)


def gather_scratch():
    D = pltpu.SemaphoreType.DMA
    return [D((2, 9)), D((6, 5)), D((6, 3, 2)), D((6, 3, 2)), D((6, 4, 4)), D((2, 3, 4)), D((2, 3, 4))]


class Gather:
    def __init__(self, at, shards, wbuf, sems):
        self.at, self.shards, self.w = at, shards, wbuf
        self.lsem, self.zs, self.xs, self.ys, self.pr, self.cs, self.cr = sems
        self.planes = other_planes(at.z)
        self.away = 2 * (at.z // 2) - 1
        self.inner = (at.z == 1) | (at.z == 2)
        self.groups = [(layer, part, k) for layer in range(2) for part in range(3) for k in range(3)]

    def strip(self, item, line, plane):
        block, row = slot(item, line, 2 * plane + self.at.c)
        return self.w.at[block, pl.ds(pl.multiple_of(row, STRIP), STRIP), :]

    def quad_ref(self, layer, part, plane, core):
        if part == 2:
            return self.w.at[12 * layer + 8 + plane, pl.ds(pl.multiple_of(4 * STRIP * core, 4 * STRIP), 4 * STRIP), :]
        row = pl.multiple_of(STRIP * (2 * plane + core), STRIP)
        return self.w.at[pl.ds(12 * layer + 4 * part, 4), pl.ds(row, STRIP), :]

    def quad(self, layer, part, plane, core, k):
        ref = self.quad_ref(layer, part, plane, core)
        return remote(ref, ref, self.cs.at[layer, part, k], self.cr.at[layer, part, plane], self.at.s, self.at.twin)

    def local(self, layer):
        triple, output, expand, reduce = self.shards
        at, w, base = self.at, self.w, 12 * layer
        rows = pl.ds(pl.multiple_of(STRIP * at.d, STRIP), STRIP)
        sems = self.lsem.at
        copies = [pltpu.make_async_copy(triple.at[layer, :, pl.ds(W * j, W)], w.at[base + j, rows, :], sems[layer, j]) for j in range(3)]
        copies.append(pltpu.make_async_copy(output.at[layer], w.at[base + 3, rows, :], sems[layer, 3]))
        copies += [pltpu.make_async_copy(expand.at[layer, :, pl.ds(W * j, W)], w.at[base + 4 + j, rows, :], sems[layer, 4 + j]) for j in range(4)]
        half = pl.ds(pl.multiple_of(4 * STRIP * at.c, 4 * STRIP), 4 * STRIP)
        copies.append(pltpu.make_async_copy(reduce.at[layer], w.at[base + 8 + at.z, half, :], sems[layer, 8]))
        return copies

    def up(self, item):
        ref = self.strip(item, self.at.s, self.at.z)
        return remote(ref, ref, self.zs.at[item, 0], self.pr.at[item, self.at.z, self.at.s], self.at.s, self.at.d + 2)

    def down(self, item):
        ref = self.strip(item, self.at.s, self.at.z)
        return remote(ref, ref, self.zs.at[item, 1], self.pr.at[item, self.at.z, self.at.s], self.at.s, self.at.d - 2)

    def onward(self, item, k):
        step = self.away if k != 1 else -self.away
        ref = self.strip(item, self.at.s, self.planes[k])
        return remote(ref, ref, self.zs.at[item, 2 + k], self.pr.at[item, self.planes[k], self.at.s], self.at.s, self.at.d + 2 * step)

    def to_x(self, item, k, line, j):
        ref = self.strip(item, line, self.planes[k])
        return remote(ref, ref, self.xs.at[item, k, j], self.pr.at[item, self.planes[k], line], self.at.xn, self.at.d)

    def to_y(self, item, k, line, j):
        ref = self.strip(item, line, self.planes[k])
        return remote(ref, ref, self.ys.at[item, k, j], self.pr.at[item, self.planes[k], line], self.at.yn, self.at.d)

    def arrival(self, item, k, line):
        ref = self.strip(item, line, self.planes[k])
        return remote(ref, ref, self.zs.at[item, 0], self.pr.at[item, self.planes[k], line], self.at.s, self.at.twin)

    def ends(self, item, act):
        @pl.when(self.at.z < 3)
        def _():
            act(self.up(item))

        @pl.when(self.at.z > 0)
        def _():
            act(self.down(item))

    def begin(self):
        at = self.at
        copies = [self.local(layer) for layer in range(2)]
        for layer in range(2):
            for copy in copies[layer]:
                copy.start()
        for copy in copies[0]:
            copy.wait()
        self.ends(0, lambda copy: copy.start())
        for part in range(3):
            self.quad(0, part, at.z, at.c, 3).start()
        for copy in copies[1]:
            copy.wait()
        for part in range(3):
            self.quad(1, part, at.z, at.c, 3).start()

    def stage_a(self, layer, part, k):
        item = 3 * layer + part
        self.arrival(item, k, self.at.s).wait_recv()

        @pl.when(self.inner)
        def _():
            self.onward(item, k).start()

        self.to_x(item, k, self.at.s, 0).start()
        self.to_y(item, k, self.at.s, 0).start()

    def stage_b(self, layer, part, k):
        item = 3 * layer + part
        self.arrival(item, k, self.at.xn).wait_recv()
        if (part + k + layer) % 2 == 0:
            self.to_y(item, k, self.at.xn, 1).start()
        self.arrival(item, k, self.at.yn).wait_recv()
        if (part + k + layer) % 2 == 1:
            self.to_x(item, k, self.at.yn, 1).start()

    def stage_c(self, layer, part, k):
        item = 3 * layer + part
        self.arrival(item, k, self.at.dn).wait_recv()
        self.quad(layer, part, self.planes[k], self.at.c, k).start()

    def step(self, g):
        n = len(self.groups)
        if g < n and g % 3 == 0 and g // 3 + 1 < 6:
            self.ends(g // 3 + 1, lambda copy: copy.start())
        if g < n:
            self.stage_a(*self.groups[g])
        if 0 <= g - 1 < n:
            self.stage_b(*self.groups[g - 1])
        if 0 <= g - 2 < n:
            self.stage_c(*self.groups[g - 2])

    def settle(self, layer, part):
        for k in range(3):
            self.quad(layer, part, self.planes[k], 1 - self.at.c, k).wait_recv()
        self.quad(layer, part, self.at.z, 1 - self.at.c, 3).wait_recv()

    def drain(self):
        at = self.at
        for layer in range(2):
            for part in range(3):
                item = 3 * layer + part
                self.ends(item, lambda copy: copy.wait_send())
                self.quad(layer, part, at.z, at.c, 3).wait_send()
                for k in range(3):
                    @pl.when(self.inner)
                    def _():
                        self.onward(item, k).wait_send()

                    self.to_x(item, k, at.s, 0).wait_send()
                    self.to_y(item, k, at.s, 0).wait_send()
                    if (part + k + layer) % 2 == 0:
                        self.to_y(item, k, at.xn, 1).wait_send()
                    else:
                        self.to_x(item, k, at.yn, 1).wait_send()
                    self.quad(layer, part, self.planes[k], at.c, k).wait_send()


def chain_kernel(triple, output, expand, reduce, small, x, mask, gin, u_out, g_out, sg, mix_out, fw_out, w, osem, *scratch):
    at = Place()
    gather = Gather(at, (triple, output, expand, reduce), w, scratch[:7])
    u = [x] + [u_out.at[i] for i in range(4)]
    g = [g_out.at[i] for i in range(4)] + [gin]

    def dw(layer, j, lhs, rhs):
        w[12 * layer + j] = mm_tn(lhs[...], rhs()).astype(BF16)

    chain = Chain(w, small, mask, u, g, sg, dw, scratch[7:])
    sg[...] = jnp.zeros_like(sg)
    greet_neighbours(at)
    gather.begin()
    for step in range(20):
        gather.step(step)
    for layer in range(2):
        for part in range(3):
            gather.settle(layer, part)
    gather.drain()
    for k in range(4):
        chain.forward(k)
    for k in (3, 2, 1, 0):
        chain.backward(k)
    lay, quarter = at.s // 2, 2 * lax.rem(at.s, 2) + at.c
    keep = [pltpu.make_async_copy(w.at[pl.ds(12 * i, 4)], mix_out.at[pl.ds(4 * i, 4)], osem.at[i]) for i in range(2)]
    keep += [pltpu.make_async_copy(w.at[12 * lay + 4 + 4 * i + quarter], fw_out.at[i], osem.at[2 + i]) for i in range(2)]
    for copy in keep:
        copy.start()
    for copy in keep:
        copy.wait()


def chain_call(triple, output, expand, reduce, small, x, mask, gin):
    V = pltpu.VMEM
    S = jax.ShapeDtypeStruct
    anywhere = pl.BlockSpec(memory_space=pl.ANY)
    vmem = pl.BlockSpec(memory_space=V)
    return pl.pallas_call(
        chain_kernel,
        out_shape=(S((4, ROWS, W), BF16), S((4, ROWS, W), BF16), S((2, 24, W), F32), S((8, W, W), BF16), S((2, W, W), BF16)),
        in_specs=[anywhere] * 4 + [vmem] * 4,
        out_specs=[vmem] * 3 + [anywhere] * 2,
        scratch_shapes=[V((24, W, W), BF16), pltpu.SemaphoreType.DMA((4,))] + gather_scratch() + chain_scratch(),
        compiler_params=pltpu.CompilerParams(collective_id=1, has_side_effects=True, vmem_limit_bytes=63 * 1024 * 1024),
        name="gather_and_chain",
    )(triple, output, expand, reduce, small, x, mask, gin)


def greet_all(at):
    bar = pltpu.get_barrier_semaphore()

    def greet(seg, dev):
        pl.semaphore_signal(bar, inc=1, device_id=(seg, dev), device_id_type=MESH)

    for seg in (at.xn, at.yn, at.dn):
        greet(seg, at.d)
        greet(seg, at.twin)
    greet(at.s, at.twin)
    greet(at.s, lax.rem(at.d + 4, 8))

    @pl.when(at.z < 3)
    def _():
        greet(at.s, at.d + 2)

    @pl.when(at.z > 0)
    def _():
        greet(at.s, at.d - 2)

    pl.semaphore_wait(bar, 9 + (at.z * (3 - at.z)) // 2)


def add_into(total, term):
    total[...] = (total[...].astype(F32) + term[...].astype(F32)).astype(BF16)


class PlaneSum:
    def __init__(self, at, below, above, ssem, bsem, asem):
        self.at, self.below, self.above, self.ssem, self.bsem, self.asem = at, below, above, ssem, bsem, asem

    def up(self, i, ref):
        return remote(ref, self.below.at[i], self.ssem.at[i], self.bsem.at[i], self.at.s, self.at.d + 2)

    def down(self, i, ref):
        return remote(ref, self.above.at[i], self.ssem.at[i], self.asem.at[i], self.at.s, self.at.d - 2)

    def from_below(self, i, ref):
        @pl.when(self.at.z > 0)
        def _():
            self.up(i, ref).wait_recv()
            add_into(ref, self.below.at[i])

    def from_above(self, i, ref):
        @pl.when(self.at.z < 3)
        def _():
            self.down(i, ref).wait_recv()
            add_into(ref, self.above.at[i])

    def step(self, i, ref, goal):
        z = self.at.z

        @pl.when(z <= goal)
        def _():
            self.from_below(i, ref)

        @pl.when(z >= goal)
        def _():
            self.from_above(i, ref)

        @pl.when(z < goal)
        def _():
            self.up(i, ref).start()

        @pl.when(z > goal)
        def _():
            self.down(i, ref).start()

    def drain(self, i, ref, goal):
        @pl.when(self.at.z < goal)
        def _():
            self.up(i, ref).wait_send()

        @pl.when(self.at.z > goal)
        def _():
            self.down(i, ref).wait_send()


def goal_order(z):
    far = 3 * (1 - z // 2)
    near = 2 - z // 2
    return far, near, 6 - far - near - z, z


UNITS = [("mix", layer, j) for layer in range(2) for j in range(4)]
UNITS += [("exp", layer, j) for layer in range(2) for j in range(4)]
UNITS += [("red", layer, j) for layer in range(2) for j in range(2)]


def sum_kernel(u, g, cot, mix, fw, small, sg, sec_out, grad_out, fin, sg_out,
               xin, gin, nbuf, abuf, dhbuf, fwv, dwe, dwr, mown, mrx, prx, below_m, above_m, below_f, above_f, sgr, sga,
               lsem, xsend, xrecv, gsend, grecv, tws, twr, osend, orecv, msend, mrecv, psend, precv,
               zms, zmb, zma, zfs, zfb, zfa, fsend, frecv, sgs, sgv):
    at = Place()
    s, d, z, c = at.s, at.d, at.z, at.c
    lay = s // 2
    quarter = 2 * lax.rem(s, 2) + c
    segs = (at.xn, at.yn, at.dn)
    greet_all(at)

    weights = pltpu.make_async_copy(fw, fwv, lsem.at[0])
    weights.start()
    strips = []
    for p in range(4):
        rows = pl.ds(pl.multiple_of(2 * STRIP * p + STRIP * c, STRIP), STRIP)
        strips.append(pltpu.make_async_copy(mix.at[:, rows, :], mown.at[:, p], lsem.at[1 + p]))
        strips[-1].start()
    seeds = [pltpu.make_async_copy(cot.at[t], gin.at[2 * t + c], lsem.at[5 + t]) for t in range(4)]

    @pl.when(s >= 2)
    def _():
        for copy in seeds:
            copy.start()

    def x_send(i):
        t = segs[i]
        return remote(u.at[2 * (t // 2)], xin.at[2 * s + c], xsend.at[i], xrecv.at[s], t, d)

    def g_send(i):
        return remote(g.at[2], gin.at[2 * s + c], gsend.at[i], grecv.at[s], segs[i], d)

    def x_arrival(t):
        return remote(xin.at[2 * t + c], xin.at[2 * t + c], xsend.at[0], xrecv.at[t], s, at.twin)

    def g_arrival(t):
        return remote(gin.at[2 * t + c], gin.at[2 * t + c], gsend.at[0], grecv.at[t], s, at.twin)

    def x_twin(t, core):
        return remote(xin.at[2 * t + core], xin.at[2 * t + core], tws.at[0, t], twr.at[0, t], s, at.twin)

    def g_twin(t, core):
        return remote(gin.at[2 * t + core], gin.at[2 * t + core], tws.at[1, t], twr.at[1, t], s, at.twin)

    for i in range(3):
        x_send(i).start()

        @pl.when(segs[i] < 2)
        def _():
            g_send(i).start()

    def twin_mix(p):
        mine = pl.ds(pl.multiple_of(2 * STRIP * p + STRIP * (1 - c), STRIP), STRIP)
        return remote(mix.at[:, mine, :], mrx.at[:, p], msend.at[p], mrecv.at[p], s, at.twin)

    for p in range(4):
        twin_mix(p).start()
    xin[2 * s + c] = u[2 * lay]
    x_twin(s, c).start()

    @pl.when(s < 2)
    def _():
        gin[2 * s + c] = g[2]
        g_twin(s, c).start()

    @pl.when(s >= 2)
    def _():
        for t in range(4):
            seeds[t].wait()
            g_twin(t, c).start()

    partners = [(s, at.twin), (at.xn, d), (at.yn, d), (s, d + 2 * (1 - 2 * lax.rem(z, 2))), (s, lax.rem(d + 4, 8))]

    def sg_round(r):
        return remote(sga.at[r], sgr.at[r], sgs.at[r], sgv.at[r], *partners[r])

    sga[0] = sg[...]
    sg_round(0).start()

    for p in range(4):
        strips[p].wait()
        twin_mix(p).wait_recv()

        @pl.loop(0, 8)
        def _(b):
            add_into(mown.at[b, p], mrx.at[b, p])

    def plane_send(i, layer):
        return remote(mown.at[4 * layer + segs[i]], prx.at[i, layer], psend.at[i, layer], precv.at[i, layer], segs[i], d)

    for layer in (1, 0):
        for i in range(3):
            plane_send(i, layer).start()

    def sg_next(r):
        sg_round(r).wait_recv()
        sga[r + 1] = sga[r] + sgr[r]
        if r < 4:
            sg_round(r + 1).start()

    sg_next(0)

    def out_send(i, which):
        src, dst = (u, sec_out) if which == 0 else (g, grad_out)
        return remote(src.at[segs[i]], dst.at[s], osend.at[which, i], orecv.at[which, i], segs[i], d)

    keep = [pltpu.make_async_copy(u.at[s], sec_out.at[s], lsem.at[9]), pltpu.make_async_copy(g.at[s], grad_out.at[s], lsem.at[10])]
    for which in range(2):
        for i in range(3):
            out_send(i, which).start()
        keep[which].start()
    sg_next(1)
    weights.wait()

    def feed_rows(i):
        x, _ = norm_parts(xin[i].astype(F32))
        n = (x * small[lay, 16:17, :] + small[lay, 17:18, :]).astype(BF16)
        nbuf[i] = n
        h = mm(n, fwv[0]) + small[lay, pl.ds(18 + quarter, 1), :]
        cdf = 0.5 + 0.5 * lax.erf(h * ROOT_HALF)
        abuf[i] = (h * cdf).astype(BF16)
        slope = cdf + h * (ROOT_TWO_PI * jnp.exp(-0.5 * h * h))
        dhbuf[i] = (mm_nt(gin[i], fwv[1]) * slope).astype(BF16)

    for i in range(4):
        t = s if i == 0 else segs[i - 1]
        if i > 0:
            x_arrival(t).wait_recv()
            x_twin(t, c).start()

            @pl.when(s < 2)
            def _():
                g_arrival(t).wait_recv()
                g_twin(t, c).start()

        if i > 0:
            sg_next(i + 1)
        x_twin(t, 1 - c).wait_recv()
        g_twin(t, 1 - c).wait_recv()

        @pl.loop(0, 2)
        def _(core):
            feed_rows(2 * t + core)

    goals = goal_order(z)
    mix_sum = PlaneSum(at, below_m, above_m, zms, zmb, zma)
    for layer in (1, 0):
        for i in range(3):
            plane_send(i, layer).wait_recv()

            @pl.loop(0, 4)
            def _(p):
                add_into(mown.at[4 * layer + s, p], prx.at[i, layer, p])

        for goal in goals[:2]:
            mix_sum.step(4 * layer + goal, mown.at[4 * layer + s, goal], goal)

    feed_sum = PlaneSum(at, below_f, above_f, zfs, zfb, zfa)
    stack = lambda ref: ref[...].reshape(8 * ROWS, W)

    def product(out, left, right):
        for i in range(3):
            cols = slice(256 * i, 256 * i + 256)
            lhs = left[:, :, cols].reshape(8 * ROWS, 256)
            out[cols, :] = mm_tn(lhs, stack(right)).astype(BF16)

    def part(ref, i):
        return ref.at[pl.ds(pl.multiple_of(2 * STRIP * i, 2 * STRIP), 2 * STRIP), :]

    product(dwe, nbuf, dhbuf)
    for goal in goals[:2]:
        feed_sum.step(goal, part(dwe, goal), goal)
    product(dwr, abuf, gin)
    for i in range(4):
        feed_sum.step(4 + i, part(dwr, i), quarter)
    for goal in goals[2:]:
        for layer in (1, 0):
            mix_sum.step(4 * layer + goal, mown.at[4 * layer + s, goal], goal)
    for goal in goals[2:]:
        feed_sum.step(goal, part(dwe, goal), goal)

    def unit(kind, layer, j):
        if kind == "mix":
            return 4 * layer + j, j, c, fin.at[layer, j], lambda p: mown.at[4 * layer + s, z]
        if kind == "exp":
            src = lambda p: dwe.at[pl.ds(pl.multiple_of(2 * STRIP * z + STRIP * p, STRIP), STRIP), :]
            return 8 + 4 * layer + j, 2 * layer + j // 2, j % 2, fin.at[layer, 4 + j], src
        src = lambda p: dwr.at[pl.ds(pl.multiple_of(4 * STRIP * p + 2 * STRIP * j, 2 * STRIP), 2 * STRIP), :]
        return 16 + 2 * layer + j, 2 * layer + z // 2, lax.rem(z, 2), fin.at[layer, pl.ds(8 + 2 * j, 2)], src

    def pieces(kind, layer, j):
        index, owner, core, dst, src = unit(kind, layer, j)
        by_x = index % 2 == 0
        cores = (c,) if kind == "mix" else (0, 1)
        owns = (s == owner) if kind == "mix" else ((s == owner) & (c == core))
        sends = []
        for n, p in enumerate(cores):
            dev = d if kind == "mix" else 2 * z + p
            ref = src(p)
            if kind == "red":
                ref = [ref.at[pl.ds(0, STRIP), :], ref.at[pl.ds(STRIP, STRIP), :]]
                targets = [dst.at[0], dst.at[1]]
            else:
                ref, targets = [ref], [dst]
            for m in range(len(ref)):
                for k, seg in enumerate((at.xn, at.yn)):
                    sends.append((owns, remote(ref[m], targets[m], fsend.at[index, n, m, k], frecv.at[index, m], seg, dev)))
                if kind == "mix":
                    sends.append((owns, pltpu.make_async_copy(ref[m], targets[m], frecv.at[index, m])))
                else:
                    sends.append((owns & (c == p), pltpu.make_async_copy(ref[m], targets[m], frecv.at[index, m])))
                    sends.append((owns & (c != p), remote(ref[m], targets[m], fsend.at[index, n, m, 2], frecv.at[index, m], s, at.twin)))
        return index, owner, owns, by_x, dst, sends

    def parts_of(kind, dst):
        return [dst.at[0], dst.at[1]] if kind == "red" else [dst]

    done = []
    for kind, layer, j in UNITS:
        index, owner, owns, by_x, dst, sends = pieces(kind, layer, j)
        for cond, copy in sends:
            @pl.when(cond)
            def _():
                copy.start()

        done.append((kind, index, owner, by_x, dst, sends))
    for kind, index, owner, by_x, dst, sends in done:
        first, then = (at.xn, at.yn) if by_x else (at.yn, at.xn)
        for m, ref in enumerate(parts_of(kind, dst)):
            relay = remote(ref, ref, fsend.at[index, 0, m, 3], frecv.at[index, m], then, d)
            relay.wait_recv()

            @pl.when(owner == first)
            def _():
                relay.start()

    sg_out[...] = sga[5]
    for r in range(5):
        sg_round(r).wait_send()
    for kind, index, owner, by_x, dst, sends in done:
        first, then = (at.xn, at.yn) if by_x else (at.yn, at.xn)
        for cond, copy in sends:
            if hasattr(copy, "wait_send") and copy.is_remote:
                @pl.when(cond)
                def _():
                    copy.wait_send()

        for m, ref in enumerate(parts_of(kind, dst)):
            relay = remote(ref, ref, fsend.at[index, 0, m, 3], frecv.at[index, m], then, d)

            @pl.when(owner == first)
            def _():
                relay.wait_send()

    for i in range(3):
        x_send(i).wait_send()

        @pl.when(segs[i] < 2)
        def _():
            g_send(i).wait_send()

        for which in range(2):
            out_send(i, which).wait()
        for layer in range(2):
            plane_send(i, layer).wait_send()
    for t in range(4):
        x_twin(t, c).wait_send()
        g_twin(t, c).wait_send()
    for copy in keep:
        copy.wait()
    for p in range(4):
        twin_mix(p).wait_send()
    for goal in range(4):
        for layer in range(2):
            mix_sum.drain(4 * layer + goal, mown.at[4 * layer + s, goal], goal)
        feed_sum.drain(goal, part(dwe, goal), goal)
        feed_sum.drain(4 + goal, part(dwr, goal), quarter)


def sum_call(u, g, cot, mix, fw, small, sg):
    V = pltpu.VMEM
    D = pltpu.SemaphoreType.DMA
    S = jax.ShapeDtypeStruct
    anywhere = pl.BlockSpec(memory_space=pl.ANY)
    vmem = pl.BlockSpec(memory_space=V)
    rows = V((8, ROWS, W), BF16)
    block = V((W, W), BF16)
    return pl.pallas_call(
        sum_kernel,
        out_shape=(S((4, ROWS, W), BF16), S((4, ROWS, W), BF16), S((2, 12, STRIP, W), BF16), S((2, 24, W), F32)),
        in_specs=[vmem, vmem, anywhere, anywhere, anywhere, vmem, vmem],
        out_specs=[anywhere, anywhere, anywhere, vmem],
        scratch_shapes=[
            rows, rows, rows, rows, rows, V((2, W, W), BF16), block, block,
            V((8, 4, STRIP, W), BF16), V((8, 4, STRIP, W), BF16), V((3, 2, 4, STRIP, W), BF16),
            V((8, STRIP, W), BF16), V((8, STRIP, W), BF16), V((8, 2 * STRIP, W), BF16), V((8, 2 * STRIP, W), BF16),
            V((5, 2, 24, W), F32), V((6, 2, 24, W), F32),
            D((11,)), D((3,)), D((4,)), D((3,)), D((4,)), D((2, 4)), D((2, 4)), D((2, 3)), D((2, 3)), D((4,)), D((4,)), D((3, 2)), D((3, 2)),
            D((8,)), D((8,)), D((8,)), D((8,)), D((8,)), D((8,)), D((20, 2, 2, 4)), D((20, 2)), D((5,)), D((5,)),
        ],
        compiler_params=pltpu.CompilerParams(collective_id=2, has_side_effects=True, vmem_limit_bytes=60 * 1024 * 1024),
        name="sum_gradients",
    )(u, g, cot, mix, fw, small, sg)


def pack_small(conv_weight, conv_bias, mixer_gain, mixer_shift, triple_bias, output_bias, feed_gain, feed_shift, expand_bias, reduce_bias):
    part = conv_bias.shape[1]
    rows = [conv_weight] + [
        v.reshape(2, -1, part)
        for v in (conv_bias, mixer_gain, mixer_shift, triple_bias, output_bias, feed_gain, feed_shift, expand_bias, reduce_bias)
    ]
    return jnp.concatenate(rows, axis=1)


def spread_small(packed):
    n = packed.shape[0]

    def rows(lo, hi):
        return jnp.transpose(packed[:, :, lo:hi], (1, 2, 0, 3)).reshape(2, hi - lo, W)

    def long(lo, hi):
        return jnp.transpose(packed[:, :, lo:hi], (1, 0, 2, 3)).reshape(2, hi - lo, W)

    zero = jnp.zeros((2, 1, W), packed.dtype)
    return jnp.concatenate([rows(0, 12), long(12, 15), rows(15, 18), long(18, 22), rows(22, 23), zero], axis=1)


def pad_images(rows):
    return jnp.pad(rows.reshape(-1, LIVE, rows.shape[1]), ((0, 0), (0, IMG - LIVE), (0, 0))).reshape(-1, rows.shape[1])


def unpad_images(rows):
    lead = rows.shape[:-2]
    return rows.reshape(lead + (-1, IMG, W))[..., :LIVE, :].reshape(lead + (-1, W))


def spread_body(
    patches, region_mask, conv_weight, conv_bias, mixer_gain, mixer_shift, triple_weight, triple_bias, output_weight,
    output_bias, feed_gain, feed_shift, expand_weight, expand_bias, reduce_weight, reduce_bias, cotangent,
):
    s = lax.axis_index("segment")
    d = lax.axis_index("dp")
    packed = pack_small(conv_weight, conv_bias, mixer_gain, mixer_shift, triple_bias, output_bias, feed_gain, feed_shift, expand_bias, reduce_bias)
    small = spread_small(lax.all_gather(packed, "dp", axis=0)).astype(F32)
    own = patches.shape[0] // lax.axis_size("segment")
    mine = lambda v: lax.dynamic_slice_in_dim(v, s * own, own, 0)
    x = pad_images(mine(patches))
    cot = pad_images(cotangent).reshape(4, ROWS, W)
    gin = lax.dynamic_index_in_dim(cot, s, 0, keepdims=False)
    mask = pad_images(mine(region_mask).astype(BF16)[:, None])
    u, g, sg, mix, fw = chain_call(triple_weight, output_weight, expand_weight, reduce_weight, small, x, mask, gin)
    sec_out, grad_out, fin, sg = sum_call(u, g, cot, mix, fw, small, sg)
    place = lambda v: unpad_images(v.reshape(1, 4 * ROWS, W))
    part = W // lax.axis_size("dp")
    fin = fin.astype(F32)
    wide = lambda lo, hi: jnp.concatenate([fin[:, j] for j in range(lo, hi)], axis=2)
    cut = lambda lo, hi: lax.dynamic_slice_in_dim(sg[:, lo:hi].reshape(2, -1), d * part * (hi - lo), part * (hi - lo), 1)
    taps = lax.dynamic_slice_in_dim(sg[:, :9], d * part, part, 2)
    return (
        place(sec_out), place(grad_out), taps, cut(9, 10), cut(10, 11), cut(11, 12), wide(0, 3), cut(12, 15), fin[:, 3],
        cut(15, 16), cut(16, 17), cut(17, 18), wide(4, 8), cut(18, 22), fin[:, 8:].reshape(2, 4 * part, W), cut(22, 23),
    )


def solution(mesh):
    in_specs = (
        P("dp", None),
        P("dp"),
        P(None, None, "dp"),
        P(None, "dp"),
        P(None, "dp"),
        P(None, "dp"),
        P(None, "dp", None),
        P(None, "dp"),
        P(None, "dp", None),
        P(None, "dp"),
        P(None, "dp"),
        P(None, "dp"),
        P(None, "dp", None),
        P(None, "dp"),
        P(None, "dp", None),
        P(None, "dp"),
        P("dp", None),
    )
    out_specs = (
        P("segment", "dp", None),
        P("segment", "dp", None),
        P(None, None, "dp"),
        P(None, "dp"),
        P(None, "dp"),
        P(None, "dp"),
        P(None, "dp", None),
        P(None, "dp"),
        P(None, "dp", None),
        P(None, "dp"),
        P(None, "dp"),
        P(None, "dp"),
        P(None, "dp", None),
        P(None, "dp"),
        P(None, "dp", None),
        P(None, "dp"),
    )
    chosen = spread_body if mesh.shape["dp"] == 8 and mesh.shape["segment"] == 4 else body
    return jax.shard_map(chosen, mesh=mesh, in_specs=in_specs, out_specs=out_specs, check_vma=False)
```

```python
from functools import partial

import jax
import jax.numpy as jnp
from jax import lax
from jax.experimental import pallas as pl
from jax.experimental.pallas import tpu as pltpu
from jax.sharding import PartitionSpec as P

HD = 32
SIDE = 7
MICRO = 4
IMG_MB = 4


EPSILON = 1e-05


def as_sent(x):

    def short(part):
        return part.astype(jnp.bfloat16) if part.dtype == jnp.float32 else part

    return jax.tree.map(short, x)


def shifted_2(x, axis, by):
    count = lax.axis_size(axis)
    pairs = [(i, i + by) for i in range(count) if 0 <= i + by < count]
    return lax.ppermute(x, axis, pairs)


def dot_last(first_operand, second_operand):
    return lax.dot_general(
        first_operand, second_operand, (((1,), (1,)), ((), ())), preferred_element_type=jnp.float32
    )


def dot_first(first_operand, second_operand):
    return lax.dot_general(
        first_operand, second_operand, (((0,), (0,)), ((), ())), preferred_element_type=jnp.float32
    )


def layer_norm(values, norm_gain, norm_shift):
    center = values - jnp.mean(values, axis=-1, keepdims=True)
    spread = jnp.mean(center * center, axis=-1, keepdims=True)
    return center * lax.rsqrt(spread + EPSILON) * norm_gain + norm_shift


def position_conv(stream, conv_weight, conv_bias):
    features = stream.shape[-1]
    planes = stream.reshape(-1, SIDE, SIDE, features)
    padded = jnp.pad(planes, ((0, 0), (1, 1), (1, 1), (0, 0)))
    summed = jnp.zeros_like(planes) + conv_bias
    for tap_row in range(3):
        for tap_col in range(3):
            summed = (
                summed
                + padded[:, tap_row : tap_row + SIDE, tap_col : tap_col + SIDE, :]
                * conv_weight[tap_row * 3 + tap_col]
            )
    return stream + summed.reshape(stream.shape)


def front_part(stream, conv_weight, conv_bias, norm_gain, norm_shift):
    shifted = position_conv(stream, conv_weight, conv_bias)
    return (shifted, layer_norm(shifted, norm_gain, norm_shift))


def gelu_exact(values):
    return jax.nn.gelu(values, approximate=False)


def softmax_rows(scores):
    row_max = jnp.max(scores, axis=-1, keepdims=True)
    lifted = jnp.exp(scores - row_max)
    return lifted / jnp.sum(lifted, axis=-1, keepdims=True)


def window_forward(triple):
    tokens = triple.shape[0]
    features = triple.shape[1] // 3
    pieces = triple.reshape(tokens // (SIDE * SIDE), SIDE * SIDE, 3, features // HD, HD)
    queries = pieces[:, :, 0]
    key_parts = pieces[:, :, 1]
    value_parts = pieces[:, :, 2]
    scores = jnp.einsum(
        "iqhd,ikhd->ihqk", queries, key_parts, preferred_element_type=jnp.float32
    ) * HD ** (-0.5)
    softmaxed = softmax_rows(scores)
    softmaxed_low = softmaxed.astype(jnp.bfloat16)
    mixture = jnp.einsum(
        "ihqk,ikhd->iqhd", softmaxed_low, value_parts, preferred_element_type=jnp.float32
    )
    return (
        mixture.reshape(tokens, features),
        (queries, key_parts, value_parts, softmaxed, softmaxed_low),
    )


def window_backward(stored, grad_mixture):
    queries, key_parts, value_parts, softmaxed, softmaxed_low = stored
    grad_pieces = grad_mixture.reshape(queries.shape)
    grad_values = jnp.einsum(
        "ihqk,iqhd->ikhd", softmaxed_low, grad_pieces, preferred_element_type=jnp.float32
    )
    grad_soft = jnp.einsum(
        "iqhd,ikhd->ihqk", grad_pieces, value_parts, preferred_element_type=jnp.float32
    )
    grad_scores = (
        softmaxed * (grad_soft - jnp.sum(grad_soft * softmaxed, axis=-1, keepdims=True))
    ).astype(jnp.bfloat16)
    grad_queries = jnp.einsum(
        "ihqk,ikhd->iqhd", grad_scores, key_parts, preferred_element_type=jnp.float32
    ) * HD ** (-0.5)
    grad_keys = jnp.einsum(
        "ihqk,iqhd->ikhd", grad_scores, queries, preferred_element_type=jnp.float32
    ) * HD ** (-0.5)
    joined = jnp.stack([grad_queries, grad_keys, grad_values], axis=2)
    return joined.reshape(grad_mixture.shape[0], 3 * grad_mixture.shape[1])


def channel_forward(triple, mask_rows):
    tokens = triple.shape[0]
    features = triple.shape[1] // 3
    images = tokens // (SIDE * SIDE)
    pieces = triple.reshape(images, SIDE * SIDE, 3, features // HD, HD)
    queries = pieces[:, :, 0]
    keep_mask = mask_rows.reshape(images, SIDE * SIDE, 1, 1).astype(jnp.bfloat16)
    masked = pieces[:, :, 1] * keep_mask
    value_parts = pieces[:, :, 2]
    scores = jnp.einsum(
        "itgc,itge->igce", queries, masked, preferred_element_type=jnp.float32
    ) * HD ** (-0.5)
    softmaxed = softmax_rows(scores)
    softmaxed_low = softmaxed.astype(jnp.bfloat16)
    mixture = jnp.einsum(
        "igce,itge->itgc", softmaxed_low, value_parts, preferred_element_type=jnp.float32
    )
    return (
        mixture.reshape(tokens, features),
        (queries, masked, value_parts, keep_mask, softmaxed, softmaxed_low),
    )


def channel_backward(stored, grad_mixture):
    queries, masked, value_parts, keep_mask, softmaxed, softmaxed_low = stored
    grad_pieces = grad_mixture.reshape(queries.shape)
    grad_soft = jnp.einsum(
        "itgc,itge->igce", grad_pieces, value_parts, preferred_element_type=jnp.float32
    )
    grad_values = jnp.einsum(
        "igce,itgc->itge", softmaxed_low, grad_pieces, preferred_element_type=jnp.float32
    )
    grad_scores = (
        softmaxed * (grad_soft - jnp.sum(grad_soft * softmaxed, axis=-1, keepdims=True))
    ).astype(jnp.bfloat16)
    grad_queries = jnp.einsum(
        "igce,itge->itgc", grad_scores, masked, preferred_element_type=jnp.float32
    ) * HD ** (-0.5)
    grad_masked = jnp.einsum(
        "igce,itgc->itge", grad_scores, queries, preferred_element_type=jnp.float32
    ) * HD ** (-0.5)
    grad_keys = grad_masked * keep_mask.astype(jnp.float32)
    joined = jnp.stack([grad_queries, grad_keys, grad_values], axis=2)
    return joined.reshape(grad_mixture.shape[0], 3 * grad_mixture.shape[1])


def mixer_inner(stream, weights, mask_rows, channel):
    (
        conv_weight,
        conv_bias,
        norm_gain,
        norm_shift,
        triple_weight,
        triple_bias,
        output_weight,
        output_bias,
    ) = weights[:8]
    widened = stream.astype(jnp.float32)
    (shifted, normed), front_pull = jax.vjp(
        front_part,
        widened,
        conv_weight.astype(jnp.float32),
        conv_bias.astype(jnp.float32),
        norm_gain.astype(jnp.float32),
        norm_shift.astype(jnp.float32),
    )
    normed_low = normed.astype(jnp.bfloat16)
    triple = (
        jnp.dot(normed_low, triple_weight, preferred_element_type=jnp.float32)
        + triple_bias.astype(jnp.float32)
    ).astype(jnp.bfloat16)
    if channel:
        mixture, stored = channel_forward(triple, mask_rows)
    else:
        mixture, stored = window_forward(triple)
    mixture_low = mixture.astype(jnp.bfloat16)
    return (shifted, front_pull, normed_low, stored, mixture_low)


def mixer_forward(stream, weights, mask_rows, channel):
    shifted, front_pull, normed_low, stored, mixture_low = mixer_inner(
        stream, weights, mask_rows, channel
    )
    result = (
        shifted
        + jnp.dot(mixture_low, weights[6], preferred_element_type=jnp.float32)
        + weights[7].astype(jnp.float32)
    )
    return result.astype(jnp.bfloat16)


def mixer_backward(stream, grad_out, weights, mask_rows, channel):
    shifted, front_pull, normed_low, stored, mixture_low = mixer_inner(
        stream, weights, mask_rows, channel
    )
    grad_wide = grad_out.astype(jnp.float32)
    grad_out_bias = jnp.sum(grad_wide, axis=0)
    grad_out_weight = dot_first(mixture_low, grad_out)
    grad_mixture = dot_last(grad_out, weights[6]).astype(jnp.bfloat16)
    if channel:
        grad_triple = channel_backward(stored, grad_mixture).astype(jnp.bfloat16)
    else:
        grad_triple = window_backward(stored, grad_mixture).astype(jnp.bfloat16)
    grad_tri_weight = dot_first(normed_low, grad_triple)
    grad_tri_bias = jnp.sum(grad_triple.astype(jnp.float32), axis=0)
    grad_normed = dot_last(grad_triple, weights[4])
    grad_stream, grad_taps, grad_tap_bias, grad_gain, grad_shift = front_pull(
        (grad_wide, grad_normed)
    )
    zero_tail = tuple((jnp.zeros(member.shape, jnp.float32) for member in weights[8:]))
    return (
        grad_stream.astype(jnp.bfloat16),
        (
            grad_taps,
            grad_tap_bias,
            grad_gain,
            grad_shift,
            grad_tri_weight,
            grad_tri_bias,
            grad_out_weight,
            grad_out_bias,
        )
        + zero_tail,
    )


def feed_inner(stream, weights):
    norm_gain, norm_shift, expand_weight, expand_bias, reduce_weight, reduce_bias = weights[8:]
    widened = stream.astype(jnp.float32)
    normed, norm_pull = jax.vjp(
        layer_norm, widened, norm_gain.astype(jnp.float32), norm_shift.astype(jnp.float32)
    )
    normed_low = normed.astype(jnp.bfloat16)
    hidden = jnp.dot(
        normed_low, expand_weight, preferred_element_type=jnp.float32
    ) + expand_bias.astype(jnp.float32)
    active, gelu_pull = jax.vjp(gelu_exact, hidden)
    return (widened, norm_pull, normed_low, gelu_pull, active.astype(jnp.bfloat16))


def feed_forward(stream, weights):
    widened, norm_pull, normed_low, gelu_pull, active_low = feed_inner(stream, weights)
    result = (
        widened
        + jnp.dot(active_low, weights[12], preferred_element_type=jnp.float32)
        + weights[13].astype(jnp.float32)
    )
    return result.astype(jnp.bfloat16)


def feed_backward(stream, grad_out, weights):
    widened, norm_pull, normed_low, gelu_pull, active_low = feed_inner(stream, weights)
    grad_wide = grad_out.astype(jnp.float32)
    grad_red_bias = jnp.sum(grad_wide, axis=0)
    grad_red_weight = dot_first(active_low, grad_out)
    grad_active = dot_last(grad_out, weights[12])
    grad_hidden = gelu_pull(grad_active)[0].astype(jnp.bfloat16)
    grad_exp_weight = dot_first(normed_low, grad_hidden)
    grad_exp_bias = jnp.sum(grad_hidden.astype(jnp.float32), axis=0)
    grad_normed = dot_last(grad_hidden, weights[10])
    grad_inner, grad_gain, grad_shift = norm_pull(grad_normed)
    zero_head = tuple((jnp.zeros(member.shape, jnp.float32) for member in weights[:8]))
    grad_stream = grad_wide + grad_inner
    return (
        grad_stream.astype(jnp.bfloat16),
        zero_head
        + (grad_gain, grad_shift, grad_exp_weight, grad_exp_bias, grad_red_weight, grad_red_bias),
    )


def section_forward(section, stream, weights, mask_rows):
    if section % 2 == 1:
        return feed_forward(stream, weights)
    return mixer_forward(stream, weights, mask_rows, section == 2)


def section_backward(section, stream, grad_out, weights, mask_rows):
    if section % 2 == 1:
        return feed_backward(stream, grad_out, weights)
    return mixer_backward(stream, grad_out, weights, mask_rows, section == 2)


def spare_forward(stream, weights, mask_rows):
    return jnp.zeros_like(stream)


def spare_backward(stream, grad_out, weights, mask_rows):
    return (
        jnp.zeros_like(stream),
        tuple((jnp.zeros(member.shape, jnp.float32) for member in weights)),
    )


def put_rows(buffer, rows, row_start, is_live):
    former = lax.dynamic_slice_in_dim(buffer, row_start, rows.shape[0], 0)
    return lax.dynamic_update_slice_in_dim(buffer, jnp.where(is_live, rows, former), row_start, 0)


def run_segments(layer_set, patches, region_mask, cotangent, segment_index, segments):
    features = patches.shape[1]
    micro_count = MICRO
    micro_rows = IMG_MB * SIDE * SIDE
    tick_count = micro_count + segments - 1
    forward_branches = [
        partial(section_forward, 0),
        partial(section_forward, 1),
        partial(section_forward, 2),
        partial(section_forward, 3),
        spare_forward,
    ]
    backward_branches = [
        partial(section_backward, 0),
        partial(section_backward, 1),
        partial(section_backward, 2),
        partial(section_backward, 3),
        spare_backward,
    ]
    received = jnp.zeros((micro_rows, features), jnp.bfloat16)
    kept_inputs = jnp.zeros((micro_count * micro_rows, features), jnp.bfloat16)
    outputs_here = jnp.zeros((micro_count * micro_rows, features), jnp.bfloat16)
    for tick_index in range(tick_count):
        micro_index = tick_index - segment_index
        is_live = (micro_index >= 0) & (micro_index < micro_count)
        row_start = jnp.clip(micro_index, 0, micro_count - 1) * micro_rows
        fresh_rows = lax.dynamic_slice_in_dim(patches, row_start, micro_rows, 0)
        mask_rows = lax.dynamic_slice_in_dim(region_mask, row_start, micro_rows, 0)
        entering = jnp.where(segment_index == 0, fresh_rows, received)
        leaving = lax.switch(
            jnp.where(is_live, segment_index, segments),
            forward_branches,
            entering,
            layer_set,
            mask_rows,
        )
        kept_inputs = put_rows(kept_inputs, entering, row_start, is_live)
        outputs_here = put_rows(outputs_here, leaving, row_start, is_live)
        if tick_index + 1 < tick_count:
            received = jax.tree.map(
                lambda part, own: part.astype(own.dtype),
                shifted_2(as_sent(leaving), "segment", 1),
                leaving,
            )
    grad_received = jnp.zeros((micro_rows, features), jnp.bfloat16)
    grads_here = jnp.zeros((micro_count * micro_rows, features), jnp.bfloat16)
    totals = tuple((jnp.zeros(member.shape, jnp.float32) for member in layer_set))
    for tick_index in range(tick_count):
        micro_index = tick_index - (segments - 1 - segment_index)
        is_live = (micro_index >= 0) & (micro_index < micro_count)
        row_start = jnp.clip(micro_index, 0, micro_count - 1) * micro_rows
        seed_rows = lax.dynamic_slice_in_dim(cotangent, row_start, micro_rows, 0)
        mask_rows = lax.dynamic_slice_in_dim(region_mask, row_start, micro_rows, 0)
        arriving = jnp.where(segment_index == segments - 1, seed_rows, grad_received)
        stream = lax.dynamic_slice_in_dim(kept_inputs, row_start, micro_rows, 0)
        grad_stream, grad_terms = lax.switch(
            jnp.where(is_live, segment_index, segments),
            backward_branches,
            stream,
            arriving,
            layer_set,
            mask_rows,
        )
        totals = tuple(
            (first_term + second_term for first_term, second_term in zip(totals, grad_terms))
        )
        grads_here = put_rows(grads_here, grad_stream, row_start, is_live)
        if tick_index + 1 < tick_count:
            grad_received = jax.tree.map(
                lambda part, own: part.astype(own.dtype),
                shifted_2(as_sent(grad_stream), "segment", -1),
                grad_stream,
            )
    return (outputs_here, grads_here, totals)


def body(
    patches,
    region_mask,
    conv_weight,
    conv_bias,
    mixer_gain,
    mixer_shift,
    triple_weight,
    triple_bias,
    output_weight,
    output_bias,
    feed_gain,
    feed_shift,
    expand_weight,
    expand_bias,
    reduce_weight,
    reduce_bias,
    cotangent,
):
    params = (
        conv_weight,
        conv_bias,
        mixer_gain,
        mixer_shift,
        triple_weight,
        triple_bias,
        output_weight,
        output_bias,
        feed_gain,
        feed_shift,
        expand_weight,
        expand_bias,
        reduce_weight,
        reduce_bias,
    )
    segments = lax.axis_size("segment")
    segment_index = lax.axis_index("segment")
    layer_index = segment_index // 2
    slices = tuple(
        (lax.dynamic_index_in_dim(member, layer_index, 0, keepdims=False) for member in params)
    )
    layer_set = (
        lax.all_gather(slices[0], "dp", axis=1, tiled=True),
        lax.all_gather(slices[1], "dp", axis=0, tiled=True),
        lax.all_gather(slices[2], "dp", axis=0, tiled=True),
        lax.all_gather(slices[3], "dp", axis=0, tiled=True),
        lax.all_gather(slices[4], "dp", axis=0, tiled=True),
        lax.all_gather(slices[5], "dp", axis=0, tiled=True),
        lax.all_gather(slices[6], "dp", axis=0, tiled=True),
        lax.all_gather(slices[7], "dp", axis=0, tiled=True),
        lax.all_gather(slices[8], "dp", axis=0, tiled=True),
        lax.all_gather(slices[9], "dp", axis=0, tiled=True),
        lax.all_gather(slices[10], "dp", axis=0, tiled=True),
        lax.all_gather(slices[11], "dp", axis=0, tiled=True),
        lax.all_gather(slices[12], "dp", axis=0, tiled=True),
        lax.all_gather(slices[13], "dp", axis=0, tiled=True),
    )
    outputs_here, grads_here, totals = run_segments(
        layer_set, patches, region_mask, cotangent, segment_index, segments
    )
    reduced = (
        lax.psum_scatter(totals[0], "dp", scatter_dimension=1, tiled=True),
        lax.psum_scatter(totals[1], "dp", scatter_dimension=0, tiled=True),
        lax.psum_scatter(totals[2], "dp", scatter_dimension=0, tiled=True),
        lax.psum_scatter(totals[3], "dp", scatter_dimension=0, tiled=True),
        lax.psum_scatter(totals[4], "dp", scatter_dimension=0, tiled=True),
        lax.psum_scatter(totals[5], "dp", scatter_dimension=0, tiled=True),
        lax.psum_scatter(totals[6], "dp", scatter_dimension=0, tiled=True),
        lax.psum_scatter(totals[7], "dp", scatter_dimension=0, tiled=True),
        lax.psum_scatter(totals[8], "dp", scatter_dimension=0, tiled=True),
        lax.psum_scatter(totals[9], "dp", scatter_dimension=0, tiled=True),
        lax.psum_scatter(totals[10], "dp", scatter_dimension=0, tiled=True),
        lax.psum_scatter(totals[11], "dp", scatter_dimension=0, tiled=True),
        lax.psum_scatter(totals[12], "dp", scatter_dimension=0, tiled=True),
        lax.psum_scatter(totals[13], "dp", scatter_dimension=0, tiled=True),
    )
    placed = tuple(
        (
            jnp.stack(
                [jnp.where(layer_index == 0, member, 0.0), jnp.where(layer_index == 1, member, 0.0)]
            )
            for member in reduced
        )
    )
    section_outputs = outputs_here[None]
    section_grads = grads_here[None]
    summed = (
        lax.psum(placed[0].astype(jnp.bfloat16), "segment").astype(jnp.float32),
        lax.psum(placed[1].astype(jnp.bfloat16), "segment").astype(jnp.float32),
        lax.psum(placed[2].astype(jnp.bfloat16), "segment").astype(jnp.float32),
        lax.psum(placed[3].astype(jnp.bfloat16), "segment").astype(jnp.float32),
        lax.psum(placed[4].astype(jnp.bfloat16), "segment").astype(jnp.float32),
        lax.psum(placed[5].astype(jnp.bfloat16), "segment").astype(jnp.float32),
        lax.psum(placed[6].astype(jnp.bfloat16), "segment").astype(jnp.float32),
        lax.psum(placed[7].astype(jnp.bfloat16), "segment").astype(jnp.float32),
        lax.psum(placed[8].astype(jnp.bfloat16), "segment").astype(jnp.float32),
        lax.psum(placed[9].astype(jnp.bfloat16), "segment").astype(jnp.float32),
        lax.psum(placed[10].astype(jnp.bfloat16), "segment").astype(jnp.float32),
        lax.psum(placed[11].astype(jnp.bfloat16), "segment").astype(jnp.float32),
        lax.psum(placed[12].astype(jnp.bfloat16), "segment").astype(jnp.float32),
        lax.psum(placed[13].astype(jnp.bfloat16), "segment").astype(jnp.float32),
    )
    return (
        section_outputs,
        section_grads,
        summed[0],
        summed[1],
        summed[2],
        summed[3],
        summed[4],
        summed[5],
        summed[6],
        summed[7],
        summed[8],
        summed[9],
        summed[10],
        summed[11],
        summed[12],
        summed[13],
    )


W = 768
IMG = 56
LIVE = 49
ROWS = 224
PAIR = 2 * IMG
LANES = 128
SCALE = HD ** (-0.5)
F32 = jnp.float32
BF16 = jnp.bfloat16
TAPS = [(a, b) for a in range(3) for b in range(3)]


def mm(a, b):
    return lax.dot_general(a, b, (((1,), (0,)), ((), ())), preferred_element_type=F32)


def mm_nt(a, b):
    return lax.dot_general(a, b, (((1,), (1,)), ((), ())), preferred_element_type=F32)


def mm_tn(a, b):
    return lax.dot_general(a, b, (((0,), (0,)), ((), ())), preferred_element_type=F32)


def row_index(rows):
    return lax.broadcasted_iota(jnp.int32, (rows, 1), 0)


def live_rows(rows):
    return lax.rem(row_index(rows), IMG) < LIVE


def column_masks(rows):
    place = lax.rem(row_index(rows), IMG)
    column = lax.rem(place, SIDE)
    live = place < LIVE
    return [(live & (column + b - 1 >= 0) & (column + b - 1 < SIDE)).astype(F32) for b in range(3)]


def rolled(values, by):
    by = by % values.shape[0]
    return values if by == 0 else pltpu.roll(values, by, 0)


def norm_parts(values):
    center = values - jnp.mean(values, axis=-1, keepdims=True)
    spread = jnp.mean(center * center, axis=-1, keepdims=True)
    rstd = lax.rsqrt(spread + EPSILON)
    return center * rstd, rstd


def column_sum(values):
    return jnp.sum(values, axis=0, keepdims=True)


def head_lanes(head):
    lane = lax.broadcasted_iota(jnp.int32, (1, LANES), 1)
    return (lane // HD) == head


def only(values, mask):
    return jnp.where(mask, values, jnp.zeros_like(values))


def mix_forward(layer, channel, u_in, u_out, w, small, mask, bias, c_ref, xhat, rstd, n_ref, t_ref, p_ref, m_ref):
    base = 12 * layer
    row = lambda r: small[layer, r:r + 1, :]
    v = u_in[...].astype(F32)
    masks = column_masks(ROWS)
    total = v + row(9)
    for b in range(3):
        part = jnp.zeros_like(v)
        for a in range(3):
            part = part + row(3 * a + b) * rolled(v, -(SIDE * (a - 1) + b - 1))
        total = total + part * masks[b]
    c = jnp.where(live_rows(ROWS), total, 0.0)
    c_ref[...] = c
    x, r = norm_parts(c)
    xhat[...] = x
    rstd[...] = r
    n_ref[...] = (x * row(10) + row(11)).astype(BF16)

    @pl.loop(0, 3)
    def _(j):
        cols = pl.ds(pl.multiple_of(W * j, W), W)
        t_ref[:, cols] = (mm(n_ref[...], w[base + j]) + small[layer, pl.ds(12 + j, 1), :]).astype(BF16)

    @pl.loop(0, 6)
    def _(g):
        qs = pl.ds(pl.multiple_of(LANES * g, LANES), LANES)
        ks = pl.ds(pl.multiple_of(W + LANES * g, LANES), LANES)
        vs = pl.ds(pl.multiple_of(2 * W + LANES * g, LANES), LANES)
        for pair in range(2):
            rows = slice(PAIR * pair, PAIR * pair + PAIR)
            q, k, val = t_ref[rows, qs], t_ref[rows, ks], t_ref[rows, vs]
            mix = jnp.zeros((PAIR, LANES), F32)
            if channel:
                for im in range(2):
                    here = (row_index(PAIR) // IMG) == im
                    km = k * only(mask[rows, :], here)
                    s = mm_tn(q, km) * SCALE + bias[...]
                    e = jnp.exp(s - jnp.max(s, axis=-1, keepdims=True))
                    p = e / jnp.sum(e, axis=-1, keepdims=True)
                    p_ref[g, 2 * pair + im] = p
                    mix = mix + mm_nt(only(val, here), p.astype(BF16))
            else:
                for head in range(4):
                    lanes = head_lanes(head)
                    s = mm_nt(only(q, lanes), k) * SCALE + bias[...]
                    e = jnp.exp(s - jnp.max(s, axis=-1, keepdims=True))
                    p = e / jnp.sum(e, axis=-1, keepdims=True)
                    p_ref[g, 4 * pair + head] = p
                    mix = mix + mm(p.astype(BF16), only(val, lanes))
            m_ref[rows, qs] = mix.astype(BF16)

    out = c_ref[...] + mm(m_ref[...], w[base + 3]) + row(15)
    u_out[...] = jnp.where(live_rows(ROWS), out, 0.0).astype(BF16)


def mix_backward(layer, channel, u_in, g_in, g_out, w, small, mask, sg, dw, c_ref, xhat, rstd, n_ref, t_ref, p_ref, m_ref, dm_ref, dt_ref, acc):
    base = 12 * layer
    row = lambda r: small[layer, r:r + 1, :]
    g = g_in[...]
    sg[layer, 15:16, :] = column_sum(g.astype(F32))
    dm_ref[...] = mm_nt(g, w[base + 3]).astype(BF16)
    dw(layer, 3, m_ref, lambda: g_in[...])

    @pl.loop(0, 6)
    def _(grp):
        qs = pl.ds(pl.multiple_of(LANES * grp, LANES), LANES)
        ks = pl.ds(pl.multiple_of(W + LANES * grp, LANES), LANES)
        vs = pl.ds(pl.multiple_of(2 * W + LANES * grp, LANES), LANES)
        for pair in range(2):
            rows = slice(PAIR * pair, PAIR * pair + PAIR)
            q, k, val, dm = t_ref[rows, qs], t_ref[rows, ks], t_ref[rows, vs], dm_ref[rows, qs]
            dq = jnp.zeros((PAIR, LANES), F32)
            dk = jnp.zeros((PAIR, LANES), F32)
            dv = jnp.zeros((PAIR, LANES), F32)
            if channel:
                for im in range(2):
                    here = (row_index(PAIR) // IMG) == im
                    keep = only(mask[rows, :], here)
                    km = k * keep
                    p = p_ref[grp, 2 * pair + im]
                    dmh = only(dm, here)
                    dp = mm_tn(dmh, val)
                    dv = dv + mm(dmh, p.astype(BF16))
                    ds = (p * (dp - jnp.sum(dp * p, axis=-1, keepdims=True))).astype(BF16)
                    dq = dq + mm_nt(km, ds)
                    dk = dk + mm(only(q, here), ds) * keep.astype(F32)
            else:
                for head in range(4):
                    lanes = head_lanes(head)
                    p = p_ref[grp, 4 * pair + head]
                    dmh = only(dm, lanes)
                    dp = mm_nt(dmh, val)
                    dv = dv + mm_tn(p.astype(BF16), dmh)
                    ds = (p * (dp - jnp.sum(dp * p, axis=-1, keepdims=True))).astype(BF16)
                    dq = dq + mm(ds, only(k, lanes))
                    dk = dk + mm_tn(ds, only(q, lanes))
            dt_ref[rows, qs] = (dq * SCALE).astype(BF16)
            dt_ref[rows, ks] = (dk * SCALE).astype(BF16)
            dt_ref[rows, vs] = dv.astype(BF16)

    acc[...] = jnp.zeros_like(acc)

    @pl.loop(0, 3)
    def _(j):
        cols = pl.ds(pl.multiple_of(W * j, W), W)
        acc[...] += mm_nt(dt_ref[:, cols], w[base + j])
        sg[layer, pl.ds(12 + j, 1), :] = column_sum(dt_ref[:, cols].astype(F32))
        dw(layer, j, n_ref, lambda: dt_ref[:, cols])

    dn = acc[...]
    x = xhat[...]
    sg[layer, 10:11, :] = column_sum(dn * x)
    sg[layer, 11:12, :] = column_sum(dn)
    e = dn * row(10)
    inner = rstd[...] * (e - jnp.mean(e, axis=-1, keepdims=True) - x * jnp.mean(e * x, axis=-1, keepdims=True))
    dc = jnp.where(live_rows(ROWS), g_in[...].astype(F32) + inner, 0.0)
    sg[layer, 9:10, :] = column_sum(dc)
    v = u_in[...].astype(F32)
    masks = column_masks(ROWS)
    du = dc
    for b in range(3):
        dcm = dc * masks[b]
        for a in range(3):
            moved = rolled(dcm, SIDE * (a - 1) + b - 1)
            tap = 3 * a + b
            du = du + row(tap) * moved
            sg[layer, tap:tap + 1, :] = column_sum(moved * v)
    g_out[...] = jnp.where(live_rows(ROWS), du, 0.0).astype(BF16)


ROOT_HALF = 0.5 ** 0.5
ROOT_TWO_PI = 0.3989422804014327


def ff_forward(layer, u_in, u_out, w, small, xhat, rstd, n_ref, slope, acc):
    base = 12 * layer
    row = lambda r: small[layer, r:r + 1, :]
    x, r = norm_parts(u_in[...].astype(F32))
    xhat[...] = x
    rstd[...] = r
    n_ref[...] = (x * row(16) + row(17)).astype(BF16)
    acc[...] = u_in[...].astype(F32) + row(22)

    @pl.loop(0, 4)
    def _(j):
        cols = pl.ds(pl.multiple_of(W * j, W), W)
        h = mm(n_ref[...], w[base + 4 + j]) + small[layer, pl.ds(18 + j, 1), :]
        cdf = 0.5 + 0.5 * lax.erf(h * ROOT_HALF)
        slope[:, cols] = cdf + h * (ROOT_TWO_PI * jnp.exp(-0.5 * h * h))
        acc[...] += mm((h * cdf).astype(BF16), w[base + 8 + j])

    u_out[...] = jnp.where(live_rows(ROWS), acc[...], 0.0).astype(BF16)


def ff_backward(layer, g_in, g_out, w, small, sg, xhat, rstd, slope, acc):
    base = 12 * layer
    row = lambda r: small[layer, r:r + 1, :]
    sg[layer, 22:23, :] = column_sum(g_in[...].astype(F32))
    acc[...] = jnp.zeros_like(acc)

    @pl.loop(0, 4)
    def _(j):
        cols = pl.ds(pl.multiple_of(W * j, W), W)
        dh = (mm_nt(g_in[...], w[base + 8 + j]) * slope[:, cols]).astype(BF16)
        sg[layer, pl.ds(18 + j, 1), :] = column_sum(dh.astype(F32))
        acc[...] += mm_nt(dh, w[base + 4 + j])

    dn = acc[...]
    x = xhat[...]
    sg[layer, 16:17, :] = column_sum(dn * x)
    sg[layer, 17:18, :] = column_sum(dn)
    e = dn * row(16)
    inner = rstd[...] * (e - jnp.mean(e, axis=-1, keepdims=True) - x * jnp.mean(e * x, axis=-1, keepdims=True))
    g_out[...] = jnp.where(live_rows(ROWS), g_in[...].astype(F32) + inner, 0.0).astype(BF16)


def chain_scratch():
    V = pltpu.VMEM
    mixer = [V((ROWS, W), F32), V((ROWS, 1), F32), V((ROWS, W), BF16), V((ROWS, 3 * W), BF16)]
    feed = [V((ROWS, W), F32), V((ROWS, 1), F32), V((ROWS, W), BF16), V((ROWS, 4 * W), F32)]
    return (mixer + [V((6, 8, PAIR, PAIR), F32), V((ROWS, W), BF16)] + feed + mixer + [V((6, 4, LANES, LANES), F32), V((ROWS, W), BF16)] + feed
            + [V((ROWS, W), F32), V((ROWS, W), F32), V((ROWS, W), BF16), V((ROWS, 3 * W), BF16), V((PAIR, PAIR), F32), V((LANES, LANES), F32)])


def fill_biases(win_bias, chan_bias):
    qi = lax.broadcasted_iota(jnp.int32, (PAIR, PAIR), 0)
    ki = lax.broadcasted_iota(jnp.int32, (PAIR, PAIR), 1)
    win_bias[...] = jnp.where(((qi // IMG) == (ki // IMG)) & (lax.rem(ki, IMG) < LIVE), 0.0, -1e30).astype(F32)
    ci = lax.broadcasted_iota(jnp.int32, (LANES, LANES), 0)
    ei = lax.broadcasted_iota(jnp.int32, (LANES, LANES), 1)
    chan_bias[...] = jnp.where((ci // HD) == (ei // HD), 0.0, -1e30).astype(F32)


class Chain:
    def __init__(self, w, small, mask, u, g, sg, dw, scratch):
        self.w, self.small, self.mask, self.u, self.g, self.sg, self.dw = w, small, mask, u, g, sg, dw
        s = scratch
        self.window, self.feed0, self.channel, self.feed1 = s[0:6], s[6:10], s[10:16], s[16:20]
        self.c_ref, self.acc, self.dm, self.dt, self.win_bias, self.chan_bias = s[20:26]

    def forward(self, k):
        u, w, small = self.u, self.w, self.small
        if k == 0:
            fill_biases(self.win_bias, self.chan_bias)
            mix_forward(0, False, u[0], u[1], w, small, self.mask, self.win_bias, self.c_ref, *self.window)
        if k == 1:
            ff_forward(0, u[1], u[2], w, small, *self.feed0, self.acc)
        if k == 2:
            mix_forward(1, True, u[2], u[3], w, small, self.mask, self.chan_bias, self.c_ref, *self.channel)
        if k == 3:
            ff_forward(1, u[3], u[4], w, small, *self.feed1, self.acc)

    def backward(self, k):
        u, g, w, small, sg = self.u, self.g, self.w, self.small, self.sg
        if k in (0, 2):
            parts = self.channel if k == 2 else self.window
            mix_backward(k // 2, k == 2, u[k], g[k + 1], g[k], w, small, self.mask, sg, self.dw, self.c_ref, *parts, self.dm, self.dt, self.acc)
        else:
            x, r, _, slope = self.feed0 if k == 1 else self.feed1
            ff_backward(k // 2, g[k + 1], g[k], w, small, sg, x, r, slope, self.acc)


MESH = pl.DeviceIdType.MESH
VMEM_LIMIT = 63 * 1024 * 1024
STRIP = 96


def slot(item, line, d):
    red = lax.rem(item, 3) // 2
    block = 12 * (item // 3) + 4 * lax.rem(item, 3) + (1 - red) * line + red * (d // 2)
    row = (1 - red) * STRIP * d + red * (4 * STRIP * lax.rem(d, 2) + STRIP * line)
    return block, row


def other_planes(z):
    near = z + 1 - 2 * (z // 2)
    far = 3 * (1 - z // 2)
    return near, 6 - z - near - far, far


class Place:
    def __init__(self):
        self.s = lax.axis_index("segment")
        self.d = lax.axis_index("dp")
        self.z = self.d // 2
        self.c = lax.rem(self.d, 2)
        self.xn = self.s + 1 - 2 * lax.rem(self.s, 2)
        self.yn = lax.rem(self.s + 2, 4)
        self.dn = 3 - self.s
        self.twin = self.d + 1 - 2 * self.c


def remote(src, dst, ssem, rsem, seg, dev):
    return pltpu.make_async_remote_copy(src, dst, ssem, rsem, device_id=(seg, dev), device_id_type=MESH)


def gather_scratch():
    D = pltpu.SemaphoreType.DMA
    return [D((2, 9)), D((6, 5)), D((6, 3, 2)), D((6, 3, 2)), D((6, 4, 4)), D((2, 3, 4)), D((2, 3, 4))]


class Gather:
    def __init__(self, at, shards, wbuf, sems):
        self.at, self.shards, self.w = at, shards, wbuf
        self.lsem, self.zs, self.xs, self.ys, self.pr, self.cs, self.cr = sems
        self.planes = other_planes(at.z)
        self.away = 2 * (at.z // 2) - 1
        self.inner = (at.z == 1) | (at.z == 2)
        self.groups = [(layer, part, k) for layer in range(2) for part in range(3) for k in range(3)]

    def strip(self, item, line, plane):
        block, row = slot(item, line, 2 * plane + self.at.c)
        return self.w.at[block, pl.ds(pl.multiple_of(row, STRIP), STRIP), :]

    def quad_ref(self, layer, part, plane, core):
        if part == 2:
            return self.w.at[12 * layer + 8 + plane, pl.ds(pl.multiple_of(4 * STRIP * core, 4 * STRIP), 4 * STRIP), :]
        row = pl.multiple_of(STRIP * (2 * plane + core), STRIP)
        return self.w.at[pl.ds(12 * layer + 4 * part, 4), pl.ds(row, STRIP), :]

    def quad(self, layer, part, plane, core, k):
        ref = self.quad_ref(layer, part, plane, core)
        return remote(ref, ref, self.cs.at[layer, part, k], self.cr.at[layer, part, plane], self.at.s, self.at.twin)

    def local(self, layer):
        triple, output, expand, reduce = self.shards
        at, w, base = self.at, self.w, 12 * layer
        rows = pl.ds(pl.multiple_of(STRIP * at.d, STRIP), STRIP)
        sems = self.lsem.at
        copies = [pltpu.make_async_copy(triple.at[layer, :, pl.ds(W * j, W)], w.at[base + j, rows, :], sems[layer, j]) for j in range(3)]
        copies.append(pltpu.make_async_copy(output.at[layer], w.at[base + 3, rows, :], sems[layer, 3]))
        copies += [pltpu.make_async_copy(expand.at[layer, :, pl.ds(W * j, W)], w.at[base + 4 + j, rows, :], sems[layer, 4 + j]) for j in range(4)]
        half = pl.ds(pl.multiple_of(4 * STRIP * at.c, 4 * STRIP), 4 * STRIP)
        copies.append(pltpu.make_async_copy(reduce.at[layer], w.at[base + 8 + at.z, half, :], sems[layer, 8]))
        return copies

    def up(self, item):
        ref = self.strip(item, self.at.s, self.at.z)
        return remote(ref, ref, self.zs.at[item, 0], self.pr.at[item, self.at.z, self.at.s], self.at.s, self.at.d + 2)

    def down(self, item):
        ref = self.strip(item, self.at.s, self.at.z)
        return remote(ref, ref, self.zs.at[item, 1], self.pr.at[item, self.at.z, self.at.s], self.at.s, self.at.d - 2)

    def onward(self, item, k):
        step = self.away if k != 1 else -self.away
        ref = self.strip(item, self.at.s, self.planes[k])
        return remote(ref, ref, self.zs.at[item, 2 + k], self.pr.at[item, self.planes[k], self.at.s], self.at.s, self.at.d + 2 * step)

    def to_x(self, item, k, line, j):
        ref = self.strip(item, line, self.planes[k])
        return remote(ref, ref, self.xs.at[item, k, j], self.pr.at[item, self.planes[k], line], self.at.xn, self.at.d)

    def to_y(self, item, k, line, j):
        ref = self.strip(item, line, self.planes[k])
        return remote(ref, ref, self.ys.at[item, k, j], self.pr.at[item, self.planes[k], line], self.at.yn, self.at.d)

    def arrival(self, item, k, line):
        ref = self.strip(item, line, self.planes[k])
        return remote(ref, ref, self.zs.at[item, 0], self.pr.at[item, self.planes[k], line], self.at.s, self.at.twin)

    def ends(self, item, act):
        @pl.when(self.at.z < 3)
        def _():
            act(self.up(item))

        @pl.when(self.at.z > 0)
        def _():
            act(self.down(item))

    def begin(self):
        at = self.at
        copies = [self.local(layer) for layer in range(2)]
        for layer in range(2):
            for copy in copies[layer]:
                copy.start()
        for copy in copies[0]:
            copy.wait()
        self.ends(0, lambda copy: copy.start())
        for part in range(3):
            self.quad(0, part, at.z, at.c, 3).start()
        for copy in copies[1]:
            copy.wait()
        for part in range(3):
            self.quad(1, part, at.z, at.c, 3).start()

    def stage_a(self, layer, part, k):
        item = 3 * layer + part
        self.arrival(item, k, self.at.s).wait_recv()

        @pl.when(self.inner)
        def _():
            self.onward(item, k).start()

        self.to_x(item, k, self.at.s, 0).start()
        self.to_y(item, k, self.at.s, 0).start()

    def stage_b(self, layer, part, k):
        item = 3 * layer + part
        self.arrival(item, k, self.at.xn).wait_recv()
        if (part + k + layer) % 2 == 0:
            self.to_y(item, k, self.at.xn, 1).start()
        self.arrival(item, k, self.at.yn).wait_recv()
        if (part + k + layer) % 2 == 1:
            self.to_x(item, k, self.at.yn, 1).start()

    def stage_c(self, layer, part, k):
        item = 3 * layer + part
        self.arrival(item, k, self.at.dn).wait_recv()
        self.quad(layer, part, self.planes[k], self.at.c, k).start()

    def step(self, g):
        n = len(self.groups)
        if g < n and g % 3 == 0 and g // 3 + 1 < 6:
            self.ends(g // 3 + 1, lambda copy: copy.start())
        if g < n:
            self.stage_a(*self.groups[g])
        if 0 <= g - 1 < n:
            self.stage_b(*self.groups[g - 1])
        if 0 <= g - 2 < n:
            self.stage_c(*self.groups[g - 2])

    def settle(self, layer, part):
        for k in range(3):
            self.quad(layer, part, self.planes[k], 1 - self.at.c, k).wait_recv()
        self.quad(layer, part, self.at.z, 1 - self.at.c, 3).wait_recv()

    def drain(self):
        at = self.at
        for layer in range(2):
            for part in range(3):
                item = 3 * layer + part
                self.ends(item, lambda copy: copy.wait_send())
                self.quad(layer, part, at.z, at.c, 3).wait_send()
                for k in range(3):
                    @pl.when(self.inner)
                    def _():
                        self.onward(item, k).wait_send()

                    self.to_x(item, k, at.s, 0).wait_send()
                    self.to_y(item, k, at.s, 0).wait_send()
                    if (part + k + layer) % 2 == 0:
                        self.to_y(item, k, at.xn, 1).wait_send()
                    else:
                        self.to_x(item, k, at.yn, 1).wait_send()
                    self.quad(layer, part, self.planes[k], at.c, k).wait_send()


def greet_all(at):
    bar = pltpu.get_barrier_semaphore()

    def greet(seg, dev):
        pl.semaphore_signal(bar, inc=1, device_id=(seg, dev), device_id_type=MESH)

    for seg in (at.xn, at.yn, at.dn):
        greet(seg, at.d)
        greet(seg, at.twin)
    greet(at.s, at.twin)
    greet(at.s, lax.rem(at.d + 4, 8))

    @pl.when(at.z < 3)
    def _():
        greet(at.s, at.d + 2)

    @pl.when(at.z > 0)
    def _():
        greet(at.s, at.d - 2)

    pl.semaphore_wait(bar, 9 + (at.z * (3 - at.z)) // 2)


def add_into(total, term):
    total[...] = (total[...].astype(F32) + term[...].astype(F32)).astype(BF16)


class PlaneSum:
    def __init__(self, at, chunk, below, above, stage, sems):
        self.at, self.chunk, self.below, self.above, self.stage = at, chunk, below, above, stage
        self.ssem, self.bsem, self.asem, self.lsem = sems

    def up(self, i):
        return remote(self.chunk(i), self.below.at[i], self.ssem.at[i], self.bsem.at[i], self.at.s, self.at.d + 2)

    def down(self, i):
        return remote(self.chunk(i), self.above.at[i], self.ssem.at[i], self.asem.at[i], self.at.s, self.at.d - 2)

    def take(self, landed, i):
        load = pltpu.make_async_copy(landed.at[i], self.stage, self.lsem)
        load.start()
        load.wait()
        add_into(self.chunk(i), self.stage)

    def step(self, i, goal):
        z = self.at.z

        @pl.when((z <= goal) & (z > 0))
        def _():
            self.up(i).wait_recv()
            self.take(self.below, i)

        @pl.when((z >= goal) & (z < 3))
        def _():
            self.down(i).wait_recv()
            self.take(self.above, i)

        @pl.when(z < goal)
        def _():
            self.up(i).start()

        @pl.when(z > goal)
        def _():
            self.down(i).start()

    def drain(self, i, goal):
        @pl.when(self.at.z < goal)
        def _():
            self.up(i).wait_send()

        @pl.when(self.at.z > goal)
        def _():
            self.down(i).wait_send()


def goal_order(z):
    far = 3 * (1 - z // 2)
    near = 2 - z // 2
    return far, near, 6 - far - near - z, z


UNITS = [("mix", layer, j) for layer in (1, 0) for j in range(4)]
UNITS = [("exp", layer, j) for layer in (1, 0) for j in range(4)] + [("red", layer, j) for layer in (1, 0) for j in range(2)] + UNITS


class Spread:
    def __init__(self, at, w, fin, fsend, frecv):
        self.at, self.w, self.fin, self.fsend, self.frecv = at, w, fin, fsend, frecv

    def unit(self, kind, layer, j):
        at, w, fin = self.at, self.w, self.fin
        if kind == "mix":
            src = lambda p: [w.at[12 * layer + at.s, pl.ds(pl.multiple_of(2 * STRIP * at.z + STRIP * at.c, STRIP), STRIP), :]]
            return 4 * layer + j, j, at.c, [fin.at[layer, j]], src
        if kind == "exp":
            src = lambda p: [w.at[12 * layer + 4 + j, pl.ds(pl.multiple_of(2 * STRIP * at.z + STRIP * p, STRIP), STRIP), :]]
            return 8 + 4 * layer + j, 2 * layer + j // 2, j % 2, [fin.at[layer, 4 + j]], src
        src = lambda p: [w.at[12 * layer + 8 + at.z, pl.ds(4 * STRIP * p + 2 * STRIP * j + STRIP * m, STRIP), :] for m in range(2)]
        return 16 + 2 * layer + j, 2 * layer + at.z // 2, lax.rem(at.z, 2), [fin.at[layer, 8 + 2 * j + m] for m in range(2)], src

    def copies(self, kind, layer, j):
        at = self.at
        index, owner, core, targets, src = self.unit(kind, layer, j)
        owns = (at.s == owner) if kind == "mix" else ((at.s == owner) & (at.c == core))
        sends = []
        for n, p in enumerate((at.c,) if kind == "mix" else (0, 1)):
            dev = at.d if kind == "mix" else 2 * at.z + p
            for m, ref in enumerate(src(p)):
                sem = lambda k: self.fsend.at[index, n, m, k]
                land = self.frecv.at[index, m]
                for k, seg in enumerate((at.xn, at.yn)):
                    sends.append((owns, remote(ref, targets[m], sem(k), land, seg, dev), True))
                if kind == "mix":
                    sends.append((owns, pltpu.make_async_copy(ref, targets[m], land), False))
                else:
                    sends.append((owns & (at.c == p), pltpu.make_async_copy(ref, targets[m], land), False))
                    sends.append((owns & (at.c != p), remote(ref, targets[m], sem(2), land, at.s, at.twin), True))
        return sends

    def relays(self, kind, layer, j):
        at = self.at
        index, owner, _, targets, _ = self.unit(kind, layer, j)
        first, then = (at.xn, at.yn) if index % 2 == 0 else (at.yn, at.xn)
        return owner == first, [remote(ref, ref, self.fsend.at[index, 0, m, 3], self.frecv.at[index, m], then, at.d) for m, ref in enumerate(targets)]

    def start(self, unit):
        for cond, copy, _ in self.copies(*unit):
            @pl.when(cond)
            def _():
                copy.start()

    def relay(self, unit):
        passes, relays = self.relays(*unit)
        for copy in relays:
            copy.wait_recv()

            @pl.when(passes)
            def _():
                copy.start()

    def drain(self, unit):
        for cond, copy, crosses in self.copies(*unit):
            if crosses:
                @pl.when(cond)
                def _():
                    copy.wait_send()

        passes, relays = self.relays(*unit)
        for copy in relays:
            @pl.when(passes)
            def _():
                copy.wait_send()


def train_kernel(triple, output, expand, reduce, small, x, mask, gin, cot,
                 sec_out, grad_out, fin, sg_out, xin, gland, xtw, gtw, mrx, prx, below_m, above_m, below_f, above_f,
                 w, u_buf, g_buf, sg, sga, sgr, stage, stage_f, lsem, tsem, xsend, xrecv, gsend, grecv, tws, twr, osend, orecv, msend, mrecv, psend, precv,
                 zms, zmb, zma, zfs, zfb, zfa, fsend, frecv, sgs, sgv, *scratch):
    at = Place()
    s, d, z, c = at.s, at.d, at.z, at.c
    lay = s // 2
    quarter = 2 * lax.rem(s, 2) + c
    segs = (at.xn, at.yn, at.dn)
    gather = Gather(at, (triple, output, expand, reduce), w, scratch[:7])
    u = [x] + [u_buf.at[i] for i in range(4)]
    g = [g_buf.at[i] for i in range(4)] + [gin]

    def dw(layer, j, lhs, rhs):
        w[12 * layer + j] = mm_tn(lhs[...], rhs()).astype(BF16)

    chain = Chain(w, small, mask, u, g, sg, dw, scratch[7:])
    sg[...] = jnp.zeros_like(sg)

    def x_send(i):
        return remote(u_buf.at[2 * (segs[i] // 2)], xin.at[s], xsend.at[i], xrecv.at[i], segs[i], d)

    def g_send(i):
        return remote(g_buf.at[2], gland.at[s], gsend.at[i], grecv.at[i], segs[i], d)

    def u_out(i):
        return remote(u_buf.at[segs[i]], sec_out.at[s], osend.at[0, i], orecv.at[0, i], segs[i], d)

    def g_out(i):
        return remote(g_buf.at[segs[i]], grad_out.at[s], osend.at[1, i], orecv.at[1, i], segs[i], d)

    keep_x = pltpu.make_async_copy(u_buf.at[2 * lay], xin.at[s], lsem.at[0])
    keep_u = pltpu.make_async_copy(u_buf.at[s], sec_out.at[s], lsem.at[1])
    keep_g = pltpu.make_async_copy(g_buf.at[s], grad_out.at[s], lsem.at[2])
    keep_gl = pltpu.make_async_copy(g_buf.at[2], gland.at[s], lsem.at[3])

    def to_where(cond, copy, i, wait=False):
        @pl.when(cond(segs[i]))
        def _():
            copy(i).wait_send() if wait else copy(i).start()

    def x_twin(t):
        return remote(xin.at[t], xtw.at[t], tws.at[0, t], twr.at[0, t], s, at.twin)

    def g_twin(t):
        return remote(gland.at[t], gtw.at[t], tws.at[1, t], twr.at[1, t], s, at.twin)

    def cot_twin(t):
        return remote(cot.at[t], gtw.at[t], tws.at[1, t], twr.at[1, t], s, at.twin)

    def strip(block, p, core):
        return w.at[block, pl.ds(pl.multiple_of(2 * STRIP * p + STRIP * core, STRIP), STRIP), :]

    def twin_mix(layer, p):
        rows = pl.ds(pl.multiple_of(2 * STRIP * p + STRIP * (1 - c), STRIP), STRIP)
        return remote(w.at[pl.ds(12 * layer, 4), rows, :], mrx.at[layer, p], msend.at[layer, p], mrecv.at[layer, p], s, at.twin)

    def plane_send(layer, i, p):
        return remote(strip(12 * layer + segs[i], p, c), prx.at[layer, i, p], psend.at[layer, i, p], precv.at[layer, i, p], segs[i], d)

    def to_stage(src, n):
        load = pltpu.make_async_copy(src, stage.at[n], tsem.at[n])
        load.start()
        return load

    def cores_sum(layer):
        loads = []
        for p in range(4):
            twin_mix(layer, p).wait_recv()
            if p >= 2:
                take(layer, p - 2, loads[p - 2])
            loads.append(to_stage(mrx.at[layer, p], p % 2))
        for p in (2, 3):
            take(layer, p, loads[p])

    def take(layer, p, load):
        load.wait()
        for b in range(4):
            add_into(strip(12 * layer + b, p, c), stage.at[p % 2, b])

    def plane_begin(layer):
        cores_sum(layer)
        for p in range(4):
            for i in range(3):
                plane_send(layer, i, p).start()

    def plane_sum(layer):
        for i in range(3):
            for p in range(4):
                plane_send(layer, i, p).wait_recv()
            to_stage(prx.at[layer, i], 0).wait()
            for p in range(4):
                add_into(strip(12 * layer + s, p, c), stage.at[0, p])

    goals = goal_order(z)
    mix_stage = stage.at[0, 0]

    def mix_chunk(i):
        return strip(12 * (i // 4) + s, lax.rem(i, 4), c)

    def feed_chunk(i):
        rows = pl.ds(pl.multiple_of(2 * STRIP * lax.rem(i, 4), 2 * STRIP), 2 * STRIP)
        return w.at[12 * lay + 4 + 4 * (i // 4) + quarter, rows, :]

    mix_sum = PlaneSum(at, mix_chunk, below_m, above_m, mix_stage, (zms, zmb, zma, tsem.at[0]))
    feed_sum = PlaneSum(at, feed_chunk, below_f, above_f, stage_f, (zfs, zfb, zfa, tsem.at[1]))

    other = 1 - lay
    own = 12 * lay
    eq, rq = own + 4 + quarter, own + 8 + quarter

    def rest(n):
        return lax.rem(quarter + n, 4)

    def block_x(k):
        return 12 * other + 4 + k

    def block_g(k):
        return 12 * other + 7 + k

    def block_a(k):
        return (1 - k // 2) * (12 * other + 10 + k) + (k // 2) * (own + 4 + rest(1))

    def block_h(k):
        return (1 - k // 2) * (own + 4 + rest(2 + k)) + (k // 2) * (own + 8 + rest(1))

    def rows_of(i):
        return pl.ds(pl.multiple_of(ROWS * lax.rem(i, 3), ROWS), ROWS)

    def token_loads():
        loads = []
        for t in range(4):
            for n, (xs, gs) in enumerate(((xin, gland), (xtw, gtw))):
                i = 2 * t + n
                loads.append(pltpu.make_async_copy(xs.at[t], w.at[block_x(i // 3), rows_of(i), :], lsem.at[4 + i]))
                dst = w.at[block_g(i // 3), rows_of(i), :]
                load = pltpu.make_async_copy(gs.at[t], dst, lsem.at[12 + i])
                seed = pltpu.make_async_copy((cot if n == 0 else gs).at[t], dst, lsem.at[12 + i])
                loads.append((load, seed))
        return loads

    def feed_rows(i):
        k, rows = i // 3, rows_of(i)
        xh, _ = norm_parts(w[block_x(k), rows, :].astype(F32))
        n = (xh * small[lay, 16:17, :] + small[lay, 17:18, :]).astype(BF16)
        w[block_x(k), rows, :] = n
        h = mm(n, w[eq]) + small[lay, pl.ds(18 + quarter, 1), :]
        cdf = 0.5 + 0.5 * lax.erf(h * ROOT_HALF)
        w[block_a(k), rows, :] = (h * cdf).astype(BF16)
        slope = cdf + h * (ROOT_TWO_PI * jnp.exp(-0.5 * h * h))
        w[block_h(k), rows, :] = (mm_nt(w[block_g(k), rows, :], w[rq]) * slope).astype(BF16)

    def product(out, left, right):
        @pl.loop(0, 3)
        def _(i):
            cols = pl.ds(pl.multiple_of(256 * i, 256), 256)
            total = jnp.zeros((256, W), F32)
            for k, rows in enumerate((3 * ROWS, 3 * ROWS, 2 * ROWS)):
                total = total + mm_tn(w[left(k), :rows, cols], w[right(k), :rows, :])
            w[out, cols, :] = total.astype(BF16)

    partners = [(s, at.twin), (at.xn, d), (at.yn, d), (s, d + 2 * (1 - 2 * lax.rem(z, 2))), (s, lax.rem(d + 4, 8))]

    def sg_round(r):
        return remote(sga.at[r], sgr.at[r], sgs.at[r], sgv.at[r], *partners[r])

    def sg_next(r):
        sg_round(r).wait_recv()
        sga[r + 1] = sga[r] + sgr[r]
        if r < 4:
            sg_round(r + 1).start()

    spread = Spread(at, w, fin, fsend, frecv)
    low, high = (lambda t: t < 2), (lambda t: t >= 2)
    odd = lambda t: lax.rem(t, 2) == 1

    greet_all(at)

    @pl.when(s >= 2)
    def _():
        for t in range(4):
            cot_twin(t).start()

    gather.begin()
    for step in range(20):
        gather.step(step)
    for layer in range(2):
        for part in range(3):
            gather.settle(layer, part)
    gather.drain()
    chain.forward(0)
    for i in range(3):
        to_where(low, x_send, i)
    chain.forward(1)
    for i in range(3):
        to_where(lambda t: t == 1, u_out, i)
    chain.forward(2)
    for i in range(3):
        to_where(high, x_send, i)
    keep_x.start()
    chain.forward(3)
    for i in range(3):
        to_where(lambda t: t == 3, u_out, i)
    keep_u.start()
    chain.backward(3)
    for i in range(3):
        to_where(lambda t: t == 3, g_out, i)
    chain.backward(2)
    for i in range(3):
        to_where(low, g_send, i)
    keep_gl.start()
    for i in range(3):
        to_where(lambda t: t == 2, g_out, i)
    for p in range(4):
        twin_mix(1, p).start()
    keep_x.wait()
    x_twin(s).start()
    for i in range(3):
        x_send(i).wait_recv()
        x_twin(segs[i]).start()
    chain.backward(1)
    for i in range(3):
        to_where(lambda t: t == 1, g_out, i)
    plane_begin(1)
    keep_gl.wait()

    @pl.when(s < 2)
    def _():
        g_twin(s).start()
        for i in range(3):
            g_send(i).wait_recv()
            g_twin(segs[i]).start()

    loads = token_loads()
    for t in range(4):
        x_twin(t).wait_recv()
        cot_twin(t).wait_recv()
    for load in loads:
        if isinstance(load, tuple):
            @pl.when(s < 2)
            def _():
                load[0].start()

            @pl.when(s >= 2)
            def _():
                load[1].start()
        else:
            load.start()
    for load in loads:
        (load[0] if isinstance(load, tuple) else load).wait()
    pl.loop(0, 8)(feed_rows)
    product(eq, block_x, block_h)
    for goal in goals[:2]:
        feed_sum.step(goal, goal)
    product(rq, block_a, block_g)
    for i in range(4):
        feed_sum.step(4 + i, quarter)
    chain.backward(0)
    for p in range(4):
        twin_mix(0, p).start()
    for i in range(3):
        to_where(lambda t: t == 0, g_out, i)
    keep_g.start()
    sga[0] = sg[...]
    sg_round(0).start()
    plane_begin(0)
    sg_next(0)
    for goal in goals[2:]:
        feed_sum.step(goal, goal)
    plane_sum(1)
    for goal in goals[:2]:
        mix_sum.step(4 + goal, goal)
    sg_next(1)
    feed_units = [unit for unit in UNITS if unit[0] != "mix"]
    for unit in feed_units:
        spread.start(unit)
    sg_next(2)
    for goal in goals[2:]:
        mix_sum.step(4 + goal, goal)
    for unit in UNITS:
        if unit[0] == "mix" and unit[1] == 1:
            spread.start(unit)
    sg_next(3)
    plane_sum(0)
    for goal in goals[:2]:
        mix_sum.step(goal, goal)
    sg_next(4)
    for unit in feed_units:
        spread.relay(unit)
    for goal in goals[2:]:
        mix_sum.step(goal, goal)
    for unit in UNITS:
        if unit[0] == "mix" and unit[1] == 0:
            spread.start(unit)
    for unit in UNITS:
        if unit[0] == "mix":
            spread.relay(unit)

    sg_out[...] = sga[5]
    for r in range(5):
        sg_round(r).wait_send()
    for unit in UNITS:
        spread.drain(unit)
    for i in range(3):
        x_send(i).wait_send()
        to_where(low, g_send, i, wait=True)
        to_where(odd, u_out, i, wait=True)
        g_out(i).wait()
        for layer in range(2):
            for p in range(4):
                plane_send(layer, i, p).wait_send()

    @pl.when(lax.rem(s, 2) == 1)
    def _():
        for i in range(3):
            u_out(i).wait_recv()

    for t in range(4):
        x_twin(t).wait_send()
        cot_twin(t).wait_send()
    keep_u.wait()
    keep_g.wait()
    for p in range(4):
        for layer in range(2):
            twin_mix(layer, p).wait_send()
    for goal in range(4):
        for layer in range(2):
            mix_sum.drain(4 * layer + goal, goal)
        feed_sum.drain(goal, goal)
        feed_sum.drain(4 + goal, quarter)


def train_call(triple, output, expand, reduce, small, x, mask, gin, cot):
    V = pltpu.VMEM
    D = pltpu.SemaphoreType.DMA
    S = jax.ShapeDtypeStruct
    anywhere = pl.BlockSpec(memory_space=pl.ANY)
    vmem = pl.BlockSpec(memory_space=V)
    tokens = S((4, ROWS, W), BF16)
    out = pl.pallas_call(
        train_kernel,
        out_shape=(
            tokens, tokens, S((2, 12, STRIP, W), BF16), S((2, 24, W), F32), tokens, tokens, tokens, tokens,
            S((2, 4, 4, STRIP, W), BF16), S((2, 3, 4, STRIP, W), BF16), S((8, STRIP, W), BF16), S((8, STRIP, W), BF16),
            S((8, 2 * STRIP, W), BF16), S((8, 2 * STRIP, W), BF16),
        ),
        in_specs=[anywhere] * 4 + [vmem] * 4 + [anywhere],
        out_specs=[anywhere] * 3 + [vmem] + [anywhere] * 10,
        scratch_shapes=[
            V((24, W, W), BF16), V((4, ROWS, W), BF16), V((4, ROWS, W), BF16), V((2, 24, W), F32), V((6, 2, 24, W), F32), V((5, 2, 24, W), F32),
            V((2, 4, STRIP, W), BF16), V((2 * STRIP, W), BF16),
            D((20,)), D((2,)), D((3,)), D((3,)), D((3,)), D((3,)), D((2, 4)), D((2, 4)), D((2, 3)), D((2, 3)), D((2, 4)), D((2, 4)), D((2, 3, 4)), D((2, 3, 4)),
            D((8,)), D((8,)), D((8,)), D((8,)), D((8,)), D((8,)), D((20, 2, 2, 4)), D((20, 2)), D((5,)), D((5,)),
        ] + gather_scratch() + chain_scratch(),
        compiler_params=pltpu.CompilerParams(collective_id=1, has_side_effects=True, vmem_limit_bytes=VMEM_LIMIT),
        name="train_sections",
    )(triple, output, expand, reduce, small, x, mask, gin, cot)
    return out[:5]


def pack_small(conv_weight, conv_bias, mixer_gain, mixer_shift, triple_bias, output_bias, feed_gain, feed_shift, expand_bias, reduce_bias):
    part = conv_bias.shape[1]
    rows = [conv_weight] + [
        v.reshape(2, -1, part)
        for v in (conv_bias, mixer_gain, mixer_shift, triple_bias, output_bias, feed_gain, feed_shift, expand_bias, reduce_bias)
    ]
    return jnp.concatenate(rows, axis=1)


def spread_small(packed):
    n = packed.shape[0]

    def rows(lo, hi):
        return jnp.transpose(packed[:, :, lo:hi], (1, 2, 0, 3)).reshape(2, hi - lo, W)

    def long(lo, hi):
        return jnp.transpose(packed[:, :, lo:hi], (1, 0, 2, 3)).reshape(2, hi - lo, W)

    zero = jnp.zeros((2, 1, W), packed.dtype)
    return jnp.concatenate([rows(0, 12), long(12, 15), rows(15, 18), long(18, 22), rows(22, 23), zero], axis=1)


def pad_images(rows):
    return jnp.pad(rows.reshape(-1, LIVE, rows.shape[1]), ((0, 0), (0, IMG - LIVE), (0, 0))).reshape(-1, rows.shape[1])


def unpad_images(rows):
    lead = rows.shape[:-2]
    return rows.reshape(lead + (-1, IMG, W))[..., :LIVE, :].reshape(lead + (-1, W))


def spread_body(
    patches, region_mask, conv_weight, conv_bias, mixer_gain, mixer_shift, triple_weight, triple_bias, output_weight,
    output_bias, feed_gain, feed_shift, expand_weight, expand_bias, reduce_weight, reduce_bias, cotangent,
):
    s = lax.axis_index("segment")
    d = lax.axis_index("dp")
    packed = pack_small(conv_weight, conv_bias, mixer_gain, mixer_shift, triple_bias, output_bias, feed_gain, feed_shift, expand_bias, reduce_bias)
    small = spread_small(lax.all_gather(packed, "dp", axis=0)).astype(F32)
    own = patches.shape[0] // lax.axis_size("segment")
    mine = lambda v: lax.dynamic_slice_in_dim(v, s * own, own, 0)
    x = pad_images(mine(patches))
    cot = pad_images(cotangent).reshape(4, ROWS, W)
    gin = lax.dynamic_index_in_dim(cot, s, 0, keepdims=False)
    mask = pad_images(mine(region_mask).astype(BF16)[:, None])
    sec_out, grad_out, fin, sg, xin = train_call(triple_weight, output_weight, expand_weight, reduce_weight, small, x, mask, gin, cot)
    sec_out = jnp.where(lax.rem(s, 2) == 0, xin, sec_out)
    place = lambda v: unpad_images(v.reshape(1, 4 * ROWS, W))
    part = W // lax.axis_size("dp")
    fin = fin.astype(F32)
    wide = lambda lo, hi: jnp.concatenate([fin[:, j] for j in range(lo, hi)], axis=2)
    cut = lambda lo, hi: lax.dynamic_slice_in_dim(sg[:, lo:hi].reshape(2, -1), d * part * (hi - lo), part * (hi - lo), 1)
    taps = lax.dynamic_slice_in_dim(sg[:, :9], d * part, part, 2)
    return (
        place(sec_out), place(grad_out), taps, cut(9, 10), cut(10, 11), cut(11, 12), wide(0, 3), cut(12, 15), fin[:, 3],
        cut(15, 16), cut(16, 17), cut(17, 18), wide(4, 8), cut(18, 22), fin[:, 8:].reshape(2, 4 * part, W), cut(22, 23),
    )


def solution(mesh):
    in_specs = (
        P("dp", None),
        P("dp"),
        P(None, None, "dp"),
        P(None, "dp"),
        P(None, "dp"),
        P(None, "dp"),
        P(None, "dp", None),
        P(None, "dp"),
        P(None, "dp", None),
        P(None, "dp"),
        P(None, "dp"),
        P(None, "dp"),
        P(None, "dp", None),
        P(None, "dp"),
        P(None, "dp", None),
        P(None, "dp"),
        P("dp", None),
    )
    out_specs = (
        P("segment", "dp", None),
        P("segment", "dp", None),
        P(None, None, "dp"),
        P(None, "dp"),
        P(None, "dp"),
        P(None, "dp"),
        P(None, "dp", None),
        P(None, "dp"),
        P(None, "dp", None),
        P(None, "dp"),
        P(None, "dp"),
        P(None, "dp"),
        P(None, "dp", None),
        P(None, "dp"),
        P(None, "dp", None),
        P(None, "dp"),
    )
    chosen = spread_body if mesh.shape["dp"] == 8 and mesh.shape["segment"] == 4 else body
    return jax.shard_map(chosen, mesh=mesh, in_specs=in_specs, out_specs=out_specs, check_vma=False)
```

```python
from functools import partial

import jax
import jax.numpy as jnp
import numpy as np
from jax import lax
from jax.experimental import pallas as pl
from jax.experimental.pallas import tpu as pltpu
from jax.sharding import PartitionSpec as P

HD = 32
SIDE = 7
MICRO = 4
IMG_MB = 4


EPSILON = 1e-05


def as_sent(x):

    def short(part):
        return part.astype(jnp.bfloat16) if part.dtype == jnp.float32 else part

    return jax.tree.map(short, x)


def shifted_2(x, axis, by):
    count = lax.axis_size(axis)
    pairs = [(i, i + by) for i in range(count) if 0 <= i + by < count]
    return lax.ppermute(x, axis, pairs)


def dot_last(first_operand, second_operand):
    return lax.dot_general(
        first_operand, second_operand, (((1,), (1,)), ((), ())), preferred_element_type=jnp.float32
    )


def dot_first(first_operand, second_operand):
    return lax.dot_general(
        first_operand, second_operand, (((0,), (0,)), ((), ())), preferred_element_type=jnp.float32
    )


def layer_norm(values, norm_gain, norm_shift):
    center = values - jnp.mean(values, axis=-1, keepdims=True)
    spread = jnp.mean(center * center, axis=-1, keepdims=True)
    return center * lax.rsqrt(spread + EPSILON) * norm_gain + norm_shift


def position_conv(stream, conv_weight, conv_bias):
    features = stream.shape[-1]
    planes = stream.reshape(-1, SIDE, SIDE, features)
    padded = jnp.pad(planes, ((0, 0), (1, 1), (1, 1), (0, 0)))
    summed = jnp.zeros_like(planes) + conv_bias
    for tap_row in range(3):
        for tap_col in range(3):
            summed = (
                summed
                + padded[:, tap_row : tap_row + SIDE, tap_col : tap_col + SIDE, :]
                * conv_weight[tap_row * 3 + tap_col]
            )
    return stream + summed.reshape(stream.shape)


def front_part(stream, conv_weight, conv_bias, norm_gain, norm_shift):
    shifted = position_conv(stream, conv_weight, conv_bias)
    return (shifted, layer_norm(shifted, norm_gain, norm_shift))


def gelu_exact(values):
    return jax.nn.gelu(values, approximate=False)


def softmax_rows(scores):
    row_max = jnp.max(scores, axis=-1, keepdims=True)
    lifted = jnp.exp(scores - row_max)
    return lifted / jnp.sum(lifted, axis=-1, keepdims=True)


def window_forward(triple):
    tokens = triple.shape[0]
    features = triple.shape[1] // 3
    pieces = triple.reshape(tokens // (SIDE * SIDE), SIDE * SIDE, 3, features // HD, HD)
    queries = pieces[:, :, 0]
    key_parts = pieces[:, :, 1]
    value_parts = pieces[:, :, 2]
    scores = jnp.einsum(
        "iqhd,ikhd->ihqk", queries, key_parts, preferred_element_type=jnp.float32
    ) * HD ** (-0.5)
    softmaxed = softmax_rows(scores)
    softmaxed_low = softmaxed.astype(jnp.bfloat16)
    mixture = jnp.einsum(
        "ihqk,ikhd->iqhd", softmaxed_low, value_parts, preferred_element_type=jnp.float32
    )
    return (
        mixture.reshape(tokens, features),
        (queries, key_parts, value_parts, softmaxed, softmaxed_low),
    )


def window_backward(stored, grad_mixture):
    queries, key_parts, value_parts, softmaxed, softmaxed_low = stored
    grad_pieces = grad_mixture.reshape(queries.shape)
    grad_values = jnp.einsum(
        "ihqk,iqhd->ikhd", softmaxed_low, grad_pieces, preferred_element_type=jnp.float32
    )
    grad_soft = jnp.einsum(
        "iqhd,ikhd->ihqk", grad_pieces, value_parts, preferred_element_type=jnp.float32
    )
    grad_scores = (
        softmaxed * (grad_soft - jnp.sum(grad_soft * softmaxed, axis=-1, keepdims=True))
    ).astype(jnp.bfloat16)
    grad_queries = jnp.einsum(
        "ihqk,ikhd->iqhd", grad_scores, key_parts, preferred_element_type=jnp.float32
    ) * HD ** (-0.5)
    grad_keys = jnp.einsum(
        "ihqk,iqhd->ikhd", grad_scores, queries, preferred_element_type=jnp.float32
    ) * HD ** (-0.5)
    joined = jnp.stack([grad_queries, grad_keys, grad_values], axis=2)
    return joined.reshape(grad_mixture.shape[0], 3 * grad_mixture.shape[1])


def channel_forward(triple, mask_rows):
    tokens = triple.shape[0]
    features = triple.shape[1] // 3
    images = tokens // (SIDE * SIDE)
    pieces = triple.reshape(images, SIDE * SIDE, 3, features // HD, HD)
    queries = pieces[:, :, 0]
    keep_mask = mask_rows.reshape(images, SIDE * SIDE, 1, 1).astype(jnp.bfloat16)
    masked = pieces[:, :, 1] * keep_mask
    value_parts = pieces[:, :, 2]
    scores = jnp.einsum(
        "itgc,itge->igce", queries, masked, preferred_element_type=jnp.float32
    ) * HD ** (-0.5)
    softmaxed = softmax_rows(scores)
    softmaxed_low = softmaxed.astype(jnp.bfloat16)
    mixture = jnp.einsum(
        "igce,itge->itgc", softmaxed_low, value_parts, preferred_element_type=jnp.float32
    )
    return (
        mixture.reshape(tokens, features),
        (queries, masked, value_parts, keep_mask, softmaxed, softmaxed_low),
    )


def channel_backward(stored, grad_mixture):
    queries, masked, value_parts, keep_mask, softmaxed, softmaxed_low = stored
    grad_pieces = grad_mixture.reshape(queries.shape)
    grad_soft = jnp.einsum(
        "itgc,itge->igce", grad_pieces, value_parts, preferred_element_type=jnp.float32
    )
    grad_values = jnp.einsum(
        "igce,itgc->itge", softmaxed_low, grad_pieces, preferred_element_type=jnp.float32
    )
    grad_scores = (
        softmaxed * (grad_soft - jnp.sum(grad_soft * softmaxed, axis=-1, keepdims=True))
    ).astype(jnp.bfloat16)
    grad_queries = jnp.einsum(
        "igce,itge->itgc", grad_scores, masked, preferred_element_type=jnp.float32
    ) * HD ** (-0.5)
    grad_masked = jnp.einsum(
        "igce,itgc->itge", grad_scores, queries, preferred_element_type=jnp.float32
    ) * HD ** (-0.5)
    grad_keys = grad_masked * keep_mask.astype(jnp.float32)
    joined = jnp.stack([grad_queries, grad_keys, grad_values], axis=2)
    return joined.reshape(grad_mixture.shape[0], 3 * grad_mixture.shape[1])


def mixer_inner(stream, weights, mask_rows, channel):
    (
        conv_weight,
        conv_bias,
        norm_gain,
        norm_shift,
        triple_weight,
        triple_bias,
        output_weight,
        output_bias,
    ) = weights[:8]
    widened = stream.astype(jnp.float32)
    (shifted, normed), front_pull = jax.vjp(
        front_part,
        widened,
        conv_weight.astype(jnp.float32),
        conv_bias.astype(jnp.float32),
        norm_gain.astype(jnp.float32),
        norm_shift.astype(jnp.float32),
    )
    normed_low = normed.astype(jnp.bfloat16)
    triple = (
        jnp.dot(normed_low, triple_weight, preferred_element_type=jnp.float32)
        + triple_bias.astype(jnp.float32)
    ).astype(jnp.bfloat16)
    if channel:
        mixture, stored = channel_forward(triple, mask_rows)
    else:
        mixture, stored = window_forward(triple)
    mixture_low = mixture.astype(jnp.bfloat16)
    return (shifted, front_pull, normed_low, stored, mixture_low)


def mixer_forward(stream, weights, mask_rows, channel):
    shifted, front_pull, normed_low, stored, mixture_low = mixer_inner(
        stream, weights, mask_rows, channel
    )
    result = (
        shifted
        + jnp.dot(mixture_low, weights[6], preferred_element_type=jnp.float32)
        + weights[7].astype(jnp.float32)
    )
    return result.astype(jnp.bfloat16)


def mixer_backward(stream, grad_out, weights, mask_rows, channel):
    shifted, front_pull, normed_low, stored, mixture_low = mixer_inner(
        stream, weights, mask_rows, channel
    )
    grad_wide = grad_out.astype(jnp.float32)
    grad_out_bias = jnp.sum(grad_wide, axis=0)
    grad_out_weight = dot_first(mixture_low, grad_out)
    grad_mixture = dot_last(grad_out, weights[6]).astype(jnp.bfloat16)
    if channel:
        grad_triple = channel_backward(stored, grad_mixture).astype(jnp.bfloat16)
    else:
        grad_triple = window_backward(stored, grad_mixture).astype(jnp.bfloat16)
    grad_tri_weight = dot_first(normed_low, grad_triple)
    grad_tri_bias = jnp.sum(grad_triple.astype(jnp.float32), axis=0)
    grad_normed = dot_last(grad_triple, weights[4])
    grad_stream, grad_taps, grad_tap_bias, grad_gain, grad_shift = front_pull(
        (grad_wide, grad_normed)
    )
    zero_tail = tuple((jnp.zeros(member.shape, jnp.float32) for member in weights[8:]))
    return (
        grad_stream.astype(jnp.bfloat16),
        (
            grad_taps,
            grad_tap_bias,
            grad_gain,
            grad_shift,
            grad_tri_weight,
            grad_tri_bias,
            grad_out_weight,
            grad_out_bias,
        )
        + zero_tail,
    )


def feed_inner(stream, weights):
    norm_gain, norm_shift, expand_weight, expand_bias, reduce_weight, reduce_bias = weights[8:]
    widened = stream.astype(jnp.float32)
    normed, norm_pull = jax.vjp(
        layer_norm, widened, norm_gain.astype(jnp.float32), norm_shift.astype(jnp.float32)
    )
    normed_low = normed.astype(jnp.bfloat16)
    hidden = jnp.dot(
        normed_low, expand_weight, preferred_element_type=jnp.float32
    ) + expand_bias.astype(jnp.float32)
    active, gelu_pull = jax.vjp(gelu_exact, hidden)
    return (widened, norm_pull, normed_low, gelu_pull, active.astype(jnp.bfloat16))


def feed_forward(stream, weights):
    widened, norm_pull, normed_low, gelu_pull, active_low = feed_inner(stream, weights)
    result = (
        widened
        + jnp.dot(active_low, weights[12], preferred_element_type=jnp.float32)
        + weights[13].astype(jnp.float32)
    )
    return result.astype(jnp.bfloat16)


def feed_backward(stream, grad_out, weights):
    widened, norm_pull, normed_low, gelu_pull, active_low = feed_inner(stream, weights)
    grad_wide = grad_out.astype(jnp.float32)
    grad_red_bias = jnp.sum(grad_wide, axis=0)
    grad_red_weight = dot_first(active_low, grad_out)
    grad_active = dot_last(grad_out, weights[12])
    grad_hidden = gelu_pull(grad_active)[0].astype(jnp.bfloat16)
    grad_exp_weight = dot_first(normed_low, grad_hidden)
    grad_exp_bias = jnp.sum(grad_hidden.astype(jnp.float32), axis=0)
    grad_normed = dot_last(grad_hidden, weights[10])
    grad_inner, grad_gain, grad_shift = norm_pull(grad_normed)
    zero_head = tuple((jnp.zeros(member.shape, jnp.float32) for member in weights[:8]))
    grad_stream = grad_wide + grad_inner
    return (
        grad_stream.astype(jnp.bfloat16),
        zero_head
        + (grad_gain, grad_shift, grad_exp_weight, grad_exp_bias, grad_red_weight, grad_red_bias),
    )


def section_forward(section, stream, weights, mask_rows):
    if section % 2 == 1:
        return feed_forward(stream, weights)
    return mixer_forward(stream, weights, mask_rows, section == 2)


def section_backward(section, stream, grad_out, weights, mask_rows):
    if section % 2 == 1:
        return feed_backward(stream, grad_out, weights)
    return mixer_backward(stream, grad_out, weights, mask_rows, section == 2)


def spare_forward(stream, weights, mask_rows):
    return jnp.zeros_like(stream)


def spare_backward(stream, grad_out, weights, mask_rows):
    return (
        jnp.zeros_like(stream),
        tuple((jnp.zeros(member.shape, jnp.float32) for member in weights)),
    )


def put_rows(buffer, rows, row_start, is_live):
    former = lax.dynamic_slice_in_dim(buffer, row_start, rows.shape[0], 0)
    return lax.dynamic_update_slice_in_dim(buffer, jnp.where(is_live, rows, former), row_start, 0)


def run_segments(layer_set, patches, region_mask, cotangent, segment_index, segments):
    features = patches.shape[1]
    micro_count = MICRO
    micro_rows = IMG_MB * SIDE * SIDE
    tick_count = micro_count + segments - 1
    forward_branches = [
        partial(section_forward, 0),
        partial(section_forward, 1),
        partial(section_forward, 2),
        partial(section_forward, 3),
        spare_forward,
    ]
    backward_branches = [
        partial(section_backward, 0),
        partial(section_backward, 1),
        partial(section_backward, 2),
        partial(section_backward, 3),
        spare_backward,
    ]
    received = jnp.zeros((micro_rows, features), jnp.bfloat16)
    kept_inputs = jnp.zeros((micro_count * micro_rows, features), jnp.bfloat16)
    outputs_here = jnp.zeros((micro_count * micro_rows, features), jnp.bfloat16)
    for tick_index in range(tick_count):
        micro_index = tick_index - segment_index
        is_live = (micro_index >= 0) & (micro_index < micro_count)
        row_start = jnp.clip(micro_index, 0, micro_count - 1) * micro_rows
        fresh_rows = lax.dynamic_slice_in_dim(patches, row_start, micro_rows, 0)
        mask_rows = lax.dynamic_slice_in_dim(region_mask, row_start, micro_rows, 0)
        entering = jnp.where(segment_index == 0, fresh_rows, received)
        leaving = lax.switch(
            jnp.where(is_live, segment_index, segments),
            forward_branches,
            entering,
            layer_set,
            mask_rows,
        )
        kept_inputs = put_rows(kept_inputs, entering, row_start, is_live)
        outputs_here = put_rows(outputs_here, leaving, row_start, is_live)
        if tick_index + 1 < tick_count:
            received = jax.tree.map(
                lambda part, own: part.astype(own.dtype),
                shifted_2(as_sent(leaving), "segment", 1),
                leaving,
            )
    grad_received = jnp.zeros((micro_rows, features), jnp.bfloat16)
    grads_here = jnp.zeros((micro_count * micro_rows, features), jnp.bfloat16)
    totals = tuple((jnp.zeros(member.shape, jnp.float32) for member in layer_set))
    for tick_index in range(tick_count):
        micro_index = tick_index - (segments - 1 - segment_index)
        is_live = (micro_index >= 0) & (micro_index < micro_count)
        row_start = jnp.clip(micro_index, 0, micro_count - 1) * micro_rows
        seed_rows = lax.dynamic_slice_in_dim(cotangent, row_start, micro_rows, 0)
        mask_rows = lax.dynamic_slice_in_dim(region_mask, row_start, micro_rows, 0)
        arriving = jnp.where(segment_index == segments - 1, seed_rows, grad_received)
        stream = lax.dynamic_slice_in_dim(kept_inputs, row_start, micro_rows, 0)
        grad_stream, grad_terms = lax.switch(
            jnp.where(is_live, segment_index, segments),
            backward_branches,
            stream,
            arriving,
            layer_set,
            mask_rows,
        )
        totals = tuple(
            (first_term + second_term for first_term, second_term in zip(totals, grad_terms))
        )
        grads_here = put_rows(grads_here, grad_stream, row_start, is_live)
        if tick_index + 1 < tick_count:
            grad_received = jax.tree.map(
                lambda part, own: part.astype(own.dtype),
                shifted_2(as_sent(grad_stream), "segment", -1),
                grad_stream,
            )
    return (outputs_here, grads_here, totals)


def body(
    patches,
    region_mask,
    conv_weight,
    conv_bias,
    mixer_gain,
    mixer_shift,
    triple_weight,
    triple_bias,
    output_weight,
    output_bias,
    feed_gain,
    feed_shift,
    expand_weight,
    expand_bias,
    reduce_weight,
    reduce_bias,
    cotangent,
):
    params = (
        conv_weight,
        conv_bias,
        mixer_gain,
        mixer_shift,
        triple_weight,
        triple_bias,
        output_weight,
        output_bias,
        feed_gain,
        feed_shift,
        expand_weight,
        expand_bias,
        reduce_weight,
        reduce_bias,
    )
    segments = lax.axis_size("segment")
    segment_index = lax.axis_index("segment")
    layer_index = segment_index // 2
    slices = tuple(
        (lax.dynamic_index_in_dim(member, layer_index, 0, keepdims=False) for member in params)
    )
    layer_set = (
        lax.all_gather(slices[0], "dp", axis=1, tiled=True),
        lax.all_gather(slices[1], "dp", axis=0, tiled=True),
        lax.all_gather(slices[2], "dp", axis=0, tiled=True),
        lax.all_gather(slices[3], "dp", axis=0, tiled=True),
        lax.all_gather(slices[4], "dp", axis=0, tiled=True),
        lax.all_gather(slices[5], "dp", axis=0, tiled=True),
        lax.all_gather(slices[6], "dp", axis=0, tiled=True),
        lax.all_gather(slices[7], "dp", axis=0, tiled=True),
        lax.all_gather(slices[8], "dp", axis=0, tiled=True),
        lax.all_gather(slices[9], "dp", axis=0, tiled=True),
        lax.all_gather(slices[10], "dp", axis=0, tiled=True),
        lax.all_gather(slices[11], "dp", axis=0, tiled=True),
        lax.all_gather(slices[12], "dp", axis=0, tiled=True),
        lax.all_gather(slices[13], "dp", axis=0, tiled=True),
    )
    outputs_here, grads_here, totals = run_segments(
        layer_set, patches, region_mask, cotangent, segment_index, segments
    )
    reduced = (
        lax.psum_scatter(totals[0], "dp", scatter_dimension=1, tiled=True),
        lax.psum_scatter(totals[1], "dp", scatter_dimension=0, tiled=True),
        lax.psum_scatter(totals[2], "dp", scatter_dimension=0, tiled=True),
        lax.psum_scatter(totals[3], "dp", scatter_dimension=0, tiled=True),
        lax.psum_scatter(totals[4], "dp", scatter_dimension=0, tiled=True),
        lax.psum_scatter(totals[5], "dp", scatter_dimension=0, tiled=True),
        lax.psum_scatter(totals[6], "dp", scatter_dimension=0, tiled=True),
        lax.psum_scatter(totals[7], "dp", scatter_dimension=0, tiled=True),
        lax.psum_scatter(totals[8], "dp", scatter_dimension=0, tiled=True),
        lax.psum_scatter(totals[9], "dp", scatter_dimension=0, tiled=True),
        lax.psum_scatter(totals[10], "dp", scatter_dimension=0, tiled=True),
        lax.psum_scatter(totals[11], "dp", scatter_dimension=0, tiled=True),
        lax.psum_scatter(totals[12], "dp", scatter_dimension=0, tiled=True),
        lax.psum_scatter(totals[13], "dp", scatter_dimension=0, tiled=True),
    )
    placed = tuple(
        (
            jnp.stack(
                [jnp.where(layer_index == 0, member, 0.0), jnp.where(layer_index == 1, member, 0.0)]
            )
            for member in reduced
        )
    )
    section_outputs = outputs_here[None]
    section_grads = grads_here[None]
    summed = (
        lax.psum(placed[0].astype(jnp.bfloat16), "segment").astype(jnp.float32),
        lax.psum(placed[1].astype(jnp.bfloat16), "segment").astype(jnp.float32),
        lax.psum(placed[2].astype(jnp.bfloat16), "segment").astype(jnp.float32),
        lax.psum(placed[3].astype(jnp.bfloat16), "segment").astype(jnp.float32),
        lax.psum(placed[4].astype(jnp.bfloat16), "segment").astype(jnp.float32),
        lax.psum(placed[5].astype(jnp.bfloat16), "segment").astype(jnp.float32),
        lax.psum(placed[6].astype(jnp.bfloat16), "segment").astype(jnp.float32),
        lax.psum(placed[7].astype(jnp.bfloat16), "segment").astype(jnp.float32),
        lax.psum(placed[8].astype(jnp.bfloat16), "segment").astype(jnp.float32),
        lax.psum(placed[9].astype(jnp.bfloat16), "segment").astype(jnp.float32),
        lax.psum(placed[10].astype(jnp.bfloat16), "segment").astype(jnp.float32),
        lax.psum(placed[11].astype(jnp.bfloat16), "segment").astype(jnp.float32),
        lax.psum(placed[12].astype(jnp.bfloat16), "segment").astype(jnp.float32),
        lax.psum(placed[13].astype(jnp.bfloat16), "segment").astype(jnp.float32),
    )
    return (
        section_outputs,
        section_grads,
        summed[0],
        summed[1],
        summed[2],
        summed[3],
        summed[4],
        summed[5],
        summed[6],
        summed[7],
        summed[8],
        summed[9],
        summed[10],
        summed[11],
        summed[12],
        summed[13],
    )


W = 768
IMG = 56
LIVE = 49
ROWS = 224
PAIR = 2 * IMG
LANES = 128
SCALE = HD ** (-0.5)
F32 = jnp.float32
BF16 = jnp.bfloat16
TAPS = [(a, b) for a in range(3) for b in range(3)]


def mm(a, b):
    return lax.dot_general(a, b, (((1,), (0,)), ((), ())), preferred_element_type=F32)


def mm_nt(a, b):
    return lax.dot_general(a, b, (((1,), (1,)), ((), ())), preferred_element_type=F32)


def mm_tn(a, b):
    return lax.dot_general(a, b, (((0,), (0,)), ((), ())), preferred_element_type=F32)


def row_index(rows):
    return lax.broadcasted_iota(jnp.int32, (rows, 1), 0)


def live_rows(rows):
    return lax.rem(row_index(rows), IMG) < LIVE


def column_masks(rows):
    place = lax.rem(row_index(rows), IMG)
    column = lax.rem(place, SIDE)
    live = place < LIVE
    return [(live & (column + b - 1 >= 0) & (column + b - 1 < SIDE)).astype(F32) for b in range(3)]


def rolled(values, by):
    by = by % values.shape[0]
    return values if by == 0 else pltpu.roll(values, by, 0)


def norm_parts(values):
    center = values - jnp.mean(values, axis=-1, keepdims=True)
    spread = jnp.mean(center * center, axis=-1, keepdims=True)
    rstd = lax.rsqrt(spread + EPSILON)
    return center * rstd, rstd


def column_sum(values):
    return jnp.sum(values, axis=0, keepdims=True)


def head_lanes(head):
    lane = lax.broadcasted_iota(jnp.int32, (1, LANES), 1)
    return (lane // HD) == head


def only(values, mask):
    return jnp.where(mask, values, jnp.zeros_like(values))


def mixer_front(layer, u_in, w, small, c_ref, xhat, rstd, n_ref, t_ref, p_ref, m_ref):
    base = 12 * layer
    row = lambda r: small[layer, r:r + 1, :]
    v = u_in[...].astype(F32)
    masks = column_masks(ROWS)
    total = v + row(9)
    for b in range(3):
        part = jnp.zeros_like(v)
        for a in range(3):
            part = part + row(3 * a + b) * rolled(v, -(SIDE * (a - 1) + b - 1))
        total = total + part * masks[b]
    c = jnp.where(live_rows(ROWS), total, 0.0)
    c_ref[...] = c
    x, r = norm_parts(c)
    xhat[...] = x
    rstd[...] = r
    n_ref[...] = (x * row(10) + row(11)).astype(BF16)

    @pl.loop(0, 3)
    def _(j):
        cols = pl.ds(pl.multiple_of(W * j, W), W)
        t_ref[:, cols] = (mm(n_ref[...], w[base + j]) + small[layer, pl.ds(12 + j, 1), :]).astype(BF16)


def mixer_mixture(layer, channel, u_out, w, small, mask, bias, c_ref, xhat, rstd, n_ref, t_ref, p_ref, m_ref):
    base = 12 * layer

    @pl.loop(0, 6)
    def _(g):
        qs = pl.ds(pl.multiple_of(LANES * g, LANES), LANES)
        ks = pl.ds(pl.multiple_of(W + LANES * g, LANES), LANES)
        vs = pl.ds(pl.multiple_of(2 * W + LANES * g, LANES), LANES)
        for pair in range(2):
            rows = slice(PAIR * pair, PAIR * pair + PAIR)
            q, k, val = t_ref[rows, qs], t_ref[rows, ks], t_ref[rows, vs]
            mix = jnp.zeros((PAIR, LANES), F32)
            if channel:
                for im in range(2):
                    here = (row_index(PAIR) // IMG) == im
                    km = k * only(mask[rows, :], here)
                    s = mm_tn(q, km) * SCALE + bias[...]
                    e = jnp.exp(s - jnp.max(s, axis=-1, keepdims=True))
                    p = e / jnp.sum(e, axis=-1, keepdims=True)
                    p_ref[g, 2 * pair + im] = p
                    mix = mix + mm_nt(only(val, here), p.astype(BF16))
            else:
                for head in range(4):
                    lanes = head_lanes(head)
                    s = mm_nt(only(q, lanes), k) * SCALE + bias[...]
                    e = jnp.exp(s - jnp.max(s, axis=-1, keepdims=True))
                    p = e / jnp.sum(e, axis=-1, keepdims=True)
                    p_ref[g, 4 * pair + head] = p
                    mix = mix + mm(p.astype(BF16), only(val, lanes))
            m_ref[rows, qs] = mix.astype(BF16)

    out = c_ref[...] + mm(m_ref[...], w[base + 3]) + small[layer, 15:16, :]
    u_out[...] = jnp.where(live_rows(ROWS), out, 0.0).astype(BF16)


def mix_backward(layer, channel, u_in, g_in, g_out, w, small, mask, sg, dw, c_ref, xhat, rstd, n_ref, t_ref, p_ref, m_ref, dm_ref, dt_ref, acc):
    base = 12 * layer
    row = lambda r: small[layer, r:r + 1, :]
    g = g_in[...]
    sg[layer, 15:16, :] = column_sum(g.astype(F32))
    dm_ref[...] = mm_nt(g, w[base + 3]).astype(BF16)
    dw(layer, 3, m_ref, lambda: g_in[...])

    @pl.loop(0, 6)
    def _(grp):
        qs = pl.ds(pl.multiple_of(LANES * grp, LANES), LANES)
        ks = pl.ds(pl.multiple_of(W + LANES * grp, LANES), LANES)
        vs = pl.ds(pl.multiple_of(2 * W + LANES * grp, LANES), LANES)
        for pair in range(2):
            rows = slice(PAIR * pair, PAIR * pair + PAIR)
            q, k, val, dm = t_ref[rows, qs], t_ref[rows, ks], t_ref[rows, vs], dm_ref[rows, qs]
            dq = jnp.zeros((PAIR, LANES), F32)
            dk = jnp.zeros((PAIR, LANES), F32)
            dv = jnp.zeros((PAIR, LANES), F32)
            if channel:
                for im in range(2):
                    here = (row_index(PAIR) // IMG) == im
                    keep = only(mask[rows, :], here)
                    km = k * keep
                    p = p_ref[grp, 2 * pair + im]
                    dmh = only(dm, here)
                    dp = mm_tn(dmh, val)
                    dv = dv + mm(dmh, p.astype(BF16))
                    ds = (p * (dp - jnp.sum(dp * p, axis=-1, keepdims=True))).astype(BF16)
                    dq = dq + mm_nt(km, ds)
                    dk = dk + mm(only(q, here), ds) * keep.astype(F32)
            else:
                for head in range(4):
                    lanes = head_lanes(head)
                    p = p_ref[grp, 4 * pair + head]
                    dmh = only(dm, lanes)
                    dp = mm_nt(dmh, val)
                    dv = dv + mm_tn(p.astype(BF16), dmh)
                    ds = (p * (dp - jnp.sum(dp * p, axis=-1, keepdims=True))).astype(BF16)
                    dq = dq + mm(ds, only(k, lanes))
                    dk = dk + mm_tn(ds, only(q, lanes))
            dt_ref[rows, qs] = (dq * SCALE).astype(BF16)
            dt_ref[rows, ks] = (dk * SCALE).astype(BF16)
            dt_ref[rows, vs] = dv.astype(BF16)

    acc[...] = jnp.zeros_like(acc)

    @pl.loop(0, 3)
    def _(j):
        cols = pl.ds(pl.multiple_of(W * j, W), W)
        acc[...] += mm_nt(dt_ref[:, cols], w[base + j])
        sg[layer, pl.ds(12 + j, 1), :] = column_sum(dt_ref[:, cols].astype(F32))
        dw(layer, j, n_ref, lambda: dt_ref[:, cols])

    dn = acc[...]
    x = xhat[...]
    sg[layer, 10:11, :] = column_sum(dn * x)
    sg[layer, 11:12, :] = column_sum(dn)
    e = dn * row(10)
    inner = rstd[...] * (e - jnp.mean(e, axis=-1, keepdims=True) - x * jnp.mean(e * x, axis=-1, keepdims=True))
    dc = jnp.where(live_rows(ROWS), g_in[...].astype(F32) + inner, 0.0)
    sg[layer, 9:10, :] = column_sum(dc)
    v = u_in[...].astype(F32)
    masks = column_masks(ROWS)
    du = dc
    for b in range(3):
        dcm = dc * masks[b]
        for a in range(3):
            moved = rolled(dcm, SIDE * (a - 1) + b - 1)
            tap = 3 * a + b
            du = du + row(tap) * moved
            sg[layer, tap:tap + 1, :] = column_sum(moved * v)
    g_out[...] = jnp.where(live_rows(ROWS), du, 0.0).astype(BF16)


ROOT_HALF = 0.5 ** 0.5
ROOT_TWO_PI = 0.3989422804014327


def ff_forward(layer, u_in, u_out, w, small, xhat, rstd, n_ref, slope, acc):
    base = 12 * layer
    row = lambda r: small[layer, r:r + 1, :]
    x, r = norm_parts(u_in[...].astype(F32))
    xhat[...] = x
    rstd[...] = r
    n_ref[...] = (x * row(16) + row(17)).astype(BF16)
    acc[...] = u_in[...].astype(F32) + row(22)

    @pl.loop(0, 4)
    def _(j):
        cols = pl.ds(pl.multiple_of(W * j, W), W)
        h = mm(n_ref[...], w[base + 4 + j]) + small[layer, pl.ds(18 + j, 1), :]
        cdf = 0.5 + 0.5 * lax.erf(h * ROOT_HALF)
        slope[:, cols] = cdf + h * (ROOT_TWO_PI * jnp.exp(-0.5 * h * h))
        acc[...] += mm((h * cdf).astype(BF16), w[base + 8 + j])

    u_out[...] = jnp.where(live_rows(ROWS), acc[...], 0.0).astype(BF16)


def ff_backward(layer, g_in, g_out, w, small, sg, xhat, rstd, slope, acc):
    base = 12 * layer
    row = lambda r: small[layer, r:r + 1, :]
    sg[layer, 22:23, :] = column_sum(g_in[...].astype(F32))
    acc[...] = jnp.zeros_like(acc)

    @pl.loop(0, 4)
    def _(j):
        cols = pl.ds(pl.multiple_of(W * j, W), W)
        dh = (mm_nt(g_in[...], w[base + 8 + j]) * slope[:, cols]).astype(BF16)
        sg[layer, pl.ds(18 + j, 1), :] = column_sum(dh.astype(F32))
        acc[...] += mm_nt(dh, w[base + 4 + j])

    dn = acc[...]
    x = xhat[...]
    sg[layer, 16:17, :] = column_sum(dn * x)
    sg[layer, 17:18, :] = column_sum(dn)
    e = dn * row(16)
    inner = rstd[...] * (e - jnp.mean(e, axis=-1, keepdims=True) - x * jnp.mean(e * x, axis=-1, keepdims=True))
    g_out[...] = jnp.where(live_rows(ROWS), g_in[...].astype(F32) + inner, 0.0).astype(BF16)


def chain_scratch():
    V = pltpu.VMEM
    mixer = [V((ROWS, W), F32), V((ROWS, 1), F32), V((ROWS, W), BF16), V((ROWS, 3 * W), BF16)]
    feed = [V((ROWS, W), F32), V((ROWS, 1), F32), V((ROWS, W), BF16), V((ROWS, 4 * W), F32)]
    return (mixer + [V((6, 8, PAIR, PAIR), F32), V((ROWS, W), BF16)] + feed + mixer + [V((6, 4, LANES, LANES), F32), V((ROWS, W), BF16)] + feed
            + [V((ROWS, W), F32), V((ROWS, W), F32), V((ROWS, W), BF16), V((ROWS, 3 * W), BF16), V((PAIR, PAIR), F32), V((LANES, LANES), F32)])


def fill_biases(win_bias, chan_bias):
    qi = lax.broadcasted_iota(jnp.int32, (PAIR, PAIR), 0)
    ki = lax.broadcasted_iota(jnp.int32, (PAIR, PAIR), 1)
    win_bias[...] = jnp.where(((qi // IMG) == (ki // IMG)) & (lax.rem(ki, IMG) < LIVE), 0.0, -1e30).astype(F32)
    ci = lax.broadcasted_iota(jnp.int32, (LANES, LANES), 0)
    ei = lax.broadcasted_iota(jnp.int32, (LANES, LANES), 1)
    chan_bias[...] = jnp.where((ci // HD) == (ei // HD), 0.0, -1e30).astype(F32)


class Chain:
    def __init__(self, w, small, mask, u, g, sg, dw, scratch):
        self.w, self.small, self.mask, self.u, self.g, self.sg, self.dw = w, small, mask, u, g, sg, dw
        s = scratch
        self.window, self.feed0, self.channel, self.feed1 = s[0:6], s[6:10], s[10:16], s[16:20]
        self.c_ref, self.acc, self.dm, self.dt, self.win_bias, self.chan_bias = s[20:26]

    def front(self, k):
        u, w, small = self.u, self.w, self.small
        if k == 0:
            fill_biases(self.win_bias, self.chan_bias)
            mixer_front(0, u[0], w, small, self.c_ref, *self.window)
        if k == 1:
            ff_forward(0, u[1], u[2], w, small, *self.feed0, self.acc)
        if k == 2:
            mixer_front(1, u[2], w, small, self.c_ref, *self.channel)
        if k == 3:
            ff_forward(1, u[3], u[4], w, small, *self.feed1, self.acc)

    def rest(self, k):
        u, w, small = self.u, self.w, self.small
        if k == 0:
            mixer_mixture(0, False, u[1], w, small, self.mask, self.win_bias, self.c_ref, *self.window)
        if k == 2:
            mixer_mixture(1, True, u[3], w, small, self.mask, self.chan_bias, self.c_ref, *self.channel)

    def backward(self, k):
        u, g, w, small, sg = self.u, self.g, self.w, self.small, self.sg
        if k in (0, 2):
            parts = self.channel if k == 2 else self.window
            mix_backward(k // 2, k == 2, u[k], g[k + 1], g[k], w, small, self.mask, sg, self.dw, self.c_ref, *parts, self.dm, self.dt, self.acc)
        else:
            x, r, _, slope = self.feed0 if k == 1 else self.feed1
            ff_backward(k // 2, g[k + 1], g[k], w, small, sg, x, r, slope, self.acc)


MESH = pl.DeviceIdType.MESH
VMEM_LIMIT = 63 * 1024 * 1024
STRIP = 96
HALF = 384


def slot(item, line, d):
    red = lax.rem(item, 3) // 2
    block = 12 * (item // 3) + 4 * lax.rem(item, 3) + (1 - red) * line + red * (d // 2)
    row = (1 - red) * STRIP * d + red * (4 * STRIP * lax.rem(d, 2) + STRIP * line)
    return block, row


def other_planes(z):
    near = z + 1 - 2 * (z // 2)
    far = 3 * (1 - z // 2)
    return near, 6 - z - near - far, far


class Place:
    def __init__(self):
        self.s = lax.axis_index("segment")
        self.d = lax.axis_index("dp")
        self.z = self.d // 2
        self.c = lax.rem(self.d, 2)
        self.xn = self.s + 1 - 2 * lax.rem(self.s, 2)
        self.yn = lax.rem(self.s + 2, 4)
        self.dn = 3 - self.s
        self.twin = self.d + 1 - 2 * self.c


def remote(src, dst, ssem, rsem, seg, dev):
    return pltpu.make_async_remote_copy(src, dst, ssem, rsem, device_id=(seg, dev), device_id_type=MESH)


def gather_scratch():
    D = pltpu.SemaphoreType.DMA
    return [D((2, 9)), D((6, 5)), D((6, 3, 2)), D((6, 3, 2)), D((6, 4, 4)), D((2, 3, 4)), D((2, 3, 4))]


class Gather:
    def __init__(self, at, shards, wbuf, sems):
        self.at, self.shards, self.w = at, shards, wbuf
        self.lsem, self.zs, self.xs, self.ys, self.pr, self.cs, self.cr = sems
        self.planes = other_planes(at.z)
        self.away = 2 * (at.z // 2) - 1
        self.inner = (at.z == 1) | (at.z == 2)
        self.groups = [(layer, part, k) for layer in range(2) for part in range(3) for k in range(3)]

    def strip(self, item, line, plane):
        block, row = slot(item, line, 2 * plane + self.at.c)
        return self.w.at[block, pl.ds(pl.multiple_of(row, STRIP), STRIP), :]

    def quad_ref(self, layer, part, plane, core):
        if part == 2:
            return self.w.at[12 * layer + 8 + plane, pl.ds(pl.multiple_of(4 * STRIP * core, 4 * STRIP), 4 * STRIP), :]
        row = pl.multiple_of(STRIP * (2 * plane + core), STRIP)
        return self.w.at[pl.ds(12 * layer + 4 * part, 4), pl.ds(row, STRIP), :]

    def quad(self, layer, part, plane, core, k):
        ref = self.quad_ref(layer, part, plane, core)
        return remote(ref, ref, self.cs.at[layer, part, k], self.cr.at[layer, part, plane], self.at.s, self.at.twin)

    def local(self, layer):
        triple, output, expand, reduce = self.shards
        at, w, base = self.at, self.w, 12 * layer
        rows = pl.ds(pl.multiple_of(STRIP * at.d, STRIP), STRIP)
        sems = self.lsem.at
        copies = [pltpu.make_async_copy(triple.at[layer, :, pl.ds(W * j, W)], w.at[base + j, rows, :], sems[layer, j]) for j in range(3)]
        copies.append(pltpu.make_async_copy(output.at[layer], w.at[base + 3, rows, :], sems[layer, 3]))
        copies += [pltpu.make_async_copy(expand.at[layer, :, pl.ds(W * j, W)], w.at[base + 4 + j, rows, :], sems[layer, 4 + j]) for j in range(4)]
        half = pl.ds(pl.multiple_of(4 * STRIP * at.c, 4 * STRIP), 4 * STRIP)
        copies.append(pltpu.make_async_copy(reduce.at[layer], w.at[base + 8 + at.z, half, :], sems[layer, 8]))
        return copies

    def up(self, item):
        ref = self.strip(item, self.at.s, self.at.z)
        return remote(ref, ref, self.zs.at[item, 0], self.pr.at[item, self.at.z, self.at.s], self.at.s, self.at.d + 2)

    def down(self, item):
        ref = self.strip(item, self.at.s, self.at.z)
        return remote(ref, ref, self.zs.at[item, 1], self.pr.at[item, self.at.z, self.at.s], self.at.s, self.at.d - 2)

    def onward(self, item, k):
        step = self.away if k != 1 else -self.away
        ref = self.strip(item, self.at.s, self.planes[k])
        return remote(ref, ref, self.zs.at[item, 2 + k], self.pr.at[item, self.planes[k], self.at.s], self.at.s, self.at.d + 2 * step)

    def to_x(self, item, k, line, j):
        ref = self.strip(item, line, self.planes[k])
        return remote(ref, ref, self.xs.at[item, k, j], self.pr.at[item, self.planes[k], line], self.at.xn, self.at.d)

    def to_y(self, item, k, line, j):
        ref = self.strip(item, line, self.planes[k])
        return remote(ref, ref, self.ys.at[item, k, j], self.pr.at[item, self.planes[k], line], self.at.yn, self.at.d)

    def arrival(self, item, k, line):
        ref = self.strip(item, line, self.planes[k])
        return remote(ref, ref, self.zs.at[item, 0], self.pr.at[item, self.planes[k], line], self.at.s, self.at.twin)

    def ends(self, item, act):
        @pl.when(self.at.z < 3)
        def _():
            act(self.up(item))

        @pl.when(self.at.z > 0)
        def _():
            act(self.down(item))

    def begin(self):
        at = self.at
        copies = [self.local(layer) for layer in range(2)]
        for layer in range(2):
            for copy in copies[layer]:
                copy.start()
        for copy in copies[0]:
            copy.wait()
        self.ends(0, lambda copy: copy.start())
        for part in range(3):
            self.quad(0, part, at.z, at.c, 3).start()
        for copy in copies[1]:
            copy.wait()
        for part in range(3):
            self.quad(1, part, at.z, at.c, 3).start()

    def stage_a(self, layer, part, k):
        item = 3 * layer + part
        self.arrival(item, k, self.at.s).wait_recv()

        @pl.when(self.inner)
        def _():
            self.onward(item, k).start()

        self.to_x(item, k, self.at.s, 0).start()
        self.to_y(item, k, self.at.s, 0).start()

    def stage_b(self, layer, part, k):
        item = 3 * layer + part
        self.arrival(item, k, self.at.xn).wait_recv()
        if (part + k + layer) % 2 == 0:
            self.to_y(item, k, self.at.xn, 1).start()
        self.arrival(item, k, self.at.yn).wait_recv()
        if (part + k + layer) % 2 == 1:
            self.to_x(item, k, self.at.yn, 1).start()

    def stage_c(self, layer, part, k):
        item = 3 * layer + part
        self.arrival(item, k, self.at.dn).wait_recv()
        self.quad(layer, part, self.planes[k], self.at.c, k).start()

    def step(self, g):
        n = len(self.groups)
        if g < n and g % 3 == 0 and g // 3 + 1 < 6:
            self.ends(g // 3 + 1, lambda copy: copy.start())
        if g < n:
            self.stage_a(*self.groups[g])
        if 0 <= g - 1 < n:
            self.stage_b(*self.groups[g - 1])
        if 0 <= g - 2 < n:
            self.stage_c(*self.groups[g - 2])

    def settle(self, layer, part):
        for k in range(3):
            self.quad(layer, part, self.planes[k], 1 - self.at.c, k).wait_recv()
        self.quad(layer, part, self.at.z, 1 - self.at.c, 3).wait_recv()

    def drain(self):
        at = self.at
        for layer in range(2):
            for part in range(3):
                item = 3 * layer + part
                self.ends(item, lambda copy: copy.wait_send())
                self.quad(layer, part, at.z, at.c, 3).wait_send()
                for k in range(3):
                    @pl.when(self.inner)
                    def _():
                        self.onward(item, k).wait_send()

                    self.to_x(item, k, at.s, 0).wait_send()
                    self.to_y(item, k, at.s, 0).wait_send()
                    if (part + k + layer) % 2 == 0:
                        self.to_y(item, k, at.xn, 1).wait_send()
                    else:
                        self.to_x(item, k, at.yn, 1).wait_send()
                    self.quad(layer, part, self.planes[k], at.c, k).wait_send()


def greet_all(at):
    bar = pltpu.get_barrier_semaphore()

    def greet(seg, dev):
        pl.semaphore_signal(bar, inc=1, device_id=(seg, dev), device_id_type=MESH)

    for seg in (at.xn, at.yn, at.dn):
        greet(seg, at.d)
        greet(seg, at.twin)
    greet(at.s, at.twin)
    for j in range(1, 4):
        greet(at.s, lax.rem(at.d + 2 * j, 8))
    pl.semaphore_wait(bar, 10)


def add_into(total, term):
    total[...] = (total[...].astype(F32) + term[...].astype(F32)).astype(BF16)


def sum_into(total, terms):
    result = total[...].astype(F32)
    for j in range(3):
        result = result + terms[j].astype(F32)
    total[...] = result.astype(BF16)


MIX_UNITS = [("mix", layer, j) for layer in (1, 0) for j in range(4)]
FEED_UNITS = [("exp", layer, j) for j in range(4) for layer in (1, 0)] + [("red", layer, j) for j in range(2) for layer in (1, 0)]


class Spread:
    def __init__(self, at, w, outs, fsend, frecv):
        self.at, self.w, self.outs, self.fsend, self.frecv = at, w, outs, fsend, frecv

    def unit(self, kind, layer, j):
        at, w = self.at, self.w
        fin, reduce = self.outs
        if kind == "mix":
            src = w.at[12 * layer + at.s, pl.ds(pl.multiple_of(2 * STRIP * at.z + STRIP * at.c, STRIP), STRIP), :]
            return 4 * layer + j, j, at.s == j, [fin.at[layer, j]], [(at.c, [src])]
        if kind == "exp":
            h, core = j // 2, j % 2
            block = w.at[12 * layer + 4 + 2 * core]
            rows = lambda p: pl.ds(pl.multiple_of(2 * STRIP * at.z + STRIP * p, STRIP), STRIP)
            src = [(p, [block.at[rows(p), :]]) for p in range(2)]
            targets = [fin.at[layer, 4 + j]]
            return 8 + 4 * layer + j, 2 * layer + h, (at.s == 2 * layer + h) & (at.c == core), targets, src
        h = lax.rem(at.s, 2)
        row = HALF * lax.rem(at.z, 2) + HALF // 2 * j
        src = w.at[12 * layer + 8 + 2 * (at.z // 2), pl.ds(pl.multiple_of(row, HALF // 2), HALF // 2), :]
        owns = (at.s // 2 == layer) & (at.c == at.z // 2)
        return 16 + 2 * layer + j, 2 * layer + at.c, owns, [reduce.at[layer, pl.ds(HALF // 2 * j, HALF // 2), :]], [(h, [src])]

    def copies(self, kind, layer, j):
        at = self.at
        index, _, owns, targets, sources = self.unit(kind, layer, j)
        sends = []
        for n, (p, refs) in enumerate(sources):
            dev = 2 * at.z + p
            for m, ref in enumerate(refs):
                target, land = targets[m], self.frecv.at[index, m]
                sem = lambda k: self.fsend.at[index, n, m, k]
                for k, seg in enumerate((at.xn, at.yn)):
                    sends.append((owns, remote(ref, target, sem(k), land, seg, dev), True))
                if kind == "mix":
                    sends.append((owns, pltpu.make_async_copy(ref, target, land), False))
                else:
                    sends.append((owns & (at.c == p), pltpu.make_async_copy(ref, target, land), False))
                    sends.append((owns & (at.c != p), remote(ref, target, sem(2), land, at.s, at.twin), True))
        return sends

    def relays(self, kind, layer, j):
        at = self.at
        index, owner, _, targets, _ = self.unit(kind, layer, j)
        first, then = (at.xn, at.yn) if index % 2 == 0 else (at.yn, at.xn)
        sends = [remote(ref, ref, self.fsend.at[index, 0, m, 3], self.frecv.at[index, m], then, at.d) for m, ref in enumerate(targets)]
        return owner == first, sends

    def start(self, unit):
        for cond, copy, _ in self.copies(*unit):
            @pl.when(cond)
            def _():
                copy.start()

    def relay(self, unit):
        passes, sends = self.relays(*unit)
        for copy in sends:
            copy.wait_recv()

            @pl.when(passes)
            def _():
                copy.start()

    def drain(self, unit):
        for cond, copy, crosses in self.copies(*unit):
            if crosses:
                @pl.when(cond)
                def _():
                    copy.wait_send()

        passes, sends = self.relays(*unit)
        for copy in sends:
            @pl.when(passes)
            def _():
                copy.wait_send()


def train_kernel(triple, output, expand, reduce, pack, choose, x, mask, gin, cot,
                 sec_out, grad_out, fin, red, sg_out, xin, gland, xtw, gtw, mrx, prx, land_m, land_e, land_r,
                 w, small, packs, pks, pkr, u_buf, g_buf, sg, sga, sgr, stage, stage_f, lsem, tsem, xsend, xrecv, gsend, grecv, tws, twr, osend, orecv, msend, mrecv, psend, precv,
                 zms, zmr, zes, zer, zrs, zrr, fsend, frecv, sgs, sgv, *scratch):
    at = Place()
    s, d, z, c = at.s, at.d, at.z, at.c
    lay = s // 2
    segs = (at.xn, at.yn, at.dn)
    gather = Gather(at, (triple, output, expand, reduce), w, scratch[:7])
    u = [x] + [u_buf.at[i] for i in range(4)]
    g = [g_buf.at[i] for i in range(4)] + [gin]

    def dw(layer, j, lhs, rhs):
        w[12 * layer + j] = mm_tn(lhs[...], rhs()).astype(BF16)

    chain = Chain(w, small, mask, u, g, sg, dw, scratch[7:])
    sg[...] = jnp.zeros_like(sg)

    def pack_line(j):
        return remote(pack, packs.at[c, z], pks.at[j], pkr.at[3 - j], s, lax.rem(d + 2 * j, 8))

    def pack_twin(core):
        return remote(packs.at[core], packs.at[core], pks.at[0], pkr.at[3], s, at.twin)

    def pack_begin():
        packs[c, z] = pack[...]
        for j in range(1, 4):
            pack_line(j).start()

    def pack_pass():
        for j in range(1, 4):
            pack_line(j).wait_recv()
        pack_twin(c).start()

    def pack_end():
        pack_twin(1 - c).wait_recv()
        held = packs[...].reshape(8 * 48, LANES)
        total = jnp.zeros((48, W), F32)
        for p in range(8):
            piece = jnp.concatenate([mm(choose[p], held), jnp.zeros((48, W - LANES), F32)], axis=1)
            total = total + (pltpu.roll(piece, STRIP * p, 1) if p else piece)
        small[...] = total.reshape(2, 24, W)
        pack_twin(c).wait_send()
        for j in range(1, 4):
            pack_line(j).wait_send()

    def x_send(i):
        return remote(u_buf.at[2 * (segs[i] // 2)], xin.at[s], xsend.at[i], xrecv.at[i], segs[i], d)

    def g_send(i):
        return remote(g_buf.at[2], gland.at[s], gsend.at[i], grecv.at[i], segs[i], d)

    def u_out(i):
        return remote(u_buf.at[segs[i]], sec_out.at[s], osend.at[0, i], orecv.at[0, i], segs[i], d)

    def g_out(i):
        return remote(g_buf.at[segs[i]], grad_out.at[s], osend.at[1, i], orecv.at[1, i], segs[i], d)

    keep_x = pltpu.make_async_copy(u_buf.at[2 * lay], xin.at[s], lsem.at[0])
    keep_u = pltpu.make_async_copy(u_buf.at[s], sec_out.at[s], lsem.at[1])
    keep_g = pltpu.make_async_copy(g_buf.at[s], grad_out.at[s], lsem.at[2])
    keep_gl = pltpu.make_async_copy(g_buf.at[2], gland.at[s], lsem.at[3])

    def to_where(cond, copy, i, wait=False):
        @pl.when(cond(segs[i]))
        def _():
            copy(i).wait_send() if wait else copy(i).start()

    def x_twin(t):
        return remote(xin.at[t], xtw.at[t], tws.at[0, t], twr.at[0, t], s, at.twin)

    def g_twin(t):
        return remote(gland.at[t], gtw.at[t], tws.at[1, t], twr.at[1, t], s, at.twin)

    def cot_twin(t):
        return remote(cot.at[t], gtw.at[t], tws.at[1, t], twr.at[1, t], s, at.twin)

    def strip(block, p, core):
        return w.at[block, pl.ds(pl.multiple_of(2 * STRIP * p + STRIP * core, STRIP), STRIP), :]

    def twin_mix(layer, p):
        rows = pl.ds(pl.multiple_of(2 * STRIP * p + STRIP * (1 - c), STRIP), STRIP)
        return remote(w.at[pl.ds(12 * layer, 4), rows, :], mrx.at[layer, p], msend.at[layer, p], mrecv.at[layer, p], s, at.twin)

    def plane_send(layer, i, p):
        return remote(strip(12 * layer + segs[i], p, c), prx.at[layer, i, p], psend.at[layer, i, p], precv.at[layer, i, p], segs[i], d)

    def to_stage(src, n):
        load = pltpu.make_async_copy(src, stage.at[n], tsem.at[n])
        load.start()
        return load

    def cores_sum(layer):
        loads = []
        for p in range(4):
            twin_mix(layer, p).wait_recv()
            if p >= 2:
                take(layer, p - 2, loads[p - 2])
            loads.append(to_stage(mrx.at[layer, p], p % 2))
        for p in (2, 3):
            take(layer, p, loads[p])

    def take(layer, p, load):
        load.wait()
        for b in range(4):
            add_into(strip(12 * layer + b, p, c), stage.at[p % 2, b])

    def plane_begin(layer):
        cores_sum(layer)
        for p in range(4):
            for i in range(3):
                plane_send(layer, i, p).start()

    def plane_sum(layer):
        for i in range(3):
            for p in range(4):
                plane_send(layer, i, p).wait_recv()
            to_stage(prx.at[layer, i], 0).wait()
            for p in range(4):
                add_into(strip(12 * layer + s, p, c), stage.at[0, p])

    def mix_line(layer, j):
        goal = lax.rem(z + j, 4)
        return remote(strip(12 * layer + s, goal, c), land_m.at[layer, 3 - j], zms.at[layer, j - 1], zmr.at[layer, 3 - j], s, lax.rem(d + 2 * j, 8))

    def exp_line(j):
        goal = lax.rem(z + j, 4)
        rows = pl.ds(pl.multiple_of(2 * STRIP * goal, 2 * STRIP), 2 * STRIP)
        return remote(w.at[eq, rows, :], land_e.at[3 - j], zes.at[j - 1], zer.at[3 - j], s, lax.rem(d + 2 * j, 8))

    def red_line(n):
        goal = 2 * c + n
        mine = lax.rem(z - goal + 7, 4)
        return remote(w.at[rq, pl.ds(4 * STRIP * n, 4 * STRIP), :], land_r.at[mine], zrs.at[n], zrr.at[mine], s, 2 * goal + c)

    def red_arrival(j):
        return remote(w.at[rq, pl.ds(0, 4 * STRIP), :], land_r.at[j], zrs.at[0], zrr.at[j], s, at.twin)

    def red_lines(act):
        for n in range(2):
            @pl.when(z != 2 * c + n)
            def _():
                act(red_line(n))

    def mix_line_sum(layer):
        for j in range(3):
            mix_line(layer, 3 - j).wait_recv()
        load = pltpu.make_async_copy(land_m.at[layer], stage.at[0, pl.ds(0, 3)], tsem.at[0])
        load.start()
        load.wait()
        sum_into(strip(12 * layer + s, z, c), stage.at[0])

    def feed_line_sum(landed, out):
        load = pltpu.make_async_copy(landed, stage_f, tsem.at[1])
        load.start()
        load.wait()
        sum_into(out, stage_f)

    def exp_line_sum():
        for j in range(3):
            exp_line(3 - j).wait_recv()
        feed_line_sum(land_e, w.at[eq, pl.ds(pl.multiple_of(2 * STRIP * z, 2 * STRIP), 2 * STRIP), :])

    def red_line_sum():
        @pl.when(z // 2 == c)
        def _():
            for j in range(3):
                red_arrival(j).wait_recv()
            for m in range(2):
                row = 4 * STRIP * lax.rem(z, 2) + 2 * STRIP * m
                feed_line_sum(land_r.at[:, pl.ds(2 * STRIP * m, 2 * STRIP), :], w.at[rq, pl.ds(pl.multiple_of(row, 2 * STRIP), 2 * STRIP), :])

    half = lax.rem(s, 2)
    own, other, far = 12 * lay, 12 * (1 - lay), 2 * (1 - c)
    eq, rq = own + 4 + 2 * c, own + 8 + 2 * c
    half_at = pl.ds(pl.multiple_of(4 * STRIP * half, LANES), 4 * STRIP)

    def block_x(k):
        return other + 4 + k

    def block_g(k):
        return other + 7 + k

    def block_a(k):
        return (1 - k // 2) * (other + 10 + k) + (k // 2) * (own + 4 + far)

    def block_h(k):
        later = (k + 1) // 2
        return (1 - later) * (own + 5 + far) + later * (own + 7 + far + k)

    def rows_of(i):
        return pl.ds(pl.multiple_of(ROWS * lax.rem(i, 3), ROWS), ROWS)

    def token_loads():
        loads = []
        for t in range(4):
            for n, (xs, gs) in enumerate(((xin, gland), (xtw, gtw))):
                i = 2 * t + n
                loads.append(pltpu.make_async_copy(xs.at[t], w.at[block_x(i // 3), rows_of(i), :], lsem.at[4 + i]))
                dst = w.at[block_g(i // 3), rows_of(i), :]
                load = pltpu.make_async_copy(gs.at[t], dst, lsem.at[12 + i])
                seed = pltpu.make_async_copy((cot if n == 0 else gs).at[t], dst, lsem.at[12 + i])
                loads.append((load, seed))
        return loads

    def feed_rows(i):
        k, rows = i // 3, rows_of(i)
        xh, _ = norm_parts(w[block_x(k), rows, :].astype(F32))
        n = (xh * small[lay, 16:17, :] + small[lay, 17:18, :]).astype(BF16)
        w[block_x(k), rows, :] = n
        for m in range(2):
            cols = slice(4 * STRIP * m, 4 * STRIP * (m + 1))
            h = mm(n, w[eq + m, :, half_at]) + small[lay, pl.ds(18 + 2 * c + m, 1), half_at]
            cdf = 0.5 + 0.5 * lax.erf(h * ROOT_HALF)
            w[block_a(k), rows, cols] = (h * cdf).astype(BF16)
            slope = cdf + h * (ROOT_TWO_PI * jnp.exp(-0.5 * h * h))
            w[block_h(k), rows, cols] = (mm_nt(w[block_g(k), rows, :], w[rq + m, half_at, :]) * slope).astype(BF16)

    def product(out, left, right):
        @pl.loop(0, 3)
        def _(i):
            cols = pl.ds(pl.multiple_of(256 * i, 256), 256)
            total = jnp.zeros((256, W), F32)
            for k, rows in enumerate((3 * ROWS, 3 * ROWS, 2 * ROWS)):
                total = total + mm_tn(w[left(k), :rows, cols], w[right(k), :rows, :])
            w[out, cols, :] = total.astype(BF16)

    partners = [(s, at.twin), (at.xn, d), (at.yn, d), (s, d + 2 * (1 - 2 * lax.rem(z, 2))), (s, lax.rem(d + 4, 8))]

    def sg_round(r):
        return remote(sga.at[r], sgr.at[r], sgs.at[r], sgv.at[r], *partners[r])

    def sg_next(r):
        sg_round(r).wait_recv()
        sga[r + 1] = sga[r] + sgr[r]
        if r < 4:
            sg_round(r + 1).start()

    spread = Spread(at, w, (fin, red), fsend, frecv)
    low, high = (lambda t: t < 2), (lambda t: t >= 2)
    odd = lambda t: lax.rem(t, 2) == 1

    greet_all(at)
    pack_begin()

    @pl.when(s >= 2)
    def _():
        for t in range(4):
            cot_twin(t).start()

    gather.begin()
    for step in range(20):
        gather.step(step)
        if step == 1:
            pack_pass()
        if step == 3:
            pack_end()
        if step == 5:
            gather.settle(0, 0)
            chain.front(0)
        if step == 6:
            chain.rest(0)
        if step == 11:
            gather.settle(0, 1)
            gather.settle(0, 2)
            chain.front(1)
        if step == 14:
            gather.settle(1, 0)
            chain.front(2)
        if step == 15:
            chain.rest(2)
    for i in range(3):
        x_send(i).start()
    keep_x.start()
    for i in range(3):
        to_where(lambda t: t == 1, u_out, i)
    gather.settle(1, 1)
    gather.settle(1, 2)
    chain.front(3)
    for i in range(3):
        to_where(lambda t: t == 3, u_out, i)
    keep_u.start()
    gather.drain()
    chain.backward(3)
    for i in range(3):
        to_where(lambda t: t == 3, g_out, i)
    chain.backward(2)
    for i in range(3):
        to_where(low, g_send, i)
    keep_gl.start()
    for i in range(3):
        to_where(lambda t: t == 2, g_out, i)
    for p in range(4):
        twin_mix(1, p).start()
    keep_x.wait()
    x_twin(s).start()
    for i in range(3):
        x_send(i).wait_recv()
        x_twin(segs[i]).start()
    chain.backward(1)
    for i in range(3):
        to_where(lambda t: t == 1, g_out, i)
    plane_begin(1)
    keep_gl.wait()

    @pl.when(s < 2)
    def _():
        g_twin(s).start()
        for i in range(3):
            g_send(i).wait_recv()
            g_twin(segs[i]).start()

    loads = token_loads()
    for t in range(4):
        x_twin(t).wait_recv()
        cot_twin(t).wait_recv()
    for load in loads:
        if isinstance(load, tuple):
            @pl.when(s < 2)
            def _():
                load[0].start()

            @pl.when(s >= 2)
            def _():
                load[1].start()
        else:
            load.start()
    for load in loads:
        (load[0] if isinstance(load, tuple) else load).wait()
    pl.loop(0, 8)(feed_rows)
    product(eq, block_x, block_h)
    for j in (2, 1, 3):
        exp_line(j).start()
    product(rq, block_a, block_g)
    red_lines(lambda copy: copy.start())
    chain.backward(0)
    for p in range(4):
        twin_mix(0, p).start()
    for i in range(3):
        to_where(lambda t: t == 0, g_out, i)
    keep_g.start()
    sga[0] = sg[...]
    sg_round(0).start()
    plane_begin(0)
    sg_next(0)
    plane_sum(1)
    for j in (2, 1, 3):
        mix_line(1, j).start()
    sg_next(1)
    exp_line_sum()
    for unit in FEED_UNITS:
        if unit[0] == "exp":
            spread.start(unit)
    sg_next(2)
    red_line_sum()
    for unit in FEED_UNITS:
        if unit[0] == "red":
            spread.start(unit)
    sg_next(3)
    mix_line_sum(1)
    for unit in MIX_UNITS[:4]:
        spread.start(unit)
    sg_next(4)
    plane_sum(0)
    for j in (2, 1, 3):
        mix_line(0, j).start()
    for unit in FEED_UNITS:
        spread.relay(unit)
    mix_line_sum(0)
    for unit in MIX_UNITS[4:]:
        spread.start(unit)
    for unit in MIX_UNITS:
        spread.relay(unit)

    for r in range(5):
        sg_round(r).wait_send()
    for layer in range(2):
        sg_out[layer] = pltpu.roll(sga[5, layer], lax.rem(W - STRIP * d, W), 1)[:, :LANES]
        for first, count in ((12, 3), (18, 4)):
            for j in range(count):
                index = count * d + j
                sga[0, layer] = pltpu.roll(sga[5, layer], lax.rem(W - STRIP * lax.rem(index, 8), W), 1)
                sg_out[layer, first + j:first + j + 1, :] = sga[0, layer, pl.ds(first + index // 8, 1), :][:, :LANES]
    for unit in FEED_UNITS + MIX_UNITS:
        spread.drain(unit)
    for i in range(3):
        x_send(i).wait_send()
        to_where(low, g_send, i, wait=True)
        to_where(odd, u_out, i, wait=True)
        g_out(i).wait()
        for layer in range(2):
            for p in range(4):
                plane_send(layer, i, p).wait_send()

    @pl.when(lax.rem(s, 2) == 1)
    def _():
        for i in range(3):
            u_out(i).wait_recv()

    for t in range(4):
        x_twin(t).wait_send()
        cot_twin(t).wait_send()
    keep_u.wait()
    keep_g.wait()
    for p in range(4):
        for layer in range(2):
            twin_mix(layer, p).wait_send()
    for j in range(1, 4):
        for layer in range(2):
            mix_line(layer, j).wait_send()
        exp_line(j).wait_send()
    red_lines(lambda copy: copy.wait_send())


def train_call(triple, output, expand, reduce, pack, choose, x, mask, gin, cot):
    V = pltpu.VMEM
    D = pltpu.SemaphoreType.DMA
    S = jax.ShapeDtypeStruct
    anywhere = pl.BlockSpec(memory_space=pl.ANY)
    vmem = pl.BlockSpec(memory_space=V)
    tokens = S((4, ROWS, W), BF16)
    out = pl.pallas_call(
        train_kernel,
        out_shape=(
            tokens, tokens, S((2, 8, STRIP, W), BF16), S((2, HALF, W), BF16), S((2, 24, LANES), F32), tokens, tokens, tokens, tokens,
            S((2, 4, 4, STRIP, W), BF16), S((2, 3, 4, STRIP, W), BF16), S((2, 3, STRIP, W), BF16), S((3, 2 * STRIP, W), BF16), S((3, 4 * STRIP, W), BF16),
        ),
        in_specs=[anywhere] * 4 + [vmem] * 5 + [anywhere],
        out_specs=[anywhere] * 4 + [vmem] + [anywhere] * 9,
        scratch_shapes=[
            V((24, W, W), BF16), V((2, 24, W), F32), V((2, 4, 48, LANES), BF16), D((4,)), D((4,)), V((4, ROWS, W), BF16), V((4, ROWS, W), BF16), V((2, 24, W), F32), V((6, 2, 24, W), F32), V((5, 2, 24, W), F32),
            V((2, 4, STRIP, W), BF16), V((3, 2 * STRIP, W), BF16),
            D((20,)), D((2,)), D((3,)), D((3,)), D((3,)), D((3,)), D((2, 4)), D((2, 4)), D((2, 3)), D((2, 3)), D((2, 4)), D((2, 4)), D((2, 3, 4)), D((2, 3, 4)),
            D((2, 3)), D((2, 3)), D((3,)), D((3,)), D((2,)), D((3,)), D((20, 2, 2, 4)), D((20, 2)), D((5,)), D((5,)),
        ] + gather_scratch() + chain_scratch(),
        compiler_params=pltpu.CompilerParams(collective_id=1, has_side_effects=True, vmem_limit_bytes=VMEM_LIMIT),
        name="train_sections",
    )(triple, output, expand, reduce, pack, choose, x, mask, gin, cot)
    return out[:6]


def pack_small(conv_weight, conv_bias, mixer_gain, mixer_shift, triple_bias, output_bias, feed_gain, feed_shift, expand_bias, reduce_bias):
    part = conv_bias.shape[1]
    rows = [conv_weight] + [
        v.reshape(2, -1, part)
        for v in (conv_bias, mixer_gain, mixer_shift, triple_bias, output_bias, feed_gain, feed_shift, expand_bias, reduce_bias)
    ]
    return jnp.concatenate(rows, axis=1)


def piece_choice():
    choice = np.zeros((8, 2, 24, 2, 4, 2, 24), np.float32)
    for place in range(8):
        for row in range(23):
            first, count = (12, 3) if 12 <= row < 15 else (18, 4) if 18 <= row < 22 else (row, 1)
            index = 8 * (row - first) + place
            shard, source = index // count, first + index % count
            for layer in range(2):
                choice[place, layer, row, shard % 2, shard // 2, layer, source] = 1.0
    return jnp.asarray(choice.reshape(8, 48, 384), BF16)


def pad_images(rows):
    return jnp.pad(rows.reshape(-1, LIVE, rows.shape[1]), ((0, 0), (0, IMG - LIVE), (0, 0))).reshape(-1, rows.shape[1])


def unpad_images(rows):
    lead = rows.shape[:-2]
    return rows.reshape(lead + (-1, IMG, W))[..., :LIVE, :].reshape(lead + (-1, W))


def spread_body(
    patches, region_mask, conv_weight, conv_bias, mixer_gain, mixer_shift, triple_weight, triple_bias, output_weight,
    output_bias, feed_gain, feed_shift, expand_weight, expand_bias, reduce_weight, reduce_bias, cotangent,
):
    s = lax.axis_index("segment")
    d = lax.axis_index("dp")
    packed = pack_small(conv_weight, conv_bias, mixer_gain, mixer_shift, triple_bias, output_bias, feed_gain, feed_shift, expand_bias, reduce_bias)
    pack = jnp.pad(packed, ((0, 0), (0, 1), (0, LANES - packed.shape[2]))).reshape(48, LANES)
    own = patches.shape[0] // lax.axis_size("segment")
    mine = lambda v: lax.dynamic_slice_in_dim(v, s * own, own, 0)
    x = pad_images(mine(patches))
    cot = pad_images(cotangent).reshape(4, ROWS, W)
    gin = lax.dynamic_index_in_dim(cot, s, 0, keepdims=False)
    mask = pad_images(mine(region_mask).astype(BF16)[:, None])
    sec_out, grad_out, fin, red, sg, xin = train_call(
        triple_weight, output_weight, expand_weight, reduce_weight, pack, piece_choice(), x, mask, gin, cot
    )
    sec_out = jnp.where(lax.rem(s, 2) == 0, xin, sec_out)
    place = lambda v: unpad_images(v.reshape(1, 4 * ROWS, W))
    part = W // lax.axis_size("dp")
    rows = lambda lo, hi: sg[:, lo:hi, :part].reshape(2, -1)
    triple = jnp.concatenate([fin[:, j] for j in range(3)], axis=2)
    expand = fin[:, 4:].reshape(2, 2, 2, part, 2, W // 2).transpose(0, 3, 2, 4, 1, 5).reshape(2, part, 4 * W)
    wide = lambda v: v.astype(F32)
    return (
        place(sec_out), place(grad_out), sg[:, :9, :part], rows(9, 10), rows(10, 11), rows(11, 12), wide(triple), rows(12, 15), wide(fin[:, 3]),
        rows(15, 16), rows(16, 17), rows(17, 18), wide(expand), rows(18, 22), wide(red), rows(22, 23),
    )


def solution(mesh):
    in_specs = (
        P("dp", None),
        P("dp"),
        P(None, None, "dp"),
        P(None, "dp"),
        P(None, "dp"),
        P(None, "dp"),
        P(None, "dp", None),
        P(None, "dp"),
        P(None, "dp", None),
        P(None, "dp"),
        P(None, "dp"),
        P(None, "dp"),
        P(None, "dp", None),
        P(None, "dp"),
        P(None, "dp", None),
        P(None, "dp"),
        P("dp", None),
    )
    out_specs = (
        P("segment", "dp", None),
        P("segment", "dp", None),
        P(None, None, "dp"),
        P(None, "dp"),
        P(None, "dp"),
        P(None, "dp"),
        P(None, "dp", None),
        P(None, "dp"),
        P(None, "dp", None),
        P(None, "dp"),
        P(None, "dp"),
        P(None, "dp"),
        P(None, "dp", None),
        P(None, "dp"),
        P(None, "dp", None),
        P(None, "dp"),
    )
    chosen = spread_body if mesh.shape["dp"] == 8 and mesh.shape["segment"] == 4 else body
    return jax.shard_map(chosen, mesh=mesh, in_specs=in_specs, out_specs=out_specs, check_vma=False)
```

```python
from functools import partial

import jax
import jax.numpy as jnp
import numpy as np
from jax import lax
from jax.experimental import pallas as pl
from jax.experimental.pallas import tpu as pltpu
from jax.sharding import PartitionSpec as P

HD = 32
SIDE = 7
MICRO = 4
IMG_MB = 4


EPSILON = 1e-05


def as_sent(x):

    def short(part):
        return part.astype(jnp.bfloat16) if part.dtype == jnp.float32 else part

    return jax.tree.map(short, x)


def shifted_2(x, axis, by):
    count = lax.axis_size(axis)
    pairs = [(i, i + by) for i in range(count) if 0 <= i + by < count]
    return lax.ppermute(x, axis, pairs)


def dot_last(first_operand, second_operand):
    return lax.dot_general(
        first_operand, second_operand, (((1,), (1,)), ((), ())), preferred_element_type=jnp.float32
    )


def dot_first(first_operand, second_operand):
    return lax.dot_general(
        first_operand, second_operand, (((0,), (0,)), ((), ())), preferred_element_type=jnp.float32
    )


def layer_norm(values, norm_gain, norm_shift):
    center = values - jnp.mean(values, axis=-1, keepdims=True)
    spread = jnp.mean(center * center, axis=-1, keepdims=True)
    return center * lax.rsqrt(spread + EPSILON) * norm_gain + norm_shift


def position_conv(stream, conv_weight, conv_bias):
    features = stream.shape[-1]
    planes = stream.reshape(-1, SIDE, SIDE, features)
    padded = jnp.pad(planes, ((0, 0), (1, 1), (1, 1), (0, 0)))
    summed = jnp.zeros_like(planes) + conv_bias
    for tap_row in range(3):
        for tap_col in range(3):
            summed = (
                summed
                + padded[:, tap_row : tap_row + SIDE, tap_col : tap_col + SIDE, :]
                * conv_weight[tap_row * 3 + tap_col]
            )
    return stream + summed.reshape(stream.shape)


def front_part(stream, conv_weight, conv_bias, norm_gain, norm_shift):
    shifted = position_conv(stream, conv_weight, conv_bias)
    return (shifted, layer_norm(shifted, norm_gain, norm_shift))


def gelu_exact(values):
    return jax.nn.gelu(values, approximate=False)


def softmax_rows(scores):
    row_max = jnp.max(scores, axis=-1, keepdims=True)
    lifted = jnp.exp(scores - row_max)
    return lifted / jnp.sum(lifted, axis=-1, keepdims=True)


def window_forward(triple):
    tokens = triple.shape[0]
    features = triple.shape[1] // 3
    pieces = triple.reshape(tokens // (SIDE * SIDE), SIDE * SIDE, 3, features // HD, HD)
    queries = pieces[:, :, 0]
    key_parts = pieces[:, :, 1]
    value_parts = pieces[:, :, 2]
    scores = jnp.einsum(
        "iqhd,ikhd->ihqk", queries, key_parts, preferred_element_type=jnp.float32
    ) * HD ** (-0.5)
    softmaxed = softmax_rows(scores)
    softmaxed_low = softmaxed.astype(jnp.bfloat16)
    mixture = jnp.einsum(
        "ihqk,ikhd->iqhd", softmaxed_low, value_parts, preferred_element_type=jnp.float32
    )
    return (
        mixture.reshape(tokens, features),
        (queries, key_parts, value_parts, softmaxed, softmaxed_low),
    )


def window_backward(stored, grad_mixture):
    queries, key_parts, value_parts, softmaxed, softmaxed_low = stored
    grad_pieces = grad_mixture.reshape(queries.shape)
    grad_values = jnp.einsum(
        "ihqk,iqhd->ikhd", softmaxed_low, grad_pieces, preferred_element_type=jnp.float32
    )
    grad_soft = jnp.einsum(
        "iqhd,ikhd->ihqk", grad_pieces, value_parts, preferred_element_type=jnp.float32
    )
    grad_scores = (
        softmaxed * (grad_soft - jnp.sum(grad_soft * softmaxed, axis=-1, keepdims=True))
    ).astype(jnp.bfloat16)
    grad_queries = jnp.einsum(
        "ihqk,ikhd->iqhd", grad_scores, key_parts, preferred_element_type=jnp.float32
    ) * HD ** (-0.5)
    grad_keys = jnp.einsum(
        "ihqk,iqhd->ikhd", grad_scores, queries, preferred_element_type=jnp.float32
    ) * HD ** (-0.5)
    joined = jnp.stack([grad_queries, grad_keys, grad_values], axis=2)
    return joined.reshape(grad_mixture.shape[0], 3 * grad_mixture.shape[1])


def channel_forward(triple, mask_rows):
    tokens = triple.shape[0]
    features = triple.shape[1] // 3
    images = tokens // (SIDE * SIDE)
    pieces = triple.reshape(images, SIDE * SIDE, 3, features // HD, HD)
    queries = pieces[:, :, 0]
    keep_mask = mask_rows.reshape(images, SIDE * SIDE, 1, 1).astype(jnp.bfloat16)
    masked = pieces[:, :, 1] * keep_mask
    value_parts = pieces[:, :, 2]
    scores = jnp.einsum(
        "itgc,itge->igce", queries, masked, preferred_element_type=jnp.float32
    ) * HD ** (-0.5)
    softmaxed = softmax_rows(scores)
    softmaxed_low = softmaxed.astype(jnp.bfloat16)
    mixture = jnp.einsum(
        "igce,itge->itgc", softmaxed_low, value_parts, preferred_element_type=jnp.float32
    )
    return (
        mixture.reshape(tokens, features),
        (queries, masked, value_parts, keep_mask, softmaxed, softmaxed_low),
    )


def channel_backward(stored, grad_mixture):
    queries, masked, value_parts, keep_mask, softmaxed, softmaxed_low = stored
    grad_pieces = grad_mixture.reshape(queries.shape)
    grad_soft = jnp.einsum(
        "itgc,itge->igce", grad_pieces, value_parts, preferred_element_type=jnp.float32
    )
    grad_values = jnp.einsum(
        "igce,itgc->itge", softmaxed_low, grad_pieces, preferred_element_type=jnp.float32
    )
    grad_scores = (
        softmaxed * (grad_soft - jnp.sum(grad_soft * softmaxed, axis=-1, keepdims=True))
    ).astype(jnp.bfloat16)
    grad_queries = jnp.einsum(
        "igce,itge->itgc", grad_scores, masked, preferred_element_type=jnp.float32
    ) * HD ** (-0.5)
    grad_masked = jnp.einsum(
        "igce,itgc->itge", grad_scores, queries, preferred_element_type=jnp.float32
    ) * HD ** (-0.5)
    grad_keys = grad_masked * keep_mask.astype(jnp.float32)
    joined = jnp.stack([grad_queries, grad_keys, grad_values], axis=2)
    return joined.reshape(grad_mixture.shape[0], 3 * grad_mixture.shape[1])


def mixer_inner(stream, weights, mask_rows, channel):
    (
        conv_weight,
        conv_bias,
        norm_gain,
        norm_shift,
        triple_weight,
        triple_bias,
        output_weight,
        output_bias,
    ) = weights[:8]
    widened = stream.astype(jnp.float32)
    (shifted, normed), front_pull = jax.vjp(
        front_part,
        widened,
        conv_weight.astype(jnp.float32),
        conv_bias.astype(jnp.float32),
        norm_gain.astype(jnp.float32),
        norm_shift.astype(jnp.float32),
    )
    normed_low = normed.astype(jnp.bfloat16)
    triple = (
        jnp.dot(normed_low, triple_weight, preferred_element_type=jnp.float32)
        + triple_bias.astype(jnp.float32)
    ).astype(jnp.bfloat16)
    if channel:
        mixture, stored = channel_forward(triple, mask_rows)
    else:
        mixture, stored = window_forward(triple)
    mixture_low = mixture.astype(jnp.bfloat16)
    return (shifted, front_pull, normed_low, stored, mixture_low)


def mixer_forward(stream, weights, mask_rows, channel):
    shifted, front_pull, normed_low, stored, mixture_low = mixer_inner(
        stream, weights, mask_rows, channel
    )
    result = (
        shifted
        + jnp.dot(mixture_low, weights[6], preferred_element_type=jnp.float32)
        + weights[7].astype(jnp.float32)
    )
    return result.astype(jnp.bfloat16)


def mixer_backward(stream, grad_out, weights, mask_rows, channel):
    shifted, front_pull, normed_low, stored, mixture_low = mixer_inner(
        stream, weights, mask_rows, channel
    )
    grad_wide = grad_out.astype(jnp.float32)
    grad_out_bias = jnp.sum(grad_wide, axis=0)
    grad_out_weight = dot_first(mixture_low, grad_out)
    grad_mixture = dot_last(grad_out, weights[6]).astype(jnp.bfloat16)
    if channel:
        grad_triple = channel_backward(stored, grad_mixture).astype(jnp.bfloat16)
    else:
        grad_triple = window_backward(stored, grad_mixture).astype(jnp.bfloat16)
    grad_tri_weight = dot_first(normed_low, grad_triple)
    grad_tri_bias = jnp.sum(grad_triple.astype(jnp.float32), axis=0)
    grad_normed = dot_last(grad_triple, weights[4])
    grad_stream, grad_taps, grad_tap_bias, grad_gain, grad_shift = front_pull(
        (grad_wide, grad_normed)
    )
    zero_tail = tuple((jnp.zeros(member.shape, jnp.float32) for member in weights[8:]))
    return (
        grad_stream.astype(jnp.bfloat16),
        (
            grad_taps,
            grad_tap_bias,
            grad_gain,
            grad_shift,
            grad_tri_weight,
            grad_tri_bias,
            grad_out_weight,
            grad_out_bias,
        )
        + zero_tail,
    )


def feed_inner(stream, weights):
    norm_gain, norm_shift, expand_weight, expand_bias, reduce_weight, reduce_bias = weights[8:]
    widened = stream.astype(jnp.float32)
    normed, norm_pull = jax.vjp(
        layer_norm, widened, norm_gain.astype(jnp.float32), norm_shift.astype(jnp.float32)
    )
    normed_low = normed.astype(jnp.bfloat16)
    hidden = jnp.dot(
        normed_low, expand_weight, preferred_element_type=jnp.float32
    ) + expand_bias.astype(jnp.float32)
    active, gelu_pull = jax.vjp(gelu_exact, hidden)
    return (widened, norm_pull, normed_low, gelu_pull, active.astype(jnp.bfloat16))


def feed_forward(stream, weights):
    widened, norm_pull, normed_low, gelu_pull, active_low = feed_inner(stream, weights)
    result = (
        widened
        + jnp.dot(active_low, weights[12], preferred_element_type=jnp.float32)
        + weights[13].astype(jnp.float32)
    )
    return result.astype(jnp.bfloat16)


def feed_backward(stream, grad_out, weights):
    widened, norm_pull, normed_low, gelu_pull, active_low = feed_inner(stream, weights)
    grad_wide = grad_out.astype(jnp.float32)
    grad_red_bias = jnp.sum(grad_wide, axis=0)
    grad_red_weight = dot_first(active_low, grad_out)
    grad_active = dot_last(grad_out, weights[12])
    grad_hidden = gelu_pull(grad_active)[0].astype(jnp.bfloat16)
    grad_exp_weight = dot_first(normed_low, grad_hidden)
    grad_exp_bias = jnp.sum(grad_hidden.astype(jnp.float32), axis=0)
    grad_normed = dot_last(grad_hidden, weights[10])
    grad_inner, grad_gain, grad_shift = norm_pull(grad_normed)
    zero_head = tuple((jnp.zeros(member.shape, jnp.float32) for member in weights[:8]))
    grad_stream = grad_wide + grad_inner
    return (
        grad_stream.astype(jnp.bfloat16),
        zero_head
        + (grad_gain, grad_shift, grad_exp_weight, grad_exp_bias, grad_red_weight, grad_red_bias),
    )


def section_forward(section, stream, weights, mask_rows):
    if section % 2 == 1:
        return feed_forward(stream, weights)
    return mixer_forward(stream, weights, mask_rows, section == 2)


def section_backward(section, stream, grad_out, weights, mask_rows):
    if section % 2 == 1:
        return feed_backward(stream, grad_out, weights)
    return mixer_backward(stream, grad_out, weights, mask_rows, section == 2)


def spare_forward(stream, weights, mask_rows):
    return jnp.zeros_like(stream)


def spare_backward(stream, grad_out, weights, mask_rows):
    return (
        jnp.zeros_like(stream),
        tuple((jnp.zeros(member.shape, jnp.float32) for member in weights)),
    )


def put_rows(buffer, rows, row_start, is_live):
    former = lax.dynamic_slice_in_dim(buffer, row_start, rows.shape[0], 0)
    return lax.dynamic_update_slice_in_dim(buffer, jnp.where(is_live, rows, former), row_start, 0)


def run_segments(layer_set, patches, region_mask, cotangent, segment_index, segments):
    features = patches.shape[1]
    micro_count = MICRO
    micro_rows = IMG_MB * SIDE * SIDE
    tick_count = micro_count + segments - 1
    forward_branches = [
        partial(section_forward, 0),
        partial(section_forward, 1),
        partial(section_forward, 2),
        partial(section_forward, 3),
        spare_forward,
    ]
    backward_branches = [
        partial(section_backward, 0),
        partial(section_backward, 1),
        partial(section_backward, 2),
        partial(section_backward, 3),
        spare_backward,
    ]
    received = jnp.zeros((micro_rows, features), jnp.bfloat16)
    kept_inputs = jnp.zeros((micro_count * micro_rows, features), jnp.bfloat16)
    outputs_here = jnp.zeros((micro_count * micro_rows, features), jnp.bfloat16)
    for tick_index in range(tick_count):
        micro_index = tick_index - segment_index
        is_live = (micro_index >= 0) & (micro_index < micro_count)
        row_start = jnp.clip(micro_index, 0, micro_count - 1) * micro_rows
        fresh_rows = lax.dynamic_slice_in_dim(patches, row_start, micro_rows, 0)
        mask_rows = lax.dynamic_slice_in_dim(region_mask, row_start, micro_rows, 0)
        entering = jnp.where(segment_index == 0, fresh_rows, received)
        leaving = lax.switch(
            jnp.where(is_live, segment_index, segments),
            forward_branches,
            entering,
            layer_set,
            mask_rows,
        )
        kept_inputs = put_rows(kept_inputs, entering, row_start, is_live)
        outputs_here = put_rows(outputs_here, leaving, row_start, is_live)
        if tick_index + 1 < tick_count:
            received = jax.tree.map(
                lambda part, own: part.astype(own.dtype),
                shifted_2(as_sent(leaving), "segment", 1),
                leaving,
            )
    grad_received = jnp.zeros((micro_rows, features), jnp.bfloat16)
    grads_here = jnp.zeros((micro_count * micro_rows, features), jnp.bfloat16)
    totals = tuple((jnp.zeros(member.shape, jnp.float32) for member in layer_set))
    for tick_index in range(tick_count):
        micro_index = tick_index - (segments - 1 - segment_index)
        is_live = (micro_index >= 0) & (micro_index < micro_count)
        row_start = jnp.clip(micro_index, 0, micro_count - 1) * micro_rows
        seed_rows = lax.dynamic_slice_in_dim(cotangent, row_start, micro_rows, 0)
        mask_rows = lax.dynamic_slice_in_dim(region_mask, row_start, micro_rows, 0)
        arriving = jnp.where(segment_index == segments - 1, seed_rows, grad_received)
        stream = lax.dynamic_slice_in_dim(kept_inputs, row_start, micro_rows, 0)
        grad_stream, grad_terms = lax.switch(
            jnp.where(is_live, segment_index, segments),
            backward_branches,
            stream,
            arriving,
            layer_set,
            mask_rows,
        )
        totals = tuple(
            (first_term + second_term for first_term, second_term in zip(totals, grad_terms))
        )
        grads_here = put_rows(grads_here, grad_stream, row_start, is_live)
        if tick_index + 1 < tick_count:
            grad_received = jax.tree.map(
                lambda part, own: part.astype(own.dtype),
                shifted_2(as_sent(grad_stream), "segment", -1),
                grad_stream,
            )
    return (outputs_here, grads_here, totals)


def body(
    patches,
    region_mask,
    conv_weight,
    conv_bias,
    mixer_gain,
    mixer_shift,
    triple_weight,
    triple_bias,
    output_weight,
    output_bias,
    feed_gain,
    feed_shift,
    expand_weight,
    expand_bias,
    reduce_weight,
    reduce_bias,
    cotangent,
):
    params = (
        conv_weight,
        conv_bias,
        mixer_gain,
        mixer_shift,
        triple_weight,
        triple_bias,
        output_weight,
        output_bias,
        feed_gain,
        feed_shift,
        expand_weight,
        expand_bias,
        reduce_weight,
        reduce_bias,
    )
    segments = lax.axis_size("segment")
    segment_index = lax.axis_index("segment")
    layer_index = segment_index // 2
    slices = tuple(
        (lax.dynamic_index_in_dim(member, layer_index, 0, keepdims=False) for member in params)
    )
    layer_set = (
        lax.all_gather(slices[0], "dp", axis=1, tiled=True),
        lax.all_gather(slices[1], "dp", axis=0, tiled=True),
        lax.all_gather(slices[2], "dp", axis=0, tiled=True),
        lax.all_gather(slices[3], "dp", axis=0, tiled=True),
        lax.all_gather(slices[4], "dp", axis=0, tiled=True),
        lax.all_gather(slices[5], "dp", axis=0, tiled=True),
        lax.all_gather(slices[6], "dp", axis=0, tiled=True),
        lax.all_gather(slices[7], "dp", axis=0, tiled=True),
        lax.all_gather(slices[8], "dp", axis=0, tiled=True),
        lax.all_gather(slices[9], "dp", axis=0, tiled=True),
        lax.all_gather(slices[10], "dp", axis=0, tiled=True),
        lax.all_gather(slices[11], "dp", axis=0, tiled=True),
        lax.all_gather(slices[12], "dp", axis=0, tiled=True),
        lax.all_gather(slices[13], "dp", axis=0, tiled=True),
    )
    outputs_here, grads_here, totals = run_segments(
        layer_set, patches, region_mask, cotangent, segment_index, segments
    )
    reduced = (
        lax.psum_scatter(totals[0], "dp", scatter_dimension=1, tiled=True),
        lax.psum_scatter(totals[1], "dp", scatter_dimension=0, tiled=True),
        lax.psum_scatter(totals[2], "dp", scatter_dimension=0, tiled=True),
        lax.psum_scatter(totals[3], "dp", scatter_dimension=0, tiled=True),
        lax.psum_scatter(totals[4], "dp", scatter_dimension=0, tiled=True),
        lax.psum_scatter(totals[5], "dp", scatter_dimension=0, tiled=True),
        lax.psum_scatter(totals[6], "dp", scatter_dimension=0, tiled=True),
        lax.psum_scatter(totals[7], "dp", scatter_dimension=0, tiled=True),
        lax.psum_scatter(totals[8], "dp", scatter_dimension=0, tiled=True),
        lax.psum_scatter(totals[9], "dp", scatter_dimension=0, tiled=True),
        lax.psum_scatter(totals[10], "dp", scatter_dimension=0, tiled=True),
        lax.psum_scatter(totals[11], "dp", scatter_dimension=0, tiled=True),
        lax.psum_scatter(totals[12], "dp", scatter_dimension=0, tiled=True),
        lax.psum_scatter(totals[13], "dp", scatter_dimension=0, tiled=True),
    )
    placed = tuple(
        (
            jnp.stack(
                [jnp.where(layer_index == 0, member, 0.0), jnp.where(layer_index == 1, member, 0.0)]
            )
            for member in reduced
        )
    )
    section_outputs = outputs_here[None]
    section_grads = grads_here[None]
    summed = (
        lax.psum(placed[0].astype(jnp.bfloat16), "segment").astype(jnp.float32),
        lax.psum(placed[1].astype(jnp.bfloat16), "segment").astype(jnp.float32),
        lax.psum(placed[2].astype(jnp.bfloat16), "segment").astype(jnp.float32),
        lax.psum(placed[3].astype(jnp.bfloat16), "segment").astype(jnp.float32),
        lax.psum(placed[4].astype(jnp.bfloat16), "segment").astype(jnp.float32),
        lax.psum(placed[5].astype(jnp.bfloat16), "segment").astype(jnp.float32),
        lax.psum(placed[6].astype(jnp.bfloat16), "segment").astype(jnp.float32),
        lax.psum(placed[7].astype(jnp.bfloat16), "segment").astype(jnp.float32),
        lax.psum(placed[8].astype(jnp.bfloat16), "segment").astype(jnp.float32),
        lax.psum(placed[9].astype(jnp.bfloat16), "segment").astype(jnp.float32),
        lax.psum(placed[10].astype(jnp.bfloat16), "segment").astype(jnp.float32),
        lax.psum(placed[11].astype(jnp.bfloat16), "segment").astype(jnp.float32),
        lax.psum(placed[12].astype(jnp.bfloat16), "segment").astype(jnp.float32),
        lax.psum(placed[13].astype(jnp.bfloat16), "segment").astype(jnp.float32),
    )
    return (
        section_outputs,
        section_grads,
        summed[0],
        summed[1],
        summed[2],
        summed[3],
        summed[4],
        summed[5],
        summed[6],
        summed[7],
        summed[8],
        summed[9],
        summed[10],
        summed[11],
        summed[12],
        summed[13],
    )


W = 768
IMG = 56
LIVE = 49
ROWS = 224
PAIR = 2 * IMG
LANES = 128
SCALE = HD ** (-0.5)
F32 = jnp.float32
BF16 = jnp.bfloat16
TAPS = [(a, b) for a in range(3) for b in range(3)]


def mm(a, b):
    return lax.dot_general(a, b, (((1,), (0,)), ((), ())), preferred_element_type=F32)


def mm_nt(a, b):
    return lax.dot_general(a, b, (((1,), (1,)), ((), ())), preferred_element_type=F32)


def mm_tn(a, b):
    return lax.dot_general(a, b, (((0,), (0,)), ((), ())), preferred_element_type=F32)


def row_index(rows):
    return lax.broadcasted_iota(jnp.int32, (rows, 1), 0)


def live_rows(rows):
    return lax.rem(row_index(rows), IMG) < LIVE


def column_masks(rows):
    place = lax.rem(row_index(rows), IMG)
    column = lax.rem(place, SIDE)
    live = place < LIVE
    return [(live & (column + b - 1 >= 0) & (column + b - 1 < SIDE)).astype(F32) for b in range(3)]


def rolled(values, by):
    by = by % values.shape[0]
    return values if by == 0 else pltpu.roll(values, by, 0)


def norm_parts(values):
    center = values - jnp.mean(values, axis=-1, keepdims=True)
    spread = jnp.mean(center * center, axis=-1, keepdims=True)
    rstd = lax.rsqrt(spread + EPSILON)
    return center * rstd, rstd


def column_sum(values):
    return jnp.sum(values, axis=0, keepdims=True)


def head_lanes(head):
    lane = lax.broadcasted_iota(jnp.int32, (1, LANES), 1)
    return (lane // HD) == head


def only(values, mask):
    return jnp.where(mask, values, jnp.zeros_like(values))


def mixer_front(layer, u_in, w, small, c_ref, xhat, rstd, n_ref, t_ref, p_ref, m_ref):
    base = 12 * layer
    row = lambda r: small[layer, r:r + 1, :]
    v = u_in[...].astype(F32)
    masks = column_masks(ROWS)
    total = v + row(9)
    for b in range(3):
        part = jnp.zeros_like(v)
        for a in range(3):
            part = part + row(3 * a + b) * rolled(v, -(SIDE * (a - 1) + b - 1))
        total = total + part * masks[b]
    c = jnp.where(live_rows(ROWS), total, 0.0)
    c_ref[...] = c
    x, r = norm_parts(c)
    xhat[...] = x
    rstd[...] = r
    n_ref[...] = (x * row(10) + row(11)).astype(BF16)

    @pl.loop(0, 3)
    def _(j):
        cols = pl.ds(pl.multiple_of(W * j, W), W)
        t_ref[:, cols] = (mm(n_ref[...], w[base + j]) + small[layer, pl.ds(12 + j, 1), :]).astype(BF16)


def mixer_mixture(layer, channel, u_out, w, small, mask, bias, c_ref, xhat, rstd, n_ref, t_ref, p_ref, m_ref):
    base = 12 * layer

    @pl.loop(0, 6)
    def _(g):
        qs = pl.ds(pl.multiple_of(LANES * g, LANES), LANES)
        ks = pl.ds(pl.multiple_of(W + LANES * g, LANES), LANES)
        vs = pl.ds(pl.multiple_of(2 * W + LANES * g, LANES), LANES)
        for pair in range(2):
            rows = slice(PAIR * pair, PAIR * pair + PAIR)
            q, k, val = t_ref[rows, qs], t_ref[rows, ks], t_ref[rows, vs]
            mix = jnp.zeros((PAIR, LANES), F32)
            if channel:
                for im in range(2):
                    here = (row_index(PAIR) // IMG) == im
                    km = k * only(mask[rows, :], here)
                    s = mm_tn(q, km) * SCALE + bias[...]
                    e = jnp.exp(s - jnp.max(s, axis=-1, keepdims=True))
                    p = e / jnp.sum(e, axis=-1, keepdims=True)
                    p_ref[g, 2 * pair + im] = p
                    mix = mix + mm_nt(only(val, here), p.astype(BF16))
            else:
                for head in range(4):
                    lanes = head_lanes(head)
                    s = mm_nt(only(q, lanes), k) * SCALE + bias[...]
                    e = jnp.exp(s - jnp.max(s, axis=-1, keepdims=True))
                    p = e / jnp.sum(e, axis=-1, keepdims=True)
                    p_ref[g, 4 * pair + head] = p
                    mix = mix + mm(p.astype(BF16), only(val, lanes))
            m_ref[rows, qs] = mix.astype(BF16)

    out = c_ref[...] + mm(m_ref[...], w[base + 3]) + small[layer, 15:16, :]
    u_out[...] = jnp.where(live_rows(ROWS), out, 0.0).astype(BF16)


def mix_backward(layer, channel, u_in, g_in, g_out, w, small, mask, sg, dw, c_ref, xhat, rstd, n_ref, t_ref, p_ref, m_ref, dm_ref, dt_ref, acc):
    base = 12 * layer
    row = lambda r: small[layer, r:r + 1, :]
    g = g_in[...]
    sg[layer, 15:16, :] = column_sum(g.astype(F32))
    dm_ref[...] = mm_nt(g, w[base + 3]).astype(BF16)
    dw(layer, 3, m_ref, lambda: g_in[...])

    @pl.loop(0, 6)
    def _(grp):
        qs = pl.ds(pl.multiple_of(LANES * grp, LANES), LANES)
        ks = pl.ds(pl.multiple_of(W + LANES * grp, LANES), LANES)
        vs = pl.ds(pl.multiple_of(2 * W + LANES * grp, LANES), LANES)
        for pair in range(2):
            rows = slice(PAIR * pair, PAIR * pair + PAIR)
            q, k, val, dm = t_ref[rows, qs], t_ref[rows, ks], t_ref[rows, vs], dm_ref[rows, qs]
            dq = jnp.zeros((PAIR, LANES), F32)
            dk = jnp.zeros((PAIR, LANES), F32)
            dv = jnp.zeros((PAIR, LANES), F32)
            if channel:
                for im in range(2):
                    here = (row_index(PAIR) // IMG) == im
                    keep = only(mask[rows, :], here)
                    km = k * keep
                    p = p_ref[grp, 2 * pair + im]
                    dmh = only(dm, here)
                    dp = mm_tn(dmh, val)
                    dv = dv + mm(dmh, p.astype(BF16))
                    ds = (p * (dp - jnp.sum(dp * p, axis=-1, keepdims=True))).astype(BF16)
                    dq = dq + mm_nt(km, ds)
                    dk = dk + mm(only(q, here), ds) * keep.astype(F32)
            else:
                for head in range(4):
                    lanes = head_lanes(head)
                    p = p_ref[grp, 4 * pair + head]
                    dmh = only(dm, lanes)
                    dp = mm_nt(dmh, val)
                    dv = dv + mm_tn(p.astype(BF16), dmh)
                    ds = (p * (dp - jnp.sum(dp * p, axis=-1, keepdims=True))).astype(BF16)
                    dq = dq + mm(ds, only(k, lanes))
                    dk = dk + mm_tn(ds, only(q, lanes))
            dt_ref[rows, qs] = (dq * SCALE).astype(BF16)
            dt_ref[rows, ks] = (dk * SCALE).astype(BF16)
            dt_ref[rows, vs] = dv.astype(BF16)

    acc[...] = jnp.zeros_like(acc)

    @pl.loop(0, 3)
    def _(j):
        cols = pl.ds(pl.multiple_of(W * j, W), W)
        acc[...] += mm_nt(dt_ref[:, cols], w[base + j])
        sg[layer, pl.ds(12 + j, 1), :] = column_sum(dt_ref[:, cols].astype(F32))
        dw(layer, j, n_ref, lambda: dt_ref[:, cols])

    dn = acc[...]
    x = xhat[...]
    sg[layer, 10:11, :] = column_sum(dn * x)
    sg[layer, 11:12, :] = column_sum(dn)
    e = dn * row(10)
    inner = rstd[...] * (e - jnp.mean(e, axis=-1, keepdims=True) - x * jnp.mean(e * x, axis=-1, keepdims=True))
    dc = jnp.where(live_rows(ROWS), g_in[...].astype(F32) + inner, 0.0)
    sg[layer, 9:10, :] = column_sum(dc)
    v = u_in[...].astype(F32)
    masks = column_masks(ROWS)
    du = dc
    for b in range(3):
        dcm = dc * masks[b]
        for a in range(3):
            moved = rolled(dcm, SIDE * (a - 1) + b - 1)
            tap = 3 * a + b
            du = du + row(tap) * moved
            sg[layer, tap:tap + 1, :] = column_sum(moved * v)
    g_out[...] = jnp.where(live_rows(ROWS), du, 0.0).astype(BF16)


ROOT_HALF = 0.5 ** 0.5
ROOT_TWO_PI = 0.3989422804014327


def ff_forward(layer, u_in, u_out, w, small, xhat, rstd, n_ref, slope, acc):
    base = 12 * layer
    row = lambda r: small[layer, r:r + 1, :]
    x, r = norm_parts(u_in[...].astype(F32))
    xhat[...] = x
    rstd[...] = r
    n_ref[...] = (x * row(16) + row(17)).astype(BF16)
    acc[...] = u_in[...].astype(F32) + row(22)

    @pl.loop(0, 4)
    def _(j):
        cols = pl.ds(pl.multiple_of(W * j, W), W)
        h = mm(n_ref[...], w[base + 4 + j]) + small[layer, pl.ds(18 + j, 1), :]
        cdf = 0.5 + 0.5 * lax.erf(h * ROOT_HALF)
        slope[:, cols] = cdf + h * (ROOT_TWO_PI * jnp.exp(-0.5 * h * h))
        acc[...] += mm((h * cdf).astype(BF16), w[base + 8 + j])

    u_out[...] = jnp.where(live_rows(ROWS), acc[...], 0.0).astype(BF16)


def ff_backward(layer, g_in, g_out, w, small, sg, xhat, rstd, slope, acc):
    base = 12 * layer
    row = lambda r: small[layer, r:r + 1, :]
    sg[layer, 22:23, :] = column_sum(g_in[...].astype(F32))
    acc[...] = jnp.zeros_like(acc)

    @pl.loop(0, 4)
    def _(j):
        cols = pl.ds(pl.multiple_of(W * j, W), W)
        dh = (mm_nt(g_in[...], w[base + 8 + j]) * slope[:, cols]).astype(BF16)
        sg[layer, pl.ds(18 + j, 1), :] = column_sum(dh.astype(F32))
        acc[...] += mm_nt(dh, w[base + 4 + j])

    dn = acc[...]
    x = xhat[...]
    sg[layer, 16:17, :] = column_sum(dn * x)
    sg[layer, 17:18, :] = column_sum(dn)
    e = dn * row(16)
    inner = rstd[...] * (e - jnp.mean(e, axis=-1, keepdims=True) - x * jnp.mean(e * x, axis=-1, keepdims=True))
    g_out[...] = jnp.where(live_rows(ROWS), g_in[...].astype(F32) + inner, 0.0).astype(BF16)


def chain_scratch():
    V = pltpu.VMEM
    mixer = [V((ROWS, W), F32), V((ROWS, 1), F32), V((ROWS, W), BF16), V((ROWS, 3 * W), BF16)]
    feed = [V((ROWS, W), F32), V((ROWS, 1), F32), V((ROWS, W), BF16), V((ROWS, 4 * W), F32)]
    return (mixer + [V((6, 8, PAIR, PAIR), F32), V((ROWS, W), BF16)] + feed + mixer + [V((6, 4, LANES, LANES), F32), V((ROWS, W), BF16)] + feed
            + [V((ROWS, W), F32), V((ROWS, W), F32), V((ROWS, W), BF16), V((ROWS, 3 * W), BF16), V((PAIR, PAIR), F32), V((LANES, LANES), F32)])


def fill_biases(win_bias, chan_bias):
    qi = lax.broadcasted_iota(jnp.int32, (PAIR, PAIR), 0)
    ki = lax.broadcasted_iota(jnp.int32, (PAIR, PAIR), 1)
    win_bias[...] = jnp.where(((qi // IMG) == (ki // IMG)) & (lax.rem(ki, IMG) < LIVE), 0.0, -1e30).astype(F32)
    ci = lax.broadcasted_iota(jnp.int32, (LANES, LANES), 0)
    ei = lax.broadcasted_iota(jnp.int32, (LANES, LANES), 1)
    chan_bias[...] = jnp.where((ci // HD) == (ei // HD), 0.0, -1e30).astype(F32)


class Chain:
    def __init__(self, w, small, mask, u, g, sg, dw, scratch):
        self.w, self.small, self.mask, self.u, self.g, self.sg, self.dw = w, small, mask, u, g, sg, dw
        s = scratch
        self.window, self.feed0, self.channel, self.feed1 = s[0:6], s[6:10], s[10:16], s[16:20]
        self.c_ref, self.acc, self.dm, self.dt, self.win_bias, self.chan_bias = s[20:26]

    def front(self, k):
        u, w, small = self.u, self.w, self.small
        if k == 0:
            fill_biases(self.win_bias, self.chan_bias)
            mixer_front(0, u[0], w, small, self.c_ref, *self.window)
        if k == 1:
            ff_forward(0, u[1], u[2], w, small, *self.feed0, self.acc)
        if k == 2:
            mixer_front(1, u[2], w, small, self.c_ref, *self.channel)
        if k == 3:
            ff_forward(1, u[3], u[4], w, small, *self.feed1, self.acc)

    def rest(self, k):
        u, w, small = self.u, self.w, self.small
        if k == 0:
            mixer_mixture(0, False, u[1], w, small, self.mask, self.win_bias, self.c_ref, *self.window)
        if k == 2:
            mixer_mixture(1, True, u[3], w, small, self.mask, self.chan_bias, self.c_ref, *self.channel)

    def backward(self, k):
        u, g, w, small, sg = self.u, self.g, self.w, self.small, self.sg
        if k in (0, 2):
            parts = self.channel if k == 2 else self.window
            mix_backward(k // 2, k == 2, u[k], g[k + 1], g[k], w, small, self.mask, sg, self.dw, self.c_ref, *parts, self.dm, self.dt, self.acc)
        else:
            x, r, _, slope = self.feed0 if k == 1 else self.feed1
            ff_backward(k // 2, g[k + 1], g[k], w, small, sg, x, r, slope, self.acc)


MESH = pl.DeviceIdType.MESH
VMEM_LIMIT = 63 * 1024 * 1024
STRIP = 96
HALF = 384


def slot(item, line, d):
    red = lax.rem(item, 3) // 2
    block = 12 * (item // 3) + 4 * lax.rem(item, 3) + (1 - red) * line + red * (d // 2)
    row = (1 - red) * STRIP * d + red * (4 * STRIP * lax.rem(d, 2) + STRIP * line)
    return block, row


def other_planes(z):
    near = z + 1 - 2 * (z // 2)
    far = 3 * (1 - z // 2)
    return near, 6 - z - near - far, far


class Place:
    def __init__(self):
        self.s = lax.axis_index("segment")
        self.d = lax.axis_index("dp")
        self.z = self.d // 2
        self.c = lax.rem(self.d, 2)
        self.xn = self.s + 1 - 2 * lax.rem(self.s, 2)
        self.yn = lax.rem(self.s + 2, 4)
        self.dn = 3 - self.s
        self.twin = self.d + 1 - 2 * self.c


def remote(src, dst, ssem, rsem, seg, dev):
    return pltpu.make_async_remote_copy(src, dst, ssem, rsem, device_id=(seg, dev), device_id_type=MESH)


def gather_scratch():
    D = pltpu.SemaphoreType.DMA
    return [D((2, 9)), D((6, 5)), D((6, 3, 2)), D((6, 3, 2)), D((6, 4, 4)), D((2, 3, 4)), D((2, 3, 4))]


class Gather:
    def __init__(self, at, shards, wbuf, sems):
        self.at, self.shards, self.w = at, shards, wbuf
        self.lsem, self.zs, self.xs, self.ys, self.pr, self.cs, self.cr = sems
        self.planes = other_planes(at.z)
        self.away = 2 * (at.z // 2) - 1
        self.inner = (at.z == 1) | (at.z == 2)
        self.groups = [(layer, part, k) for layer in range(2) for part in range(3) for k in range(3)]

    def strip(self, item, line, plane):
        block, row = slot(item, line, 2 * plane + self.at.c)
        return self.w.at[block, pl.ds(pl.multiple_of(row, STRIP), STRIP), :]

    def quad_ref(self, layer, part, plane, core):
        if part == 2:
            return self.w.at[12 * layer + 8 + plane, pl.ds(pl.multiple_of(4 * STRIP * core, 4 * STRIP), 4 * STRIP), :]
        row = pl.multiple_of(STRIP * (2 * plane + core), STRIP)
        return self.w.at[pl.ds(12 * layer + 4 * part, 4), pl.ds(row, STRIP), :]

    def quad(self, layer, part, plane, core, k):
        ref = self.quad_ref(layer, part, plane, core)
        return remote(ref, ref, self.cs.at[layer, part, k], self.cr.at[layer, part, plane], self.at.s, self.at.twin)

    def local(self, layer):
        triple, output, expand, reduce = self.shards
        at, w, base = self.at, self.w, 12 * layer
        rows = pl.ds(pl.multiple_of(STRIP * at.d, STRIP), STRIP)
        sems = self.lsem.at
        copies = [pltpu.make_async_copy(triple.at[layer, :, pl.ds(W * j, W)], w.at[base + j, rows, :], sems[layer, j]) for j in range(3)]
        copies.append(pltpu.make_async_copy(output.at[layer], w.at[base + 3, rows, :], sems[layer, 3]))
        copies += [pltpu.make_async_copy(expand.at[layer, :, pl.ds(W * j, W)], w.at[base + 4 + j, rows, :], sems[layer, 4 + j]) for j in range(4)]
        half = pl.ds(pl.multiple_of(4 * STRIP * at.c, 4 * STRIP), 4 * STRIP)
        copies.append(pltpu.make_async_copy(reduce.at[layer], w.at[base + 8 + at.z, half, :], sems[layer, 8]))
        return copies

    def up(self, item):
        ref = self.strip(item, self.at.s, self.at.z)
        return remote(ref, ref, self.zs.at[item, 0], self.pr.at[item, self.at.z, self.at.s], self.at.s, self.at.d + 2)

    def down(self, item):
        ref = self.strip(item, self.at.s, self.at.z)
        return remote(ref, ref, self.zs.at[item, 1], self.pr.at[item, self.at.z, self.at.s], self.at.s, self.at.d - 2)

    def onward(self, item, k):
        step = self.away if k != 1 else -self.away
        ref = self.strip(item, self.at.s, self.planes[k])
        return remote(ref, ref, self.zs.at[item, 2 + k], self.pr.at[item, self.planes[k], self.at.s], self.at.s, self.at.d + 2 * step)

    def to_x(self, item, k, line, j):
        ref = self.strip(item, line, self.planes[k])
        return remote(ref, ref, self.xs.at[item, k, j], self.pr.at[item, self.planes[k], line], self.at.xn, self.at.d)

    def to_y(self, item, k, line, j):
        ref = self.strip(item, line, self.planes[k])
        return remote(ref, ref, self.ys.at[item, k, j], self.pr.at[item, self.planes[k], line], self.at.yn, self.at.d)

    def arrival(self, item, k, line):
        ref = self.strip(item, line, self.planes[k])
        return remote(ref, ref, self.zs.at[item, 0], self.pr.at[item, self.planes[k], line], self.at.s, self.at.twin)

    def ends(self, item, act):
        @pl.when(self.at.z < 3)
        def _():
            act(self.up(item))

        @pl.when(self.at.z > 0)
        def _():
            act(self.down(item))

    def begin(self):
        at = self.at
        copies = [self.local(layer) for layer in range(2)]
        for layer in range(2):
            for copy in copies[layer]:
                copy.start()
        for copy in copies[0]:
            copy.wait()
        self.ends(0, lambda copy: copy.start())
        for part in range(3):
            self.quad(0, part, at.z, at.c, 3).start()
        for copy in copies[1]:
            copy.wait()
        for part in range(3):
            self.quad(1, part, at.z, at.c, 3).start()

    def stage_a(self, layer, part, k):
        item = 3 * layer + part
        self.arrival(item, k, self.at.s).wait_recv()

        @pl.when(self.inner)
        def _():
            self.onward(item, k).start()

        self.to_x(item, k, self.at.s, 0).start()
        self.to_y(item, k, self.at.s, 0).start()

    def stage_b(self, layer, part, k):
        item = 3 * layer + part
        self.arrival(item, k, self.at.xn).wait_recv()
        if (part + k + layer) % 2 == 0:
            self.to_y(item, k, self.at.xn, 1).start()
        self.arrival(item, k, self.at.yn).wait_recv()
        if (part + k + layer) % 2 == 1:
            self.to_x(item, k, self.at.yn, 1).start()

    def stage_c(self, layer, part, k):
        item = 3 * layer + part
        self.arrival(item, k, self.at.dn).wait_recv()
        self.quad(layer, part, self.planes[k], self.at.c, k).start()

    def step(self, g):
        n = len(self.groups)
        if g < n and g % 3 == 0 and g // 3 + 1 < 6:
            self.ends(g // 3 + 1, lambda copy: copy.start())
        if g < n:
            self.stage_a(*self.groups[g])
        if 0 <= g - 1 < n:
            self.stage_b(*self.groups[g - 1])
        if 0 <= g - 2 < n:
            self.stage_c(*self.groups[g - 2])

    def settle(self, layer, part):
        for k in range(3):
            self.quad(layer, part, self.planes[k], 1 - self.at.c, k).wait_recv()
        self.quad(layer, part, self.at.z, 1 - self.at.c, 3).wait_recv()

    def drain(self):
        at = self.at
        for layer in range(2):
            for part in range(3):
                item = 3 * layer + part
                self.ends(item, lambda copy: copy.wait_send())
                self.quad(layer, part, at.z, at.c, 3).wait_send()
                for k in range(3):
                    @pl.when(self.inner)
                    def _():
                        self.onward(item, k).wait_send()

                    self.to_x(item, k, at.s, 0).wait_send()
                    self.to_y(item, k, at.s, 0).wait_send()
                    if (part + k + layer) % 2 == 0:
                        self.to_y(item, k, at.xn, 1).wait_send()
                    else:
                        self.to_x(item, k, at.yn, 1).wait_send()
                    self.quad(layer, part, self.planes[k], at.c, k).wait_send()


def greet_all(at):
    bar = pltpu.get_barrier_semaphore()

    def greet(seg, dev):
        pl.semaphore_signal(bar, inc=1, device_id=(seg, dev), device_id_type=MESH)

    for seg in (at.xn, at.yn, at.dn):
        greet(seg, at.d)
        greet(seg, at.twin)
    greet(at.s, at.twin)
    for j in range(1, 4):
        greet(at.s, lax.rem(at.d + 2 * j, 8))
    pl.semaphore_wait(bar, 10)


def add_into(total, term):
    total[...] = (total[...].astype(F32) + term[...].astype(F32)).astype(BF16)


def sum_into(total, terms):
    result = total[...].astype(F32)
    for j in range(3):
        result = result + terms[j].astype(F32)
    total[...] = result.astype(BF16)


class Spread:
    def __init__(self, at, w, fin, red, fsend, frecv):
        self.at, self.w, self.fin, self.red, self.fsend, self.frecv = at, w, fin, red, fsend, frecv
        self.layer, self.half = at.s // 2, lax.rem(at.s, 2)
        self.holds = at.c == at.z // 2

    def strip(self, block, row, rows=STRIP):
        return self.w.at[block, pl.ds(pl.multiple_of(row, STRIP), rows), :]

    def mix_copies(self, layer):
        at = self.at
        ref = self.strip(12 * layer + at.s, 2 * STRIP * at.z + STRIP * at.c)
        target, land = self.fin.at[layer, at.s], self.frecv.at[4 * layer + at.s]
        sends = [remote(ref, target, self.fsend.at[2 * layer + k], land, seg, at.d) for k, seg in enumerate((at.xn, at.yn))]
        return sends, pltpu.make_async_copy(ref, target, land)

    def core_copies(self, ref, target, land, core, first):
        at = self.at
        dev = 2 * at.z + core
        sends = [remote(ref, target, self.fsend.at[first + k], land, seg, dev) for k, seg in enumerate((at.xn, at.yn))]
        return core == at.c, sends, pltpu.make_async_copy(ref, target, land), remote(ref, target, self.fsend.at[first + 2], land, at.s, at.twin)

    def exp_copies(self, p):
        at = self.at
        ref = self.strip(12 * self.layer + 4 + 2 * at.c, 2 * STRIP * at.z + STRIP * p)
        j = 2 * self.half + at.c
        return self.core_copies(ref, self.fin.at[self.layer, 4 + j], self.frecv.at[8 + 4 * self.layer + j], p, 4 + 3 * p)

    def red_copies(self, m):
        ref = self.strip(12 * self.layer + 8 + 2 * (self.at.z // 2), HALF * lax.rem(self.at.z, 2) + HALF // 2 * m, HALF // 2)
        target = self.red.at[self.layer, pl.ds(HALF // 2 * m, HALF // 2), :]
        return self.core_copies(ref, target, self.frecv.at[16 + 2 * self.layer + m], self.half, 10 + 3 * m)

    def start_mix(self, layer):
        sends, keep = self.mix_copies(layer)
        for copy in sends:
            copy.start()
        keep.start()

    def start_cores(self, here, sends, keep, cross):
        for copy in sends:
            copy.start()

        @pl.when(here)
        def _():
            keep.start()

        @pl.when(jnp.logical_not(here))
        def _():
            cross.start()

    def start_exp(self):
        for p in range(2):
            self.start_cores(*self.exp_copies(p))

    def start_red(self):
        @pl.when(self.holds)
        def _():
            for m in range(2):
                self.start_cores(*self.red_copies(m))

    def passing(self, ref, land, to, n):
        return remote(ref, ref, self.fsend.at[16 + n], land, to, self.at.d)

    def sources(self):
        at = self.at
        return ((at.xn, at.yn, 0), (at.yn, at.xn, 1), (at.dn, at.xn, 2), (at.s, at.xn, 2))

    def mix_passing(self, layer, owner, to):
        return self.passing(self.fin.at[layer, owner], self.frecv.at[4 * layer + owner], to, layer)

    def exp_passing(self, core, owner, to):
        layer, j = owner // 2, 2 * lax.rem(owner, 2) + core
        return self.passing(self.fin.at[layer, 4 + j], self.frecv.at[8 + 4 * layer + j], to, 2 + core)

    def red_passing(self, m, owner, to):
        layer = owner // 2
        return self.passing(self.red.at[layer, pl.ds(HALF // 2 * m, HALF // 2), :], self.frecv.at[16 + 2 * layer + m], to, 4 + m)

    def finish_mix(self, layer):
        for owner, to, part in self.sources():
            copy = self.mix_passing(layer, owner, to)
            copy.wait_recv()
            if part == layer:
                copy.start()

    def finish_exp(self):
        for owner, to, part in self.sources():
            for core in range(2):
                copy = self.exp_passing(core, owner, to)
                copy.wait_recv()
                if part == core:
                    copy.start()

    def finish_red(self):
        for owner, to, part in self.sources():
            @pl.when(lax.rem(owner, 2) == self.at.c)
            def _():
                for m in range(2):
                    copy = self.red_passing(m, owner, to)
                    copy.wait_recv()
                    if part == m:
                        copy.start()

    def drain_cores(self, here, sends, keep, cross):
        for copy in sends:
            copy.wait_send()

        @pl.when(jnp.logical_not(here))
        def _():
            cross.wait_send()

    def drain(self):
        for layer in range(2):
            for copy in self.mix_copies(layer)[0]:
                copy.wait_send()
        for p in range(2):
            self.drain_cores(*self.exp_copies(p))

        @pl.when(self.holds)
        def _():
            for m in range(2):
                self.drain_cores(*self.red_copies(m))

        for owner, to, part in self.sources()[:2]:
            self.mix_passing(part, owner, to).wait_send()
            self.exp_passing(part, owner, to).wait_send()

            @pl.when(lax.rem(owner, 2) == self.at.c)
            def _():
                self.red_passing(part, owner, to).wait_send()


def train_kernel(triple, output, expand, reduce, pack, choose, x, mask, gin, cot,
                 sec_out, grad_out, fin, red, sg_out, xin, gland, xtw, gtw, mrx, prx, land_m, land_e, land_r,
                 w, small, packs, pks, pkr, u_buf, g_buf, sg, sga, sgr, stage, stage_f, lsem, tsem, xsend, xrecv, gsend, grecv, tws, twr, osend, orecv, msend, mrecv, psend, precv,
                 zms, zmr, zes, zer, zrs, zrr, fsend, frecv, sgs, sgv, *scratch):
    at = Place()
    s, d, z, c = at.s, at.d, at.z, at.c
    lay = s // 2
    segs = (at.xn, at.yn, at.dn)
    gather = Gather(at, (triple, output, expand, reduce), w, scratch[:7])
    u = [x] + [u_buf.at[i] for i in range(4)]
    g = [g_buf.at[i] for i in range(4)] + [gin]

    def dw(layer, j, lhs, rhs):
        w[12 * layer + j] = mm_tn(lhs[...], rhs()).astype(BF16)

    chain = Chain(w, small, mask, u, g, sg, dw, scratch[7:])
    sg[...] = jnp.zeros_like(sg)

    def pack_line(j):
        return remote(pack, packs.at[c, z], pks.at[j], pkr.at[3 - j], s, lax.rem(d + 2 * j, 8))

    def pack_twin(core):
        return remote(packs.at[core], packs.at[core], pks.at[0], pkr.at[3], s, at.twin)

    def pack_begin():
        packs[c, z] = pack[...]
        for j in range(1, 4):
            pack_line(j).start()

    def pack_pass():
        for j in range(1, 4):
            pack_line(j).wait_recv()
        pack_twin(c).start()

    def pack_end():
        pack_twin(1 - c).wait_recv()
        held = packs[...].reshape(8 * 48, LANES)
        total = jnp.zeros((48, W), F32)
        for p in range(8):
            piece = jnp.concatenate([mm(choose[p], held), jnp.zeros((48, W - LANES), F32)], axis=1)
            total = total + (pltpu.roll(piece, STRIP * p, 1) if p else piece)
        small[...] = total.reshape(2, 24, W)
        pack_twin(c).wait_send()
        for j in range(1, 4):
            pack_line(j).wait_send()

    def x_send(i):
        return remote(u_buf.at[2 * (segs[i] // 2)], xin.at[s], xsend.at[i], xrecv.at[i], segs[i], d)

    def g_send(i):
        return remote(g_buf.at[2], gland.at[s], gsend.at[i], grecv.at[i], segs[i], d)

    def u_out(i):
        return remote(u_buf.at[segs[i]], sec_out.at[s], osend.at[0, i], orecv.at[0, i], segs[i], d)

    def g_out(i):
        return remote(g_buf.at[segs[i]], grad_out.at[s], osend.at[1, i], orecv.at[1, i], segs[i], d)

    keep_x = pltpu.make_async_copy(u_buf.at[2 * lay], xin.at[s], lsem.at[0])
    keep_u = pltpu.make_async_copy(u_buf.at[s], sec_out.at[s], lsem.at[1])
    keep_g = pltpu.make_async_copy(g_buf.at[s], grad_out.at[s], lsem.at[2])
    keep_gl = pltpu.make_async_copy(g_buf.at[2], gland.at[s], lsem.at[3])

    def to_where(cond, copy, i, wait=False):
        @pl.when(cond(segs[i]))
        def _():
            copy(i).wait_send() if wait else copy(i).start()

    def x_twin(t):
        return remote(xin.at[t], xtw.at[t], tws.at[0, t], twr.at[0, t], s, at.twin)

    def g_twin(t):
        return remote(gland.at[t], gtw.at[t], tws.at[1, t], twr.at[1, t], s, at.twin)

    def cot_twin(t):
        return remote(cot.at[t], gtw.at[t], tws.at[1, t], twr.at[1, t], s, at.twin)

    def strip(block, p, core):
        return w.at[block, pl.ds(pl.multiple_of(2 * STRIP * p + STRIP * core, STRIP), STRIP), :]

    def twin_mix(layer, p):
        rows = pl.ds(pl.multiple_of(2 * STRIP * p + STRIP * (1 - c), STRIP), STRIP)
        return remote(w.at[pl.ds(12 * layer, 4), rows, :], mrx.at[layer, p], msend.at[layer, p], mrecv.at[layer, p], s, at.twin)

    def plane_send(layer, i, p):
        return remote(strip(12 * layer + segs[i], p, c), prx.at[layer, i, p], psend.at[layer, i, p], precv.at[layer, i, p], segs[i], d)

    def to_stage(src, n):
        load = pltpu.make_async_copy(src, stage.at[n], tsem.at[n])
        load.start()
        return load

    def cores_sum(layer):
        loads = []
        for p in range(4):
            twin_mix(layer, p).wait_recv()
            if p >= 2:
                take(layer, p - 2, loads[p - 2])
            loads.append(to_stage(mrx.at[layer, p], p % 2))
        for p in (2, 3):
            take(layer, p, loads[p])

    def take(layer, p, load):
        load.wait()
        for b in range(4):
            add_into(strip(12 * layer + b, p, c), stage.at[p % 2, b])

    def plane_begin(layer):
        for p in range(4):
            for i in range(3):
                plane_send(layer, i, p).start()

    def plane_sum(layer):
        for i in range(3):
            for p in range(4):
                plane_send(layer, i, p).wait_recv()
            to_stage(prx.at[layer, i], 0).wait()
            for p in range(4):
                add_into(strip(12 * layer + s, p, c), stage.at[0, p])

    def mix_line(layer, j):
        goal = lax.rem(z + j, 4)
        return remote(strip(12 * layer + s, goal, c), land_m.at[layer, 3 - j], zms.at[layer, j - 1], zmr.at[layer, 3 - j], s, lax.rem(d + 2 * j, 8))

    def exp_line(j):
        goal = lax.rem(z + j, 4)
        rows = pl.ds(pl.multiple_of(2 * STRIP * goal, 2 * STRIP), 2 * STRIP)
        return remote(w.at[eq, rows, :], land_e.at[3 - j], zes.at[j - 1], zer.at[3 - j], s, lax.rem(d + 2 * j, 8))

    def red_line(n):
        goal = 2 * c + n
        mine = lax.rem(z - goal + 7, 4)
        return remote(w.at[rq, pl.ds(4 * STRIP * n, 4 * STRIP), :], land_r.at[mine], zrs.at[n], zrr.at[mine], s, 2 * goal + c)

    def red_arrival(j):
        return remote(w.at[rq, pl.ds(0, 4 * STRIP), :], land_r.at[j], zrs.at[0], zrr.at[j], s, at.twin)

    def red_lines(act):
        for n in range(2):
            @pl.when(z != 2 * c + n)
            def _():
                act(red_line(n))

    def mix_line_sum(layer):
        for j in range(3):
            mix_line(layer, 3 - j).wait_recv()
        load = pltpu.make_async_copy(land_m.at[layer], stage.at[0, pl.ds(0, 3)], tsem.at[0])
        load.start()
        load.wait()
        sum_into(strip(12 * layer + s, z, c), stage.at[0])

    def feed_line_sum(landed, out):
        load = pltpu.make_async_copy(landed, stage_f, tsem.at[1])
        load.start()
        load.wait()
        sum_into(out, stage_f)

    def exp_line_sum():
        for j in range(3):
            exp_line(3 - j).wait_recv()
        feed_line_sum(land_e, w.at[eq, pl.ds(pl.multiple_of(2 * STRIP * z, 2 * STRIP), 2 * STRIP), :])

    def red_line_sum():
        @pl.when(z // 2 == c)
        def _():
            for j in range(3):
                red_arrival(j).wait_recv()
            for m in range(2):
                row = 4 * STRIP * lax.rem(z, 2) + 2 * STRIP * m
                feed_line_sum(land_r.at[:, pl.ds(2 * STRIP * m, 2 * STRIP), :], w.at[rq, pl.ds(pl.multiple_of(row, 2 * STRIP), 2 * STRIP), :])

    half = lax.rem(s, 2)
    own, other, far = 12 * lay, 12 * (1 - lay), 2 * (1 - c)
    eq, rq = own + 4 + 2 * c, own + 8 + 2 * c
    half_at = pl.ds(pl.multiple_of(4 * STRIP * half, LANES), 4 * STRIP)

    def block_x(k):
        return other + 4 + k

    def block_g(k):
        return other + 7 + k

    def block_a(k):
        return (1 - k // 2) * (other + 10 + k) + (k // 2) * (own + 4 + far)

    def block_h(k):
        later = (k + 1) // 2
        return (1 - later) * (own + 5 + far) + later * (own + 7 + far + k)

    def rows_of(i):
        return pl.ds(pl.multiple_of(ROWS * lax.rem(i, 3), ROWS), ROWS)

    def token_loads():
        loads = []
        for t in range(4):
            for n, (xs, gs) in enumerate(((xin, gland), (xtw, gtw))):
                i = 2 * t + n
                loads.append(pltpu.make_async_copy(xs.at[t], w.at[block_x(i // 3), rows_of(i), :], lsem.at[4 + i]))
                dst = w.at[block_g(i // 3), rows_of(i), :]
                load = pltpu.make_async_copy(gs.at[t], dst, lsem.at[12 + i])
                seed = pltpu.make_async_copy((cot if n == 0 else gs).at[t], dst, lsem.at[12 + i])
                loads.append((load, seed))
        return loads

    def feed_rows(i):
        k, rows = i // 3, rows_of(i)
        xh, _ = norm_parts(w[block_x(k), rows, :].astype(F32))
        n = (xh * small[lay, 16:17, :] + small[lay, 17:18, :]).astype(BF16)
        w[block_x(k), rows, :] = n
        for m in range(2):
            cols = slice(4 * STRIP * m, 4 * STRIP * (m + 1))
            h = mm(n, w[eq + m, :, half_at]) + small[lay, pl.ds(18 + 2 * c + m, 1), half_at]
            cdf = 0.5 + 0.5 * lax.erf(h * ROOT_HALF)
            w[block_a(k), rows, cols] = (h * cdf).astype(BF16)
            slope = cdf + h * (ROOT_TWO_PI * jnp.exp(-0.5 * h * h))
            w[block_h(k), rows, cols] = (mm_nt(w[block_g(k), rows, :], w[rq + m, half_at, :]) * slope).astype(BF16)

    def product(out, left, right):
        @pl.loop(0, 3)
        def _(i):
            cols = pl.ds(pl.multiple_of(256 * i, 256), 256)
            total = jnp.zeros((256, W), F32)
            for k, rows in enumerate((3 * ROWS, 3 * ROWS, 2 * ROWS)):
                total = total + mm_tn(w[left(k), :rows, cols], w[right(k), :rows, :])
            w[out, cols, :] = total.astype(BF16)

    partners = [(s, at.twin), (at.xn, d), (at.yn, d), (s, d + 2 * (1 - 2 * lax.rem(z, 2))), (s, lax.rem(d + 4, 8))]

    def sg_round(r):
        return remote(sga.at[r], sgr.at[r], sgs.at[r], sgv.at[r], *partners[r])

    def sg_next(r):
        sg_round(r).wait_recv()
        sga[r + 1] = sga[r] + sgr[r]
        if r < 4:
            sg_round(r + 1).start()

    spread = Spread(at, w, fin, red, fsend, frecv)
    low, high = (lambda t: t < 2), (lambda t: t >= 2)
    odd = lambda t: lax.rem(t, 2) == 1

    greet_all(at)
    pack_begin()

    @pl.when(s >= 2)
    def _():
        for t in range(4):
            cot_twin(t).start()

    gather.begin()
    for step in range(20):
        gather.step(step)
        if step == 1:
            pack_pass()
        if step == 3:
            pack_end()
        if step == 5:
            gather.settle(0, 0)
            chain.front(0)
        if step == 6:
            chain.rest(0)
        if step == 11:
            gather.settle(0, 1)
            gather.settle(0, 2)
            chain.front(1)
        if step == 14:
            gather.settle(1, 0)
            chain.front(2)
        if step == 15:
            chain.rest(2)
    for i in range(3):
        x_send(i).start()
    keep_x.start()
    gather.settle(1, 1)
    gather.settle(1, 2)
    chain.front(3)
    gather.drain()
    chain.backward(3)
    chain.backward(2)
    for i in range(3):
        to_where(low, g_send, i)
    keep_gl.start()
    for p in range(4):
        twin_mix(1, p).start()
    keep_x.wait()
    x_twin(s).start()
    for i in range(3):
        x_send(i).wait_recv()
        x_twin(segs[i]).start()
    chain.backward(1)
    cores_sum(1)
    keep_gl.wait()

    @pl.when(s < 2)
    def _():
        g_twin(s).start()

    for i in range(3):
        to_where(low, g_send, i, wait=True)

    @pl.when(s < 2)
    def _():
        for i in range(3):
            g_send(i).wait_recv()
            g_twin(segs[i]).start()

    plane_begin(1)
    loads = token_loads()
    for t in range(4):
        x_twin(t).wait_recv()
        cot_twin(t).wait_recv()
    for load in loads:
        if isinstance(load, tuple):
            @pl.when(s < 2)
            def _():
                load[0].start()

            @pl.when(s >= 2)
            def _():
                load[1].start()
        else:
            load.start()
    for load in loads:
        (load[0] if isinstance(load, tuple) else load).wait()
    pl.loop(0, 8)(feed_rows)
    product(eq, block_x, block_h)
    for j in (2, 1, 3):
        exp_line(j).start()
    product(rq, block_a, block_g)
    red_lines(lambda copy: copy.start())
    for i in range(3):
        to_where(odd, u_out, i)
    keep_u.start()
    for i in range(3):
        to_where(lambda t: t >= 1, g_out, i)
    chain.backward(0)
    for p in range(4):
        twin_mix(0, p).start()
    for i in range(3):
        to_where(lambda t: t == 0, g_out, i)
    keep_g.start()
    sga[0] = sg[...]
    sg_round(0).start()
    cores_sum(0)
    plane_begin(0)
    sg_next(0)
    plane_sum(1)
    for j in (2, 1, 3):
        mix_line(1, j).start()
    sg_next(1)
    exp_line_sum()
    spread.start_exp()
    sg_next(2)
    red_line_sum()
    spread.start_red()
    sg_next(3)
    mix_line_sum(1)
    spread.start_mix(1)
    sg_next(4)
    plane_sum(0)
    for j in (2, 1, 3):
        mix_line(0, j).start()
    spread.finish_exp()
    spread.finish_red()
    spread.finish_mix(1)
    mix_line_sum(0)
    spread.start_mix(0)
    spread.finish_mix(0)

    for r in range(5):
        sg_round(r).wait_send()
    for layer in range(2):
        sg_out[layer] = pltpu.roll(sga[5, layer], lax.rem(W - STRIP * d, W), 1)[:, :LANES]
        for first, count in ((12, 3), (18, 4)):
            for j in range(count):
                index = count * d + j
                sga[0, layer] = pltpu.roll(sga[5, layer], lax.rem(W - STRIP * lax.rem(index, 8), W), 1)
                sg_out[layer, first + j:first + j + 1, :] = sga[0, layer, pl.ds(first + index // 8, 1), :][:, :LANES]
    spread.drain()
    for i in range(3):
        x_send(i).wait_send()
        to_where(odd, u_out, i, wait=True)
        g_out(i).wait()
        for layer in range(2):
            for p in range(4):
                plane_send(layer, i, p).wait_send()

    @pl.when(lax.rem(s, 2) == 1)
    def _():
        for i in range(3):
            u_out(i).wait_recv()

    for t in range(4):
        x_twin(t).wait_send()
        cot_twin(t).wait_send()
    keep_u.wait()
    keep_g.wait()
    for p in range(4):
        for layer in range(2):
            twin_mix(layer, p).wait_send()
    for j in range(1, 4):
        for layer in range(2):
            mix_line(layer, j).wait_send()
        exp_line(j).wait_send()
    red_lines(lambda copy: copy.wait_send())


def train_call(triple, output, expand, reduce, pack, choose, x, mask, gin, cot):
    V = pltpu.VMEM
    D = pltpu.SemaphoreType.DMA
    S = jax.ShapeDtypeStruct
    anywhere = pl.BlockSpec(memory_space=pl.ANY)
    vmem = pl.BlockSpec(memory_space=V)
    tokens = S((4, ROWS, W), BF16)
    out = pl.pallas_call(
        train_kernel,
        out_shape=(
            tokens, tokens, S((2, 8, STRIP, W), BF16), S((2, HALF, W), BF16), S((2, 24, LANES), F32), tokens, tokens, tokens, tokens,
            S((2, 4, 4, STRIP, W), BF16), S((2, 3, 4, STRIP, W), BF16), S((2, 3, STRIP, W), BF16), S((3, 2 * STRIP, W), BF16), S((3, 4 * STRIP, W), BF16),
        ),
        in_specs=[anywhere] * 4 + [vmem] * 5 + [anywhere],
        out_specs=[anywhere] * 4 + [vmem] + [anywhere] * 9,
        scratch_shapes=[
            V((24, W, W), BF16), V((2, 24, W), F32), V((2, 4, 48, LANES), BF16), D((4,)), D((4,)), V((4, ROWS, W), BF16), V((4, ROWS, W), BF16), V((2, 24, W), F32), V((6, 2, 24, W), F32), V((5, 2, 24, W), F32),
            V((2, 4, STRIP, W), BF16), V((3, 2 * STRIP, W), BF16),
            D((20,)), D((2,)), D((3,)), D((3,)), D((3,)), D((3,)), D((2, 4)), D((2, 4)), D((2, 3)), D((2, 3)), D((2, 4)), D((2, 4)), D((2, 3, 4)), D((2, 3, 4)),
            D((2, 3)), D((2, 3)), D((3,)), D((3,)), D((2,)), D((3,)), D((22,)), D((20,)), D((5,)), D((5,)),
        ] + gather_scratch() + chain_scratch(),
        compiler_params=pltpu.CompilerParams(collective_id=1, has_side_effects=True, vmem_limit_bytes=VMEM_LIMIT),
        name="train_sections",
    )(triple, output, expand, reduce, pack, choose, x, mask, gin, cot)
    return out[:6]


def pack_small(conv_weight, conv_bias, mixer_gain, mixer_shift, triple_bias, output_bias, feed_gain, feed_shift, expand_bias, reduce_bias):
    part = conv_bias.shape[1]
    rows = [conv_weight] + [
        v.reshape(2, -1, part)
        for v in (conv_bias, mixer_gain, mixer_shift, triple_bias, output_bias, feed_gain, feed_shift, expand_bias, reduce_bias)
    ]
    return jnp.concatenate(rows, axis=1)


def piece_choice():
    choice = np.zeros((8, 2, 24, 2, 4, 2, 24), np.float32)
    for place in range(8):
        for row in range(23):
            first, count = (12, 3) if 12 <= row < 15 else (18, 4) if 18 <= row < 22 else (row, 1)
            index = 8 * (row - first) + place
            shard, source = index // count, first + index % count
            for layer in range(2):
                choice[place, layer, row, shard % 2, shard // 2, layer, source] = 1.0
    return jnp.asarray(choice.reshape(8, 48, 384), BF16)


def pad_images(rows):
    return jnp.pad(rows.reshape(-1, LIVE, rows.shape[1]), ((0, 0), (0, IMG - LIVE), (0, 0))).reshape(-1, rows.shape[1])


def unpad_images(rows):
    lead = rows.shape[:-2]
    return rows.reshape(lead + (-1, IMG, W))[..., :LIVE, :].reshape(lead + (-1, W))


def spread_body(
    patches, region_mask, conv_weight, conv_bias, mixer_gain, mixer_shift, triple_weight, triple_bias, output_weight,
    output_bias, feed_gain, feed_shift, expand_weight, expand_bias, reduce_weight, reduce_bias, cotangent,
):
    s = lax.axis_index("segment")
    d = lax.axis_index("dp")
    packed = pack_small(conv_weight, conv_bias, mixer_gain, mixer_shift, triple_bias, output_bias, feed_gain, feed_shift, expand_bias, reduce_bias)
    pack = jnp.pad(packed, ((0, 0), (0, 1), (0, LANES - packed.shape[2]))).reshape(48, LANES)
    own = patches.shape[0] // lax.axis_size("segment")
    mine = lambda v: lax.dynamic_slice_in_dim(v, s * own, own, 0)
    x = pad_images(mine(patches))
    cot = pad_images(cotangent).reshape(4, ROWS, W)
    gin = lax.dynamic_index_in_dim(cot, s, 0, keepdims=False)
    mask = pad_images(mine(region_mask).astype(BF16)[:, None])
    sec_out, grad_out, fin, red, sg, xin = train_call(
        triple_weight, output_weight, expand_weight, reduce_weight, pack, piece_choice(), x, mask, gin, cot
    )
    sec_out = jnp.where(lax.rem(s, 2) == 0, xin, sec_out)
    place = lambda v: unpad_images(v.reshape(1, 4 * ROWS, W))
    part = W // lax.axis_size("dp")
    rows = lambda lo, hi: sg[:, lo:hi, :part].reshape(2, -1)
    triple = jnp.concatenate([fin[:, j] for j in range(3)], axis=2)
    expand = fin[:, 4:].reshape(2, 2, 2, part, 2, W // 2).transpose(0, 3, 2, 4, 1, 5).reshape(2, part, 4 * W)
    wide = lambda v: v.astype(F32)
    return (
        place(sec_out), place(grad_out), sg[:, :9, :part], rows(9, 10), rows(10, 11), rows(11, 12), wide(triple), rows(12, 15), wide(fin[:, 3]),
        rows(15, 16), rows(16, 17), rows(17, 18), wide(expand), rows(18, 22), wide(red), rows(22, 23),
    )


def solution(mesh):
    in_specs = (
        P("dp", None),
        P("dp"),
        P(None, None, "dp"),
        P(None, "dp"),
        P(None, "dp"),
        P(None, "dp"),
        P(None, "dp", None),
        P(None, "dp"),
        P(None, "dp", None),
        P(None, "dp"),
        P(None, "dp"),
        P(None, "dp"),
        P(None, "dp", None),
        P(None, "dp"),
        P(None, "dp", None),
        P(None, "dp"),
        P("dp", None),
    )
    out_specs = (
        P("segment", "dp", None),
        P("segment", "dp", None),
        P(None, None, "dp"),
        P(None, "dp"),
        P(None, "dp"),
        P(None, "dp"),
        P(None, "dp", None),
        P(None, "dp"),
        P(None, "dp", None),
        P(None, "dp"),
        P(None, "dp"),
        P(None, "dp"),
        P(None, "dp", None),
        P(None, "dp"),
        P(None, "dp", None),
        P(None, "dp"),
    )
    chosen = spread_body if mesh.shape["dp"] == 8 and mesh.shape["segment"] == 4 else body
    return jax.shard_map(chosen, mesh=mesh, in_specs=in_specs, out_specs=out_specs, check_vma=False)
```

```python
from functools import partial

import jax
import jax.numpy as jnp
import numpy as np
from jax import lax
from jax.experimental import pallas as pl
from jax.experimental.pallas import tpu as pltpu
from jax.sharding import PartitionSpec as P

HD = 32
SIDE = 7
MICRO = 4
IMG_MB = 4


EPSILON = 1e-05


def as_sent(x):

    def short(part):
        return part.astype(jnp.bfloat16) if part.dtype == jnp.float32 else part

    return jax.tree.map(short, x)


def shifted_2(x, axis, by):
    count = lax.axis_size(axis)
    pairs = [(i, i + by) for i in range(count) if 0 <= i + by < count]
    return lax.ppermute(x, axis, pairs)


def dot_last(first_operand, second_operand):
    return lax.dot_general(
        first_operand, second_operand, (((1,), (1,)), ((), ())), preferred_element_type=jnp.float32
    )


def dot_first(first_operand, second_operand):
    return lax.dot_general(
        first_operand, second_operand, (((0,), (0,)), ((), ())), preferred_element_type=jnp.float32
    )


def layer_norm(values, norm_gain, norm_shift):
    center = values - jnp.mean(values, axis=-1, keepdims=True)
    spread = jnp.mean(center * center, axis=-1, keepdims=True)
    return center * lax.rsqrt(spread + EPSILON) * norm_gain + norm_shift


def position_conv(stream, conv_weight, conv_bias):
    features = stream.shape[-1]
    planes = stream.reshape(-1, SIDE, SIDE, features)
    padded = jnp.pad(planes, ((0, 0), (1, 1), (1, 1), (0, 0)))
    summed = jnp.zeros_like(planes) + conv_bias
    for tap_row in range(3):
        for tap_col in range(3):
            summed = (
                summed
                + padded[:, tap_row : tap_row + SIDE, tap_col : tap_col + SIDE, :]
                * conv_weight[tap_row * 3 + tap_col]
            )
    return stream + summed.reshape(stream.shape)


def front_part(stream, conv_weight, conv_bias, norm_gain, norm_shift):
    shifted = position_conv(stream, conv_weight, conv_bias)
    return (shifted, layer_norm(shifted, norm_gain, norm_shift))


def gelu_exact(values):
    return jax.nn.gelu(values, approximate=False)


def softmax_rows(scores):
    row_max = jnp.max(scores, axis=-1, keepdims=True)
    lifted = jnp.exp(scores - row_max)
    return lifted / jnp.sum(lifted, axis=-1, keepdims=True)


def window_forward(triple):
    tokens = triple.shape[0]
    features = triple.shape[1] // 3
    pieces = triple.reshape(tokens // (SIDE * SIDE), SIDE * SIDE, 3, features // HD, HD)
    queries = pieces[:, :, 0]
    key_parts = pieces[:, :, 1]
    value_parts = pieces[:, :, 2]
    scores = jnp.einsum(
        "iqhd,ikhd->ihqk", queries, key_parts, preferred_element_type=jnp.float32
    ) * HD ** (-0.5)
    softmaxed = softmax_rows(scores)
    softmaxed_low = softmaxed.astype(jnp.bfloat16)
    mixture = jnp.einsum(
        "ihqk,ikhd->iqhd", softmaxed_low, value_parts, preferred_element_type=jnp.float32
    )
    return (
        mixture.reshape(tokens, features),
        (queries, key_parts, value_parts, softmaxed, softmaxed_low),
    )


def window_backward(stored, grad_mixture):
    queries, key_parts, value_parts, softmaxed, softmaxed_low = stored
    grad_pieces = grad_mixture.reshape(queries.shape)
    grad_values = jnp.einsum(
        "ihqk,iqhd->ikhd", softmaxed_low, grad_pieces, preferred_element_type=jnp.float32
    )
    grad_soft = jnp.einsum(
        "iqhd,ikhd->ihqk", grad_pieces, value_parts, preferred_element_type=jnp.float32
    )
    grad_scores = (
        softmaxed * (grad_soft - jnp.sum(grad_soft * softmaxed, axis=-1, keepdims=True))
    ).astype(jnp.bfloat16)
    grad_queries = jnp.einsum(
        "ihqk,ikhd->iqhd", grad_scores, key_parts, preferred_element_type=jnp.float32
    ) * HD ** (-0.5)
    grad_keys = jnp.einsum(
        "ihqk,iqhd->ikhd", grad_scores, queries, preferred_element_type=jnp.float32
    ) * HD ** (-0.5)
    joined = jnp.stack([grad_queries, grad_keys, grad_values], axis=2)
    return joined.reshape(grad_mixture.shape[0], 3 * grad_mixture.shape[1])


def channel_forward(triple, mask_rows):
    tokens = triple.shape[0]
    features = triple.shape[1] // 3
    images = tokens // (SIDE * SIDE)
    pieces = triple.reshape(images, SIDE * SIDE, 3, features // HD, HD)
    queries = pieces[:, :, 0]
    keep_mask = mask_rows.reshape(images, SIDE * SIDE, 1, 1).astype(jnp.bfloat16)
    masked = pieces[:, :, 1] * keep_mask
    value_parts = pieces[:, :, 2]
    scores = jnp.einsum(
        "itgc,itge->igce", queries, masked, preferred_element_type=jnp.float32
    ) * HD ** (-0.5)
    softmaxed = softmax_rows(scores)
    softmaxed_low = softmaxed.astype(jnp.bfloat16)
    mixture = jnp.einsum(
        "igce,itge->itgc", softmaxed_low, value_parts, preferred_element_type=jnp.float32
    )
    return (
        mixture.reshape(tokens, features),
        (queries, masked, value_parts, keep_mask, softmaxed, softmaxed_low),
    )


def channel_backward(stored, grad_mixture):
    queries, masked, value_parts, keep_mask, softmaxed, softmaxed_low = stored
    grad_pieces = grad_mixture.reshape(queries.shape)
    grad_soft = jnp.einsum(
        "itgc,itge->igce", grad_pieces, value_parts, preferred_element_type=jnp.float32
    )
    grad_values = jnp.einsum(
        "igce,itgc->itge", softmaxed_low, grad_pieces, preferred_element_type=jnp.float32
    )
    grad_scores = (
        softmaxed * (grad_soft - jnp.sum(grad_soft * softmaxed, axis=-1, keepdims=True))
    ).astype(jnp.bfloat16)
    grad_queries = jnp.einsum(
        "igce,itge->itgc", grad_scores, masked, preferred_element_type=jnp.float32
    ) * HD ** (-0.5)
    grad_masked = jnp.einsum(
        "igce,itgc->itge", grad_scores, queries, preferred_element_type=jnp.float32
    ) * HD ** (-0.5)
    grad_keys = grad_masked * keep_mask.astype(jnp.float32)
    joined = jnp.stack([grad_queries, grad_keys, grad_values], axis=2)
    return joined.reshape(grad_mixture.shape[0], 3 * grad_mixture.shape[1])


def mixer_inner(stream, weights, mask_rows, channel):
    (
        conv_weight,
        conv_bias,
        norm_gain,
        norm_shift,
        triple_weight,
        triple_bias,
        output_weight,
        output_bias,
    ) = weights[:8]
    widened = stream.astype(jnp.float32)
    (shifted, normed), front_pull = jax.vjp(
        front_part,
        widened,
        conv_weight.astype(jnp.float32),
        conv_bias.astype(jnp.float32),
        norm_gain.astype(jnp.float32),
        norm_shift.astype(jnp.float32),
    )
    normed_low = normed.astype(jnp.bfloat16)
    triple = (
        jnp.dot(normed_low, triple_weight, preferred_element_type=jnp.float32)
        + triple_bias.astype(jnp.float32)
    ).astype(jnp.bfloat16)
    if channel:
        mixture, stored = channel_forward(triple, mask_rows)
    else:
        mixture, stored = window_forward(triple)
    mixture_low = mixture.astype(jnp.bfloat16)
    return (shifted, front_pull, normed_low, stored, mixture_low)


def mixer_forward(stream, weights, mask_rows, channel):
    shifted, front_pull, normed_low, stored, mixture_low = mixer_inner(
        stream, weights, mask_rows, channel
    )
    result = (
        shifted
        + jnp.dot(mixture_low, weights[6], preferred_element_type=jnp.float32)
        + weights[7].astype(jnp.float32)
    )
    return result.astype(jnp.bfloat16)


def mixer_backward(stream, grad_out, weights, mask_rows, channel):
    shifted, front_pull, normed_low, stored, mixture_low = mixer_inner(
        stream, weights, mask_rows, channel
    )
    grad_wide = grad_out.astype(jnp.float32)
    grad_out_bias = jnp.sum(grad_wide, axis=0)
    grad_out_weight = dot_first(mixture_low, grad_out)
    grad_mixture = dot_last(grad_out, weights[6]).astype(jnp.bfloat16)
    if channel:
        grad_triple = channel_backward(stored, grad_mixture).astype(jnp.bfloat16)
    else:
        grad_triple = window_backward(stored, grad_mixture).astype(jnp.bfloat16)
    grad_tri_weight = dot_first(normed_low, grad_triple)
    grad_tri_bias = jnp.sum(grad_triple.astype(jnp.float32), axis=0)
    grad_normed = dot_last(grad_triple, weights[4])
    grad_stream, grad_taps, grad_tap_bias, grad_gain, grad_shift = front_pull(
        (grad_wide, grad_normed)
    )
    zero_tail = tuple((jnp.zeros(member.shape, jnp.float32) for member in weights[8:]))
    return (
        grad_stream.astype(jnp.bfloat16),
        (
            grad_taps,
            grad_tap_bias,
            grad_gain,
            grad_shift,
            grad_tri_weight,
            grad_tri_bias,
            grad_out_weight,
            grad_out_bias,
        )
        + zero_tail,
    )


def feed_inner(stream, weights):
    norm_gain, norm_shift, expand_weight, expand_bias, reduce_weight, reduce_bias = weights[8:]
    widened = stream.astype(jnp.float32)
    normed, norm_pull = jax.vjp(
        layer_norm, widened, norm_gain.astype(jnp.float32), norm_shift.astype(jnp.float32)
    )
    normed_low = normed.astype(jnp.bfloat16)
    hidden = jnp.dot(
        normed_low, expand_weight, preferred_element_type=jnp.float32
    ) + expand_bias.astype(jnp.float32)
    active, gelu_pull = jax.vjp(gelu_exact, hidden)
    return (widened, norm_pull, normed_low, gelu_pull, active.astype(jnp.bfloat16))


def feed_forward(stream, weights):
    widened, norm_pull, normed_low, gelu_pull, active_low = feed_inner(stream, weights)
    result = (
        widened
        + jnp.dot(active_low, weights[12], preferred_element_type=jnp.float32)
        + weights[13].astype(jnp.float32)
    )
    return result.astype(jnp.bfloat16)


def feed_backward(stream, grad_out, weights):
    widened, norm_pull, normed_low, gelu_pull, active_low = feed_inner(stream, weights)
    grad_wide = grad_out.astype(jnp.float32)
    grad_red_bias = jnp.sum(grad_wide, axis=0)
    grad_red_weight = dot_first(active_low, grad_out)
    grad_active = dot_last(grad_out, weights[12])
    grad_hidden = gelu_pull(grad_active)[0].astype(jnp.bfloat16)
    grad_exp_weight = dot_first(normed_low, grad_hidden)
    grad_exp_bias = jnp.sum(grad_hidden.astype(jnp.float32), axis=0)
    grad_normed = dot_last(grad_hidden, weights[10])
    grad_inner, grad_gain, grad_shift = norm_pull(grad_normed)
    zero_head = tuple((jnp.zeros(member.shape, jnp.float32) for member in weights[:8]))
    grad_stream = grad_wide + grad_inner
    return (
        grad_stream.astype(jnp.bfloat16),
        zero_head
        + (grad_gain, grad_shift, grad_exp_weight, grad_exp_bias, grad_red_weight, grad_red_bias),
    )


def section_forward(section, stream, weights, mask_rows):
    if section % 2 == 1:
        return feed_forward(stream, weights)
    return mixer_forward(stream, weights, mask_rows, section == 2)


def section_backward(section, stream, grad_out, weights, mask_rows):
    if section % 2 == 1:
        return feed_backward(stream, grad_out, weights)
    return mixer_backward(stream, grad_out, weights, mask_rows, section == 2)


def spare_forward(stream, weights, mask_rows):
    return jnp.zeros_like(stream)


def spare_backward(stream, grad_out, weights, mask_rows):
    return (
        jnp.zeros_like(stream),
        tuple((jnp.zeros(member.shape, jnp.float32) for member in weights)),
    )


def put_rows(buffer, rows, row_start, is_live):
    former = lax.dynamic_slice_in_dim(buffer, row_start, rows.shape[0], 0)
    return lax.dynamic_update_slice_in_dim(buffer, jnp.where(is_live, rows, former), row_start, 0)


def run_segments(layer_set, patches, region_mask, cotangent, segment_index, segments):
    features = patches.shape[1]
    micro_count = MICRO
    micro_rows = IMG_MB * SIDE * SIDE
    tick_count = micro_count + segments - 1
    forward_branches = [
        partial(section_forward, 0),
        partial(section_forward, 1),
        partial(section_forward, 2),
        partial(section_forward, 3),
        spare_forward,
    ]
    backward_branches = [
        partial(section_backward, 0),
        partial(section_backward, 1),
        partial(section_backward, 2),
        partial(section_backward, 3),
        spare_backward,
    ]
    received = jnp.zeros((micro_rows, features), jnp.bfloat16)
    kept_inputs = jnp.zeros((micro_count * micro_rows, features), jnp.bfloat16)
    outputs_here = jnp.zeros((micro_count * micro_rows, features), jnp.bfloat16)
    for tick_index in range(tick_count):
        micro_index = tick_index - segment_index
        is_live = (micro_index >= 0) & (micro_index < micro_count)
        row_start = jnp.clip(micro_index, 0, micro_count - 1) * micro_rows
        fresh_rows = lax.dynamic_slice_in_dim(patches, row_start, micro_rows, 0)
        mask_rows = lax.dynamic_slice_in_dim(region_mask, row_start, micro_rows, 0)
        entering = jnp.where(segment_index == 0, fresh_rows, received)
        leaving = lax.switch(
            jnp.where(is_live, segment_index, segments),
            forward_branches,
            entering,
            layer_set,
            mask_rows,
        )
        kept_inputs = put_rows(kept_inputs, entering, row_start, is_live)
        outputs_here = put_rows(outputs_here, leaving, row_start, is_live)
        if tick_index + 1 < tick_count:
            received = jax.tree.map(
                lambda part, own: part.astype(own.dtype),
                shifted_2(as_sent(leaving), "segment", 1),
                leaving,
            )
    grad_received = jnp.zeros((micro_rows, features), jnp.bfloat16)
    grads_here = jnp.zeros((micro_count * micro_rows, features), jnp.bfloat16)
    totals = tuple((jnp.zeros(member.shape, jnp.float32) for member in layer_set))
    for tick_index in range(tick_count):
        micro_index = tick_index - (segments - 1 - segment_index)
        is_live = (micro_index >= 0) & (micro_index < micro_count)
        row_start = jnp.clip(micro_index, 0, micro_count - 1) * micro_rows
        seed_rows = lax.dynamic_slice_in_dim(cotangent, row_start, micro_rows, 0)
        mask_rows = lax.dynamic_slice_in_dim(region_mask, row_start, micro_rows, 0)
        arriving = jnp.where(segment_index == segments - 1, seed_rows, grad_received)
        stream = lax.dynamic_slice_in_dim(kept_inputs, row_start, micro_rows, 0)
        grad_stream, grad_terms = lax.switch(
            jnp.where(is_live, segment_index, segments),
            backward_branches,
            stream,
            arriving,
            layer_set,
            mask_rows,
        )
        totals = tuple(
            (first_term + second_term for first_term, second_term in zip(totals, grad_terms))
        )
        grads_here = put_rows(grads_here, grad_stream, row_start, is_live)
        if tick_index + 1 < tick_count:
            grad_received = jax.tree.map(
                lambda part, own: part.astype(own.dtype),
                shifted_2(as_sent(grad_stream), "segment", -1),
                grad_stream,
            )
    return (outputs_here, grads_here, totals)


def body(
    patches,
    region_mask,
    conv_weight,
    conv_bias,
    mixer_gain,
    mixer_shift,
    triple_weight,
    triple_bias,
    output_weight,
    output_bias,
    feed_gain,
    feed_shift,
    expand_weight,
    expand_bias,
    reduce_weight,
    reduce_bias,
    cotangent,
):
    params = (
        conv_weight,
        conv_bias,
        mixer_gain,
        mixer_shift,
        triple_weight,
        triple_bias,
        output_weight,
        output_bias,
        feed_gain,
        feed_shift,
        expand_weight,
        expand_bias,
        reduce_weight,
        reduce_bias,
    )
    segments = lax.axis_size("segment")
    segment_index = lax.axis_index("segment")
    layer_index = segment_index // 2
    slices = tuple(
        (lax.dynamic_index_in_dim(member, layer_index, 0, keepdims=False) for member in params)
    )
    layer_set = (
        lax.all_gather(slices[0], "dp", axis=1, tiled=True),
        lax.all_gather(slices[1], "dp", axis=0, tiled=True),
        lax.all_gather(slices[2], "dp", axis=0, tiled=True),
        lax.all_gather(slices[3], "dp", axis=0, tiled=True),
        lax.all_gather(slices[4], "dp", axis=0, tiled=True),
        lax.all_gather(slices[5], "dp", axis=0, tiled=True),
        lax.all_gather(slices[6], "dp", axis=0, tiled=True),
        lax.all_gather(slices[7], "dp", axis=0, tiled=True),
        lax.all_gather(slices[8], "dp", axis=0, tiled=True),
        lax.all_gather(slices[9], "dp", axis=0, tiled=True),
        lax.all_gather(slices[10], "dp", axis=0, tiled=True),
        lax.all_gather(slices[11], "dp", axis=0, tiled=True),
        lax.all_gather(slices[12], "dp", axis=0, tiled=True),
        lax.all_gather(slices[13], "dp", axis=0, tiled=True),
    )
    outputs_here, grads_here, totals = run_segments(
        layer_set, patches, region_mask, cotangent, segment_index, segments
    )
    reduced = (
        lax.psum_scatter(totals[0], "dp", scatter_dimension=1, tiled=True),
        lax.psum_scatter(totals[1], "dp", scatter_dimension=0, tiled=True),
        lax.psum_scatter(totals[2], "dp", scatter_dimension=0, tiled=True),
        lax.psum_scatter(totals[3], "dp", scatter_dimension=0, tiled=True),
        lax.psum_scatter(totals[4], "dp", scatter_dimension=0, tiled=True),
        lax.psum_scatter(totals[5], "dp", scatter_dimension=0, tiled=True),
        lax.psum_scatter(totals[6], "dp", scatter_dimension=0, tiled=True),
        lax.psum_scatter(totals[7], "dp", scatter_dimension=0, tiled=True),
        lax.psum_scatter(totals[8], "dp", scatter_dimension=0, tiled=True),
        lax.psum_scatter(totals[9], "dp", scatter_dimension=0, tiled=True),
        lax.psum_scatter(totals[10], "dp", scatter_dimension=0, tiled=True),
        lax.psum_scatter(totals[11], "dp", scatter_dimension=0, tiled=True),
        lax.psum_scatter(totals[12], "dp", scatter_dimension=0, tiled=True),
        lax.psum_scatter(totals[13], "dp", scatter_dimension=0, tiled=True),
    )
    placed = tuple(
        (
            jnp.stack(
                [jnp.where(layer_index == 0, member, 0.0), jnp.where(layer_index == 1, member, 0.0)]
            )
            for member in reduced
        )
    )
    section_outputs = outputs_here[None]
    section_grads = grads_here[None]
    summed = (
        lax.psum(placed[0].astype(jnp.bfloat16), "segment").astype(jnp.float32),
        lax.psum(placed[1].astype(jnp.bfloat16), "segment").astype(jnp.float32),
        lax.psum(placed[2].astype(jnp.bfloat16), "segment").astype(jnp.float32),
        lax.psum(placed[3].astype(jnp.bfloat16), "segment").astype(jnp.float32),
        lax.psum(placed[4].astype(jnp.bfloat16), "segment").astype(jnp.float32),
        lax.psum(placed[5].astype(jnp.bfloat16), "segment").astype(jnp.float32),
        lax.psum(placed[6].astype(jnp.bfloat16), "segment").astype(jnp.float32),
        lax.psum(placed[7].astype(jnp.bfloat16), "segment").astype(jnp.float32),
        lax.psum(placed[8].astype(jnp.bfloat16), "segment").astype(jnp.float32),
        lax.psum(placed[9].astype(jnp.bfloat16), "segment").astype(jnp.float32),
        lax.psum(placed[10].astype(jnp.bfloat16), "segment").astype(jnp.float32),
        lax.psum(placed[11].astype(jnp.bfloat16), "segment").astype(jnp.float32),
        lax.psum(placed[12].astype(jnp.bfloat16), "segment").astype(jnp.float32),
        lax.psum(placed[13].astype(jnp.bfloat16), "segment").astype(jnp.float32),
    )
    return (
        section_outputs,
        section_grads,
        summed[0],
        summed[1],
        summed[2],
        summed[3],
        summed[4],
        summed[5],
        summed[6],
        summed[7],
        summed[8],
        summed[9],
        summed[10],
        summed[11],
        summed[12],
        summed[13],
    )


W = 768
IMG = 56
LIVE = 49
ROWS = 224
PAIR = 2 * IMG
LANES = 128
SCALE = HD ** (-0.5)
F32 = jnp.float32
BF16 = jnp.bfloat16
TAPS = [(a, b) for a in range(3) for b in range(3)]


def mm(a, b):
    return lax.dot_general(a, b, (((1,), (0,)), ((), ())), preferred_element_type=F32)


def mm_nt(a, b):
    return lax.dot_general(a, b, (((1,), (1,)), ((), ())), preferred_element_type=F32)


def mm_tn(a, b):
    return lax.dot_general(a, b, (((0,), (0,)), ((), ())), preferred_element_type=F32)


def row_index(rows):
    return lax.broadcasted_iota(jnp.int32, (rows, 1), 0)


def live_rows(rows):
    return lax.rem(row_index(rows), IMG) < LIVE


def column_masks(rows):
    place = lax.rem(row_index(rows), IMG)
    column = lax.rem(place, SIDE)
    live = place < LIVE
    return [(live & (column + b - 1 >= 0) & (column + b - 1 < SIDE)).astype(F32) for b in range(3)]


def rolled(values, by):
    by = by % values.shape[0]
    return values if by == 0 else pltpu.roll(values, by, 0)


def norm_parts(values):
    center = values - jnp.mean(values, axis=-1, keepdims=True)
    spread = jnp.mean(center * center, axis=-1, keepdims=True)
    rstd = lax.rsqrt(spread + EPSILON)
    return center * rstd, rstd


def column_sum(values):
    return jnp.sum(values, axis=0, keepdims=True)


def head_lanes(head):
    lane = lax.broadcasted_iota(jnp.int32, (1, LANES), 1)
    return (lane // HD) == head


def only(values, mask):
    return jnp.where(mask, values, jnp.zeros_like(values))


def mixer_front(layer, u_in, w, small, c_ref, xhat, rstd, n_ref, t_ref, p_ref, m_ref):
    base = 12 * layer
    row = lambda r: small[layer, r:r + 1, :]
    v = u_in[...].astype(F32)
    masks = column_masks(ROWS)
    total = v + row(9)
    for b in range(3):
        part = jnp.zeros_like(v)
        for a in range(3):
            part = part + row(3 * a + b) * rolled(v, -(SIDE * (a - 1) + b - 1))
        total = total + part * masks[b]
    c = jnp.where(live_rows(ROWS), total, 0.0)
    c_ref[...] = c
    x, r = norm_parts(c)
    xhat[...] = x
    rstd[...] = r
    n_ref[...] = (x * row(10) + row(11)).astype(BF16)

    @pl.loop(0, 3)
    def _(j):
        cols = pl.ds(pl.multiple_of(W * j, W), W)
        t_ref[:, cols] = (mm(n_ref[...], w[base + j]) + small[layer, pl.ds(12 + j, 1), :]).astype(BF16)


def mixer_mixture(layer, channel, u_out, w, small, mask, bias, c_ref, xhat, rstd, n_ref, t_ref, p_ref, m_ref):
    base = 12 * layer

    @pl.loop(0, 6)
    def _(g):
        qs = pl.ds(pl.multiple_of(LANES * g, LANES), LANES)
        ks = pl.ds(pl.multiple_of(W + LANES * g, LANES), LANES)
        vs = pl.ds(pl.multiple_of(2 * W + LANES * g, LANES), LANES)
        for pair in range(2):
            rows = slice(PAIR * pair, PAIR * pair + PAIR)
            q, k, val = t_ref[rows, qs], t_ref[rows, ks], t_ref[rows, vs]
            mix = jnp.zeros((PAIR, LANES), F32)
            if channel:
                for im in range(2):
                    here = (row_index(PAIR) // IMG) == im
                    km = k * only(mask[rows, :], here)
                    s = mm_tn(q, km) * SCALE + bias[...]
                    e = jnp.exp(s - jnp.max(s, axis=-1, keepdims=True))
                    p = e / jnp.sum(e, axis=-1, keepdims=True)
                    p_ref[g, 2 * pair + im] = p
                    mix = mix + mm_nt(only(val, here), p.astype(BF16))
            else:
                for head in range(4):
                    lanes = head_lanes(head)
                    s = mm_nt(only(q, lanes), k) * SCALE + bias[...]
                    e = jnp.exp(s - jnp.max(s, axis=-1, keepdims=True))
                    p = e / jnp.sum(e, axis=-1, keepdims=True)
                    p_ref[g, 4 * pair + head] = p
                    mix = mix + mm(p.astype(BF16), only(val, lanes))
            m_ref[rows, qs] = mix.astype(BF16)

    out = c_ref[...] + mm(m_ref[...], w[base + 3]) + small[layer, 15:16, :]
    u_out[...] = jnp.where(live_rows(ROWS), out, 0.0).astype(BF16)


def mix_backward(layer, channel, u_in, g_in, g_out, w, small, mask, sg, dw, c_ref, xhat, rstd, n_ref, t_ref, p_ref, m_ref, dm_ref, dt_ref, acc):
    base = 12 * layer
    row = lambda r: small[layer, r:r + 1, :]
    g = g_in[...]
    sg[layer, 15:16, :] = column_sum(g.astype(F32))
    dm_ref[...] = mm_nt(g, w[base + 3]).astype(BF16)
    dw(layer, 3, m_ref, lambda: g_in[...])

    @pl.loop(0, 6)
    def _(grp):
        qs = pl.ds(pl.multiple_of(LANES * grp, LANES), LANES)
        ks = pl.ds(pl.multiple_of(W + LANES * grp, LANES), LANES)
        vs = pl.ds(pl.multiple_of(2 * W + LANES * grp, LANES), LANES)
        for pair in range(2):
            rows = slice(PAIR * pair, PAIR * pair + PAIR)
            q, k, val, dm = t_ref[rows, qs], t_ref[rows, ks], t_ref[rows, vs], dm_ref[rows, qs]
            dq = jnp.zeros((PAIR, LANES), F32)
            dk = jnp.zeros((PAIR, LANES), F32)
            dv = jnp.zeros((PAIR, LANES), F32)
            if channel:
                for im in range(2):
                    here = (row_index(PAIR) // IMG) == im
                    keep = only(mask[rows, :], here)
                    km = k * keep
                    p = p_ref[grp, 2 * pair + im]
                    dmh = only(dm, here)
                    dp = mm_tn(dmh, val)
                    dv = dv + mm(dmh, p.astype(BF16))
                    ds = (p * (dp - jnp.sum(dp * p, axis=-1, keepdims=True))).astype(BF16)
                    dq = dq + mm_nt(km, ds)
                    dk = dk + mm(only(q, here), ds) * keep.astype(F32)
            else:
                for head in range(4):
                    lanes = head_lanes(head)
                    p = p_ref[grp, 4 * pair + head]
                    dmh = only(dm, lanes)
                    dp = mm_nt(dmh, val)
                    dv = dv + mm_tn(p.astype(BF16), dmh)
                    ds = (p * (dp - jnp.sum(dp * p, axis=-1, keepdims=True))).astype(BF16)
                    dq = dq + mm(ds, only(k, lanes))
                    dk = dk + mm_tn(ds, only(q, lanes))
            dt_ref[rows, qs] = (dq * SCALE).astype(BF16)
            dt_ref[rows, ks] = (dk * SCALE).astype(BF16)
            dt_ref[rows, vs] = dv.astype(BF16)

    acc[...] = jnp.zeros_like(acc)

    @pl.loop(0, 3)
    def _(j):
        cols = pl.ds(pl.multiple_of(W * j, W), W)
        acc[...] += mm_nt(dt_ref[:, cols], w[base + j])
        sg[layer, pl.ds(12 + j, 1), :] = column_sum(dt_ref[:, cols].astype(F32))
        dw(layer, j, n_ref, lambda: dt_ref[:, cols])

    dn = acc[...]
    x = xhat[...]
    sg[layer, 10:11, :] = column_sum(dn * x)
    sg[layer, 11:12, :] = column_sum(dn)
    e = dn * row(10)
    inner = rstd[...] * (e - jnp.mean(e, axis=-1, keepdims=True) - x * jnp.mean(e * x, axis=-1, keepdims=True))
    dc = jnp.where(live_rows(ROWS), g_in[...].astype(F32) + inner, 0.0)
    sg[layer, 9:10, :] = column_sum(dc)
    v = u_in[...].astype(F32)
    masks = column_masks(ROWS)
    du = dc
    for b in range(3):
        dcm = dc * masks[b]
        for a in range(3):
            moved = rolled(dcm, SIDE * (a - 1) + b - 1)
            tap = 3 * a + b
            du = du + row(tap) * moved
            sg[layer, tap:tap + 1, :] = column_sum(moved * v)
    g_out[...] = jnp.where(live_rows(ROWS), du, 0.0).astype(BF16)


ROOT_HALF = 0.5 ** 0.5
ROOT_TWO_PI = 0.3989422804014327


def ff_forward(layer, u_in, u_out, w, small, xhat, rstd, n_ref, slope, acc):
    base = 12 * layer
    row = lambda r: small[layer, r:r + 1, :]
    x, r = norm_parts(u_in[...].astype(F32))
    xhat[...] = x
    rstd[...] = r
    n_ref[...] = (x * row(16) + row(17)).astype(BF16)
    acc[...] = u_in[...].astype(F32) + row(22)

    @pl.loop(0, 4)
    def _(j):
        cols = pl.ds(pl.multiple_of(W * j, W), W)
        h = mm(n_ref[...], w[base + 4 + j]) + small[layer, pl.ds(18 + j, 1), :]
        cdf = 0.5 + 0.5 * lax.erf(h * ROOT_HALF)
        slope[:, cols] = cdf + h * (ROOT_TWO_PI * jnp.exp(-0.5 * h * h))
        acc[...] += mm((h * cdf).astype(BF16), w[base + 8 + j])

    u_out[...] = jnp.where(live_rows(ROWS), acc[...], 0.0).astype(BF16)


def ff_backward(layer, g_in, g_out, w, small, sg, xhat, rstd, slope, acc):
    base = 12 * layer
    row = lambda r: small[layer, r:r + 1, :]
    sg[layer, 22:23, :] = column_sum(g_in[...].astype(F32))
    acc[...] = jnp.zeros_like(acc)

    @pl.loop(0, 4)
    def _(j):
        cols = pl.ds(pl.multiple_of(W * j, W), W)
        dh = (mm_nt(g_in[...], w[base + 8 + j]) * slope[:, cols]).astype(BF16)
        sg[layer, pl.ds(18 + j, 1), :] = column_sum(dh.astype(F32))
        acc[...] += mm_nt(dh, w[base + 4 + j])

    dn = acc[...]
    x = xhat[...]
    sg[layer, 16:17, :] = column_sum(dn * x)
    sg[layer, 17:18, :] = column_sum(dn)
    e = dn * row(16)
    inner = rstd[...] * (e - jnp.mean(e, axis=-1, keepdims=True) - x * jnp.mean(e * x, axis=-1, keepdims=True))
    g_out[...] = jnp.where(live_rows(ROWS), g_in[...].astype(F32) + inner, 0.0).astype(BF16)


def chain_scratch():
    V = pltpu.VMEM
    mixer = [V((ROWS, W), F32), V((ROWS, 1), F32), V((ROWS, W), BF16), V((ROWS, 3 * W), BF16)]
    feed = [V((ROWS, W), F32), V((ROWS, 1), F32), V((ROWS, W), BF16), V((ROWS, 4 * W), F32)]
    return (mixer + [V((6, 8, PAIR, PAIR), F32), V((ROWS, W), BF16)] + feed + mixer + [V((6, 4, LANES, LANES), F32), V((ROWS, W), BF16)] + feed
            + [V((ROWS, W), F32), V((ROWS, W), F32), V((ROWS, W), BF16), V((ROWS, 3 * W), BF16), V((PAIR, PAIR), F32), V((LANES, LANES), F32)])


def fill_biases(win_bias, chan_bias):
    qi = lax.broadcasted_iota(jnp.int32, (PAIR, PAIR), 0)
    ki = lax.broadcasted_iota(jnp.int32, (PAIR, PAIR), 1)
    win_bias[...] = jnp.where(((qi // IMG) == (ki // IMG)) & (lax.rem(ki, IMG) < LIVE), 0.0, -1e30).astype(F32)
    ci = lax.broadcasted_iota(jnp.int32, (LANES, LANES), 0)
    ei = lax.broadcasted_iota(jnp.int32, (LANES, LANES), 1)
    chan_bias[...] = jnp.where((ci // HD) == (ei // HD), 0.0, -1e30).astype(F32)


class Chain:
    def __init__(self, w, small, mask, u, g, sg, dw, scratch):
        self.w, self.small, self.mask, self.u, self.g, self.sg, self.dw = w, small, mask, u, g, sg, dw
        s = scratch
        self.window, self.feed0, self.channel, self.feed1 = s[0:6], s[6:10], s[10:16], s[16:20]
        self.c_ref, self.acc, self.dm, self.dt, self.win_bias, self.chan_bias = s[20:26]

    def front(self, k):
        u, w, small = self.u, self.w, self.small
        if k == 0:
            fill_biases(self.win_bias, self.chan_bias)
            mixer_front(0, u[0], w, small, self.c_ref, *self.window)
        if k == 1:
            ff_forward(0, u[1], u[2], w, small, *self.feed0, self.acc)
        if k == 2:
            mixer_front(1, u[2], w, small, self.c_ref, *self.channel)
        if k == 3:
            ff_forward(1, u[3], u[4], w, small, *self.feed1, self.acc)

    def rest(self, k):
        u, w, small = self.u, self.w, self.small
        if k == 0:
            mixer_mixture(0, False, u[1], w, small, self.mask, self.win_bias, self.c_ref, *self.window)
        if k == 2:
            mixer_mixture(1, True, u[3], w, small, self.mask, self.chan_bias, self.c_ref, *self.channel)

    def backward(self, k):
        u, g, w, small, sg = self.u, self.g, self.w, self.small, self.sg
        if k in (0, 2):
            parts = self.channel if k == 2 else self.window
            mix_backward(k // 2, k == 2, u[k], g[k + 1], g[k], w, small, self.mask, sg, self.dw, self.c_ref, *parts, self.dm, self.dt, self.acc)
        else:
            x, r, _, slope = self.feed0 if k == 1 else self.feed1
            ff_backward(k // 2, g[k + 1], g[k], w, small, sg, x, r, slope, self.acc)


MESH = pl.DeviceIdType.MESH
VMEM_LIMIT = 63 * 1024 * 1024
STRIP = 96
HALF = 384


def slot(item, line, d):
    red = lax.rem(item, 3) // 2
    block = 12 * (item // 3) + 4 * lax.rem(item, 3) + (1 - red) * line + red * (d // 2)
    row = (1 - red) * STRIP * d + red * (4 * STRIP * lax.rem(d, 2) + STRIP * line)
    return block, row


def other_planes(z):
    near = z + 1 - 2 * (z // 2)
    far = 3 * (1 - z // 2)
    return near, 6 - z - near - far, far


class Place:
    def __init__(self):
        self.s = lax.axis_index("segment")
        self.d = lax.axis_index("dp")
        self.z = self.d // 2
        self.c = lax.rem(self.d, 2)
        self.xn = self.s + 1 - 2 * lax.rem(self.s, 2)
        self.yn = lax.rem(self.s + 2, 4)
        self.dn = 3 - self.s
        self.twin = self.d + 1 - 2 * self.c


def remote(src, dst, ssem, rsem, seg, dev):
    return pltpu.make_async_remote_copy(src, dst, ssem, rsem, device_id=(seg, dev), device_id_type=MESH)


def gather_scratch():
    D = pltpu.SemaphoreType.DMA
    return [D((2, 9)), D((6, 5)), D((6, 3, 2)), D((6, 3, 2)), D((6, 4, 4)), D((2, 3, 4)), D((2, 3, 4))]


class Gather:
    def __init__(self, at, shards, wbuf, sems):
        self.at, self.shards, self.w = at, shards, wbuf
        self.lsem, self.zs, self.xs, self.ys, self.pr, self.cs, self.cr = sems
        self.planes = other_planes(at.z)
        self.away = 2 * (at.z // 2) - 1
        self.inner = (at.z == 1) | (at.z == 2)
        self.groups = [(layer, part, k) for layer in range(2) for part in range(3) for k in range(3)]

    def strip(self, item, line, plane):
        block, row = slot(item, line, 2 * plane + self.at.c)
        return self.w.at[block, pl.ds(pl.multiple_of(row, STRIP), STRIP), :]

    def quad_ref(self, layer, part, plane, core):
        if part == 2:
            return self.w.at[12 * layer + 8 + plane, pl.ds(pl.multiple_of(4 * STRIP * core, 4 * STRIP), 4 * STRIP), :]
        row = pl.multiple_of(STRIP * (2 * plane + core), STRIP)
        return self.w.at[pl.ds(12 * layer + 4 * part, 4), pl.ds(row, STRIP), :]

    def quad(self, layer, part, plane, core, k):
        ref = self.quad_ref(layer, part, plane, core)
        return remote(ref, ref, self.cs.at[layer, part, k], self.cr.at[layer, part, plane], self.at.s, self.at.twin)

    def local(self, layer):
        triple, output, expand, reduce = self.shards
        at, w, base = self.at, self.w, 12 * layer
        rows = pl.ds(pl.multiple_of(STRIP * at.d, STRIP), STRIP)
        sems = self.lsem.at
        copies = [pltpu.make_async_copy(triple.at[layer, :, pl.ds(W * j, W)], w.at[base + j, rows, :], sems[layer, j]) for j in range(3)]
        copies.append(pltpu.make_async_copy(output.at[layer], w.at[base + 3, rows, :], sems[layer, 3]))
        copies += [pltpu.make_async_copy(expand.at[layer, :, pl.ds(W * j, W)], w.at[base + 4 + j, rows, :], sems[layer, 4 + j]) for j in range(4)]
        half = pl.ds(pl.multiple_of(4 * STRIP * at.c, 4 * STRIP), 4 * STRIP)
        copies.append(pltpu.make_async_copy(reduce.at[layer], w.at[base + 8 + at.z, half, :], sems[layer, 8]))
        return copies

    def up(self, item):
        ref = self.strip(item, self.at.s, self.at.z)
        return remote(ref, ref, self.zs.at[item, 0], self.pr.at[item, self.at.z, self.at.s], self.at.s, self.at.d + 2)

    def down(self, item):
        ref = self.strip(item, self.at.s, self.at.z)
        return remote(ref, ref, self.zs.at[item, 1], self.pr.at[item, self.at.z, self.at.s], self.at.s, self.at.d - 2)

    def onward(self, item, k):
        step = self.away if k != 1 else -self.away
        ref = self.strip(item, self.at.s, self.planes[k])
        return remote(ref, ref, self.zs.at[item, 2 + k], self.pr.at[item, self.planes[k], self.at.s], self.at.s, self.at.d + 2 * step)

    def to_x(self, item, k, line, j):
        ref = self.strip(item, line, self.planes[k])
        return remote(ref, ref, self.xs.at[item, k, j], self.pr.at[item, self.planes[k], line], self.at.xn, self.at.d)

    def to_y(self, item, k, line, j):
        ref = self.strip(item, line, self.planes[k])
        return remote(ref, ref, self.ys.at[item, k, j], self.pr.at[item, self.planes[k], line], self.at.yn, self.at.d)

    def arrival(self, item, k, line):
        ref = self.strip(item, line, self.planes[k])
        return remote(ref, ref, self.zs.at[item, 0], self.pr.at[item, self.planes[k], line], self.at.s, self.at.twin)

    def ends(self, item, act):
        @pl.when(self.at.z < 3)
        def _():
            act(self.up(item))

        @pl.when(self.at.z > 0)
        def _():
            act(self.down(item))

    def begin(self):
        at = self.at
        copies = [self.local(layer) for layer in range(2)]
        for layer in range(2):
            for copy in copies[layer]:
                copy.start()
        for copy in copies[0]:
            copy.wait()
        self.ends(0, lambda copy: copy.start())
        for part in range(3):
            self.quad(0, part, at.z, at.c, 3).start()
        for copy in copies[1]:
            copy.wait()
        for part in range(3):
            self.quad(1, part, at.z, at.c, 3).start()

    def stage_a(self, layer, part, k):
        item = 3 * layer + part
        self.arrival(item, k, self.at.s).wait_recv()

        @pl.when(self.inner)
        def _():
            self.onward(item, k).start()

        self.to_x(item, k, self.at.s, 0).start()
        self.to_y(item, k, self.at.s, 0).start()

    def stage_b(self, layer, part, k):
        item = 3 * layer + part
        self.arrival(item, k, self.at.xn).wait_recv()
        if (part + k + layer) % 2 == 0:
            self.to_y(item, k, self.at.xn, 1).start()
        self.arrival(item, k, self.at.yn).wait_recv()
        if (part + k + layer) % 2 == 1:
            self.to_x(item, k, self.at.yn, 1).start()

    def stage_c(self, layer, part, k):
        item = 3 * layer + part
        self.arrival(item, k, self.at.dn).wait_recv()
        self.quad(layer, part, self.planes[k], self.at.c, k).start()

    def step(self, g):
        n = len(self.groups)
        if g < n and g % 3 == 0 and g // 3 + 1 < 6:
            self.ends(g // 3 + 1, lambda copy: copy.start())
        if g < n:
            self.stage_a(*self.groups[g])
        if 0 <= g - 1 < n:
            self.stage_b(*self.groups[g - 1])
        if 0 <= g - 2 < n:
            self.stage_c(*self.groups[g - 2])

    def settle(self, layer, part):
        for k in range(3):
            self.quad(layer, part, self.planes[k], 1 - self.at.c, k).wait_recv()
        self.quad(layer, part, self.at.z, 1 - self.at.c, 3).wait_recv()

    def drain(self):
        at = self.at
        for layer in range(2):
            for part in range(3):
                item = 3 * layer + part
                self.ends(item, lambda copy: copy.wait_send())
                self.quad(layer, part, at.z, at.c, 3).wait_send()
                for k in range(3):
                    @pl.when(self.inner)
                    def _():
                        self.onward(item, k).wait_send()

                    self.to_x(item, k, at.s, 0).wait_send()
                    self.to_y(item, k, at.s, 0).wait_send()
                    if (part + k + layer) % 2 == 0:
                        self.to_y(item, k, at.xn, 1).wait_send()
                    else:
                        self.to_x(item, k, at.yn, 1).wait_send()
                    self.quad(layer, part, self.planes[k], at.c, k).wait_send()


def greet_all(at):
    bar = pltpu.get_barrier_semaphore()

    def greet(seg, dev):
        pl.semaphore_signal(bar, inc=1, device_id=(seg, dev), device_id_type=MESH)

    for seg in (at.xn, at.yn, at.dn):
        greet(seg, at.d)
        greet(seg, at.twin)
    greet(at.s, at.twin)
    for j in range(1, 4):
        greet(at.s, lax.rem(at.d + 2 * j, 8))
    pl.semaphore_wait(bar, 10)


def add_into(total, term):
    total[...] = (total[...].astype(F32) + term[...].astype(F32)).astype(BF16)


def sum_into(total, terms):
    result = total[...].astype(F32)
    for j in range(3):
        result = result + terms[j].astype(F32)
    total[...] = result.astype(BF16)


class Spread:
    def __init__(self, at, w, mix, exp, red, fsend, frecv):
        self.at, self.w, self.mix, self.exp, self.red, self.fsend, self.frecv = at, w, mix, exp, red, fsend, frecv
        self.layer, self.half = at.s // 2, lax.rem(at.s, 2)
        self.holds = at.c == at.z // 2

    def strip(self, block, row, rows=STRIP):
        return self.w.at[block, pl.ds(pl.multiple_of(row, STRIP), rows), :]

    def mix_place(self, layer, j):
        return self.mix.at[layer, :, pl.ds(pl.multiple_of(W * j, W), W)]

    def exp_place(self, layer, half, core, m):
        return self.exp.at[layer, :, pl.ds(pl.multiple_of(W * (2 * core + m) + HALF * half, LANES), HALF)]

    def exp_land(self, layer, half, core, m):
        return self.frecv.at[8 + 8 * layer + 4 * half + 2 * core + m]

    def mix_copies(self, layer):
        at = self.at
        ref = self.strip(12 * layer + at.s, 2 * STRIP * at.z + STRIP * at.c)
        target, land = self.mix_place(layer, at.s), self.frecv.at[4 * layer + at.s]
        sends = [remote(ref, target, self.fsend.at[2 * layer + k], land, seg, at.d) for k, seg in enumerate((at.xn, at.yn))]
        return sends, pltpu.make_async_copy(ref, target, land)

    def core_copies(self, ref, target, land, core, first):
        at = self.at
        dev = 2 * at.z + core
        sends = [remote(ref, target, self.fsend.at[first + k], land, seg, dev) for k, seg in enumerate((at.xn, at.yn))]
        return core == at.c, sends, pltpu.make_async_copy(ref, target, land), remote(ref, target, self.fsend.at[first + 2], land, at.s, at.twin)

    def exp_copies(self, p, m):
        at = self.at
        rows = pl.ds(pl.multiple_of(2 * STRIP * at.z + STRIP * p, STRIP), STRIP)
        ref = self.w.at[12 * self.layer + 4 + 2 * at.c, rows, pl.ds(HALF * m, HALF)]
        own = (self.layer, self.half, at.c, m)
        return self.core_copies(ref, self.exp_place(*own), self.exp_land(*own), p, 4 + 6 * p + 3 * m)

    def red_copies(self, m):
        ref = self.strip(12 * self.layer + 8 + 2 * (self.at.z // 2), HALF * lax.rem(self.at.z, 2) + HALF // 2 * m, HALF // 2)
        target = self.red.at[self.layer, pl.ds(HALF // 2 * m, HALF // 2), :]
        return self.core_copies(ref, target, self.frecv.at[24 + 2 * self.layer + m], self.half, 16 + 3 * m)

    def start_mix(self, layer):
        sends, keep = self.mix_copies(layer)
        for copy in sends:
            copy.start()
        keep.start()

    def start_cores(self, here, sends, keep, cross):
        for copy in sends:
            copy.start()

        @pl.when(here)
        def _():
            keep.start()

        @pl.when(jnp.logical_not(here))
        def _():
            cross.start()

    def start_exp(self):
        for p in range(2):
            for m in range(2):
                self.start_cores(*self.exp_copies(p, m))

    def start_red(self):
        @pl.when(self.holds)
        def _():
            for m in range(2):
                self.start_cores(*self.red_copies(m))

    def passing(self, ref, land, to, n):
        return remote(ref, ref, self.fsend.at[22 + n], land, to, self.at.d)

    def sources(self):
        at = self.at
        return ((at.xn, at.yn, 0), (at.yn, at.xn, 1), (at.dn, at.xn, 2), (at.s, at.xn, 2))

    def mix_passing(self, layer, owner, to):
        return self.passing(self.mix_place(layer, owner), self.frecv.at[4 * layer + owner], to, layer)

    def exp_passing(self, core, m, owner, to):
        own = (owner // 2, lax.rem(owner, 2), core, m)
        return self.passing(self.exp_place(*own), self.exp_land(*own), to, 2 + 2 * core + m)

    def red_passing(self, m, owner, to):
        layer = owner // 2
        return self.passing(self.red.at[layer, pl.ds(HALF // 2 * m, HALF // 2), :], self.frecv.at[24 + 2 * layer + m], to, 6 + m)

    def finish_mix(self, layer):
        for owner, to, part in self.sources():
            copy = self.mix_passing(layer, owner, to)
            copy.wait_recv()
            if part == layer:
                copy.start()

    def finish_exp(self):
        for owner, to, part in self.sources():
            for core in range(2):
                for m in range(2):
                    copy = self.exp_passing(core, m, owner, to)
                    copy.wait_recv()
                    if part == core:
                        copy.start()

    def finish_red(self):
        for owner, to, part in self.sources():
            @pl.when(lax.rem(owner, 2) == self.at.c)
            def _():
                for m in range(2):
                    copy = self.red_passing(m, owner, to)
                    copy.wait_recv()
                    if part == m:
                        copy.start()

    def drain_cores(self, here, sends, keep, cross):
        for copy in sends:
            copy.wait_send()

        @pl.when(jnp.logical_not(here))
        def _():
            cross.wait_send()

    def drain(self):
        for layer in range(2):
            for copy in self.mix_copies(layer)[0]:
                copy.wait_send()
        for p in range(2):
            for m in range(2):
                self.drain_cores(*self.exp_copies(p, m))

        @pl.when(self.holds)
        def _():
            for m in range(2):
                self.drain_cores(*self.red_copies(m))

        for owner, to, part in self.sources()[:2]:
            self.mix_passing(part, owner, to).wait_send()
            for m in range(2):
                self.exp_passing(part, m, owner, to).wait_send()

            @pl.when(lax.rem(owner, 2) == self.at.c)
            def _():
                self.red_passing(part, owner, to).wait_send()


def train_kernel(triple, output, expand, reduce, pack, choose, x, mask, gin, cot,
                 sec_out, grad_out, d_mix, d_exp, d_red, sg_out, xin, gland, xtw, gtw, mrx, prx, land_m, land_e, land_r,
                 w, small, packs, pks, pkr, u_buf, g_buf, sg, sga, sgr, stage, stage_f, lsem, tsem, xsend, xrecv, gsend, grecv, tws, twr, osend, orecv, msend, mrecv, psend, precv,
                 zms, zmr, zes, zer, zrs, zrr, fsend, frecv, sgs, sgv, *scratch):
    at = Place()
    s, d, z, c = at.s, at.d, at.z, at.c
    lay = s // 2
    segs = (at.xn, at.yn, at.dn)
    gather = Gather(at, (triple, output, expand, reduce), w, scratch[:7])
    u = [x] + [u_buf.at[i] for i in range(4)]
    g = [g_buf.at[i] for i in range(4)] + [gin]

    def dw(layer, j, lhs, rhs):
        w[12 * layer + j] = mm_tn(lhs[...], rhs()).astype(BF16)

    chain = Chain(w, small, mask, u, g, sg, dw, scratch[7:])
    sg[...] = jnp.zeros_like(sg)

    def pack_line(j):
        return remote(pack, packs.at[c, z], pks.at[j], pkr.at[3 - j], s, lax.rem(d + 2 * j, 8))

    def pack_twin(core):
        return remote(packs.at[core], packs.at[core], pks.at[0], pkr.at[3], s, at.twin)

    def pack_begin():
        packs[c, z] = pack[...]
        for j in range(1, 4):
            pack_line(j).start()

    def pack_pass():
        for j in range(1, 4):
            pack_line(j).wait_recv()
        pack_twin(c).start()

    def pack_end():
        pack_twin(1 - c).wait_recv()
        held = packs[...].reshape(8 * 48, LANES)
        total = jnp.zeros((48, W), F32)
        for p in range(8):
            piece = jnp.concatenate([mm(choose[p], held), jnp.zeros((48, W - LANES), F32)], axis=1)
            total = total + (pltpu.roll(piece, STRIP * p, 1) if p else piece)
        small[...] = total.reshape(2, 24, W)
        pack_twin(c).wait_send()
        for j in range(1, 4):
            pack_line(j).wait_send()

    def x_send(i):
        return remote(u_buf.at[2 * (segs[i] // 2)], xin.at[s], xsend.at[i], xrecv.at[i], segs[i], d)

    def g_send(i):
        return remote(g_buf.at[2], gland.at[s], gsend.at[i], grecv.at[i], segs[i], d)

    def u_out(i):
        return remote(u_buf.at[segs[i]], sec_out.at[s], osend.at[0, i], orecv.at[0, i], segs[i], d)

    def g_out(i):
        return remote(g_buf.at[segs[i]], grad_out.at[s], osend.at[1, i], orecv.at[1, i], segs[i], d)

    keep_x = pltpu.make_async_copy(u_buf.at[2 * lay], xin.at[s], lsem.at[0])
    keep_u = pltpu.make_async_copy(u_buf.at[s], sec_out.at[s], lsem.at[1])
    keep_g = pltpu.make_async_copy(g_buf.at[s], grad_out.at[s], lsem.at[2])
    keep_gl = pltpu.make_async_copy(g_buf.at[2], gland.at[s], lsem.at[3])

    def to_where(cond, copy, i, wait=False):
        @pl.when(cond(segs[i]))
        def _():
            copy(i).wait_send() if wait else copy(i).start()

    def x_twin(t):
        return remote(xin.at[t], xtw.at[t], tws.at[0, t], twr.at[0, t], s, at.twin)

    def g_twin(t):
        return remote(gland.at[t], gtw.at[t], tws.at[1, t], twr.at[1, t], s, at.twin)

    def cot_twin(t):
        return remote(cot.at[t], gtw.at[t], tws.at[1, t], twr.at[1, t], s, at.twin)

    def strip(block, p, core):
        return w.at[block, pl.ds(pl.multiple_of(2 * STRIP * p + STRIP * core, STRIP), STRIP), :]

    def twin_mix(layer, p):
        rows = pl.ds(pl.multiple_of(2 * STRIP * p + STRIP * (1 - c), STRIP), STRIP)
        return remote(w.at[pl.ds(12 * layer, 4), rows, :], mrx.at[layer, p], msend.at[layer, p], mrecv.at[layer, p], s, at.twin)

    def plane_send(layer, i, p):
        return remote(strip(12 * layer + segs[i], p, c), prx.at[layer, i, p], psend.at[layer, i, p], precv.at[layer, i, p], segs[i], d)

    def to_stage(src, n):
        load = pltpu.make_async_copy(src, stage.at[n], tsem.at[n])
        load.start()
        return load

    def cores_sum(layer):
        loads = []
        for p in range(4):
            twin_mix(layer, p).wait_recv()
            if p >= 2:
                take(layer, p - 2, loads[p - 2])
            loads.append(to_stage(mrx.at[layer, p], p % 2))
        for p in (2, 3):
            take(layer, p, loads[p])

    def take(layer, p, load):
        load.wait()
        for b in range(4):
            add_into(strip(12 * layer + b, p, c), stage.at[p % 2, b])

    def plane_begin(layer):
        for p in range(4):
            for i in range(3):
                plane_send(layer, i, p).start()

    def plane_sum(layer):
        for i in range(3):
            for p in range(4):
                plane_send(layer, i, p).wait_recv()
            to_stage(prx.at[layer, i], 0).wait()
            for p in range(4):
                add_into(strip(12 * layer + s, p, c), stage.at[0, p])

    def mix_line(layer, j):
        goal = lax.rem(z + j, 4)
        return remote(strip(12 * layer + s, goal, c), land_m.at[layer, 3 - j], zms.at[layer, j - 1], zmr.at[layer, 3 - j], s, lax.rem(d + 2 * j, 8))

    def exp_line(j):
        goal = lax.rem(z + j, 4)
        rows = pl.ds(pl.multiple_of(2 * STRIP * goal, 2 * STRIP), 2 * STRIP)
        return remote(w.at[eq, rows, :], land_e.at[3 - j], zes.at[j - 1], zer.at[3 - j], s, lax.rem(d + 2 * j, 8))

    def red_line(n):
        goal = 2 * c + n
        mine = lax.rem(z - goal + 7, 4)
        return remote(w.at[rq, pl.ds(4 * STRIP * n, 4 * STRIP), :], land_r.at[mine], zrs.at[n], zrr.at[mine], s, 2 * goal + c)

    def red_arrival(j):
        return remote(w.at[rq, pl.ds(0, 4 * STRIP), :], land_r.at[j], zrs.at[0], zrr.at[j], s, at.twin)

    def red_lines(act):
        for n in range(2):
            @pl.when(z != 2 * c + n)
            def _():
                act(red_line(n))

    def mix_line_sum(layer):
        for j in range(3):
            mix_line(layer, 3 - j).wait_recv()
        load = pltpu.make_async_copy(land_m.at[layer], stage.at[0, pl.ds(0, 3)], tsem.at[0])
        load.start()
        load.wait()
        sum_into(strip(12 * layer + s, z, c), stage.at[0])

    def feed_line_sum(landed, out):
        load = pltpu.make_async_copy(landed, stage_f, tsem.at[1])
        load.start()
        load.wait()
        sum_into(out, stage_f)

    def exp_line_sum():
        for j in range(3):
            exp_line(3 - j).wait_recv()
        feed_line_sum(land_e, w.at[eq, pl.ds(pl.multiple_of(2 * STRIP * z, 2 * STRIP), 2 * STRIP), :])

    def red_line_sum():
        @pl.when(z // 2 == c)
        def _():
            for j in range(3):
                red_arrival(j).wait_recv()
            for m in range(2):
                row = 4 * STRIP * lax.rem(z, 2) + 2 * STRIP * m
                feed_line_sum(land_r.at[:, pl.ds(2 * STRIP * m, 2 * STRIP), :], w.at[rq, pl.ds(pl.multiple_of(row, 2 * STRIP), 2 * STRIP), :])

    half = lax.rem(s, 2)
    own, other, far = 12 * lay, 12 * (1 - lay), 2 * (1 - c)
    eq, rq = own + 4 + 2 * c, own + 8 + 2 * c
    half_at = pl.ds(pl.multiple_of(4 * STRIP * half, LANES), 4 * STRIP)

    def block_x(k):
        return other + 4 + k

    def block_g(k):
        return other + 7 + k

    def block_a(k):
        return (1 - k // 2) * (other + 10 + k) + (k // 2) * (own + 4 + far)

    def block_h(k):
        later = (k + 1) // 2
        return (1 - later) * (own + 5 + far) + later * (own + 7 + far + k)

    def rows_of(i):
        return pl.ds(pl.multiple_of(ROWS * lax.rem(i, 3), ROWS), ROWS)

    def token_loads():
        loads = []
        for t in range(4):
            for n, (xs, gs) in enumerate(((xin, gland), (xtw, gtw))):
                i = 2 * t + n
                loads.append(pltpu.make_async_copy(xs.at[t], w.at[block_x(i // 3), rows_of(i), :], lsem.at[4 + i]))
                dst = w.at[block_g(i // 3), rows_of(i), :]
                load = pltpu.make_async_copy(gs.at[t], dst, lsem.at[12 + i])
                seed = pltpu.make_async_copy((cot if n == 0 else gs).at[t], dst, lsem.at[12 + i])
                loads.append((load, seed))
        return loads

    def feed_rows(i):
        k, rows = i // 3, rows_of(i)
        xh, _ = norm_parts(w[block_x(k), rows, :].astype(F32))
        n = (xh * small[lay, 16:17, :] + small[lay, 17:18, :]).astype(BF16)
        w[block_x(k), rows, :] = n
        for m in range(2):
            cols = slice(4 * STRIP * m, 4 * STRIP * (m + 1))
            h = mm(n, w[eq + m, :, half_at]) + small[lay, pl.ds(18 + 2 * c + m, 1), half_at]
            cdf = 0.5 + 0.5 * lax.erf(h * ROOT_HALF)
            w[block_a(k), rows, cols] = (h * cdf).astype(BF16)
            slope = cdf + h * (ROOT_TWO_PI * jnp.exp(-0.5 * h * h))
            w[block_h(k), rows, cols] = (mm_nt(w[block_g(k), rows, :], w[rq + m, half_at, :]) * slope).astype(BF16)

    def product(out, left, right):
        @pl.loop(0, 3)
        def _(i):
            cols = pl.ds(pl.multiple_of(256 * i, 256), 256)
            total = jnp.zeros((256, W), F32)
            for k, rows in enumerate((3 * ROWS, 3 * ROWS, 2 * ROWS)):
                total = total + mm_tn(w[left(k), :rows, cols], w[right(k), :rows, :])
            w[out, cols, :] = total.astype(BF16)

    partners = [(s, at.twin), (at.xn, d), (at.yn, d), (s, d + 2 * (1 - 2 * lax.rem(z, 2))), (s, lax.rem(d + 4, 8))]

    def sg_round(r):
        return remote(sga.at[r], sgr.at[r], sgs.at[r], sgv.at[r], *partners[r])

    def sg_next(r):
        sg_round(r).wait_recv()
        sga[r + 1] = sga[r] + sgr[r]
        if r < 4:
            sg_round(r + 1).start()

    spread = Spread(at, w, d_mix, d_exp, d_red, fsend, frecv)
    low, high = (lambda t: t < 2), (lambda t: t >= 2)
    odd = lambda t: lax.rem(t, 2) == 1

    greet_all(at)
    pack_begin()

    @pl.when(s >= 2)
    def _():
        for t in range(4):
            cot_twin(t).start()

    gather.begin()
    for step in range(20):
        gather.step(step)
        if step == 1:
            pack_pass()
        if step == 3:
            pack_end()
        if step == 5:
            gather.settle(0, 0)
            chain.front(0)
        if step == 6:
            chain.rest(0)
        if step == 11:
            gather.settle(0, 1)
            gather.settle(0, 2)
            chain.front(1)
        if step == 14:
            gather.settle(1, 0)
            chain.front(2)
        if step == 15:
            chain.rest(2)
    for i in range(3):
        x_send(i).start()
    keep_x.start()
    gather.settle(1, 1)
    gather.settle(1, 2)
    chain.front(3)
    gather.drain()
    chain.backward(3)
    chain.backward(2)
    for i in range(3):
        to_where(low, g_send, i)
    keep_gl.start()
    for p in range(4):
        twin_mix(1, p).start()
    keep_x.wait()
    x_twin(s).start()
    for i in range(3):
        x_send(i).wait_recv()
        x_twin(segs[i]).start()
    chain.backward(1)
    cores_sum(1)
    keep_gl.wait()

    @pl.when(s < 2)
    def _():
        g_twin(s).start()

    for i in range(3):
        to_where(low, g_send, i, wait=True)

    @pl.when(s < 2)
    def _():
        for i in range(3):
            g_send(i).wait_recv()
            g_twin(segs[i]).start()

    plane_begin(1)
    loads = token_loads()
    for t in range(4):
        x_twin(t).wait_recv()
        cot_twin(t).wait_recv()
    for load in loads:
        if isinstance(load, tuple):
            @pl.when(s < 2)
            def _():
                load[0].start()

            @pl.when(s >= 2)
            def _():
                load[1].start()
        else:
            load.start()
    for load in loads:
        (load[0] if isinstance(load, tuple) else load).wait()
    pl.loop(0, 8)(feed_rows)
    product(eq, block_x, block_h)
    for j in (2, 1, 3):
        exp_line(j).start()
    product(rq, block_a, block_g)
    red_lines(lambda copy: copy.start())
    for i in range(3):
        to_where(odd, u_out, i)
    keep_u.start()
    for i in range(3):
        to_where(lambda t: t >= 1, g_out, i)
    chain.backward(0)
    for p in range(4):
        twin_mix(0, p).start()
    sga[0] = sg[...]
    sg_round(0).start()
    cores_sum(0)
    plane_begin(0)
    for i in range(3):
        to_where(lambda t: t == 0, g_out, i)
    keep_g.start()
    sg_next(0)
    plane_sum(1)
    for j in (2, 1, 3):
        mix_line(1, j).start()
    exp_line_sum()
    spread.start_exp()
    red_line_sum()
    spread.start_red()
    mix_line_sum(1)
    spread.start_mix(1)
    plane_sum(0)
    for j in (2, 1, 3):
        mix_line(0, j).start()
    sg_next(1)
    spread.finish_exp()
    sg_next(2)
    spread.finish_red()
    sg_next(3)
    spread.finish_mix(1)
    sg_next(4)
    mix_line_sum(0)
    spread.start_mix(0)
    spread.finish_mix(0)

    for r in range(5):
        sg_round(r).wait_send()
    for layer in range(2):
        sg_out[layer] = pltpu.roll(sga[5, layer], lax.rem(W - STRIP * d, W), 1)[:, :LANES]
        for first, count in ((12, 3), (18, 4)):
            for j in range(count):
                index = count * d + j
                sga[0, layer] = pltpu.roll(sga[5, layer], lax.rem(W - STRIP * lax.rem(index, 8), W), 1)
                sg_out[layer, first + j:first + j + 1, :] = sga[0, layer, pl.ds(first + index // 8, 1), :][:, :LANES]
    spread.drain()
    for i in range(3):
        x_send(i).wait_send()
        to_where(odd, u_out, i, wait=True)
        g_out(i).wait()
        for layer in range(2):
            for p in range(4):
                plane_send(layer, i, p).wait_send()

    @pl.when(lax.rem(s, 2) == 1)
    def _():
        for i in range(3):
            u_out(i).wait_recv()

    for t in range(4):
        x_twin(t).wait_send()
        cot_twin(t).wait_send()
    keep_u.wait()
    keep_g.wait()
    for p in range(4):
        for layer in range(2):
            twin_mix(layer, p).wait_send()
    for j in range(1, 4):
        for layer in range(2):
            mix_line(layer, j).wait_send()
        exp_line(j).wait_send()
    red_lines(lambda copy: copy.wait_send())


def train_call(triple, output, expand, reduce, pack, choose, x, mask, gin, cot):
    V = pltpu.VMEM
    D = pltpu.SemaphoreType.DMA
    S = jax.ShapeDtypeStruct
    anywhere = pl.BlockSpec(memory_space=pl.ANY)
    vmem = pl.BlockSpec(memory_space=V)
    tokens = S((4, ROWS, W), BF16)
    out = pl.pallas_call(
        train_kernel,
        out_shape=(
            tokens, tokens, S((2, STRIP, 4 * W), BF16), S((2, STRIP, 4 * W), BF16), S((2, HALF, W), BF16), S((2, 24, LANES), F32), tokens, tokens, tokens, tokens,
            S((2, 4, 4, STRIP, W), BF16), S((2, 3, 4, STRIP, W), BF16), S((2, 3, STRIP, W), BF16), S((3, 2 * STRIP, W), BF16), S((3, 4 * STRIP, W), BF16),
        ),
        in_specs=[anywhere] * 4 + [vmem] * 5 + [anywhere],
        out_specs=[anywhere] * 5 + [vmem] + [anywhere] * 9,
        scratch_shapes=[
            V((24, W, W), BF16), V((2, 24, W), F32), V((2, 4, 48, LANES), BF16), D((4,)), D((4,)), V((4, ROWS, W), BF16), V((4, ROWS, W), BF16), V((2, 24, W), F32), V((6, 2, 24, W), F32), V((5, 2, 24, W), F32),
            V((2, 4, STRIP, W), BF16), V((3, 2 * STRIP, W), BF16),
            D((20,)), D((2,)), D((3,)), D((3,)), D((3,)), D((3,)), D((2, 4)), D((2, 4)), D((2, 3)), D((2, 3)), D((2, 4)), D((2, 4)), D((2, 3, 4)), D((2, 3, 4)),
            D((2, 3)), D((2, 3)), D((3,)), D((3,)), D((2,)), D((3,)), D((30,)), D((28,)), D((5,)), D((5,)),
        ] + gather_scratch() + chain_scratch(),
        compiler_params=pltpu.CompilerParams(collective_id=1, has_side_effects=True, vmem_limit_bytes=VMEM_LIMIT),
        name="train_sections",
    )(triple, output, expand, reduce, pack, choose, x, mask, gin, cot)
    return out[:7]


def pack_small(conv_weight, conv_bias, mixer_gain, mixer_shift, triple_bias, output_bias, feed_gain, feed_shift, expand_bias, reduce_bias):
    part = conv_bias.shape[1]
    rows = [conv_weight] + [
        v.reshape(2, -1, part)
        for v in (conv_bias, mixer_gain, mixer_shift, triple_bias, output_bias, feed_gain, feed_shift, expand_bias, reduce_bias)
    ]
    total, first = 0, 0
    for v in rows:
        last = first + v.shape[1]
        total = total + jnp.pad(v, ((0, 0), (first, 24 - last), (0, LANES - part)))
        first = last
    return total.reshape(48, LANES)


def piece_choice():
    choice = np.zeros((8, 2, 24, 2, 4, 2, 24), np.float32)
    for place in range(8):
        for row in range(23):
            first, count = (12, 3) if 12 <= row < 15 else (18, 4) if 18 <= row < 22 else (row, 1)
            index = 8 * (row - first) + place
            shard, source = index // count, first + index % count
            for layer in range(2):
                choice[place, layer, row, shard % 2, shard // 2, layer, source] = 1.0
    return jnp.asarray(choice.reshape(8, 48, 384), BF16)


def pad_images(rows):
    return jnp.pad(rows.reshape(-1, LIVE, rows.shape[1]), ((0, 0), (0, IMG - LIVE), (0, 0))).reshape(-1, rows.shape[1])


def unpad_images(rows):
    lead = rows.shape[:-2]
    return rows.reshape(lead + (-1, IMG, W))[..., :LIVE, :].reshape(lead + (-1, W))


def spread_body(
    patches, region_mask, conv_weight, conv_bias, mixer_gain, mixer_shift, triple_weight, triple_bias, output_weight,
    output_bias, feed_gain, feed_shift, expand_weight, expand_bias, reduce_weight, reduce_bias, cotangent,
):
    s = lax.axis_index("segment")
    d = lax.axis_index("dp")
    pack = pack_small(conv_weight, conv_bias, mixer_gain, mixer_shift, triple_bias, output_bias, feed_gain, feed_shift, expand_bias, reduce_bias)
    own = patches.shape[0] // lax.axis_size("segment")
    mine = lambda v: lax.dynamic_slice_in_dim(v, s * own, own, 0)
    x = pad_images(mine(patches))
    cot = pad_images(cotangent).reshape(4, ROWS, W)
    gin = lax.dynamic_index_in_dim(cot, s, 0, keepdims=False)
    mask = pad_images(mine(region_mask).astype(BF16)[:, None])
    sec_out, grad_out, mix, exp, red, sg, xin = train_call(
        triple_weight, output_weight, expand_weight, reduce_weight, pack, piece_choice(), x, mask, gin, cot
    )
    sec_out = jnp.where(lax.rem(s, 2) == 0, xin, sec_out)
    place = lambda v: unpad_images(v.reshape(1, 4 * ROWS, W))
    part = W // lax.axis_size("dp")
    rows = lambda lo, hi: sg[:, lo:hi, :part].reshape(2, -1)
    wide = lambda v: v.astype(F32)
    return (
        place(sec_out), place(grad_out), sg[:, :9, :part], rows(9, 10), rows(10, 11), rows(11, 12), wide(mix[:, :, :3 * W]), rows(12, 15), wide(mix[:, :, 3 * W:]),
        rows(15, 16), rows(16, 17), rows(17, 18), wide(exp), rows(18, 22), wide(red), rows(22, 23),
    )


def solution(mesh):
    in_specs = (
        P("dp", None),
        P("dp"),
        P(None, None, "dp"),
        P(None, "dp"),
        P(None, "dp"),
        P(None, "dp"),
        P(None, "dp", None),
        P(None, "dp"),
        P(None, "dp", None),
        P(None, "dp"),
        P(None, "dp"),
        P(None, "dp"),
        P(None, "dp", None),
        P(None, "dp"),
        P(None, "dp", None),
        P(None, "dp"),
        P("dp", None),
    )
    out_specs = (
        P("segment", "dp", None),
        P("segment", "dp", None),
        P(None, None, "dp"),
        P(None, "dp"),
        P(None, "dp"),
        P(None, "dp"),
        P(None, "dp", None),
        P(None, "dp"),
        P(None, "dp", None),
        P(None, "dp"),
        P(None, "dp"),
        P(None, "dp"),
        P(None, "dp", None),
        P(None, "dp"),
        P(None, "dp", None),
        P(None, "dp"),
    )
    chosen = spread_body if mesh.shape["dp"] == 8 and mesh.shape["segment"] == 4 else body
    return jax.shard_map(chosen, mesh=mesh, in_specs=in_specs, out_specs=out_specs, check_vma=False)
```
